32 devices in a mesh: mem: 4 (over y, x), tok: 8 (over z, core).
Axes of the slice: x: 2, y: 2, z: 4, core: 2. Of those that a mesh axis runs over, the one named last changes fastest.
Arguments:
- ens_state: bfloat16 [16, 4096, 256], P('mem', 'tok'), may hold values from -8 to 8
- attn_gain: float32 [256], replicated, may hold values from 0.1 to 1.9
- ffn_gain: float32 [256], replicated, may hold values from 0.1 to 1.9
- w_query: bfloat16 [256, 256], replicated, may hold values from -2 to 2
- w_key: bfloat16 [256, 256], replicated, may hold values from -2 to 2
- w_value: bfloat16 [256, 256], replicated, may hold values from -0.375 to 0.375
- w_out: bfloat16 [256, 256], replicated, may hold values from -0.375 to 0.375
- w_gate: bfloat16 [256, 1024], replicated, may hold values from -0.375 to 0.375
- w_up: bfloat16 [256, 1024], replicated, may hold values from -0.375 to 0.375
- down_weight: bfloat16 [1024, 256], replicated, may hold values from -0.1875 to 0.1875
- head_window: int32 [4], replicated, may hold values from 32 to 256, as said below
- obs_token: int32 [32768], P('tok'), may hold values from 0 to 4095, as said below
- obs_channel: int32 [32768], P('tok'), may hold values from 0 to 255
- obs_value: float32 [32768], P('tok'), may hold values from -6 to 6
- obs_var: float32 [32768], P('tok'), may hold values from 1 to 16
Outputs:
- analysis: bfloat16 [16, 4096, 256], P('mem', 'tok')
The draws below stay inside these ranges and needn't reach their ends.
Inputs may be any that keep to these rules, and one draw needn't show every extreme that they name: `head_window`: one head's window is exactly 256. `obs_token`: sample o lies on a token of block o // 4096, that is between (o // 4096) * 512 and that plus 512 - 1; the first sample is on token 0 and the last on token 4095.
All inputs are finite; a program needn't handle non-finite values.
Results may differ from the reference program's by a relative error of at most 0.012.
Values may be sent and summed in bfloat16 or wider, within the bound.
No kernel may reach another device: no remote copies, remote signals or barrier semaphores. Data moves between devices by JAX's collectives and lax.ppermute only.
A program may use at most 128 MiB of HBM per device.

```python
import math
import jax
import jax.numpy as jnp
from jax import lax

FEATURE_COUNT = 256
FF = 1024
HEADS = 4
WIN = 256
MEM_DEV = 4
TOK_DEV = 512
OBS_DEV = 4096
NS_STEPS = 8
ENS = 16
SAMPLE_LENGTH = 4096
OBS = 32768


def shared_matrix(key):
    return jax.random.normal(jax.random.fold_in(key, 11), (FEATURE_COUNT, FEATURE_COUNT), jnp.float32)


def draw_w_query(key, part):
    common = shared_matrix(key)
    return jnp.clip(common / math.sqrt(FEATURE_COUNT), -2.0, 2.0).astype(jnp.bfloat16)


def draw_w_key(key, part):
    key = jax.random.fold_in(key, 6)
    fresh_noise = jax.random.normal(key, (FEATURE_COUNT, FEATURE_COUNT), jnp.float32)
    return jnp.clip(fresh_noise / math.sqrt(FEATURE_COUNT), -2.0, 2.0).astype(jnp.bfloat16)


def draw_ens_state(key, part):
    key = jax.random.fold_in(key, 21)
    key_common = jax.random.fold_in(key, 1)
    key_scale = jax.random.fold_in(key, 2)
    key_fresh = jax.random.fold_in(key, 3)
    key_mixing = jax.random.fold_in(key, 5)
    key_weight = jax.random.fold_in(key, 6)
    key_pattern = jax.random.fold_in(key, 7)
    common = jnp.clip(jax.random.normal(key_common, (SAMPLE_LENGTH, FEATURE_COUNT), jnp.float32), -4.0, 4.0)
    member_scale = jnp.exp(jax.random.uniform(key_scale, (ENS, 1, 1), jnp.float32, math.log(0.2), 0.0))
    mixing = jax.random.randint(key_mixing, (ENS, 16), -3, 4).astype(jnp.float32)
    pattern_weight = 0.5 + 0.5 * jax.random.randint(key_weight, (16,), 0, 2).astype(jnp.float32)
    patterns = jax.random.randint(key_pattern, (16, SAMPLE_LENGTH, FEATURE_COUNT), -7, 8).astype(jnp.float32)
    structured = jnp.einsum('kr,rtd->ktd', mixing * pattern_weight[None, :], patterns, precision=lax.Precision.HIGHEST) / 32.0
    fresh = jnp.clip(jax.random.normal(key_fresh, (ENS, SAMPLE_LENGTH, FEATURE_COUNT), jnp.float32), -4.0, 4.0)
    perturbation = structured + 0.3 * fresh
    return jnp.clip(common[None] + member_scale * perturbation, -8.0, 8.0).astype(jnp.bfloat16)


def draw_head_window(key, part):
    key = jax.random.fold_in(key, 31)
    key_width = jax.random.fold_in(key, 1)
    key_chosen = jax.random.fold_in(key, 2)
    widths = jax.random.randint(key_width, (HEADS,), WIN // 8, WIN + 1)
    chosen = jax.random.randint(key_chosen, (), 0, HEADS)
    return jnp.where(jnp.arange(HEADS) == chosen, WIN, widths).astype(jnp.int32)


def draw_obs_token(key, part):
    key = jax.random.fold_in(key, 41)
    position = jnp.arange(OBS, dtype=jnp.int32)
    block_start = position // OBS_DEV * TOK_DEV
    token_pos = block_start + jax.random.randint(key, (OBS,), 0, TOK_DEV)
    token_pos = jnp.where(position == 0, 0, token_pos)
    token_pos = jnp.where(position == OBS - 1, SAMPLE_LENGTH - 1, token_pos)
    return token_pos.astype(jnp.int32)


def plant(entries, own_key, least, largest):
    longest = entries.shape.index(max(entries.shape))
    spots = []
    for shift in (0, 1):
        where = [jax.random.randint(jax.random.fold_in(own_key, axis), (), 0, length) for axis, length in enumerate(entries.shape)]
        where[longest] = (where[longest] + shift) % entries.shape[longest]
        spots.append(tuple(where))
    return entries.at[spots[0]].set(least).at[spots[1]].set(largest)


def level_of(rng, shape, shards, least, high):
    loudness, own = 1.0, jax.random.fold_in(rng, 6)
    for axis_at, parts in shards:
        draws = jnp.exp(jax.random.uniform(jax.random.fold_in(own, axis_at), (parts,), jnp.float32, least / len(shards), high / len(shards)))
        loudness = loudness * jnp.repeat(draws, shape[axis_at] // parts).reshape([-1 if axis == axis_at else 1 for axis in range(len(shape))])
    return loudness


def noise(stream_key, extent, spread, most, cuts=(), kind=jnp.bfloat16):
    values = spread * jax.random.normal(stream_key, extent, jnp.float32)
    if cuts:
        values = values * level_of(stream_key, extent, cuts, -0.22, 0.18)
    return jnp.clip(values, -most, most).astype(kind)


def setup_inputs(seed: int = 0) -> dict:
    seeds = jax.random.split(jax.random.key(seed), 16)
    return {
        "ens_state": draw_ens_state(jax.random.fold_in(seeds[15], 71), 0),
        "attn_gain": jnp.clip(1.0 + 0.18 * jax.random.normal(seeds[1], (FEATURE_COUNT,), jnp.float32), 0.1, 1.9),
        "ffn_gain": jnp.clip(1.0 + 0.18 * jax.random.normal(seeds[2], (FEATURE_COUNT,), jnp.float32), 0.1, 1.9),
        "w_query": draw_w_query(jax.random.fold_in(seeds[15], 71), 0),
        "w_key": draw_w_key(jax.random.fold_in(seeds[15], 71), 0),
        "w_value": noise(seeds[5], (FEATURE_COUNT, FEATURE_COUNT), FEATURE_COUNT ** -0.5, 0.375),
        "w_out": noise(seeds[6], (FEATURE_COUNT, FEATURE_COUNT), FEATURE_COUNT ** -0.5, 0.375),
        "w_gate": noise(seeds[7], (FEATURE_COUNT, FF), FEATURE_COUNT ** -0.5, 0.375),
        "w_up": noise(seeds[8], (FEATURE_COUNT, FF), FEATURE_COUNT ** -0.5, 0.375),
        "down_weight": noise(seeds[9], (FF, FEATURE_COUNT), FF ** -0.5, 0.1875),
        "head_window": draw_head_window(jax.random.fold_in(seeds[15], 71), 0),
        "obs_token": draw_obs_token(jax.random.fold_in(seeds[15], 71), 0),
        "obs_channel": plant(jax.random.randint(seeds[12], (OBS,), 0, FEATURE_COUNT), jax.random.fold_in(seeds[12], 1), 0, FEATURE_COUNT - 1).astype(jnp.int32),
        "obs_value": noise(seeds[13], (OBS,), 1.0, 6.0, ((0, 8),), jnp.float32),
        "obs_var": jnp.clip(jnp.exp(math.log(16.0) - 2.7725887 * jax.random.uniform(seeds[14], (OBS,), jnp.float32) ** level_of(seeds[14], (OBS,), ((0, 8),), -0.2, 0.2)), 1.0, 16.0),
    }


EPS = 1e-05

def rounded(values):
    return lax.optimization_barrier(values.astype(jnp.bfloat16))

def rms_scaled(values, gain):
    return values * lax.rsqrt(lax.optimization_barrier(jnp.mean(values * values, axis=-1, keepdims=True)) + EPS) * gain

def attend(queries, key_rows, value_rows, head_window, first_pos, total_len, reach):
    groups, row_count, feat_width = queries.shape
    head_count = head_window.shape[0]
    head_size = feat_width // head_count
    block_rows = min(512, row_count)
    key_count = block_rows + 2 * reach
    logit_scale = 1.0 / math.sqrt(head_size)

    def one_block(block_index):
        block_start = block_index * block_rows
        query_block = lax.dynamic_slice_in_dim(queries, block_start, block_rows, 1).astype(jnp.float32)
        key_block = lax.dynamic_slice_in_dim(key_rows, block_start, key_count, 1).astype(jnp.float32)
        value_block = lax.dynamic_slice_in_dim(value_rows, block_start, key_count, 1).astype(jnp.float32)
        q_pos = first_pos + block_start + jnp.arange(block_rows, dtype=jnp.int32)
        k_pos = first_pos - reach + block_start + jnp.arange(key_count, dtype=jnp.int32)
        apart = jnp.abs(q_pos[:, None] - k_pos[None, :])
        inside = (k_pos >= 0) & (k_pos < total_len)
        head_outputs = []
        for head in range(head_count):
            lower_column = head * head_size
            upper_column = lower_column + head_size
            score_matrix = jnp.einsum('alx,adx->ald', query_block[:, :, lower_column:upper_column], key_block[:, :, lower_column:upper_column]) * logit_scale
            allowed = (apart <= head_window[head]) & inside[None, :]
            score_matrix = jnp.where(allowed[None], score_matrix, -1e+30)
            row_top = lax.optimization_barrier(jnp.max(score_matrix, axis=-1, keepdims=True))
            expo = jnp.exp(score_matrix - row_top)
            row_total = lax.optimization_barrier(jnp.sum(expo, axis=-1, keepdims=True))
            softmax_weights = rounded(expo / row_total).astype(jnp.float32)
            head_outputs.append(jnp.einsum('pol,plj->poj', softmax_weights, value_block[:, :, lower_column:upper_column]))
        return jnp.concatenate(head_outputs, axis=-1).astype(jnp.bfloat16)
    pieces = lax.map(one_block, jnp.arange(row_count // block_rows, dtype=jnp.int32))
    return jnp.moveaxis(pieces, 0, 1).reshape(groups, row_count, feat_width)

def apply_projection(values, matrix):
    return jnp.einsum('gsd,de->gse', values.astype(jnp.float32), matrix.astype(jnp.float32))

def forward(group_state, attn_gain, ffn_gain, w_query, w_key, w_value, w_out, w_gate, w_up, down_weight, head_window):
    normed_in = rounded(rms_scaled(group_state.astype(jnp.float32), attn_gain))
    queries = rounded(apply_projection(normed_in, w_query))
    key_rows = rounded(apply_projection(normed_in, w_key))
    value_rows = rounded(apply_projection(normed_in, w_value))
    pad_shape = ((0, 0), (WIN, WIN), (0, 0))
    mixed_heads = attend(queries, jnp.pad(key_rows, pad_shape), jnp.pad(value_rows, pad_shape), head_window, 0, SAMPLE_LENGTH, WIN)
    after_attention_state = rounded(group_state.astype(jnp.float32) + apply_projection(mixed_heads, w_out))
    normed_mid = rounded(rms_scaled(after_attention_state.astype(jnp.float32), ffn_gain))
    hidden_neurons = rounded(jax.nn.silu(apply_projection(normed_mid, w_gate)) * apply_projection(normed_mid, w_up))
    return rounded(after_attention_state.astype(jnp.float32) + apply_projection(hidden_neurons, down_weight))

def ensemble_transform(gram, proj):
    ensemble_fields = gram.shape[0]
    identity = jnp.eye(ensemble_fields, dtype=jnp.float32)
    mean_mat = jnp.full((ensemble_fields, ensemble_fields), 1.0 / ensemble_fields, dtype=jnp.float32)
    system = gram + (ensemble_fields - 1.0) * identity
    factor = jnp.linalg.cholesky(system)
    mean_weights = jax.scipy.linalg.cho_solve((factor, True), proj)
    mean_level = jnp.trace(system) / ensemble_fields
    lifted = system + (mean_level - (ensemble_fields - 1.0)) * mean_mat
    frobenius = jnp.sqrt(jnp.sum(lifted * lifted))
    root_iter = lifted / frobenius
    inv_iter = identity
    for sweep in range(NS_STEPS):
        correction = 1.5 * identity - 0.5 * jnp.dot(inv_iter, root_iter, precision=lax.Precision.HIGHEST)
        root_iter = jnp.dot(root_iter, correction, precision=lax.Precision.HIGHEST)
        inv_iter = jnp.dot(correction, inv_iter, precision=lax.Precision.HIGHEST)
    inv_root = inv_iter / jnp.sqrt(frobenius) + (1.0 / math.sqrt(ensemble_fields - 1.0) - 1.0 / jnp.sqrt(mean_level)) * mean_mat
    spread_part = math.sqrt(ensemble_fields - 1.0) * inv_root
    return mean_mat + jnp.dot(identity - mean_mat, mean_weights[:, None] + spread_part, precision=lax.Precision.HIGHEST)

def reference(ens_state, attn_gain, ffn_gain, w_query, w_key, w_value, w_out, w_gate, w_up, down_weight, head_window, obs_token, obs_channel, obs_value, obs_var):
    ensemble_fields = ens_state.shape[0]
    gathered_lines = ens_state.reshape(ensemble_fields // MEM_DEV, MEM_DEV, SAMPLE_LENGTH, FEATURE_COUNT)

    def worker_team(group_state):
        return forward(group_state, attn_gain, ffn_gain, w_query, w_key, w_value, w_out, w_gate, w_up, down_weight, head_window)
    prior_field = lax.map(worker_team, gathered_lines).reshape(ensemble_fields, SAMPLE_LENGTH, FEATURE_COUNT)
    serial_position = (obs_token * FEATURE_COUNT + obs_channel).astype(jnp.int32)
    measurement_vector = prior_field.reshape(ensemble_fields, -1)[:, serial_position].astype(jnp.float32)
    seen_mean = lax.optimization_barrier(jnp.mean(measurement_vector, axis=0))
    inv_err = lax.rsqrt(obs_var)
    scaled = (measurement_vector - seen_mean[None, :]) * inv_err[None, :]
    innovation = (obs_value - seen_mean) * inv_err
    gram = jnp.dot(scaled, scaled.T, precision=lax.Precision.HIGHEST)
    proj = jnp.dot(scaled, innovation, precision=lax.Precision.HIGHEST)
    analysis_operator = ensemble_transform(gram, proj)
    mixed_result = jnp.einsum('ts,tnm->snm', analysis_operator, prior_field.astype(jnp.float32), precision=lax.Precision.HIGHEST)
    return mixed_result.astype(jnp.bfloat16)
```

```python
import math

import jax
import jax.numpy as jnp
from jax import lax
from jax.experimental import pallas as pl
from jax.experimental.pallas import tpu as pltpu
from jax.sharding import PartitionSpec as P

WIN = 256
NS_STEPS = 8
EPS = 1e-05
Q_ROWS = 128
GROUP = 16
LANES = 128
VMEM_LIMIT = 50 * 1024 * 1024

F32 = jnp.float32
BF16 = jnp.bfloat16


def dot(a, b, contract=((1,), (0,)), precision=None):
    return lax.dot_general(a, b, (contract, ((), ())), precision=precision, preferred_element_type=F32)


def exact_dot(a, b, contract=((1,), (0,))):
    return dot(a, b, contract, lax.Precision.HIGHEST)


def iota(shape, axis):
    return lax.broadcasted_iota(jnp.int32, shape, axis)


def halves(values):
    high = values.astype(BF16)
    return high, (values - high.astype(F32)).astype(BF16)


def rms_scaled(values, gain):
    return values * lax.rsqrt(jnp.mean(values * values, axis=-1, keepdims=True) + EPS) * gain


def vmem_spec():
    return pl.BlockSpec(memory_space=pltpu.VMEM)


def smem_spec():
    return pl.BlockSpec(memory_space=pltpu.SMEM)


def sample_grid_kernel(start_ref, token_ref, channel_ref, value_ref, var_ref, out_ref):
    rows, feat_width = out_ref.shape[1:]
    count = token_ref.shape[1]
    chunk = min(1024, count)
    total = jnp.zeros((4 * rows, feat_width), F32)
    for lower in range(0, count, chunk):
        part = slice(lower, lower + chunk)
        inv_var = 1.0 / var_ref[:, part]
        weighted = value_ref[:, part] * inv_var
        here = iota((rows, chunk), 0) == token_ref[:, part] - start_ref[0]
        pieces = []
        for row in (inv_var, weighted):
            high = row.astype(BF16).astype(F32)
            pieces.append(jnp.where(here, high, 0.0).astype(BF16))
            pieces.append(jnp.where(here, row - high, 0.0).astype(BF16))
        channel_hot = jnp.where(iota((feat_width, chunk), 0) == channel_ref[:, part], 1.0, 0.0).astype(BF16)
        total += dot(jnp.concatenate(pieces, axis=0), channel_hot, ((1,), (1,)))
    out_ref[0] = total[:rows] + total[rows : 2 * rows]
    out_ref[1] = total[2 * rows : 3 * rows] + total[3 * rows :]


def sample_grid(start, obs_token, obs_channel, obs_value, obs_var, rows, feat_width):
    count = obs_token.shape[0]
    return pl.pallas_call(
        sample_grid_kernel,
        out_shape=jax.ShapeDtypeStruct((2, rows, feat_width), F32),
        in_specs=[smem_spec()] + [vmem_spec()] * 4,
        out_specs=vmem_spec(),
        compiler_params=pltpu.CompilerParams(vmem_limit_bytes=VMEM_LIMIT),
        cost_estimate=pl.CostEstimate(flops=8 * rows * count * feat_width, bytes_accessed=16 * count, transcendentals=0),
        name="sample_grid",
    )(start, *(v.reshape(1, count) for v in (obs_token, obs_channel, obs_value, obs_var)))


def forward_kernel(
    place_ref,
    window_ref,
    own_ref,
    left_ref,
    right_ref,
    attn_gain_ref,
    ffn_gain_ref,
    w_query_ref,
    w_key_ref,
    w_value_ref,
    w_out_ref,
    w_gate_ref,
    w_up_ref,
    down_weight_ref,
    out_ref,
    query_buf,
    key_buf,
    value_buf,
    apart_buf,
    mixed_buf,
):
    row_count, feat_width = own_ref.shape[1:]
    reach = left_ref.shape[1]
    head_count = window_ref.shape[0]
    head_size = feat_width // head_count
    blocks = row_count // Q_ROWS
    key_count = Q_ROWS + 2 * reach

    @pl.when(pl.program_id(0) == 0)
    def _():
        rel = jnp.abs(iota((Q_ROWS, key_count), 1) - reach - iota((Q_ROWS, key_count), 0))
        for block in range(blocks):
            k_pos = place_ref[0] - reach + block * Q_ROWS + iota((Q_ROWS, key_count), 1)
            inside = (k_pos >= 0) & (k_pos < place_ref[1])
            apart_buf[block] = jnp.where(inside, rel, 1 << 20)

    attn_gain = attn_gain_ref[...]
    for source, lower, rows in ((left_ref, 0, reach), (own_ref, reach, row_count), (right_ref, reach + row_count, reach)):
        normed = rms_scaled(source[0].astype(F32), attn_gain).astype(BF16)
        key_buf[lower : lower + rows] = dot(normed, w_key_ref[...]).astype(BF16)
        value_buf[lower : lower + rows] = dot(normed, w_value_ref[...]).astype(BF16)
        if source is own_ref:
            queries = dot(normed, w_query_ref[...]).astype(BF16)
            query_buf[...] = queries * jnp.asarray(1.0 / math.sqrt(head_size), BF16)

    column_head = iota((1, feat_width), 1) // head_size

    def one_block(block, carry):
        start = pl.multiple_of(block * Q_ROWS, Q_ROWS)
        queries = query_buf[pl.ds(start, Q_ROWS), :]
        stacked = jnp.concatenate(
            [queries * (column_head == head).astype(F32).astype(BF16) for head in range(head_count)], axis=0
        )
        scores = dot(stacked, key_buf[pl.ds(start, key_count), :], ((1,), (1,)))
        apart = apart_buf[block]
        weights, scales = [], []
        for head in range(head_count):
            score_matrix = scores[head * Q_ROWS : (head + 1) * Q_ROWS]
            score_matrix = jnp.where(apart <= window_ref[head], score_matrix, -1e30)
            expo = jnp.exp(score_matrix - jnp.max(score_matrix, axis=-1, keepdims=True))
            scales.append(1.0 / jnp.sum(expo, axis=-1, keepdims=True))
            weights.append(expo.astype(BF16))
        mixed_all = dot(jnp.concatenate(weights, axis=0), value_buf[pl.ds(start, key_count), :])
        mixed = jnp.zeros((Q_ROWS, feat_width), F32)
        for head in range(head_count):
            mixed = jnp.where(column_head == head, mixed_all[head * Q_ROWS : (head + 1) * Q_ROWS] * scales[head], mixed)
        mixed_buf[pl.ds(start, Q_ROWS), :] = mixed.astype(BF16)
        return carry

    lax.fori_loop(0, blocks, one_block, 0)

    after = (own_ref[0].astype(F32) + dot(mixed_buf[...], w_out_ref[...])).astype(BF16)
    normed_mid = rms_scaled(after.astype(F32), ffn_gain_ref[...]).astype(BF16)
    gate = dot(normed_mid, w_gate_ref[...])
    hidden = (gate * (0.5 + 0.5 * jnp.tanh(0.5 * gate)) * dot(normed_mid, w_up_ref[...])).astype(BF16)
    forecast = (after.astype(F32) + dot(hidden, down_weight_ref[...])).astype(BF16)
    shares, _, share_rows, _ = out_ref.shape
    for share in range(shares):
        out_ref[share, 0] = forecast[share * share_rows : (share + 1) * share_rows]


def forward(place, head_window, own, left, right, gains, weights, shares):
    members, row_count, feat_width = own.shape
    reach = left.shape[1]
    key_count = Q_ROWS + 2 * reach
    hidden_width = weights[4].shape[1]
    macs = members * row_count * feat_width * (6 * feat_width + 3 * hidden_width + 8 * key_count)
    return pl.pallas_call(
        forward_kernel,
        grid=(members,),
        out_shape=jax.ShapeDtypeStruct((shares, members, row_count // shares, feat_width), BF16),
        in_specs=[
            smem_spec(),
            smem_spec(),
            pl.BlockSpec((1, row_count, feat_width), lambda m: (m, 0, 0)),
            pl.BlockSpec((1, reach, feat_width), lambda m: (m, 0, 0)),
            pl.BlockSpec((1, reach, feat_width), lambda m: (m, 0, 0)),
        ]
        + [vmem_spec()] * (len(gains) + len(weights)),
        out_specs=pl.BlockSpec((shares, 1, row_count // shares, feat_width), lambda m: (0, m, 0, 0)),
        scratch_shapes=[
            pltpu.VMEM((row_count, feat_width), BF16),
            pltpu.VMEM((row_count + 2 * reach, feat_width), BF16),
            pltpu.VMEM((row_count + 2 * reach, feat_width), BF16),
            pltpu.VMEM((row_count // Q_ROWS, Q_ROWS, key_count), jnp.int32),
            pltpu.VMEM((row_count, feat_width), BF16),
        ],
        compiler_params=pltpu.CompilerParams(vmem_limit_bytes=VMEM_LIMIT),
        cost_estimate=pl.CostEstimate(flops=2 * macs, bytes_accessed=5 * own.size, transcendentals=0),
        name="forward",
    )(place, head_window, own, left, right, *gains, *weights)


def gram_kernel(share_ref, grid_ref, out_ref):
    members, rows, feat_width = share_ref.shape
    stack = members * GROUP
    total = jnp.zeros((stack, stack), F32)
    proj = jnp.zeros((members, GROUP, feat_width), F32)
    for lower in range(0, rows, GROUP):
        part = slice(lower, lower + GROUP)
        fields = share_ref[:, part, :].astype(F32)
        mean = jnp.sum(fields, axis=0) * (1.0 / members)
        spread = fields - mean[None]
        weight = grid_ref[0, part, :]
        proj += spread * (grid_ref[1, part, :] - weight * mean)[None]
        high, low = halves(spread.reshape(stack, feat_width))
        w_high, w_low = halves((spread * weight[None]).reshape(stack, feat_width))
        last = ((1,), (1,))
        total += dot(w_high, high, last) + dot(w_high, low, last) + dot(w_low, high, last)
    same = iota((stack, stack), 0) % GROUP == iota((stack, stack), 1) % GROUP
    by_row = jnp.sum(jnp.where(same, total, 0.0).reshape(members, GROUP, stack), axis=1)
    folded = (iota((stack, LANES), 0) // GROUP == iota((stack, LANES), 1) % members).astype(F32)
    tiled = exact_dot(by_row, folded)
    per_row = LANES // members
    keep = iota((members, LANES), 0) % per_row == iota((members, LANES), 1) // members
    packed = jnp.sum(jnp.where(keep, tiled, 0.0).reshape(members // per_row, per_row, LANES), axis=1)
    proj_col = jnp.sum(jnp.sum(proj, axis=1), axis=1, keepdims=True)
    proj_row = jnp.sum(
        jnp.where(iota((members, LANES), 0) == iota((members, LANES), 1), proj_col, 0.0), axis=0, keepdims=True
    )
    filled = members // per_row + 1
    blank = jnp.zeros((out_ref.shape[0] - filled, LANES), F32)
    out_ref[...] = jnp.concatenate([packed, proj_row, blank], axis=0)


def gram_partial(share, grid):
    members = share.shape[0]
    filled = members * members // LANES + 1
    return pl.pallas_call(
        gram_kernel,
        out_shape=jax.ShapeDtypeStruct((-(-filled // 8) * 8, LANES), F32),
        in_specs=[vmem_spec()] * 2,
        out_specs=vmem_spec(),
        compiler_params=pltpu.CompilerParams(vmem_limit_bytes=VMEM_LIMIT),
        cost_estimate=pl.CostEstimate(
            flops=6 * GROUP * members * share.size, bytes_accessed=2 * share.size, transcendentals=0
        ),
        name="gram",
    )(share, grid)


def ensemble_transform(gram, proj):
    members = gram.shape[0]
    row, column = iota((members, members), 0), iota((members, members), 1)
    identity = (row == column).astype(F32)
    system = gram + (members - 1.0) * identity
    left, right = system, proj
    for pivot in range(members):
        is_pivot = iota((members, 1), 0) == pivot
        scale = 1.0 / left[pivot : pivot + 1, pivot : pivot + 1]
        pivot_row = left[pivot : pivot + 1, :] * scale
        pivot_right = right[pivot : pivot + 1, :] * scale
        factor = left[:, pivot : pivot + 1]
        left = jnp.where(is_pivot, pivot_row, left - factor * pivot_row)
        right = jnp.where(is_pivot, pivot_right, right - factor * pivot_right)
    mean_weights = right
    mean_level = jnp.sum(jnp.sum(system * identity, axis=1, keepdims=True), axis=0, keepdims=True) / members
    lifted = system + (mean_level - (members - 1.0)) * (1.0 / members)
    frobenius = jnp.sqrt(jnp.sum(jnp.sum(lifted * lifted, axis=1, keepdims=True), axis=0, keepdims=True))
    root_iter = lifted / frobenius
    inv_iter = identity
    for sweep in range(NS_STEPS):
        product = root_iter if sweep == 0 else exact_dot(inv_iter, root_iter)
        correction = 1.5 * identity - 0.5 * product
        inv_iter = correction if sweep == 0 else exact_dot(correction, inv_iter)
        if sweep < NS_STEPS - 1:
            root_iter = exact_dot(root_iter, correction)
    inv_root = inv_iter / jnp.sqrt(frobenius) + (1.0 / math.sqrt(members - 1.0) - 1.0 / jnp.sqrt(mean_level)) * (
        1.0 / members
    )
    moved = mean_weights + math.sqrt(members - 1.0) * inv_root
    return 1.0 / members + moved - jnp.sum(moved, axis=0, keepdims=True) * (1.0 / members)


def combine_kernel(partial_ref, share_ref, out_ref):
    members, rows, feat_width = share_ref.shape
    stack = members * GROUP
    per_row = LANES // members
    sums = jnp.sum(partial_ref[...], axis=0)
    spread_rows = jnp.concatenate(
        [jnp.broadcast_to(sums[r : r + 1], (per_row, LANES)) for r in range(members // per_row)], axis=0
    )
    keep = iota((members, LANES), 0) % per_row == iota((members, LANES), 1) // members
    folded = (iota((LANES, members), 0) % members == iota((LANES, members), 1)).astype(F32)
    gram = exact_dot(jnp.where(keep, spread_rows, 0.0), folded)
    proj_row = jnp.broadcast_to(sums[members // per_row : members // per_row + 1], (members, LANES))
    on_diagonal = iota((members, LANES), 0) == iota((members, LANES), 1)
    proj = jnp.sum(jnp.where(on_diagonal, proj_row, 0.0), axis=1, keepdims=True)
    transform = ensemble_transform(gram, proj)
    pick = (iota((stack, members), 0) // GROUP == iota((stack, members), 1)).astype(F32).astype(BF16)
    same = iota((stack, stack), 0) % GROUP == iota((stack, stack), 1) % GROUP
    mixers = []
    for piece in halves(transform):
        rows_of = dot(pick, piece, ((1,), (1,))).astype(BF16)
        mixers.append(jnp.where(same, dot(rows_of, pick, ((1,), (1,))), 0.0).astype(BF16))
    for lower in range(0, rows, GROUP):
        fields = share_ref[:, lower : lower + GROUP, :].reshape(stack, feat_width)
        mixed = dot(mixers[0], fields) + dot(mixers[1], fields)
        out_ref[:, lower : lower + GROUP, :] = mixed.astype(BF16).reshape(members, GROUP, feat_width)


def combine(partials, share):
    members = share.shape[0]
    return pl.pallas_call(
        combine_kernel,
        out_shape=jax.ShapeDtypeStruct(share.shape, BF16),
        in_specs=[vmem_spec()] * 2,
        out_specs=vmem_spec(),
        compiler_params=pltpu.CompilerParams(vmem_limit_bytes=VMEM_LIMIT),
        cost_estimate=pl.CostEstimate(
            flops=4 * GROUP * members * share.size, bytes_accessed=4 * share.size, transcendentals=0
        ),
        name="combine",
    )(partials, share)


def local(
    ens_state,
    attn_gain,
    ffn_gain,
    w_query,
    w_key,
    w_value,
    w_out,
    w_gate,
    w_up,
    down_weight,
    head_window,
    obs_token,
    obs_channel,
    obs_value,
    obs_var,
):
    own_members, row_count, feat_width = ens_state.shape
    mem_count = lax.axis_size("mem")
    tok_count = lax.axis_size("tok")
    device_count = mem_count * tok_count
    members = own_members * mem_count
    share_rows = row_count // mem_count
    first_pos = lax.axis_index("tok") * row_count
    up = [(i, i + 1) for i in range(tok_count - 1)]
    down = [(i + 1, i) for i in range(tok_count - 1)]
    left = lax.ppermute(ens_state[:, row_count - WIN :], "tok", up)
    right = lax.ppermute(ens_state[:, :WIN], "tok", down)
    share_start = first_pos + lax.axis_index("mem") * share_rows
    grid = sample_grid(
        share_start.astype(jnp.int32).reshape(1), obs_token, obs_channel, obs_value, obs_var, share_rows, feat_width
    )
    place = jnp.stack([first_pos, row_count * tok_count]).astype(jnp.int32)
    forecast = forward(
        place,
        head_window,
        ens_state,
        left,
        right,
        [attn_gain.reshape(1, -1), ffn_gain.reshape(1, -1)],
        [w_query, w_key, w_value, w_out, w_gate, w_up, down_weight],
        mem_count,
    )
    share = lax.all_to_all(forecast, "mem", split_axis=0, concat_axis=0, tiled=True)
    share = share.reshape(members, share_rows, feat_width)
    partial = gram_partial(share, grid)
    partials = lax.all_to_all(
        jnp.broadcast_to(partial[None], (device_count, *partial.shape)),
        ("mem", "tok"),
        split_axis=0,
        concat_axis=0,
        tiled=True,
    )
    mixed = combine(partials, share).reshape(mem_count, own_members, share_rows, feat_width)
    mixed = lax.all_to_all(mixed, "mem", split_axis=0, concat_axis=0, tiled=True)
    return jnp.moveaxis(mixed, 0, 1).reshape(own_members, row_count, feat_width)


def solution(mesh):
    in_specs = (P("mem", "tok", None), *[P()] * 10, *[P("tok")] * 4)
    return jax.shard_map(local, mesh=mesh, in_specs=in_specs, out_specs=P("mem", "tok", None), check_vma=False)
```

```python
import math

import jax
import jax.numpy as jnp
from jax import lax
from jax.experimental import pallas as pl
from jax.experimental.pallas import tpu as pltpu
from jax.sharding import PartitionSpec as P

WIN = 256
NS_STEPS = 8
EPS = 1e-05
Q_ROWS = 128
GROUP = 16
LANES = 128
VMEM_LIMIT = 50 * 1024 * 1024

F32 = jnp.float32
BF16 = jnp.bfloat16


def dot(a, b, contract=((1,), (0,)), precision=None):
    return lax.dot_general(a, b, (contract, ((), ())), precision=precision, preferred_element_type=F32)


def exact_dot(a, b, contract=((1,), (0,))):
    return dot(a, b, contract, lax.Precision.HIGHEST)


def iota(shape, axis):
    return lax.broadcasted_iota(jnp.int32, shape, axis)


def halves(values):
    high = values.astype(BF16)
    return high, (values - high.astype(F32)).astype(BF16)


def rms_scaled(values, gain):
    return values * lax.rsqrt(jnp.mean(values * values, axis=-1, keepdims=True) + EPS) * gain


def vmem_spec():
    return pl.BlockSpec(memory_space=pltpu.VMEM)


def smem_spec():
    return pl.BlockSpec(memory_space=pltpu.SMEM)


def sample_grid_kernel(start_ref, token_ref, channel_ref, value_ref, var_ref, out_ref):
    rows, feat_width = out_ref.shape[1:]
    count = token_ref.shape[1]
    chunk = min(1024, count)
    total = jnp.zeros((4 * rows, feat_width), F32)
    for lower in range(0, count, chunk):
        part = slice(lower, lower + chunk)
        inv_var = 1.0 / var_ref[:, part]
        weighted = value_ref[:, part] * inv_var
        here = iota((rows, chunk), 0) == token_ref[:, part] - start_ref[0]
        pieces = []
        for row in (inv_var, weighted):
            high = row.astype(BF16).astype(F32)
            pieces.append(jnp.where(here, high, 0.0).astype(BF16))
            pieces.append(jnp.where(here, row - high, 0.0).astype(BF16))
        channel_hot = jnp.where(iota((feat_width, chunk), 0) == channel_ref[:, part], 1.0, 0.0).astype(BF16)
        total += dot(jnp.concatenate(pieces, axis=0), channel_hot, ((1,), (1,)))
    out_ref[0] = total[:rows] + total[rows : 2 * rows]
    out_ref[1] = total[2 * rows : 3 * rows] + total[3 * rows :]


def sample_grid(start, obs_token, obs_channel, obs_value, obs_var, rows, feat_width):
    count = obs_token.shape[0]
    return pl.pallas_call(
        sample_grid_kernel,
        out_shape=jax.ShapeDtypeStruct((2, rows, feat_width), F32),
        in_specs=[smem_spec()] + [vmem_spec()] * 4,
        out_specs=vmem_spec(),
        compiler_params=pltpu.CompilerParams(vmem_limit_bytes=VMEM_LIMIT),
        cost_estimate=pl.CostEstimate(flops=8 * rows * count * feat_width, bytes_accessed=16 * count, transcendentals=0),
        name="sample_grid",
    )(start, *(v.reshape(1, count) for v in (obs_token, obs_channel, obs_value, obs_var)))


def forward_kernel(
    place_ref,
    window_ref,
    own_ref,
    left_ref,
    right_ref,
    attn_gain_ref,
    ffn_gain_ref,
    w_query_ref,
    w_key_ref,
    w_value_ref,
    w_out_ref,
    w_gate_ref,
    w_up_ref,
    down_weight_ref,
    out_ref,
    query_buf,
    key_buf,
    value_buf,
    apart_buf,
    mixed_buf,
):
    row_count, feat_width = own_ref.shape[1:]
    reach = left_ref.shape[1]
    head_count = window_ref.shape[0]
    head_size = feat_width // head_count
    blocks = row_count // Q_ROWS
    key_count = Q_ROWS + 2 * reach

    @pl.when(pl.program_id(0) == 0)
    def _():
        rel = jnp.abs(iota((Q_ROWS, key_count), 1) - reach - iota((Q_ROWS, key_count), 0))
        for block in range(blocks):
            k_pos = place_ref[0] - reach + block * Q_ROWS + iota((Q_ROWS, key_count), 1)
            inside = (k_pos >= 0) & (k_pos < place_ref[1])
            apart_buf[block] = jnp.where(inside, rel, 1 << 20)

    attn_gain = attn_gain_ref[...]
    for source, lower, rows in ((left_ref, 0, reach), (own_ref, reach, row_count), (right_ref, reach + row_count, reach)):
        normed = rms_scaled(source[0].astype(F32), attn_gain).astype(BF16)
        key_buf[lower : lower + rows] = dot(normed, w_key_ref[...]).astype(BF16)
        value_buf[lower : lower + rows] = dot(normed, w_value_ref[...]).astype(BF16)
        if source is own_ref:
            queries = dot(normed, w_query_ref[...]).astype(BF16)
            query_buf[...] = queries * jnp.asarray(1.0 / math.sqrt(head_size), BF16)

    column_head = iota((1, feat_width), 1) // head_size

    def one_block(block, carry):
        start = pl.multiple_of(block * Q_ROWS, Q_ROWS)
        queries = query_buf[pl.ds(start, Q_ROWS), :]
        stacked = jnp.concatenate(
            [queries * (column_head == head).astype(F32).astype(BF16) for head in range(head_count)], axis=0
        )
        scores = dot(stacked, key_buf[pl.ds(start, key_count), :], ((1,), (1,)))
        apart = apart_buf[block]
        weights, scales = [], []
        for head in range(head_count):
            score_matrix = scores[head * Q_ROWS : (head + 1) * Q_ROWS]
            score_matrix = jnp.where(apart <= window_ref[head], score_matrix, -1e30)
            expo = jnp.exp(score_matrix - jnp.max(score_matrix, axis=-1, keepdims=True))
            scales.append(1.0 / jnp.sum(expo, axis=-1, keepdims=True))
            weights.append(expo.astype(BF16))
        mixed_all = dot(jnp.concatenate(weights, axis=0), value_buf[pl.ds(start, key_count), :])
        mixed = jnp.zeros((Q_ROWS, feat_width), F32)
        for head in range(head_count):
            mixed = jnp.where(column_head == head, mixed_all[head * Q_ROWS : (head + 1) * Q_ROWS] * scales[head], mixed)
        mixed_buf[pl.ds(start, Q_ROWS), :] = mixed.astype(BF16)
        return carry

    lax.fori_loop(0, blocks, one_block, 0)

    after = (own_ref[0].astype(F32) + dot(mixed_buf[...], w_out_ref[...])).astype(BF16)
    normed_mid = rms_scaled(after.astype(F32), ffn_gain_ref[...]).astype(BF16)
    gate = dot(normed_mid, w_gate_ref[...])
    hidden = (gate * (0.5 + 0.5 * jnp.tanh(0.5 * gate)) * dot(normed_mid, w_up_ref[...])).astype(BF16)
    forecast = (after.astype(F32) + dot(hidden, down_weight_ref[...])).astype(BF16)
    shares, _, share_rows, _ = out_ref.shape
    for share in range(shares):
        out_ref[share, 0] = forecast[share * share_rows : (share + 1) * share_rows]


def forward(place, head_window, own, left, right, gains, weights, shares, first, members):
    _, row_count, feat_width = own.shape
    reach = left.shape[1]
    key_count = Q_ROWS + 2 * reach
    hidden_width = weights[4].shape[1]
    macs = members * row_count * feat_width * (6 * feat_width + 3 * hidden_width + 8 * key_count)
    return pl.pallas_call(
        forward_kernel,
        grid=(members,),
        out_shape=jax.ShapeDtypeStruct((shares, members, row_count // shares, feat_width), BF16),
        in_specs=[
            smem_spec(),
            smem_spec(),
            pl.BlockSpec((1, row_count, feat_width), lambda m: (first + m, 0, 0)),
            pl.BlockSpec((1, reach, feat_width), lambda m: (first + m, 0, 0)),
            pl.BlockSpec((1, reach, feat_width), lambda m: (first + m, 0, 0)),
        ]
        + [vmem_spec()] * (len(gains) + len(weights)),
        out_specs=pl.BlockSpec((shares, 1, row_count // shares, feat_width), lambda m: (0, m, 0, 0)),
        scratch_shapes=[
            pltpu.VMEM((row_count, feat_width), BF16),
            pltpu.VMEM((row_count + 2 * reach, feat_width), BF16),
            pltpu.VMEM((row_count + 2 * reach, feat_width), BF16),
            pltpu.VMEM((row_count // Q_ROWS, Q_ROWS, key_count), jnp.int32),
            pltpu.VMEM((row_count, feat_width), BF16),
        ],
        compiler_params=pltpu.CompilerParams(vmem_limit_bytes=VMEM_LIMIT),
        cost_estimate=pl.CostEstimate(flops=2 * macs, bytes_accessed=6 * members * row_count * feat_width, transcendentals=0),
        name="forward",
    )(place, head_window, own, left, right, *gains, *weights)


def gram_kernel(index_ref, *refs):
    share_refs, grid_ref, out_ref = refs[:-2], refs[-2], refs[-1]
    rows, feat_width = grid_ref.shape[1:]
    members = sum(math.prod(ref.shape[:-2]) for ref in share_refs)
    stack = members * GROUP
    total = jnp.zeros((stack, stack), F32)
    proj = jnp.zeros((members, GROUP, feat_width), F32)
    for lower in range(0, rows, GROUP):
        part = slice(lower, lower + GROUP)
        fields = jnp.concatenate(
            [ref[..., part, :].reshape(-1, GROUP, feat_width).astype(F32) for ref in share_refs], axis=0
        )
        mean = jnp.sum(fields, axis=0) * (1.0 / members)
        spread = fields - mean[None]
        weight = grid_ref[0, part, :]
        proj += spread * (grid_ref[1, part, :] - weight * mean)[None]
        high, low = halves(spread.reshape(stack, feat_width))
        w_high, w_low = halves((spread * weight[None]).reshape(stack, feat_width))
        last = ((1,), (1,))
        total += dot(w_high, high, last) + dot(w_high, low, last) + dot(w_low, high, last)
    same = iota((stack, stack), 0) % GROUP == iota((stack, stack), 1) % GROUP
    by_row = jnp.sum(jnp.where(same, total, 0.0).reshape(members, GROUP, stack), axis=1)
    folded = (iota((stack, LANES), 0) // GROUP == iota((stack, LANES), 1) % members).astype(F32)
    tiled = exact_dot(by_row, folded)
    per_row = LANES // members
    keep = iota((members, LANES), 0) % per_row == iota((members, LANES), 1) // members
    packed = jnp.sum(jnp.where(keep, tiled, 0.0).reshape(members // per_row, per_row, LANES), axis=1)
    proj_col = jnp.sum(jnp.sum(proj, axis=1), axis=1, keepdims=True)
    proj_row = jnp.sum(
        jnp.where(iota((members, LANES), 0) == iota((members, LANES), 1), proj_col, 0.0), axis=0, keepdims=True
    )
    filled = members // per_row + 1
    blank = jnp.zeros((out_ref.shape[0] - filled, LANES), F32)
    out_ref[...] = jnp.concatenate([packed, proj_row, blank], axis=0)


def gram_partial(index, gathered, shares, grid):
    def here(array):
        block = (array.shape[0], 1, *array.shape[2:])
        return pl.BlockSpec(block, lambda i, index: (0, index[0], 0, 0, 0))

    def whole(array):
        return pl.BlockSpec(array.shape, lambda i, index: (0,) * array.ndim)

    members = sum(v.shape[0] * v.shape[2] for v in gathered) + sum(v.shape[0] * v.shape[1] for v in shares)
    filled = members * members // LANES + 1
    out_shape = (-(-filled // 8) * 8, LANES)
    return pl.pallas_call(
        gram_kernel,
        grid_spec=pltpu.PrefetchScalarGridSpec(
            num_scalar_prefetch=1,
            grid=(1,),
            in_specs=[here(v) for v in gathered] + [whole(v) for v in (*shares, grid)],
            out_specs=pl.BlockSpec(out_shape, lambda i, index: (0, 0)),
        ),
        out_shape=jax.ShapeDtypeStruct(out_shape, F32),
        compiler_params=pltpu.CompilerParams(vmem_limit_bytes=VMEM_LIMIT),
        cost_estimate=pl.CostEstimate(
            flops=3 * GROUP * members * members * grid.size, bytes_accessed=members * grid.size, transcendentals=0
        ),
        name="gram",
    )(index, *gathered, *shares, grid)


def ensemble_transform(gram, proj):
    members = gram.shape[0]
    row, column = iota((members, members), 0), iota((members, members), 1)
    identity = (row == column).astype(F32)
    system = gram + (members - 1.0) * identity
    left, right = system, proj
    for pivot in range(members):
        is_pivot = iota((members, 1), 0) == pivot
        scale = 1.0 / left[pivot : pivot + 1, pivot : pivot + 1]
        pivot_row = left[pivot : pivot + 1, :] * scale
        pivot_right = right[pivot : pivot + 1, :] * scale
        factor = left[:, pivot : pivot + 1]
        left = jnp.where(is_pivot, pivot_row, left - factor * pivot_row)
        right = jnp.where(is_pivot, pivot_right, right - factor * pivot_right)
    mean_weights = right
    mean_level = jnp.sum(jnp.sum(system * identity, axis=1, keepdims=True), axis=0, keepdims=True) / members
    lifted = system + (mean_level - (members - 1.0)) * (1.0 / members)
    frobenius = jnp.sqrt(jnp.sum(jnp.sum(lifted * lifted, axis=1, keepdims=True), axis=0, keepdims=True))
    root_iter = lifted / frobenius
    inv_iter = identity
    for sweep in range(NS_STEPS):
        product = root_iter if sweep == 0 else exact_dot(inv_iter, root_iter)
        correction = 1.5 * identity - 0.5 * product
        inv_iter = correction if sweep == 0 else exact_dot(correction, inv_iter)
        if sweep < NS_STEPS - 1:
            root_iter = exact_dot(root_iter, correction)
    inv_root = inv_iter / jnp.sqrt(frobenius) + (1.0 / math.sqrt(members - 1.0) - 1.0 / jnp.sqrt(mean_level)) * (
        1.0 / members
    )
    moved = mean_weights + math.sqrt(members - 1.0) * inv_root
    return 1.0 / members + moved - jnp.sum(moved, axis=0, keepdims=True) * (1.0 / members)


def solve_kernel(partial_ref, out_ref):
    members = out_ref.shape[0]
    per_row = LANES // members
    sums = jnp.sum(partial_ref[...], axis=0)
    spread_rows = jnp.concatenate(
        [jnp.broadcast_to(sums[r : r + 1], (per_row, LANES)) for r in range(members // per_row)], axis=0
    )
    keep = iota((members, LANES), 0) % per_row == iota((members, LANES), 1) // members
    folded = (iota((LANES, members), 0) % members == iota((LANES, members), 1)).astype(F32)
    gram = exact_dot(jnp.where(keep, spread_rows, 0.0), folded)
    proj_row = jnp.broadcast_to(sums[members // per_row : members // per_row + 1], (members, LANES))
    on_diagonal = iota((members, LANES), 0) == iota((members, LANES), 1)
    proj = jnp.sum(jnp.where(on_diagonal, proj_row, 0.0), axis=1, keepdims=True)
    out_ref[...] = ensemble_transform(gram, proj)


def solve(partials, members):
    return pl.pallas_call(
        solve_kernel,
        out_shape=jax.ShapeDtypeStruct((members, members), F32),
        in_specs=[vmem_spec()],
        out_specs=vmem_spec(),
        compiler_params=pltpu.CompilerParams(vmem_limit_bytes=VMEM_LIMIT),
        cost_estimate=pl.CostEstimate(flops=10**9, bytes_accessed=partials.size * 4, transcendentals=0),
        name="solve",
    )(partials)


def combine_kernel(index_ref, transform_ref, *refs):
    field_refs, out_ref = refs[:-1], refs[-1]
    own_members, rows, feat_width = out_ref.shape
    members = transform_ref.shape[0]
    stack, own_stack = members * GROUP, own_members * GROUP
    own = iota((own_stack, members), 0) // GROUP
    place, first, base = jnp.zeros_like(own), 0, 0
    for ref in field_refs:
        part = ref.shape[2]
        inside = (own >= first) & (own < first + part)
        place = jnp.where(inside, base + index_ref[0] * part + own - first, place)
        first, base = first + part, base + part * ref.shape[0]
    pick_own = (place == iota((own_stack, members), 1)).astype(F32).astype(BF16)
    pick = (iota((stack, members), 0) // GROUP == iota((stack, members), 1)).astype(F32).astype(BF16)
    same = iota((own_stack, stack), 0) % GROUP == iota((own_stack, stack), 1) % GROUP
    mixers = []
    for piece in halves(transform_ref[...]):
        rows_of = dot(pick_own, piece, ((1,), (1,))).astype(BF16)
        mixers.append(jnp.where(same, dot(rows_of, pick, ((1,), (1,))), 0.0).astype(BF16))
    mixer = jnp.concatenate(mixers, axis=0)
    share_rows = field_refs[0].shape[3]
    for share in range(rows // share_rows):
        for lower in range(0, share_rows, GROUP):
            fields = jnp.concatenate(
                [ref[:, share, :, lower : lower + GROUP, :].reshape(-1, feat_width) for ref in field_refs], axis=0
            )
            mixed = dot(mixer, fields)
            mixed = (mixed[:own_stack] + mixed[own_stack:]).astype(BF16)
            start = share * share_rows + lower
            out_ref[:, start : start + GROUP, :] = mixed.reshape(own_members, GROUP, feat_width)


def combine(index, transform, gathered):
    own_members = sum(v.shape[2] for v in gathered)
    shares, _, share_rows, feat_width = gathered[0].shape[1:]
    out_shape = (own_members, shares * share_rows, feat_width)
    size = sum(v.size for v in gathered)
    return pl.pallas_call(
        combine_kernel,
        out_shape=jax.ShapeDtypeStruct(out_shape, BF16),
        in_specs=[smem_spec()] + [vmem_spec()] * (1 + len(gathered)),
        out_specs=vmem_spec(),
        compiler_params=pltpu.CompilerParams(vmem_limit_bytes=VMEM_LIMIT),
        cost_estimate=pl.CostEstimate(flops=4 * GROUP * own_members * size, bytes_accessed=3 * size, transcendentals=0),
        name="combine",
    )(index, transform, *gathered)


def local(
    ens_state,
    attn_gain,
    ffn_gain,
    w_query,
    w_key,
    w_value,
    w_out,
    w_gate,
    w_up,
    down_weight,
    head_window,
    obs_token,
    obs_channel,
    obs_value,
    obs_var,
):
    own_members, row_count, feat_width = ens_state.shape
    mem_count = lax.axis_size("mem")
    tok_count = lax.axis_size("tok")
    device_count = mem_count * tok_count
    members = own_members * mem_count
    share_rows = row_count // mem_count
    first_pos = lax.axis_index("tok") * row_count
    up = [(i, i + 1) for i in range(tok_count - 1)]
    down = [(i + 1, i) for i in range(tok_count - 1)]
    left = lax.ppermute(ens_state[:, row_count - WIN :], "tok", up)
    right = lax.ppermute(ens_state[:, :WIN], "tok", down)
    share_start = first_pos + lax.axis_index("mem") * share_rows
    grid = sample_grid(
        share_start.astype(jnp.int32).reshape(1), obs_token, obs_channel, obs_value, obs_var, share_rows, feat_width
    )
    place = jnp.stack([first_pos, row_count * tok_count]).astype(jnp.int32)
    index = lax.axis_index("mem").astype(jnp.int32).reshape(1)
    half = own_members // 2

    def forecast_of(first, count):
        return forward(
            place,
            head_window,
            ens_state,
            left,
            right,
            [attn_gain.reshape(1, -1), ffn_gain.reshape(1, -1)],
            [w_query, w_key, w_value, w_out, w_gate, w_up, down_weight],
            mem_count,
            first,
            count,
        )

    early = forecast_of(0, half)
    early_all = lax.all_gather(early, "mem")
    late = forecast_of(half, own_members - half)
    late_share = lax.all_to_all(late, "mem", split_axis=0, concat_axis=0, tiled=True)
    late, late_share = lax.optimization_barrier((late, late_share))
    late_all = lax.all_gather(late, "mem")
    partial = gram_partial(index, [early_all], [late_share], grid)
    partials = lax.all_to_all(
        jnp.broadcast_to(partial[None], (device_count, *partial.shape)),
        ("mem", "tok"),
        split_axis=0,
        concat_axis=0,
        tiled=True,
    )
    return combine(index, solve(partials, members), [early_all, late_all])


def solution(mesh):
    in_specs = (P("mem", "tok", None), *[P()] * 10, *[P("tok")] * 4)
    return jax.shard_map(local, mesh=mesh, in_specs=in_specs, out_specs=P("mem", "tok", None), check_vma=False)
```

```python
import functools
import math

import jax
import jax.numpy as jnp
from jax import lax
from jax.experimental import pallas as pl
from jax.experimental.pallas import tpu as pltpu
from jax.sharding import PartitionSpec as P

WIN = 256
NS_STEPS = 8
EPS = 1e-05
Q_ROWS = 128
GROUP = 16
LANES = 128
VMEM_LIMIT = 50 * 1024 * 1024

F32 = jnp.float32
BF16 = jnp.bfloat16


def dot(a, b, contract=((1,), (0,)), precision=None):
    return lax.dot_general(a, b, (contract, ((), ())), precision=precision, preferred_element_type=F32)


def exact_dot(a, b, contract=((1,), (0,))):
    return dot(a, b, contract, lax.Precision.HIGHEST)


def iota(shape, axis):
    return lax.broadcasted_iota(jnp.int32, shape, axis)


def halves(values):
    high = values.astype(BF16)
    return high, (values - high.astype(F32)).astype(BF16)


def rms_scaled(values, gain):
    return values * lax.rsqrt(jnp.mean(values * values, axis=-1, keepdims=True) + EPS) * gain


def vmem_spec():
    return pl.BlockSpec(memory_space=pltpu.VMEM)


def smem_spec():
    return pl.BlockSpec(memory_space=pltpu.SMEM)


def sample_grid_kernel(start_ref, token_ref, channel_ref, value_ref, var_ref, out_ref):
    rows, feat_width = out_ref.shape[1:]
    count = token_ref.shape[1]
    chunk = min(1024, count)
    total = jnp.zeros((4 * rows, feat_width), F32)
    for lower in range(0, count, chunk):
        part = slice(lower, lower + chunk)
        inv_var = 1.0 / var_ref[:, part]
        weighted = value_ref[:, part] * inv_var
        here = iota((rows, chunk), 0) == token_ref[:, part] - start_ref[0]
        pieces = []
        for row in (inv_var, weighted):
            high = row.astype(BF16).astype(F32)
            pieces.append(jnp.where(here, high, 0.0).astype(BF16))
            pieces.append(jnp.where(here, row - high, 0.0).astype(BF16))
        channel_hot = jnp.where(iota((feat_width, chunk), 0) == channel_ref[:, part], 1.0, 0.0).astype(BF16)
        total += dot(jnp.concatenate(pieces, axis=0), channel_hot, ((1,), (1,)))
    out_ref[0] = total[:rows] + total[rows : 2 * rows]
    out_ref[1] = total[2 * rows : 3 * rows] + total[3 * rows :]


def sample_grid(start, obs_token, obs_channel, obs_value, obs_var, rows, feat_width):
    count = obs_token.shape[0]
    return pl.pallas_call(
        sample_grid_kernel,
        out_shape=jax.ShapeDtypeStruct((2, rows, feat_width), F32),
        in_specs=[smem_spec()] + [vmem_spec()] * 4,
        out_specs=vmem_spec(),
        compiler_params=pltpu.CompilerParams(vmem_limit_bytes=VMEM_LIMIT),
        cost_estimate=pl.CostEstimate(flops=8 * rows * count * feat_width, bytes_accessed=16 * count, transcendentals=0),
        name="sample_grid",
    )(start, *(v.reshape(1, count) for v in (obs_token, obs_channel, obs_value, obs_var)))


def forward_kernel(
    members,
    place_ref,
    window_ref,
    own_ref,
    left_ref,
    right_ref,
    attn_gain_ref,
    ffn_gain_ref,
    w_query_ref,
    w_key_ref,
    w_value_ref,
    w_out_ref,
    w_gate_ref,
    w_up_ref,
    down_weight_ref,
    *refs,
):
    out_refs, (query_buf, key_buf, value_buf, apart_buf, mixed_buf) = refs[:-5], refs[-5:]
    row_count, feat_width = own_ref.shape[1:]
    reach = left_ref.shape[1]
    head_count = window_ref.shape[0]
    head_size = feat_width // head_count
    blocks = row_count // Q_ROWS
    key_count = Q_ROWS + 2 * reach

    @pl.when(pl.program_id(0) == 0)
    def _():
        rel = jnp.abs(iota((Q_ROWS, key_count), 1) - reach - iota((Q_ROWS, key_count), 0))
        for block in range(blocks):
            k_pos = place_ref[0] - reach + block * Q_ROWS + iota((Q_ROWS, key_count), 1)
            inside = (k_pos >= 0) & (k_pos < place_ref[1])
            apart_buf[block] = jnp.where(inside, rel, 1 << 20)

    attn_gain = attn_gain_ref[...]
    for source, lower, rows in ((left_ref, 0, reach), (own_ref, reach, row_count), (right_ref, reach + row_count, reach)):
        normed = rms_scaled(source[0].astype(F32), attn_gain).astype(BF16)
        key_buf[lower : lower + rows] = dot(normed, w_key_ref[...]).astype(BF16)
        value_buf[lower : lower + rows] = dot(normed, w_value_ref[...]).astype(BF16)
        if source is own_ref:
            queries = dot(normed, w_query_ref[...]).astype(BF16)
            query_buf[...] = queries * jnp.asarray(1.0 / math.sqrt(head_size), BF16)

    column_head = iota((1, feat_width), 1) // head_size

    def one_block(block, carry):
        start = pl.multiple_of(block * Q_ROWS, Q_ROWS)
        queries = query_buf[pl.ds(start, Q_ROWS), :]
        stacked = jnp.concatenate(
            [queries * (column_head == head).astype(F32).astype(BF16) for head in range(head_count)], axis=0
        )
        scores = dot(stacked, key_buf[pl.ds(start, key_count), :], ((1,), (1,)))
        apart = apart_buf[block]
        weights, scales = [], []
        for head in range(head_count):
            score_matrix = scores[head * Q_ROWS : (head + 1) * Q_ROWS]
            score_matrix = jnp.where(apart <= window_ref[head], score_matrix, -1e30)
            expo = jnp.exp(score_matrix - jnp.max(score_matrix, axis=-1, keepdims=True))
            scales.append(1.0 / jnp.sum(expo, axis=-1, keepdims=True))
            weights.append(expo.astype(BF16))
        mixed_all = dot(jnp.concatenate(weights, axis=0), value_buf[pl.ds(start, key_count), :])
        mixed = jnp.zeros((Q_ROWS, feat_width), F32)
        for head in range(head_count):
            mixed = jnp.where(column_head == head, mixed_all[head * Q_ROWS : (head + 1) * Q_ROWS] * scales[head], mixed)
        mixed_buf[pl.ds(start, Q_ROWS), :] = mixed.astype(BF16)
        return carry

    lax.fori_loop(0, blocks, one_block, 0)

    after = (own_ref[0].astype(F32) + dot(mixed_buf[...], w_out_ref[...])).astype(BF16)
    normed_mid = rms_scaled(after.astype(F32), ffn_gain_ref[...]).astype(BF16)
    gate = dot(normed_mid, w_gate_ref[...])
    hidden = (gate * (0.5 + 0.5 * jnp.tanh(0.5 * gate)) * dot(normed_mid, w_up_ref[...])).astype(BF16)
    forecast = (after.astype(F32) + dot(hidden, down_weight_ref[...])).astype(BF16)
    shares, share_rows, _ = out_refs[0].shape
    for member, out_ref in enumerate(out_refs[:members]):

        @pl.when(pl.program_id(0) == member)
        def _():
            for share in range(shares):
                out_ref[share] = forecast[share * share_rows : (share + 1) * share_rows]

    for out_ref in out_refs[members:]:
        for share in range(shares):
            out_ref[share, 0] = forecast[share * share_rows : (share + 1) * share_rows]


def forward(place, head_window, own, left, right, gains, weights, shares, first, members, joined):
    _, row_count, feat_width = own.shape
    reach = left.shape[1]
    key_count = Q_ROWS + 2 * reach
    hidden_width = weights[4].shape[1]
    macs = members * row_count * feat_width * (6 * feat_width + 3 * hidden_width + 8 * key_count)
    share_rows = row_count // shares
    out_shape = [jax.ShapeDtypeStruct((shares, share_rows, feat_width), BF16)] * members
    out_specs = [pl.BlockSpec((shares, share_rows, feat_width), lambda m: (0, 0, 0))] * members
    if joined:
        out_shape.append(jax.ShapeDtypeStruct((shares, members, share_rows, feat_width), BF16))
        out_specs.append(pl.BlockSpec((shares, 1, share_rows, feat_width), lambda m: (0, m, 0, 0)))
    return pl.pallas_call(
        functools.partial(forward_kernel, members),
        grid=(members,),
        out_shape=out_shape,
        in_specs=[
            smem_spec(),
            smem_spec(),
            pl.BlockSpec((1, row_count, feat_width), lambda m: (first + m, 0, 0)),
            pl.BlockSpec((1, reach, feat_width), lambda m: (first + m, 0, 0)),
            pl.BlockSpec((1, reach, feat_width), lambda m: (first + m, 0, 0)),
        ]
        + [vmem_spec()] * (len(gains) + len(weights)),
        out_specs=out_specs,
        scratch_shapes=[
            pltpu.VMEM((row_count, feat_width), BF16),
            pltpu.VMEM((row_count + 2 * reach, feat_width), BF16),
            pltpu.VMEM((row_count + 2 * reach, feat_width), BF16),
            pltpu.VMEM((row_count // Q_ROWS, Q_ROWS, key_count), jnp.int32),
            pltpu.VMEM((row_count, feat_width), BF16),
        ],
        compiler_params=pltpu.CompilerParams(vmem_limit_bytes=VMEM_LIMIT),
        cost_estimate=pl.CostEstimate(flops=2 * macs, bytes_accessed=6 * members * row_count * feat_width, transcendentals=0),
        name="forward",
    )(place, head_window, own, left, right, *gains, *weights)


def gram_kernel(gathered, index_ref, *refs):
    share_refs, grid_ref, out_ref = refs[:-2], refs[-2], refs[-1]
    rows, feat_width = grid_ref.shape[1:]
    members = sum(math.prod(ref.shape[:-2]) for ref in share_refs)
    stack = members * GROUP
    total = jnp.zeros((stack, stack), F32)
    proj = jnp.zeros((members, GROUP, feat_width), F32)
    for lower in range(0, rows, GROUP):
        part = slice(lower, lower + GROUP)
        pieces = []
        for member, ref in enumerate(share_refs[:gathered]):
            for source in range(ref.shape[0] * ref.shape[1]):
                pieces.append(piece_of(ref, member, source)[0, part, :].reshape(1, GROUP, feat_width))
        pieces += [ref[..., part, :].reshape(-1, GROUP, feat_width) for ref in share_refs[gathered:]]
        fields = jnp.concatenate(pieces, axis=0).astype(F32)
        mean = jnp.sum(fields, axis=0) * (1.0 / members)
        spread = fields - mean[None]
        weight = grid_ref[0, part, :]
        proj += spread * (grid_ref[1, part, :] - weight * mean)[None]
        high, low = halves(spread.reshape(stack, feat_width))
        w_high, w_low = halves((spread * weight[None]).reshape(stack, feat_width))
        last = ((1,), (1,))
        total += dot(w_high, high, last) + dot(w_high, low, last) + dot(w_low, high, last)
    same = iota((stack, stack), 0) % GROUP == iota((stack, stack), 1) % GROUP
    by_row = jnp.sum(jnp.where(same, total, 0.0).reshape(members, GROUP, stack), axis=1)
    folded = (iota((stack, LANES), 0) // GROUP == iota((stack, LANES), 1) % members).astype(F32)
    tiled = exact_dot(by_row, folded)
    per_row = LANES // members
    keep = iota((members, LANES), 0) % per_row == iota((members, LANES), 1) // members
    packed = jnp.sum(jnp.where(keep, tiled, 0.0).reshape(members // per_row, per_row, LANES), axis=1)
    proj_col = jnp.sum(jnp.sum(proj, axis=1), axis=1, keepdims=True)
    proj_row = jnp.sum(
        jnp.where(iota((members, LANES), 0) == iota((members, LANES), 1), proj_col, 0.0), axis=0, keepdims=True
    )
    filled = members // per_row + 1
    blank = jnp.zeros((out_ref.shape[0] - filled, LANES), F32)
    out_ref[...] = jnp.concatenate([packed, proj_row, blank], axis=0)


def gram_partial(index, gathered, shares, grid):
    def here(array):
        block = (*array.shape[:2], 1, *array.shape[3:])
        return pl.BlockSpec(block, lambda i, index: (0, 0, index[0], 0, 0))

    def whole(array):
        return pl.BlockSpec(array.shape, lambda i, index: (0,) * array.ndim)

    members = sum(v.shape[0] * v.shape[1] for v in gathered) + sum(v.shape[0] * v.shape[1] for v in shares)
    filled = members * members // LANES + 1
    out_shape = (-(-filled // 8) * 8, LANES)
    return pl.pallas_call(
        functools.partial(gram_kernel, len(gathered)),
        grid_spec=pltpu.PrefetchScalarGridSpec(
            num_scalar_prefetch=1,
            grid=(1,),
            in_specs=[here(v) for v in gathered] + [whole(v) for v in (*shares, grid)],
            out_specs=pl.BlockSpec(out_shape, lambda i, index: (0, 0)),
        ),
        out_shape=jax.ShapeDtypeStruct(out_shape, F32),
        compiler_params=pltpu.CompilerParams(vmem_limit_bytes=VMEM_LIMIT),
        cost_estimate=pl.CostEstimate(
            flops=3 * GROUP * members * members * grid.size, bytes_accessed=members * grid.size, transcendentals=0
        ),
        name="gram",
    )(index, *gathered, *shares, grid)


def ensemble_transform(gram, proj):
    members = gram.shape[0]
    row, column = iota((members, members), 0), iota((members, members), 1)
    identity = (row == column).astype(F32)
    system = gram + (members - 1.0) * identity
    left, right = system, proj
    for pivot in range(members):
        is_pivot = iota((members, 1), 0) == pivot
        scale = 1.0 / left[pivot : pivot + 1, pivot : pivot + 1]
        pivot_row = left[pivot : pivot + 1, :] * scale
        pivot_right = right[pivot : pivot + 1, :] * scale
        factor = left[:, pivot : pivot + 1]
        left = jnp.where(is_pivot, pivot_row, left - factor * pivot_row)
        right = jnp.where(is_pivot, pivot_right, right - factor * pivot_right)
    mean_weights = right
    mean_level = jnp.sum(jnp.sum(system * identity, axis=1, keepdims=True), axis=0, keepdims=True) / members
    lifted = system + (mean_level - (members - 1.0)) * (1.0 / members)
    frobenius = jnp.sqrt(jnp.sum(jnp.sum(lifted * lifted, axis=1, keepdims=True), axis=0, keepdims=True))
    root_iter = lifted / frobenius
    inv_iter = identity
    for sweep in range(NS_STEPS):
        product = root_iter if sweep == 0 else exact_dot(inv_iter, root_iter)
        correction = 1.5 * identity - 0.5 * product
        inv_iter = correction if sweep == 0 else exact_dot(correction, inv_iter)
        if sweep < NS_STEPS - 1:
            root_iter = exact_dot(root_iter, correction)
    inv_root = inv_iter / jnp.sqrt(frobenius) + (1.0 / math.sqrt(members - 1.0) - 1.0 / jnp.sqrt(mean_level)) * (
        1.0 / members
    )
    moved = mean_weights + math.sqrt(members - 1.0) * inv_root
    return 1.0 / members + moved - jnp.sum(moved, axis=0, keepdims=True) * (1.0 / members)


def solve_kernel(partial_ref, out_ref):
    members = out_ref.shape[0]
    per_row = LANES // members
    sums = jnp.sum(partial_ref[...], axis=0)
    spread_rows = jnp.concatenate(
        [jnp.broadcast_to(sums[r : r + 1], (per_row, LANES)) for r in range(members // per_row)], axis=0
    )
    keep = iota((members, LANES), 0) % per_row == iota((members, LANES), 1) // members
    folded = (iota((LANES, members), 0) % members == iota((LANES, members), 1)).astype(F32)
    gram = exact_dot(jnp.where(keep, spread_rows, 0.0), folded)
    proj_row = jnp.broadcast_to(sums[members // per_row : members // per_row + 1], (members, LANES))
    on_diagonal = iota((members, LANES), 0) == iota((members, LANES), 1)
    proj = jnp.sum(jnp.where(on_diagonal, proj_row, 0.0), axis=1, keepdims=True)
    out_ref[...] = ensemble_transform(gram, proj)


def solve(partials, members):
    return pl.pallas_call(
        solve_kernel,
        out_shape=jax.ShapeDtypeStruct((members, members), F32),
        in_specs=[vmem_spec()],
        out_specs=vmem_spec(),
        compiler_params=pltpu.CompilerParams(vmem_limit_bytes=VMEM_LIMIT),
        cost_estimate=pl.CostEstimate(flops=10**9, bytes_accessed=partials.size * 4, transcendentals=0),
        name="solve",
    )(partials)


def combine_kernel(groups, index_ref, transform_ref, *refs):
    field_refs, out_ref = refs[:-1], refs[-1]
    own_members, rows, feat_width = out_ref.shape
    members = transform_ref.shape[0]
    stack, own_stack = members * GROUP, own_members * GROUP
    own = iota((own_stack, members), 0) // GROUP
    sources = members // own_members
    place = jnp.zeros_like(own)
    base = 0
    for group in groups:
        first = base // sources
        inside = (own >= first) & (own < first + group)
        place = jnp.where(inside, base + index_ref[0] * group + own - first, place)
        base += group * sources
    pick_own = (place == iota((own_stack, members), 1)).astype(F32).astype(BF16)
    pick = (iota((stack, members), 0) // GROUP == iota((stack, members), 1)).astype(F32).astype(BF16)
    same = iota((own_stack, stack), 0) % GROUP == iota((own_stack, stack), 1) % GROUP
    mixers = []
    for piece in halves(transform_ref[...]):
        rows_of = dot(pick_own, piece, ((1,), (1,))).astype(BF16)
        mixers.append(jnp.where(same, dot(rows_of, pick, ((1,), (1,))), 0.0).astype(BF16))
    mixer = jnp.concatenate(mixers, axis=0)
    share_rows = field_refs[0].shape[-2]
    for share in range(rows // share_rows):
        for lower in range(0, share_rows, GROUP):
            part = slice(lower, lower + GROUP)
            pieces, first = [], 0
            for group in groups:
                for source in range(sources):
                    for member in range(first, first + group):
                        pieces.append(piece_of(field_refs[member], member, source)[share, part, :])
                first += group
            mixed = dot(mixer, jnp.concatenate(pieces, axis=0))
            mixed = (mixed[:own_stack] + mixed[own_stack:]).astype(BF16)
            start = share * share_rows + lower
            out_ref[:, start : start + GROUP, :] = mixed.reshape(own_members, GROUP, feat_width)


def combine(index, transform, gathered, groups):
    own_members = len(gathered)
    shares, share_rows, feat_width = gathered[0].shape[2:]
    out_shape = (own_members, shares * share_rows, feat_width)
    size = sum(v.size for v in gathered)
    return pl.pallas_call(
        functools.partial(combine_kernel, groups),
        out_shape=jax.ShapeDtypeStruct(out_shape, BF16),
        in_specs=[smem_spec()] + [vmem_spec()] * (1 + len(gathered)),
        out_specs=vmem_spec(),
        compiler_params=pltpu.CompilerParams(vmem_limit_bytes=VMEM_LIMIT),
        cost_estimate=pl.CostEstimate(flops=4 * GROUP * own_members * size, bytes_accessed=3 * size, transcendentals=0),
        name="combine",
    )(index, transform, *gathered)


def mem_grid(count):
    fine = max(n for n in range(1, math.isqrt(count) + 1) if count % n == 0)
    coarse = count // fine
    along_fine = [[a * fine + b for b in range(fine)] for a in range(coarse)]
    along_coarse = [[a * fine + b for a in range(coarse)] for b in range(fine)]
    return along_fine, along_coarse


def gathered_over_mem(fields, member):
    ways = mem_grid(lax.axis_size("mem"))
    for way in ways if member % 2 == 0 else ways[::-1]:
        fields = lax.all_gather(fields, "mem", axis_index_groups=way)
    return fields


def piece_of(ref, member, source):
    if member % 2 == 0:
        return ref.at[source // ref.shape[1], source % ref.shape[1]]
    return ref.at[source % ref.shape[0], source // ref.shape[0]]


def local(
    ens_state,
    attn_gain,
    ffn_gain,
    w_query,
    w_key,
    w_value,
    w_out,
    w_gate,
    w_up,
    down_weight,
    head_window,
    obs_token,
    obs_channel,
    obs_value,
    obs_var,
):
    own_members, row_count, feat_width = ens_state.shape
    mem_count = lax.axis_size("mem")
    tok_count = lax.axis_size("tok")
    device_count = mem_count * tok_count
    members = own_members * mem_count
    share_rows = row_count // mem_count
    first_pos = lax.axis_index("tok") * row_count
    up = [(i, i + 1) for i in range(tok_count - 1)]
    down = [(i + 1, i) for i in range(tok_count - 1)]
    left = lax.ppermute(ens_state[:, row_count - WIN :], "tok", up)
    right = lax.ppermute(ens_state[:, :WIN], "tok", down)
    share_start = first_pos + lax.axis_index("mem") * share_rows
    grid = sample_grid(
        share_start.astype(jnp.int32).reshape(1), obs_token, obs_channel, obs_value, obs_var, share_rows, feat_width
    )
    place = jnp.stack([first_pos, row_count * tok_count]).astype(jnp.int32)
    index = lax.axis_index("mem").astype(jnp.int32).reshape(1)
    half = own_members // 2

    def forecast_of(first, count, joined):
        return forward(
            place,
            head_window,
            ens_state,
            left,
            right,
            [attn_gain.reshape(1, -1), ffn_gain.reshape(1, -1)],
            [w_query, w_key, w_value, w_out, w_gate, w_up, down_weight],
            mem_count,
            first,
            count,
            joined,
        )

    early = forecast_of(0, half, False)
    early_all = [gathered_over_mem(v, m) for m, v in enumerate(early)]
    *late, late_joined = forecast_of(half, own_members - half, True)
    late_share = lax.all_to_all(late_joined, "mem", split_axis=0, concat_axis=0, tiled=True)
    late, late_share = lax.optimization_barrier((late, late_share))
    late_all = [gathered_over_mem(v, half + m) for m, v in enumerate(late)]
    partial = gram_partial(index, early_all, [late_share], grid)
    partials = lax.all_to_all(
        jnp.broadcast_to(partial[None], (device_count, *partial.shape)),
        ("mem", "tok"),
        split_axis=0,
        concat_axis=0,
        tiled=True,
    )
    groups = (1,) * half + (own_members - half,)
    return combine(index, solve(partials, members), early_all + late_all, groups)


def solution(mesh):
    in_specs = (P("mem", "tok", None), *[P()] * 10, *[P("tok")] * 4)
    return jax.shard_map(local, mesh=mesh, in_specs=in_specs, out_specs=P("mem", "tok", None), check_vma=False)
```

```python
import functools
import math

import jax
import jax.numpy as jnp
from jax import lax
from jax.experimental import pallas as pl
from jax.experimental.pallas import tpu as pltpu
from jax.sharding import PartitionSpec as P

WIN = 256
NS_STEPS = 8
EPS = 1e-05
Q_ROWS = 128
GROUP = 16
LANES = 128
VMEM_LIMIT = 50 * 1024 * 1024

F32 = jnp.float32
BF16 = jnp.bfloat16


def dot(a, b, contract=((1,), (0,)), precision=None):
    return lax.dot_general(a, b, (contract, ((), ())), precision=precision, preferred_element_type=F32)


def exact_dot(a, b, contract=((1,), (0,))):
    return dot(a, b, contract, lax.Precision.HIGHEST)


def iota(shape, axis):
    return lax.broadcasted_iota(jnp.int32, shape, axis)


def halves(values):
    high = values.astype(BF16)
    return high, (values - high.astype(F32)).astype(BF16)


def rms_scaled(values, gain):
    return values * lax.rsqrt(jnp.mean(values * values, axis=-1, keepdims=True) + EPS) * gain


def vmem_spec():
    return pl.BlockSpec(memory_space=pltpu.VMEM)


def smem_spec():
    return pl.BlockSpec(memory_space=pltpu.SMEM)


def edges_kernel(own_ref, head_ref, tail_ref, sems):
    members, reach, _ = head_ref.shape
    rows = own_ref.shape[1]
    copies = []
    for member in range(members):
        for which, (lower, out_ref) in enumerate(((rows - reach, tail_ref), (0, head_ref))):
            copies.append(
                pltpu.make_async_copy(
                    own_ref.at[member, pl.ds(lower, reach)], out_ref.at[member], sems.at[which, member]
                )
            )
    for copy in copies:
        copy.start()
    for copy in copies:
        copy.wait()


def edges(own, reach):
    members, _, feat_width = own.shape
    return pl.pallas_call(
        edges_kernel,
        out_shape=[jax.ShapeDtypeStruct((members, reach, feat_width), own.dtype)] * 2,
        in_specs=[pl.BlockSpec(memory_space=pl.ANY)],
        out_specs=[pl.BlockSpec(memory_space=pl.ANY)] * 2,
        scratch_shapes=[pltpu.SemaphoreType.DMA((2, members))],
        cost_estimate=pl.CostEstimate(flops=0, bytes_accessed=8 * members * reach * feat_width, transcendentals=0),
        name="edges",
    )(own)


def sample_grid_kernel(stride, start_ref, token_ref, channel_ref, value_ref, var_ref, out_ref):
    rows, feat_width = out_ref.shape[1:]
    share_rows = rows // 2
    count = token_ref.shape[1]
    chunk = min(1024, count)
    total = jnp.zeros((4 * rows, feat_width), F32)
    for lower in range(0, count, chunk):
        part = slice(lower, lower + chunk)
        inv_var = 1.0 / var_ref[:, part]
        weighted = value_ref[:, part] * inv_var
        row = iota((rows, chunk), 0)
        row = jnp.where(row < share_rows, row, row + (stride - share_rows))
        here = row == token_ref[:, part] - start_ref[0]
        pieces = []
        for values in (inv_var, weighted):
            high = values.astype(BF16).astype(F32)
            pieces.append(jnp.where(here, high, 0.0).astype(BF16))
            pieces.append(jnp.where(here, values - high, 0.0).astype(BF16))
        channel_hot = jnp.where(iota((feat_width, chunk), 0) == channel_ref[:, part], 1.0, 0.0).astype(BF16)
        total += dot(jnp.concatenate(pieces, axis=0), channel_hot, ((1,), (1,)))
    out_ref[0] = total[:rows] + total[rows : 2 * rows]
    out_ref[1] = total[2 * rows : 3 * rows] + total[3 * rows :]


def sample_grid(start, obs_token, obs_channel, obs_value, obs_var, share_rows, stride, feat_width):
    count = obs_token.shape[0]
    rows = 2 * share_rows
    return pl.pallas_call(
        functools.partial(sample_grid_kernel, stride),
        out_shape=jax.ShapeDtypeStruct((2, rows, feat_width), F32),
        in_specs=[smem_spec()] + [vmem_spec()] * 4,
        out_specs=vmem_spec(),
        compiler_params=pltpu.CompilerParams(vmem_limit_bytes=VMEM_LIMIT),
        cost_estimate=pl.CostEstimate(flops=8 * rows * count * feat_width, bytes_accessed=16 * count, transcendentals=0),
        name="sample_grid",
    )(start, *(v.reshape(1, count) for v in (obs_token, obs_channel, obs_value, obs_var)))


def project_kernel(
    heads, own_ref, gain_ref, w_query_ref, w_key_ref, w_value_ref, query_ref, key_ref, value_ref, turned_ref
):
    @pl.when(pl.program_id(0) == 0)
    def _():
        turned_ref[...] = w_value_ref[...].astype(F32).T.astype(BF16)

    scale = math.log2(math.e) / math.sqrt(own_ref.shape[2] // heads)
    normed = rms_scaled(own_ref[0].astype(F32), gain_ref[...]).astype(BF16)
    query_ref[0] = (dot(normed, w_query_ref[...]) * scale).astype(BF16)
    key_ref[0] = dot(normed, w_key_ref[...]).astype(BF16)
    value_ref[0] = dot(turned_ref[...], normed, ((1,), (1,))).astype(BF16)


def project(own, heads, gain, w_query, w_key, w_value):
    members, rows, feat_width = own.shape
    block = pl.BlockSpec((1, rows, feat_width), lambda m: (m, 0, 0))
    return pl.pallas_call(
        functools.partial(project_kernel, heads),
        grid=(members,),
        out_shape=[
            jax.ShapeDtypeStruct((members, rows, feat_width), BF16),
            jax.ShapeDtypeStruct((members, rows, feat_width), BF16),
            jax.ShapeDtypeStruct((members, feat_width, rows), BF16),
        ],
        in_specs=[block] + [vmem_spec()] * 4,
        out_specs=[block, block, pl.BlockSpec((1, feat_width, rows), lambda m: (m, 0, 0))],
        scratch_shapes=[pltpu.VMEM((feat_width, feat_width), BF16)],
        compiler_params=pltpu.CompilerParams(vmem_limit_bytes=VMEM_LIMIT),
        cost_estimate=pl.CostEstimate(
            flops=6 * own.size * feat_width, bytes_accessed=8 * own.size, transcendentals=0
        ),
        name="project",
    )(own, gain, w_query, w_key, w_value)


def forward_kernel(
    halo_first,
    place_ref,
    window_ref,
    state_ref,
    query_ref,
    key_ref,
    value_ref,
    halo_ref,
    attn_gain_ref,
    ffn_gain_ref,
    w_key_ref,
    w_value_ref,
    w_out_ref,
    w_gate_ref,
    w_up_ref,
    down_weight_ref,
    out_ref,
    key_buf,
    value_buf,
    turned_buf,
    bias_buf,
    mixed_buf,
):
    rows, feat_width = state_ref.shape[1:]
    reach = halo_ref.shape[1]
    own_rows = key_ref.shape[1]
    head_count = window_ref.shape[0]
    head_size = feat_width // head_count
    blocks = rows // Q_ROWS
    key_count = Q_ROWS + 2 * reach

    @pl.when(pl.program_id(0) == 0)
    def _():
        turned_buf[...] = w_value_ref[...].astype(F32).T.astype(BF16)
        value_buf[feat_width:, :] = jnp.ones((value_buf.shape[0] - feat_width, value_buf.shape[1]), BF16)
        apart = jnp.abs(iota((key_count, Q_ROWS), 0) - reach - iota((key_count, Q_ROWS), 1))
        for block in range(blocks):
            k_pos = place_ref[0] + block * Q_ROWS + iota((key_count, Q_ROWS), 0)
            inside = (k_pos >= 0) & (k_pos < place_ref[1])
            for head in range(head_count):
                bias_buf[block, head] = jnp.where(inside & (apart <= window_ref[head]), 0.0, -1e30)

    own_at, halo_at = (reach, 0) if halo_first else (0, own_rows)
    normed = rms_scaled(halo_ref[0].astype(F32), attn_gain_ref[...]).astype(BF16)
    key_buf[own_at : own_at + own_rows] = key_ref[0]
    value_buf[:feat_width, own_at : own_at + own_rows] = value_ref[0]
    key_buf[halo_at : halo_at + reach] = dot(normed, w_key_ref[...]).astype(BF16)
    value_buf[:feat_width, halo_at : halo_at + reach] = dot(turned_buf[...], normed, ((1,), (1,))).astype(BF16)

    column_head = iota((1, feat_width), 1) // head_size
    for block in range(blocks):
        start = block * Q_ROWS
        queries = query_ref[0, start : start + Q_ROWS, :]
        stacked = jnp.concatenate(
            [queries * (column_head == head).astype(F32).astype(BF16) for head in range(head_count)], axis=0
        )
        scores = dot(key_buf[start : start + key_count, :], stacked, ((1,), (1,)))
        weights = []
        for head in range(head_count):
            score_matrix = scores[:, head * Q_ROWS : (head + 1) * Q_ROWS] + bias_buf[block, head]
            row_top = jnp.max(score_matrix, axis=0, keepdims=True)
            weights.append(jnp.exp2((score_matrix - row_top).astype(BF16)))
        mixed_all = dot(value_buf[:, start : start + key_count], jnp.concatenate(weights, axis=1))
        mixed = []
        for head in range(head_count):
            columns = slice(head * Q_ROWS, (head + 1) * Q_ROWS)
            total = mixed_all[feat_width : feat_width + 1, columns]
            mixed.append(mixed_all[head * head_size : (head + 1) * head_size, columns] * (1.0 / total))
        mixed_buf[start : start + Q_ROWS, :] = jnp.concatenate(mixed, axis=0).T.astype(BF16)

    after = (state_ref[0].astype(F32) + dot(mixed_buf[...], w_out_ref[...])).astype(BF16)
    normed_mid = rms_scaled(after.astype(F32), ffn_gain_ref[...]).astype(BF16)
    gate = dot(normed_mid, w_gate_ref[...])
    hidden = (gate * (0.5 + 0.5 * jnp.tanh(0.5 * gate)) * dot(normed_mid, w_up_ref[...])).astype(BF16)
    forecast = (after.astype(F32) + dot(hidden, down_weight_ref[...])).astype(BF16)
    targets, _, out_rows, _ = out_ref.shape
    for target in range(targets):
        lower = target * out_rows if targets * out_rows == rows else 0
        out_ref[target, 0] = forecast[lower : lower + out_rows]


def forward(place, head_window, own, projected, halo, gains, weights, half, targets, out_rows):
    members, row_count, feat_width = own.shape
    rows, reach = row_count // 2, halo.shape[1]
    key_count = Q_ROWS + 2 * reach
    hidden_width = weights[3].shape[1]
    macs = members * rows * feat_width * (2 * feat_width + 3 * hidden_width + 8 * key_count)
    here = pl.BlockSpec((1, rows, feat_width), lambda m: (m, half, 0))
    ones_rows = 16
    return pl.pallas_call(
        functools.partial(forward_kernel, half == 0),
        grid=(members,),
        out_shape=jax.ShapeDtypeStruct((targets, members, out_rows, feat_width), BF16),
        in_specs=[
            smem_spec(),
            smem_spec(),
            here,
            here,
            pl.BlockSpec((1, row_count, feat_width), lambda m: (m, 0, 0)),
            pl.BlockSpec((1, feat_width, row_count), lambda m: (m, 0, 0)),
            pl.BlockSpec((1, reach, feat_width), lambda m: (m, 0, 0)),
        ]
        + [vmem_spec()] * (len(gains) + len(weights)),
        out_specs=pl.BlockSpec((targets, 1, out_rows, feat_width), lambda m: (0, m, 0, 0)),
        scratch_shapes=[
            pltpu.VMEM((row_count + reach, feat_width), BF16),
            pltpu.VMEM((feat_width + ones_rows, row_count + reach), BF16),
            pltpu.VMEM((feat_width, feat_width), BF16),
            pltpu.VMEM((rows // Q_ROWS, head_window.shape[0], key_count, Q_ROWS), F32),
            pltpu.VMEM((rows, feat_width), BF16),
        ],
        compiler_params=pltpu.CompilerParams(vmem_limit_bytes=VMEM_LIMIT),
        cost_estimate=pl.CostEstimate(flops=2 * macs, bytes_accessed=6 * own.size, transcendentals=0),
        name="forward",
    )(place, head_window, own, *projected, halo, *gains, *weights)


def gram_kernel(index_ref, early_ref, late_ref, grid_ref, out_ref):
    share_rows, feat_width = late_ref.shape[2:]
    members = late_ref.shape[0] * late_ref.shape[1]
    stack = members * GROUP
    total = jnp.zeros((stack, stack), F32)
    proj = jnp.zeros((members, GROUP, feat_width), F32)
    for half, ref in enumerate((early_ref, late_ref)):
        for lower in range(0, share_rows, GROUP):
            fields = ref[:, :, lower : lower + GROUP, :].reshape(members, GROUP, feat_width).astype(F32)
            mean = jnp.sum(fields, axis=0) * (1.0 / members)
            spread = fields - mean[None]
            part = slice(half * share_rows + lower, half * share_rows + lower + GROUP)
            weight = grid_ref[0, part, :]
            proj += spread * (grid_ref[1, part, :] - weight * mean)[None]
            high, low = halves(spread.reshape(stack, feat_width))
            w_high, w_low = halves((spread * weight[None]).reshape(stack, feat_width))
            last = ((1,), (1,))
            total += dot(w_high, high, last) + dot(w_high, low, last) + dot(w_low, high, last)
    same = iota((stack, stack), 0) % GROUP == iota((stack, stack), 1) % GROUP
    by_row = jnp.sum(jnp.where(same, total, 0.0).reshape(members, GROUP, stack), axis=1)
    folded = (iota((stack, LANES), 0) // GROUP == iota((stack, LANES), 1) % members).astype(F32)
    tiled = exact_dot(by_row, folded)
    per_row = LANES // members
    keep = iota((members, LANES), 0) % per_row == iota((members, LANES), 1) // members
    packed = jnp.sum(jnp.where(keep, tiled, 0.0).reshape(members // per_row, per_row, LANES), axis=1)
    proj_col = jnp.sum(jnp.sum(proj, axis=1), axis=1, keepdims=True)
    proj_row = jnp.sum(
        jnp.where(iota((members, LANES), 0) == iota((members, LANES), 1), proj_col, 0.0), axis=0, keepdims=True
    )
    filled = members // per_row + 1
    blank = jnp.zeros((out_ref.shape[0] - filled, LANES), F32)
    out_ref[...] = jnp.concatenate([packed, proj_row, blank], axis=0)


def gram_partial(index, early_all, late_share, grid):
    members = late_share.shape[0] * late_share.shape[1]
    filled = members * members // LANES + 1
    out_shape = (-(-filled // 8) * 8, LANES)
    return pl.pallas_call(
        gram_kernel,
        grid_spec=pltpu.PrefetchScalarGridSpec(
            num_scalar_prefetch=1,
            grid=(1,),
            in_specs=[
                pl.BlockSpec(late_share.shape, lambda i, index: (0, 0, index[0], 0)),
                pl.BlockSpec(late_share.shape, lambda i, index: (0, 0, 0, 0)),
                pl.BlockSpec(grid.shape, lambda i, index: (0, 0, 0)),
            ],
            out_specs=pl.BlockSpec(out_shape, lambda i, index: (0, 0)),
        ),
        out_shape=jax.ShapeDtypeStruct(out_shape, F32),
        compiler_params=pltpu.CompilerParams(vmem_limit_bytes=VMEM_LIMIT),
        cost_estimate=pl.CostEstimate(
            flops=3 * GROUP * members * members * grid.size, bytes_accessed=members * grid.size, transcendentals=0
        ),
        name="gram",
    )(index, early_all, late_share, grid)


def ensemble_transform(gram, proj):
    members = gram.shape[0]
    row, column = iota((members, members), 0), iota((members, members), 1)
    identity = (row == column).astype(F32)
    system = gram + (members - 1.0) * identity
    left, right = system, proj
    for pivot in range(members):
        is_pivot = iota((members, 1), 0) == pivot
        scale = 1.0 / left[pivot : pivot + 1, pivot : pivot + 1]
        pivot_row = left[pivot : pivot + 1, :] * scale
        pivot_right = right[pivot : pivot + 1, :] * scale
        factor = left[:, pivot : pivot + 1]
        left = jnp.where(is_pivot, pivot_row, left - factor * pivot_row)
        right = jnp.where(is_pivot, pivot_right, right - factor * pivot_right)
    mean_weights = right
    mean_level = jnp.sum(jnp.sum(system * identity, axis=1, keepdims=True), axis=0, keepdims=True) / members
    lifted = system + (mean_level - (members - 1.0)) * (1.0 / members)
    frobenius = jnp.sqrt(jnp.sum(jnp.sum(lifted * lifted, axis=1, keepdims=True), axis=0, keepdims=True))
    root_iter = lifted / frobenius
    inv_iter = identity
    for sweep in range(NS_STEPS):
        product = root_iter if sweep == 0 else exact_dot(inv_iter, root_iter)
        correction = 1.5 * identity - 0.5 * product
        inv_iter = correction if sweep == 0 else exact_dot(correction, inv_iter)
        if sweep < NS_STEPS - 1:
            root_iter = exact_dot(root_iter, correction)
    inv_root = inv_iter / jnp.sqrt(frobenius) + (1.0 / math.sqrt(members - 1.0) - 1.0 / jnp.sqrt(mean_level)) * (
        1.0 / members
    )
    moved = mean_weights + math.sqrt(members - 1.0) * inv_root
    return 1.0 / members + moved - jnp.sum(moved, axis=0, keepdims=True) * (1.0 / members)


def mixers(transform, first, count):
    members = transform.shape[0]
    shape = (count * GROUP, members * GROUP)
    pick_out = (iota((shape[0], members), 0) // GROUP + first == iota((shape[0], members), 1)).astype(F32).astype(BF16)
    pick_in = (iota((shape[1], members), 0) // GROUP == iota((shape[1], members), 1)).astype(F32).astype(BF16)
    same = iota(shape, 0) % GROUP == iota(shape, 1) % GROUP
    pieces = []
    for piece in halves(transform):
        rows_of = dot(pick_out, piece, ((1,), (1,))).astype(BF16)
        pieces.append(jnp.where(same, dot(rows_of, pick_in, ((1,), (1,))), 0.0).astype(BF16))
    return jnp.concatenate(pieces, axis=0)


def mix(mixer, fields):
    mixed = dot(mixer, fields)
    count = mixed.shape[0] // 2
    return (mixed[:count] + mixed[count:]).astype(BF16)


def solve_kernel(partial_ref, share_ref, transform_ref, out_ref):
    members = transform_ref.shape[0]
    share_rows, feat_width = share_ref.shape[2:]
    per_row = LANES // members
    sums = jnp.sum(partial_ref[...], axis=0)
    spread_rows = jnp.concatenate(
        [jnp.broadcast_to(sums[r : r + 1], (per_row, LANES)) for r in range(members // per_row)], axis=0
    )
    keep = iota((members, LANES), 0) % per_row == iota((members, LANES), 1) // members
    folded = (iota((LANES, members), 0) % members == iota((LANES, members), 1)).astype(F32)
    gram = exact_dot(jnp.where(keep, spread_rows, 0.0), folded)
    proj_row = jnp.broadcast_to(sums[members // per_row : members // per_row + 1], (members, LANES))
    on_diagonal = iota((members, LANES), 0) == iota((members, LANES), 1)
    proj = jnp.sum(jnp.where(on_diagonal, proj_row, 0.0), axis=1, keepdims=True)
    transform = ensemble_transform(gram, proj)
    transform_ref[...] = transform
    mixer = mixers(transform, 0, members)
    for lower in range(0, share_rows, GROUP):
        fields = share_ref[:, :, lower : lower + GROUP, :].reshape(members * GROUP, feat_width)
        out_ref[:, :, lower : lower + GROUP, :] = mix(mixer, fields).reshape(*share_ref.shape[:2], GROUP, feat_width)


def solve(partials, share):
    members = share.shape[0] * share.shape[1]
    return pl.pallas_call(
        solve_kernel,
        out_shape=[jax.ShapeDtypeStruct((members, members), F32), jax.ShapeDtypeStruct(share.shape, BF16)],
        in_specs=[vmem_spec()] * 2,
        out_specs=[vmem_spec()] * 2,
        compiler_params=pltpu.CompilerParams(vmem_limit_bytes=VMEM_LIMIT),
        cost_estimate=pl.CostEstimate(flops=10**9, bytes_accessed=partials.size * 4, transcendentals=0),
        name="solve",
    )(partials, share)


def combine_kernel(index_ref, transform_ref, fields_ref, out_ref, mixer_buf):
    sources, own_members, rows, feat_width = fields_ref.shape

    @pl.when(pl.program_id(0) == 0)
    def _():
        mixer_buf[...] = mixers(transform_ref[...], index_ref[0] * own_members, own_members)

    mixer = mixer_buf[...]
    for lower in range(0, rows, GROUP):
        fields = fields_ref[:, :, lower : lower + GROUP, :].reshape(sources * own_members * GROUP, feat_width)
        out_ref[:, lower : lower + GROUP, :] = mix(mixer, fields).reshape(own_members, GROUP, feat_width)


def combine(index, transform, fields):
    sources, own_members, rows, feat_width = fields.shape
    block = min(64, rows)
    return pl.pallas_call(
        combine_kernel,
        grid=(rows // block,),
        out_shape=jax.ShapeDtypeStruct((own_members, 2 * rows, feat_width), BF16),
        in_specs=[
            smem_spec(),
            vmem_spec(),
            pl.BlockSpec((sources, own_members, block, feat_width), lambda i: (0, 0, i, 0)),
        ],
        out_specs=pl.BlockSpec((own_members, block, feat_width), lambda i: (0, i, 0)),
        scratch_shapes=[pltpu.VMEM((2 * own_members * GROUP, transform.shape[0] * GROUP), BF16)],
        compiler_params=pltpu.CompilerParams(vmem_limit_bytes=VMEM_LIMIT),
        cost_estimate=pl.CostEstimate(
            flops=4 * GROUP * own_members * fields.size, bytes_accessed=3 * fields.size, transcendentals=0
        ),
        name="combine",
    )(index, transform, fields)


def local(
    ens_state,
    attn_gain,
    ffn_gain,
    w_query,
    w_key,
    w_value,
    w_out,
    w_gate,
    w_up,
    down_weight,
    head_window,
    obs_token,
    obs_channel,
    obs_value,
    obs_var,
):
    own_members, row_count, feat_width = ens_state.shape
    mem_count = lax.axis_size("mem")
    tok_count = lax.axis_size("tok")
    device_count = mem_count * tok_count
    half_rows = row_count // 2
    share_rows = half_rows // mem_count
    first_pos = lax.axis_index("tok") * row_count
    index = lax.axis_index("mem").astype(jnp.int32).reshape(1)
    head, tail = edges(ens_state, WIN)
    left = lax.ppermute(tail, "tok", [(i, i + 1) for i in range(tok_count - 1)])
    right = lax.ppermute(head, "tok", [(i + 1, i) for i in range(tok_count - 1)])
    gains = [attn_gain.reshape(1, -1), ffn_gain.reshape(1, -1)]
    projected = project(ens_state, head_window.shape[0], gains[0], w_query, w_key, w_value)
    share_start = (first_pos + index * share_rows).astype(jnp.int32)
    grid = sample_grid(share_start, obs_token, obs_channel, obs_value, obs_var, share_rows, half_rows, feat_width)

    def forecast_of(half, halo, out_rows):
        ext_start = first_pos + half * half_rows - WIN
        place = jnp.stack([ext_start, row_count * tok_count]).astype(jnp.int32)
        weights = [w_key, w_value, w_out, w_gate, w_up, down_weight]
        return forward(place, head_window, ens_state, projected, halo, gains, weights, half, mem_count, out_rows)

    def exchanged(fields, axes="mem"):
        return lax.all_to_all(fields, axes, split_axis=0, concat_axis=0, tiled=True)

    early_all = exchanged(forecast_of(0, left, half_rows))
    late_share = exchanged(forecast_of(1, right, share_rows))
    partial = gram_partial(index, early_all, late_share, grid)
    partials = exchanged(jnp.broadcast_to(partial[None], (device_count, *partial.shape)), ("mem", "tok"))
    transform, late_mixed = solve(partials, late_share)
    late_back = exchanged(late_mixed)
    analysis = combine(index, transform, early_all)
    late_back = jnp.moveaxis(late_back, 0, 1).reshape(own_members, half_rows, feat_width)
    return lax.dynamic_update_slice(analysis, late_back, (0, half_rows, 0))


def solution(mesh):
    in_specs = (P("mem", "tok", None), *[P()] * 10, *[P("tok")] * 4)
    return jax.shard_map(local, mesh=mesh, in_specs=in_specs, out_specs=P("mem", "tok", None), check_vma=False)
```

```python
import functools
import math

import jax
import jax.numpy as jnp
from jax import lax
from jax.experimental import pallas as pl
from jax.experimental.pallas import tpu as pltpu
from jax.sharding import PartitionSpec as P

WIN = 256
NS_STEPS = 8
EPS = 1e-05
Q_ROWS = 128
GROUP = 16
LANES = 128
VMEM_LIMIT = 60 * 1024 * 1024

F32 = jnp.float32
BF16 = jnp.bfloat16


def dot(a, b, contract=((1,), (0,)), precision=None):
    return lax.dot_general(a, b, (contract, ((), ())), precision=precision, preferred_element_type=F32)


def exact_dot(a, b, contract=((1,), (0,))):
    return dot(a, b, contract, lax.Precision.HIGHEST)


def iota(shape, axis):
    return lax.broadcasted_iota(jnp.int32, shape, axis)


def halves(values):
    high = values.astype(BF16)
    return high, (values - high.astype(F32)).astype(BF16)


def rms_scaled(values, gain):
    return values * lax.rsqrt(jnp.mean(values * values, axis=-1, keepdims=True) + EPS) * gain


def vmem_spec():
    return pl.BlockSpec(memory_space=pltpu.VMEM)


def smem_spec():
    return pl.BlockSpec(memory_space=pltpu.SMEM)


def edges_kernel(own_ref, head_ref, tail_ref):
    reach = head_ref.shape[1]
    head_ref[...] = own_ref[:, :reach, :]
    tail_ref[...] = own_ref[:, own_ref.shape[1] - reach :, :]


def edges(own, reach):
    members, rows, feat_width = own.shape
    edge = pl.BlockSpec((1, reach, feat_width), lambda m: (m, 0, 0))
    return pl.pallas_call(
        edges_kernel,
        grid=(members,),
        out_shape=[jax.ShapeDtypeStruct((members, reach, feat_width), own.dtype)] * 2,
        in_specs=[pl.BlockSpec((1, rows, feat_width), lambda m: (m, 0, 0))],
        out_specs=[edge] * 2,
        compiler_params=pltpu.CompilerParams(vmem_limit_bytes=VMEM_LIMIT),
        cost_estimate=pl.CostEstimate(flops=0, bytes_accessed=8 * members * reach * feat_width, transcendentals=0),
        name="edges",
    )(own)


def sample_grid_kernel(stride, start_ref, token_ref, channel_ref, value_ref, var_ref, out_ref):
    rows, feat_width = out_ref.shape[1:]
    share_rows = rows // 2
    count = token_ref.shape[1]
    chunk = min(1024, count)
    total = jnp.zeros((4 * rows, feat_width), F32)
    for lower in range(0, count, chunk):
        part = slice(lower, lower + chunk)
        inv_var = 1.0 / var_ref[:, part]
        weighted = value_ref[:, part] * inv_var
        row = iota((rows, chunk), 0)
        row = jnp.where(row < share_rows, row, row + (stride - share_rows))
        here = row == token_ref[:, part] - start_ref[0]
        pieces = []
        for values in (inv_var, weighted):
            high = values.astype(BF16).astype(F32)
            pieces.append(jnp.where(here, high, 0.0).astype(BF16))
            pieces.append(jnp.where(here, values - high, 0.0).astype(BF16))
        channel_hot = jnp.where(iota((feat_width, chunk), 0) == channel_ref[:, part], 1.0, 0.0).astype(BF16)
        total += dot(jnp.concatenate(pieces, axis=0), channel_hot, ((1,), (1,)))
    out_ref[0] = total[:rows] + total[rows : 2 * rows]
    out_ref[1] = total[2 * rows : 3 * rows] + total[3 * rows :]


def sample_grid(start, obs_token, obs_channel, obs_value, obs_var, share_rows, stride, feat_width):
    count = obs_token.shape[0]
    rows = 2 * share_rows
    return pl.pallas_call(
        functools.partial(sample_grid_kernel, stride),
        out_shape=jax.ShapeDtypeStruct((2, rows, feat_width), F32),
        in_specs=[smem_spec()] + [vmem_spec()] * 4,
        out_specs=vmem_spec(),
        compiler_params=pltpu.CompilerParams(vmem_limit_bytes=VMEM_LIMIT),
        cost_estimate=pl.CostEstimate(flops=8 * rows * count * feat_width, bytes_accessed=16 * count, transcendentals=0),
        name="sample_grid",
    )(start, *(v.reshape(1, count) for v in (obs_token, obs_channel, obs_value, obs_var)))


def project_kernel(
    heads, own_ref, gain_ref, w_query_ref, w_key_ref, w_value_ref, query_ref, key_ref, value_ref, turned_ref
):
    @pl.when(pl.program_id(0) == 0)
    def _():
        turned_ref[...] = w_value_ref[...].astype(F32).T.astype(BF16)

    scale = math.log2(math.e) / math.sqrt(own_ref.shape[2] // heads)
    normed = rms_scaled(own_ref[0].astype(F32), gain_ref[...]).astype(BF16)
    query_ref[0] = (dot(normed, w_query_ref[...]) * scale).astype(BF16)
    key_ref[0] = dot(normed, w_key_ref[...]).astype(BF16)
    value_ref[0] = dot(turned_ref[...], normed, ((1,), (1,))).astype(BF16)


def project(own, heads, gain, w_query, w_key, w_value):
    members, rows, feat_width = own.shape
    block = pl.BlockSpec((1, rows, feat_width), lambda m: (m, 0, 0))
    return pl.pallas_call(
        functools.partial(project_kernel, heads),
        grid=(members,),
        out_shape=[
            jax.ShapeDtypeStruct((members, rows, feat_width), BF16),
            jax.ShapeDtypeStruct((members, rows, feat_width), BF16),
            jax.ShapeDtypeStruct((members, feat_width, rows), BF16),
        ],
        in_specs=[block] + [vmem_spec()] * 4,
        out_specs=[block, block, pl.BlockSpec((1, feat_width, rows), lambda m: (m, 0, 0))],
        scratch_shapes=[pltpu.VMEM((feat_width, feat_width), BF16)],
        compiler_params=pltpu.CompilerParams(vmem_limit_bytes=VMEM_LIMIT),
        cost_estimate=pl.CostEstimate(
            flops=6 * own.size * feat_width, bytes_accessed=8 * own.size, transcendentals=0
        ),
        name="project",
    )(own, gain, w_query, w_key, w_value)


def forward_kernel(
    halo_first,
    place_ref,
    window_ref,
    state_ref,
    query_ref,
    key_ref,
    value_ref,
    halo_ref,
    attn_gain_ref,
    ffn_gain_ref,
    w_key_ref,
    w_value_ref,
    w_out_ref,
    w_gate_ref,
    w_up_ref,
    down_weight_ref,
    *refs,
):
    out_ref, key_buf, value_buf, turned_buf, bias_buf, mixed_buf = refs[-6:]
    rows, feat_width = state_ref.shape[1:]
    reach = halo_ref.shape[1]
    own_rows = key_ref.shape[1]
    head_count = window_ref.shape[0]
    head_size = feat_width // head_count
    blocks = rows // Q_ROWS
    key_count = Q_ROWS + 2 * reach

    @pl.when(pl.program_id(0) == 0)
    def _():
        turned_buf[...] = w_value_ref[...].astype(F32).T.astype(BF16)
        value_buf[feat_width:, :] = jnp.ones((value_buf.shape[0] - feat_width, value_buf.shape[1]), BF16)
        apart = jnp.abs(iota((key_count, Q_ROWS), 0) - reach - iota((key_count, Q_ROWS), 1))
        for block in range(blocks):
            k_pos = place_ref[0] + block * Q_ROWS + iota((key_count, Q_ROWS), 0)
            inside = (k_pos >= 0) & (k_pos < place_ref[1])
            for head in range(head_count):
                bias_buf[block, head] = jnp.where(inside & (apart <= window_ref[head]), 0.0, -1e30)

    own_at, halo_at = (reach, 0) if halo_first else (0, own_rows)
    normed = rms_scaled(halo_ref[0].astype(F32), attn_gain_ref[...]).astype(BF16)
    key_buf[own_at : own_at + own_rows] = key_ref[0]
    value_buf[:feat_width, own_at : own_at + own_rows] = value_ref[0]
    key_buf[halo_at : halo_at + reach] = dot(normed, w_key_ref[...]).astype(BF16)
    value_buf[:feat_width, halo_at : halo_at + reach] = dot(turned_buf[...], normed, ((1,), (1,))).astype(BF16)

    column_head = iota((1, feat_width), 1) // head_size
    for block in range(blocks):
        start = block * Q_ROWS
        queries = query_ref[0, start : start + Q_ROWS, :]
        stacked = jnp.concatenate(
            [queries * (column_head == head).astype(F32).astype(BF16) for head in range(head_count)], axis=0
        )
        scores = dot(key_buf[start : start + key_count, :], stacked, ((1,), (1,)))
        weights = []
        for head in range(head_count):
            score_matrix = scores[:, head * Q_ROWS : (head + 1) * Q_ROWS] + bias_buf[block, head]
            row_top = jnp.max(score_matrix, axis=0, keepdims=True)
            weights.append(jnp.exp2((score_matrix - row_top).astype(BF16)))
        mixed_all = dot(value_buf[:, start : start + key_count], jnp.concatenate(weights, axis=1))
        mixed = []
        for head in range(head_count):
            columns = slice(head * Q_ROWS, (head + 1) * Q_ROWS)
            total = mixed_all[feat_width : feat_width + 1, columns]
            mixed.append(mixed_all[head * head_size : (head + 1) * head_size, columns] * (1.0 / total))
        mixed_buf[start : start + Q_ROWS, :] = jnp.concatenate(mixed, axis=0).T.astype(BF16)

    after = (state_ref[0].astype(F32) + dot(mixed_buf[...], w_out_ref[...])).astype(BF16)
    normed_mid = rms_scaled(after.astype(F32), ffn_gain_ref[...]).astype(BF16)
    gate = dot(normed_mid, w_gate_ref[...])
    hidden = (gate * (0.5 + 0.5 * jnp.tanh(0.5 * gate)) * dot(normed_mid, w_up_ref[...])).astype(BF16)
    forecast = (after.astype(F32) + dot(hidden, down_weight_ref[...])).astype(BF16)
    targets, _, out_rows, _ = out_ref.shape
    for target in range(targets):
        lower = target * out_rows if targets * out_rows == rows else 0
        out_ref[target, 0] = forecast[lower : lower + out_rows]


def forward(place, head_window, own, projected, halo, gains, weights, half, targets, out_rows, earlier):
    members, row_count, feat_width = own.shape
    rows, reach = row_count // 2, halo.shape[1]
    key_count = Q_ROWS + 2 * reach
    hidden_width = weights[3].shape[1]
    macs = members * rows * feat_width * (2 * feat_width + 3 * hidden_width + 8 * key_count)
    here = pl.BlockSpec((1, rows, feat_width), lambda m: (m, half, 0))
    ones_rows = 16
    return pl.pallas_call(
        functools.partial(forward_kernel, half == 0),
        grid=(members,),
        out_shape=jax.ShapeDtypeStruct((targets, members, out_rows, feat_width), BF16),
        in_specs=[
            smem_spec(),
            smem_spec(),
            here,
            here,
            pl.BlockSpec((1, row_count, feat_width), lambda m: (m, 0, 0)),
            pl.BlockSpec((1, feat_width, row_count), lambda m: (m, 0, 0)),
            pl.BlockSpec((1, reach, feat_width), lambda m: (m, 0, 0)),
        ]
        + [vmem_spec()] * (len(gains) + len(weights))
        + [pl.BlockSpec(memory_space=pl.ANY)] * len(earlier),
        out_specs=pl.BlockSpec((targets, 1, out_rows, feat_width), lambda m: (0, m, 0, 0)),
        scratch_shapes=[
            pltpu.VMEM((row_count + reach, feat_width), BF16),
            pltpu.VMEM((feat_width + ones_rows, row_count + reach), BF16),
            pltpu.VMEM((feat_width, feat_width), BF16),
            pltpu.VMEM((rows // Q_ROWS, head_window.shape[0], key_count, Q_ROWS), F32),
            pltpu.VMEM((rows, feat_width), BF16),
        ],
        compiler_params=pltpu.CompilerParams(vmem_limit_bytes=VMEM_LIMIT),
        cost_estimate=pl.CostEstimate(flops=2 * macs, bytes_accessed=6 * own.size, transcendentals=0),
        name="forward",
    )(place, head_window, own, *projected, halo, *gains, *weights, *earlier)


def gram_kernel(index_ref, early_ref, late_ref, grid_ref, out_ref):
    share_rows, feat_width = late_ref.shape[2:]
    members = late_ref.shape[0] * late_ref.shape[1]
    stack = members * GROUP
    total = jnp.zeros((stack, stack), F32)
    proj = jnp.zeros((members, GROUP, feat_width), F32)
    for half, ref in enumerate((early_ref, late_ref)):
        for lower in range(0, share_rows, GROUP):
            fields = ref[:, :, lower : lower + GROUP, :].reshape(members, GROUP, feat_width).astype(F32)
            mean = jnp.sum(fields, axis=0) * (1.0 / members)
            spread = fields - mean[None]
            part = slice(half * share_rows + lower, half * share_rows + lower + GROUP)
            weight = grid_ref[0, part, :]
            proj += spread * (grid_ref[1, part, :] - weight * mean)[None]
            high, low = halves(spread.reshape(stack, feat_width))
            w_high, w_low = halves((spread * weight[None]).reshape(stack, feat_width))
            last = ((1,), (1,))
            total += dot(w_high, high, last) + dot(w_high, low, last) + dot(w_low, high, last)
    same = iota((stack, stack), 0) % GROUP == iota((stack, stack), 1) % GROUP
    by_row = jnp.sum(jnp.where(same, total, 0.0).reshape(members, GROUP, stack), axis=1)
    folded = (iota((stack, LANES), 0) // GROUP == iota((stack, LANES), 1) % members).astype(F32)
    tiled = exact_dot(by_row, folded)
    per_row = LANES // members
    keep = iota((members, LANES), 0) % per_row == iota((members, LANES), 1) // members
    packed = jnp.sum(jnp.where(keep, tiled, 0.0).reshape(members // per_row, per_row, LANES), axis=1)
    proj_col = jnp.sum(jnp.sum(proj, axis=1), axis=1, keepdims=True)
    proj_row = jnp.sum(
        jnp.where(iota((members, LANES), 0) == iota((members, LANES), 1), proj_col, 0.0), axis=0, keepdims=True
    )
    filled = members // per_row + 1
    blank = jnp.zeros((out_ref.shape[0] - filled, LANES), F32)
    out_ref[...] = jnp.concatenate([packed, proj_row, blank], axis=0)


def gram_partial(index, early_all, late_share, grid):
    members = late_share.shape[0] * late_share.shape[1]
    filled = members * members // LANES + 1
    out_shape = (-(-filled // 8) * 8, LANES)
    return pl.pallas_call(
        gram_kernel,
        grid_spec=pltpu.PrefetchScalarGridSpec(
            num_scalar_prefetch=1,
            grid=(1,),
            in_specs=[
                pl.BlockSpec(late_share.shape, lambda i, index: (0, 0, index[0], 0)),
                pl.BlockSpec(late_share.shape, lambda i, index: (0, 0, 0, 0)),
                pl.BlockSpec(grid.shape, lambda i, index: (0, 0, 0)),
            ],
            out_specs=pl.BlockSpec(out_shape, lambda i, index: (0, 0)),
        ),
        out_shape=jax.ShapeDtypeStruct(out_shape, F32),
        compiler_params=pltpu.CompilerParams(vmem_limit_bytes=VMEM_LIMIT),
        cost_estimate=pl.CostEstimate(
            flops=3 * GROUP * members * members * grid.size, bytes_accessed=members * grid.size, transcendentals=0
        ),
        name="gram",
    )(index, early_all, late_share, grid)


def ensemble_transform(gram, proj):
    members = gram.shape[0]
    row, column = iota((members, members), 0), iota((members, members), 1)
    identity = (row == column).astype(F32)
    system = gram + (members - 1.0) * identity
    left, right = system, proj
    for pivot in range(members):
        is_pivot = iota((members, 1), 0) == pivot
        scale = 1.0 / left[pivot : pivot + 1, pivot : pivot + 1]
        pivot_row = left[pivot : pivot + 1, :] * scale
        pivot_right = right[pivot : pivot + 1, :] * scale
        factor = left[:, pivot : pivot + 1]
        left = jnp.where(is_pivot, pivot_row, left - factor * pivot_row)
        right = jnp.where(is_pivot, pivot_right, right - factor * pivot_right)
    mean_weights = right
    mean_level = jnp.sum(jnp.sum(system * identity, axis=1, keepdims=True), axis=0, keepdims=True) / members
    lifted = system + (mean_level - (members - 1.0)) * (1.0 / members)
    frobenius = jnp.sqrt(jnp.sum(jnp.sum(lifted * lifted, axis=1, keepdims=True), axis=0, keepdims=True))
    root_iter = lifted / frobenius
    inv_iter = identity
    for sweep in range(NS_STEPS):
        product = root_iter if sweep == 0 else exact_dot(inv_iter, root_iter)
        correction = 1.5 * identity - 0.5 * product
        inv_iter = correction if sweep == 0 else exact_dot(correction, inv_iter)
        if sweep < NS_STEPS - 1:
            root_iter = exact_dot(root_iter, correction)
    inv_root = inv_iter / jnp.sqrt(frobenius) + (1.0 / math.sqrt(members - 1.0) - 1.0 / jnp.sqrt(mean_level)) * (
        1.0 / members
    )
    moved = mean_weights + math.sqrt(members - 1.0) * inv_root
    return 1.0 / members + moved - jnp.sum(moved, axis=0, keepdims=True) * (1.0 / members)


def mixers(transform, first, count):
    members = transform.shape[0]
    shape = (count * GROUP, members * GROUP)
    pick_out = (iota((shape[0], members), 0) // GROUP + first == iota((shape[0], members), 1)).astype(F32).astype(BF16)
    pick_in = (iota((shape[1], members), 0) // GROUP == iota((shape[1], members), 1)).astype(F32).astype(BF16)
    same = iota(shape, 0) % GROUP == iota(shape, 1) % GROUP
    pieces = []
    for piece in halves(transform):
        rows_of = dot(pick_out, piece, ((1,), (1,))).astype(BF16)
        pieces.append(jnp.where(same, dot(rows_of, pick_in, ((1,), (1,))), 0.0).astype(BF16))
    return jnp.concatenate(pieces, axis=0)


def mix(mixer, fields):
    mixed = dot(mixer, fields)
    count = mixed.shape[0] // 2
    return (mixed[:count] + mixed[count:]).astype(BF16)


def solve_kernel(partial_ref, share_ref, transform_ref, out_ref):
    members = transform_ref.shape[0]
    share_rows, feat_width = share_ref.shape[2:]
    per_row = LANES // members
    sums = jnp.sum(partial_ref[...], axis=0)
    spread_rows = jnp.concatenate(
        [jnp.broadcast_to(sums[r : r + 1], (per_row, LANES)) for r in range(members // per_row)], axis=0
    )
    keep = iota((members, LANES), 0) % per_row == iota((members, LANES), 1) // members
    folded = (iota((LANES, members), 0) % members == iota((LANES, members), 1)).astype(F32)
    gram = exact_dot(jnp.where(keep, spread_rows, 0.0), folded)
    proj_row = jnp.broadcast_to(sums[members // per_row : members // per_row + 1], (members, LANES))
    on_diagonal = iota((members, LANES), 0) == iota((members, LANES), 1)
    proj = jnp.sum(jnp.where(on_diagonal, proj_row, 0.0), axis=1, keepdims=True)
    transform = ensemble_transform(gram, proj)
    transform_ref[...] = transform
    mixer = mixers(transform, 0, members)
    for lower in range(0, share_rows, GROUP):
        fields = share_ref[:, :, lower : lower + GROUP, :].reshape(members * GROUP, feat_width)
        out_ref[:, :, lower : lower + GROUP, :] = mix(mixer, fields).reshape(*share_ref.shape[:2], GROUP, feat_width)


def solve(partials, share):
    members = share.shape[0] * share.shape[1]
    return pl.pallas_call(
        solve_kernel,
        out_shape=[jax.ShapeDtypeStruct((members, members), F32), jax.ShapeDtypeStruct(share.shape, BF16)],
        in_specs=[vmem_spec()] * 2,
        out_specs=[vmem_spec()] * 2,
        compiler_params=pltpu.CompilerParams(vmem_limit_bytes=VMEM_LIMIT),
        cost_estimate=pl.CostEstimate(flops=10**9, bytes_accessed=partials.size * 4, transcendentals=0),
        name="solve",
    )(partials, share)


def combine_kernel(index_ref, transform_ref, fields_ref, out_ref, mixer_buf):
    sources, own_members, rows, feat_width = fields_ref.shape

    @pl.when(pl.program_id(0) == 0)
    def _():
        mixer_buf[...] = mixers(transform_ref[...], index_ref[0] * own_members, own_members)

    mixer = mixer_buf[...]
    for lower in range(0, rows, GROUP):
        fields = fields_ref[:, :, lower : lower + GROUP, :].reshape(sources * own_members * GROUP, feat_width)
        out_ref[:, lower : lower + GROUP, :] = mix(mixer, fields).reshape(own_members, GROUP, feat_width)


def combine(index, transform, fields):
    sources, own_members, rows, feat_width = fields.shape
    block = min(64, rows)
    return pl.pallas_call(
        combine_kernel,
        grid=(rows // block,),
        out_shape=jax.ShapeDtypeStruct((own_members, 2 * rows, feat_width), BF16),
        in_specs=[
            smem_spec(),
            vmem_spec(),
            pl.BlockSpec((sources, own_members, block, feat_width), lambda i: (0, 0, i, 0)),
        ],
        out_specs=pl.BlockSpec((own_members, block, feat_width), lambda i: (0, i, 0)),
        scratch_shapes=[pltpu.VMEM((2 * own_members * GROUP, transform.shape[0] * GROUP), BF16)],
        compiler_params=pltpu.CompilerParams(vmem_limit_bytes=VMEM_LIMIT),
        cost_estimate=pl.CostEstimate(
            flops=4 * GROUP * own_members * fields.size, bytes_accessed=3 * fields.size, transcendentals=0
        ),
        name="combine",
    )(index, transform, fields)


def local(
    ens_state,
    attn_gain,
    ffn_gain,
    w_query,
    w_key,
    w_value,
    w_out,
    w_gate,
    w_up,
    down_weight,
    head_window,
    obs_token,
    obs_channel,
    obs_value,
    obs_var,
):
    own_members, row_count, feat_width = ens_state.shape
    mem_count = lax.axis_size("mem")
    tok_count = lax.axis_size("tok")
    device_count = mem_count * tok_count
    half_rows = row_count // 2
    share_rows = half_rows // mem_count
    first_pos = lax.axis_index("tok") * row_count
    index = lax.axis_index("mem").astype(jnp.int32).reshape(1)
    head, tail = edges(ens_state, WIN)
    left = lax.ppermute(tail, "tok", [(i, i + 1) for i in range(tok_count - 1)])
    right = lax.ppermute(head, "tok", [(i + 1, i) for i in range(tok_count - 1)])
    gains = [attn_gain.reshape(1, -1), ffn_gain.reshape(1, -1)]
    projected = project(ens_state, head_window.shape[0], gains[0], w_query, w_key, w_value)
    share_start = (first_pos + index * share_rows).astype(jnp.int32)
    grid = sample_grid(share_start, obs_token, obs_channel, obs_value, obs_var, share_rows, half_rows, feat_width)

    def forecast_of(half, halo, out_rows, earlier=()):
        ext_start = first_pos + half * half_rows - WIN
        place = jnp.stack([ext_start, row_count * tok_count]).astype(jnp.int32)
        weights = [w_key, w_value, w_out, w_gate, w_up, down_weight]
        return forward(
            place, head_window, ens_state, projected, halo, gains, weights, half, mem_count, out_rows, earlier
        )

    def exchanged(fields, axes="mem"):
        return lax.all_to_all(fields, axes, split_axis=0, concat_axis=0, tiled=True)

    early = forecast_of(0, left, half_rows)
    early_all = exchanged(early)
    late_share = exchanged(forecast_of(1, right, share_rows, (early,)))
    partial = gram_partial(index, early_all, late_share, grid)
    partials = exchanged(jnp.broadcast_to(partial[None], (device_count, *partial.shape)), ("mem", "tok"))
    transform, late_mixed = solve(partials, late_share)
    late_back = exchanged(late_mixed)
    analysis = combine(index, transform, early_all)
    late_back = jnp.moveaxis(late_back, 0, 1).reshape(own_members, half_rows, feat_width)
    return lax.dynamic_update_slice(analysis, late_back, (0, half_rows, 0))


def solution(mesh):
    in_specs = (P("mem", "tok", None), *[P()] * 10, *[P("tok")] * 4)
    return jax.shard_map(local, mesh=mesh, in_specs=in_specs, out_specs=P("mem", "tok", None), check_vma=False)
```

```python
import functools
import math

import jax
import jax.numpy as jnp
from jax import lax
from jax.experimental import pallas as pl
from jax.experimental.pallas import tpu as pltpu
from jax.sharding import PartitionSpec as P

WIN = 256
NS_STEPS = 8
EPS = 1e-05
Q_ROWS = 128
GROUP = 16
LANES = 128
VMEM_LIMIT = 32 * 1024 * 1024
SAFE_SCORE = 56.0
HIDDEN_CHUNK = 256

F32 = jnp.float32
BF16 = jnp.bfloat16


def dot(a, b, contract=((1,), (0,)), precision=None):
    return lax.dot_general(a, b, (contract, ((), ())), precision=precision, preferred_element_type=F32)


def exact_dot(a, b, contract=((1,), (0,))):
    return dot(a, b, contract, lax.Precision.HIGHEST)


def iota(shape, axis):
    return lax.broadcasted_iota(jnp.int32, shape, axis)


def halves(values):
    high = values.astype(BF16)
    return high, (values - high.astype(F32)).astype(BF16)


def rms_scaled(values, gain):
    return values * lax.rsqrt(jnp.mean(values * values, axis=-1, keepdims=True) + EPS) * gain


def vmem_spec():
    return pl.BlockSpec(memory_space=pltpu.VMEM)


def smem_spec():
    return pl.BlockSpec(memory_space=pltpu.SMEM)


def sample_grid_kernel(start_ref, token_ref, channel_ref, value_ref, var_ref, out_ref):
    rows, feat_width = out_ref.shape[1:]
    count = token_ref.shape[1]
    chunk = min(1024, count)
    total = jnp.zeros((4 * rows, feat_width), F32)
    for lower in range(0, count, chunk):
        part = slice(lower, lower + chunk)
        inv_var = 1.0 / var_ref[:, part]
        weighted = value_ref[:, part] * inv_var
        here = iota((rows, chunk), 0) == token_ref[:, part] - start_ref[0]
        pieces = []
        for row in (inv_var, weighted):
            high = row.astype(BF16).astype(F32)
            pieces.append(jnp.where(here, high, 0.0).astype(BF16))
            pieces.append(jnp.where(here, row - high, 0.0).astype(BF16))
        channel_hot = jnp.where(iota((feat_width, chunk), 0) == channel_ref[:, part], 1.0, 0.0).astype(BF16)
        total += dot(jnp.concatenate(pieces, axis=0), channel_hot, ((1,), (1,)))
    out_ref[0] = total[:rows] + total[rows : 2 * rows]
    out_ref[1] = total[2 * rows : 3 * rows] + total[3 * rows :]


def sample_grid(start, obs_token, obs_channel, obs_value, obs_var, rows, feat_width):
    count = obs_token.shape[0]
    return pl.pallas_call(
        sample_grid_kernel,
        out_shape=jax.ShapeDtypeStruct((2, rows, feat_width), F32),
        in_specs=[smem_spec()] + [vmem_spec()] * 4,
        out_specs=vmem_spec(),
        compiler_params=pltpu.CompilerParams(vmem_limit_bytes=VMEM_LIMIT),
        cost_estimate=pl.CostEstimate(flops=8 * rows * count * feat_width, bytes_accessed=16 * count, transcendentals=0),
        name="sample_grid",
    )(start, *(v.reshape(1, count) for v in (obs_token, obs_channel, obs_value, obs_var)))


def project_kernel(heads, own_ref, gain_ref, w_query_ref, w_key_ref, w_value_ref, query_ref, key_ref, value_ref):
    scale = math.log2(math.e) / math.sqrt(own_ref.shape[2] // heads)
    normed = rms_scaled(own_ref[0].astype(F32), gain_ref[...]).astype(BF16)
    query_ref[0] = (dot(normed, w_query_ref[...]) * scale).astype(BF16)
    key_ref[0] = dot(normed, w_key_ref[...]).astype(BF16)
    value_ref[0] = dot(normed, w_value_ref[...]).astype(BF16)


def project(own, heads, gain, w_query, w_key, w_value):
    members, rows, feat_width = own.shape
    block = pl.BlockSpec((1, rows, feat_width), lambda m: (m, 0, 0))
    return pl.pallas_call(
        functools.partial(project_kernel, heads),
        grid=(members,),
        out_shape=[jax.ShapeDtypeStruct((members, rows, feat_width), BF16)] * 3,
        in_specs=[block] + [vmem_spec()] * 4,
        out_specs=[block] * 3,
        compiler_params=pltpu.CompilerParams(vmem_limit_bytes=VMEM_LIMIT),
        cost_estimate=pl.CostEstimate(
            flops=6 * own.size * feat_width, bytes_accessed=8 * own.size, transcendentals=0
        ),
        name="project",
    )(own, gain, w_query, w_key, w_value)


def forward_kernel(
    place_ref,
    window_ref,
    state_ref,
    query_ref,
    key_ref,
    value_ref,
    left_ref,
    right_ref,
    attn_gain_ref,
    ffn_gain_ref,
    w_key_ref,
    w_value_ref,
    w_out_ref,
    w_gate_ref,
    w_up_ref,
    down_weight_ref,
    out_ref,
    key_buf,
    value_buf,
    bias_buf,
    mixed_buf,
):
    rows, feat_width = state_ref.shape[1:]
    reach = left_ref.shape[1]
    head_count = window_ref.shape[0]
    head_size = feat_width // head_count
    blocks = rows // Q_ROWS
    key_count = Q_ROWS + 2 * reach

    @pl.when(pl.program_id(0) == 0)
    def _():
        apart = jnp.abs(iota((Q_ROWS, key_count), 1) - reach - iota((Q_ROWS, key_count), 0))
        for block in range(blocks):
            k_pos = place_ref[0] - reach + block * Q_ROWS + iota((Q_ROWS, key_count), 1)
            inside = (k_pos >= 0) & (k_pos < place_ref[1])
            for head in range(head_count):
                bias_buf[block, head] = jnp.where(inside & (apart <= window_ref[head]), 0.0, -1e30)

    key_buf[reach : reach + rows] = key_ref[0]
    value_buf[reach : reach + rows] = value_ref[0]
    for ref, lower in ((left_ref, 0), (right_ref, reach + rows)):
        normed = rms_scaled(ref[0].astype(F32), attn_gain_ref[...]).astype(BF16)
        key_buf[lower : lower + reach] = dot(normed, w_key_ref[...]).astype(BF16)
        value_buf[lower : lower + reach] = dot(normed, w_value_ref[...]).astype(BF16)

    column_head = iota((1, feat_width), 1) // head_size
    head_masks = [(column_head == head).astype(F32).astype(BF16) for head in range(head_count)]
    by_head = (iota((feat_width, LANES), 0) // head_size == iota((feat_width, LANES), 1)).astype(F32).astype(BF16)

    def largest_norm(values):
        squares = values.astype(F32)
        return jnp.max(dot((squares * squares).astype(BF16), by_head), axis=0, keepdims=True)

    bound = jnp.max(largest_norm(query_ref[0]) * largest_norm(key_buf[...])) * 1.02
    safe = bound <= SAFE_SCORE * SAFE_SCORE

    def joined_heads(mixed_all, totals, count):
        mixed = mixed_all[:count] * (1.0 / totals[0])
        for head in range(1, head_count):
            part = mixed_all[head * count : (head + 1) * count] * (1.0 / totals[head])
            mixed = jnp.where(column_head == head, part, mixed)
        return mixed.astype(BF16)

    @pl.when(safe)
    def _():
        pair = 2 * Q_ROWS
        span = pair + 2 * reach
        corner = jnp.zeros((Q_ROWS, Q_ROWS), BF16)
        for start in range(0, rows, pair):
            queries = query_ref[0, start : start + pair, :]
            stacked = jnp.concatenate([queries * mask for mask in head_masks], axis=0)
            scores = dot(stacked, key_buf[start : start + span, :], ((1,), (1,)))
            weights, totals = [], []
            for head in range(head_count):
                top = head * pair
                bias = [bias_buf[start // Q_ROWS + part, head] for part in range(2)]
                upper = jnp.exp2(scores[top : top + Q_ROWS, :key_count] + bias[0])
                lower = jnp.exp2(scores[top + Q_ROWS : top + pair, Q_ROWS:] + bias[1])
                totals.append(
                    jnp.concatenate([jnp.sum(v, axis=-1, keepdims=True) for v in (upper, lower)], axis=0)
                )
                weights.append(jnp.concatenate([upper.astype(BF16), corner], axis=1))
                weights.append(jnp.concatenate([corner, lower.astype(BF16)], axis=1))
            mixed_all = dot(jnp.concatenate(weights, axis=0), value_buf[start : start + span, :])
            mixed_buf[start : start + pair, :] = joined_heads(mixed_all, totals, pair)

    @pl.when(jnp.logical_not(safe))
    def _():
        def one_block(block, carry):
            start = pl.multiple_of(block * Q_ROWS, Q_ROWS)
            queries = query_ref[0, pl.ds(start, Q_ROWS), :]
            stacked = jnp.concatenate([queries * mask for mask in head_masks], axis=0)
            scores = dot(stacked, key_buf[pl.ds(start, key_count), :], ((1,), (1,)))
            weights, totals = [], []
            for head in range(head_count):
                score_matrix = scores[head * Q_ROWS : (head + 1) * Q_ROWS] + bias_buf[block, head]
                expo = jnp.exp2(score_matrix - jnp.max(score_matrix, axis=-1, keepdims=True))
                totals.append(jnp.sum(expo, axis=-1, keepdims=True))
                weights.append(expo.astype(BF16))
            mixed_all = dot(jnp.concatenate(weights, axis=0), value_buf[pl.ds(start, key_count), :])
            mixed_buf[pl.ds(start, Q_ROWS), :] = joined_heads(mixed_all, totals, Q_ROWS)
            return carry

        lax.fori_loop(0, blocks, one_block, 0)

    after = (state_ref[0].astype(F32) + dot(mixed_buf[...], w_out_ref[...])).astype(BF16)
    normed_mid = rms_scaled(after.astype(F32), ffn_gain_ref[...]).astype(BF16)
    forecast = after.astype(F32)
    for lower in range(0, w_gate_ref.shape[1], HIDDEN_CHUNK):
        part = slice(lower, lower + HIDDEN_CHUNK)
        gate = dot(normed_mid, w_gate_ref[:, part])
        hidden = (gate * (0.5 + 0.5 * jnp.tanh(0.5 * gate)) * dot(normed_mid, w_up_ref[:, part])).astype(BF16)
        forecast += dot(hidden, down_weight_ref[part, :])
    forecast = forecast.astype(BF16)
    shares, _, share_rows, _ = out_ref.shape
    for share in range(shares):
        out_ref[share, 0] = forecast[share * share_rows : (share + 1) * share_rows]


def forward(place, head_window, own, projected, left, right, gains, weights, shares):
    members, row_count, feat_width = own.shape
    reach = left.shape[1]
    key_count = Q_ROWS + 2 * reach
    hidden_width = weights[3].shape[1]
    macs = members * row_count * feat_width * (3 * feat_width + 3 * hidden_width + 8 * key_count)
    member_block = pl.BlockSpec((1, row_count, feat_width), lambda m: (m, 0, 0))
    edge_block = pl.BlockSpec((1, reach, feat_width), lambda m: (m, 0, 0))
    return pl.pallas_call(
        forward_kernel,
        grid=(members,),
        out_shape=jax.ShapeDtypeStruct((shares, members, row_count // shares, feat_width), BF16),
        in_specs=[smem_spec()] * 2
        + [member_block] * (1 + len(projected))
        + [edge_block] * 2
        + [vmem_spec()] * (len(gains) + len(weights)),
        out_specs=pl.BlockSpec((shares, 1, row_count // shares, feat_width), lambda m: (0, m, 0, 0)),
        scratch_shapes=[
            pltpu.VMEM((row_count + 2 * reach, feat_width), BF16),
            pltpu.VMEM((row_count + 2 * reach, feat_width), BF16),
            pltpu.VMEM((row_count // Q_ROWS, head_window.shape[0], Q_ROWS, key_count), F32),
            pltpu.VMEM((row_count, feat_width), BF16),
        ],
        compiler_params=pltpu.CompilerParams(vmem_limit_bytes=VMEM_LIMIT),
        cost_estimate=pl.CostEstimate(flops=2 * macs, bytes_accessed=10 * own.size, transcendentals=0),
        name="forward",
    )(place, head_window, own, *projected, left, right, *gains, *weights)


def gram_kernel(share_ref, grid_ref, out_ref):
    members, rows, feat_width = share_ref.shape
    stack = members * GROUP
    total = jnp.zeros((stack, stack), F32)
    proj = jnp.zeros((members, GROUP, feat_width), F32)
    for lower in range(0, rows, GROUP):
        part = slice(lower, lower + GROUP)
        fields = share_ref[:, part, :].astype(F32)
        mean = jnp.sum(fields, axis=0) * (1.0 / members)
        spread = fields - mean[None]
        weight = grid_ref[0, part, :]
        proj += spread * (grid_ref[1, part, :] - weight * mean)[None]
        high, low = halves(spread.reshape(stack, feat_width))
        w_high, w_low = halves((spread * weight[None]).reshape(stack, feat_width))
        last = ((1,), (1,))
        total += dot(w_high, high, last) + dot(w_high, low, last) + dot(w_low, high, last)
    same = iota((stack, stack), 0) % GROUP == iota((stack, stack), 1) % GROUP
    by_row = jnp.sum(jnp.where(same, total, 0.0).reshape(members, GROUP, stack), axis=1)
    folded = (iota((stack, LANES), 0) // GROUP == iota((stack, LANES), 1) % members).astype(F32)
    tiled = exact_dot(by_row, folded)
    per_row = LANES // members
    keep = iota((members, LANES), 0) % per_row == iota((members, LANES), 1) // members
    packed = jnp.sum(jnp.where(keep, tiled, 0.0).reshape(members // per_row, per_row, LANES), axis=1)
    proj_col = jnp.sum(jnp.sum(proj, axis=1), axis=1, keepdims=True)
    proj_row = jnp.sum(
        jnp.where(iota((members, LANES), 0) == iota((members, LANES), 1), proj_col, 0.0), axis=0, keepdims=True
    )
    filled = members // per_row + 1
    blank = jnp.zeros((out_ref.shape[0] - filled, LANES), F32)
    out_ref[...] = jnp.concatenate([packed, proj_row, blank], axis=0)


def gram_partial(share, grid):
    members = share.shape[0]
    filled = members * members // LANES + 1
    return pl.pallas_call(
        gram_kernel,
        out_shape=jax.ShapeDtypeStruct((-(-filled // 8) * 8, LANES), F32),
        in_specs=[vmem_spec()] * 2,
        out_specs=vmem_spec(),
        compiler_params=pltpu.CompilerParams(vmem_limit_bytes=VMEM_LIMIT),
        cost_estimate=pl.CostEstimate(
            flops=6 * GROUP * members * share.size, bytes_accessed=2 * share.size, transcendentals=0
        ),
        name="gram",
    )(share, grid)


def ensemble_transform(gram, proj):
    members = gram.shape[0]
    row, column = iota((members, members), 0), iota((members, members), 1)
    identity = (row == column).astype(F32)
    system = gram + (members - 1.0) * identity
    left, right = system, proj
    for pivot in range(members):
        is_pivot = iota((members, 1), 0) == pivot
        scale = 1.0 / left[pivot : pivot + 1, pivot : pivot + 1]
        pivot_row = left[pivot : pivot + 1, :] * scale
        pivot_right = right[pivot : pivot + 1, :] * scale
        factor = left[:, pivot : pivot + 1]
        left = jnp.where(is_pivot, pivot_row, left - factor * pivot_row)
        right = jnp.where(is_pivot, pivot_right, right - factor * pivot_right)
    mean_weights = right
    mean_level = jnp.sum(jnp.sum(system * identity, axis=1, keepdims=True), axis=0, keepdims=True) / members
    lifted = system + (mean_level - (members - 1.0)) * (1.0 / members)
    frobenius = jnp.sqrt(jnp.sum(jnp.sum(lifted * lifted, axis=1, keepdims=True), axis=0, keepdims=True))
    root_iter = lifted / frobenius
    inv_iter = identity
    for sweep in range(NS_STEPS):
        product = root_iter if sweep == 0 else exact_dot(inv_iter, root_iter)
        correction = 1.5 * identity - 0.5 * product
        inv_iter = correction if sweep == 0 else exact_dot(correction, inv_iter)
        if sweep < NS_STEPS - 1:
            root_iter = exact_dot(root_iter, correction)
    inv_root = inv_iter / jnp.sqrt(frobenius) + (1.0 / math.sqrt(members - 1.0) - 1.0 / jnp.sqrt(mean_level)) * (
        1.0 / members
    )
    moved = mean_weights + math.sqrt(members - 1.0) * inv_root
    return 1.0 / members + moved - jnp.sum(moved, axis=0, keepdims=True) * (1.0 / members)


def combine_kernel(partial_ref, share_ref, out_ref):
    members, rows, feat_width = share_ref.shape
    stack = members * GROUP
    per_row = LANES // members
    sums = jnp.sum(partial_ref[...], axis=0)
    spread_rows = jnp.concatenate(
        [jnp.broadcast_to(sums[r : r + 1], (per_row, LANES)) for r in range(members // per_row)], axis=0
    )
    keep = iota((members, LANES), 0) % per_row == iota((members, LANES), 1) // members
    folded = (iota((LANES, members), 0) % members == iota((LANES, members), 1)).astype(F32)
    gram = exact_dot(jnp.where(keep, spread_rows, 0.0), folded)
    proj_row = jnp.broadcast_to(sums[members // per_row : members // per_row + 1], (members, LANES))
    on_diagonal = iota((members, LANES), 0) == iota((members, LANES), 1)
    proj = jnp.sum(jnp.where(on_diagonal, proj_row, 0.0), axis=1, keepdims=True)
    transform = ensemble_transform(gram, proj)
    pick = (iota((stack, members), 0) // GROUP == iota((stack, members), 1)).astype(F32).astype(BF16)
    same = iota((stack, stack), 0) % GROUP == iota((stack, stack), 1) % GROUP
    mixers = []
    for piece in halves(transform):
        rows_of = dot(pick, piece, ((1,), (1,))).astype(BF16)
        mixers.append(jnp.where(same, dot(rows_of, pick, ((1,), (1,))), 0.0).astype(BF16))
    for lower in range(0, rows, GROUP):
        fields = share_ref[:, lower : lower + GROUP, :].reshape(stack, feat_width)
        mixed = dot(mixers[0], fields) + dot(mixers[1], fields)
        out_ref[:, lower : lower + GROUP, :] = mixed.astype(BF16).reshape(members, GROUP, feat_width)


def combine(partials, share):
    members = share.shape[0]
    return pl.pallas_call(
        combine_kernel,
        out_shape=jax.ShapeDtypeStruct(share.shape, BF16),
        in_specs=[vmem_spec()] * 2,
        out_specs=vmem_spec(),
        compiler_params=pltpu.CompilerParams(vmem_limit_bytes=VMEM_LIMIT),
        cost_estimate=pl.CostEstimate(
            flops=4 * GROUP * members * share.size, bytes_accessed=4 * share.size, transcendentals=0
        ),
        name="combine",
    )(partials, share)


def local(
    ens_state,
    attn_gain,
    ffn_gain,
    w_query,
    w_key,
    w_value,
    w_out,
    w_gate,
    w_up,
    down_weight,
    head_window,
    obs_token,
    obs_channel,
    obs_value,
    obs_var,
):
    own_members, row_count, feat_width = ens_state.shape
    mem_count = lax.axis_size("mem")
    tok_count = lax.axis_size("tok")
    device_count = mem_count * tok_count
    members = own_members * mem_count
    share_rows = row_count // mem_count
    first_pos = lax.axis_index("tok") * row_count
    up = [(i, i + 1) for i in range(tok_count - 1)]
    down = [(i + 1, i) for i in range(tok_count - 1)]
    left = lax.ppermute(ens_state[:, row_count - WIN :], "tok", up)
    right = lax.ppermute(ens_state[:, :WIN], "tok", down)
    share_start = first_pos + lax.axis_index("mem") * share_rows
    grid = sample_grid(
        share_start.astype(jnp.int32).reshape(1), obs_token, obs_channel, obs_value, obs_var, share_rows, feat_width
    )
    place = jnp.stack([first_pos, row_count * tok_count]).astype(jnp.int32)
    gains = [attn_gain.reshape(1, -1), ffn_gain.reshape(1, -1)]
    projected = project(ens_state, head_window.shape[0], gains[0], w_query, w_key, w_value)
    weights = [w_key, w_value, w_out, w_gate, w_up, down_weight]
    forecast = forward(place, head_window, ens_state, projected, left, right, gains, weights, mem_count)
    share = lax.all_to_all(forecast, "mem", split_axis=0, concat_axis=0, tiled=True)
    share = share.reshape(members, share_rows, feat_width)
    partial = gram_partial(share, grid)
    partials = lax.all_to_all(
        jnp.broadcast_to(partial[None], (device_count, *partial.shape)),
        ("mem", "tok"),
        split_axis=0,
        concat_axis=0,
        tiled=True,
    )
    mixed = combine(partials, share).reshape(mem_count, own_members, share_rows, feat_width)
    mixed = lax.all_to_all(mixed, "mem", split_axis=0, concat_axis=0, tiled=True)
    return jnp.moveaxis(mixed, 0, 1).reshape(own_members, row_count, feat_width)


def solution(mesh):
    in_specs = (P("mem", "tok", None), *[P()] * 10, *[P("tok")] * 4)
    return jax.shard_map(local, mesh=mesh, in_specs=in_specs, out_specs=P("mem", "tok", None), check_vma=False)
```

```python
import functools
import math

import jax
import jax.numpy as jnp
from jax import lax
from jax.experimental import pallas as pl
from jax.experimental.pallas import tpu as pltpu
from jax.sharding import PartitionSpec as P

WIN = 256
NS_STEPS = 8
EPS = 1e-05
Q_ROWS = 128
GROUP = 16
LANES = 128
VMEM_LIMIT = 32 * 1024 * 1024
SAFE_SCORE = 56.0
HIDDEN_CHUNK = 256

F32 = jnp.float32
BF16 = jnp.bfloat16


def dot(a, b, contract=((1,), (0,)), precision=None):
    return lax.dot_general(a, b, (contract, ((), ())), precision=precision, preferred_element_type=F32)


def exact_dot(a, b, contract=((1,), (0,))):
    return dot(a, b, contract, lax.Precision.HIGHEST)


def iota(shape, axis):
    return lax.broadcasted_iota(jnp.int32, shape, axis)


def halves(values):
    high = values.astype(BF16)
    return high, (values - high.astype(F32)).astype(BF16)


def rms_scaled(values, gain):
    return values * lax.rsqrt(jnp.mean(values * values, axis=-1, keepdims=True) + EPS) * gain


def vmem_spec():
    return pl.BlockSpec(memory_space=pltpu.VMEM)


def smem_spec():
    return pl.BlockSpec(memory_space=pltpu.SMEM)


def sample_grid_kernel(start_ref, token_ref, channel_ref, value_ref, var_ref, out_ref):
    rows, feat_width = out_ref.shape[1:]
    count = token_ref.shape[1]
    chunk = min(1024, count)
    total = jnp.zeros((4 * rows, feat_width), F32)
    for lower in range(0, count, chunk):
        part = slice(lower, lower + chunk)
        inv_var = 1.0 / var_ref[:, part]
        weighted = value_ref[:, part] * inv_var
        here = iota((rows, chunk), 0) == token_ref[:, part] - start_ref[0]
        pieces = []
        for row in (inv_var, weighted):
            high = row.astype(BF16).astype(F32)
            pieces.append(jnp.where(here, high, 0.0).astype(BF16))
            pieces.append(jnp.where(here, row - high, 0.0).astype(BF16))
        channel_hot = jnp.where(iota((feat_width, chunk), 0) == channel_ref[:, part], 1.0, 0.0).astype(BF16)
        total += dot(jnp.concatenate(pieces, axis=0), channel_hot, ((1,), (1,)))
    out_ref[0] = total[:rows] + total[rows : 2 * rows]
    out_ref[1] = total[2 * rows : 3 * rows] + total[3 * rows :]


def sample_grid(start, obs_token, obs_channel, obs_value, obs_var, rows, feat_width):
    count = obs_token.shape[0]
    return pl.pallas_call(
        sample_grid_kernel,
        out_shape=jax.ShapeDtypeStruct((2, rows, feat_width), F32),
        in_specs=[smem_spec()] + [vmem_spec()] * 4,
        out_specs=vmem_spec(),
        compiler_params=pltpu.CompilerParams(vmem_limit_bytes=VMEM_LIMIT),
        cost_estimate=pl.CostEstimate(flops=8 * rows * count * feat_width, bytes_accessed=16 * count, transcendentals=0),
        name="sample_grid",
    )(start, *(v.reshape(1, count) for v in (obs_token, obs_channel, obs_value, obs_var)))


def head_lanes(feat_width, heads):
    lane_head = iota((feat_width, LANES), 0) // (feat_width // heads)
    return (lane_head == iota((feat_width, LANES), 1)).astype(F32).astype(BF16)


def largest_norms(values, heads):
    squares = dot((values * values).astype(BF16), head_lanes(values.shape[1], heads))
    return jnp.max(squares, axis=0, keepdims=True)


def project_kernel(
    heads, own_ref, gain_ref, w_query_ref, w_key_ref, w_value_ref, query_ref, key_ref, value_ref, norm_ref
):
    scale = math.log2(math.e) / math.sqrt(own_ref.shape[2] // heads)
    normed = rms_scaled(own_ref[0].astype(F32), gain_ref[...]).astype(BF16)
    queries = dot(normed, w_query_ref[...]) * scale
    keys = dot(normed, w_key_ref[...])
    query_ref[0] = queries.astype(BF16)
    key_ref[0] = keys.T.astype(BF16)
    value_ref[0] = dot(normed, w_value_ref[...]).astype(BF16)
    blank = jnp.zeros((norm_ref.shape[1] - 2, LANES), F32)
    norm_ref[0] = jnp.concatenate([largest_norms(queries, heads), largest_norms(keys, heads), blank], axis=0)


def project(own, heads, gain, w_query, w_key, w_value):
    members, rows, feat_width = own.shape
    upright = (members, rows, feat_width)
    shapes = [upright, (members, feat_width, rows), upright]
    norm_shape = (members, 8, LANES)

    def spec(shape):
        return pl.BlockSpec((1, *shape[1:]), lambda m: (m, 0, 0))

    return pl.pallas_call(
        functools.partial(project_kernel, heads),
        grid=(members,),
        out_shape=[jax.ShapeDtypeStruct(v, BF16) for v in shapes] + [jax.ShapeDtypeStruct(norm_shape, F32)],
        in_specs=[spec(upright)] + [vmem_spec()] * 4,
        out_specs=[spec(v) for v in (*shapes, norm_shape)],
        compiler_params=pltpu.CompilerParams(vmem_limit_bytes=VMEM_LIMIT),
        cost_estimate=pl.CostEstimate(
            flops=6 * own.size * feat_width, bytes_accessed=8 * own.size, transcendentals=0
        ),
        name="project",
    )(own, gain, w_query, w_key, w_value)


def forward_kernel(
    place_ref,
    window_ref,
    state_ref,
    query_ref,
    key_ref,
    value_ref,
    norm_ref,
    left_ref,
    right_ref,
    attn_gain_ref,
    ffn_gain_ref,
    w_key_ref,
    w_value_ref,
    w_out_ref,
    w_gate_ref,
    w_up_ref,
    down_weight_ref,
    out_ref,
    key_buf,
    value_buf,
    bias_buf,
    mixed_buf,
):
    rows, feat_width = state_ref.shape[1:]
    reach = left_ref.shape[1]
    head_count = window_ref.shape[0]
    head_size = feat_width // head_count
    group_heads = LANES // head_size
    blocks = rows // Q_ROWS
    key_count = Q_ROWS + 2 * reach

    @pl.when(pl.program_id(0) == 0)
    def _():
        apart = jnp.abs(iota((Q_ROWS, key_count), 1) - reach - iota((Q_ROWS, key_count), 0))
        for block in range(blocks):
            k_pos = place_ref[0] - reach + block * Q_ROWS + iota((Q_ROWS, key_count), 1)
            inside = (k_pos >= 0) & (k_pos < place_ref[1])
            for head in range(head_count):
                bias_buf[block, head] = jnp.where(inside & (apart <= window_ref[head]), 0.0, -1e30)

    key_buf[:, reach : reach + rows] = key_ref[0]
    value_buf[reach : reach + rows] = value_ref[0]
    key_norms = norm_ref[0, 1:2, :]
    for ref, lower in ((left_ref, 0), (right_ref, reach + rows)):
        normed = rms_scaled(ref[0].astype(F32), attn_gain_ref[...]).astype(BF16)
        keys = dot(normed, w_key_ref[...])
        key_norms = jnp.maximum(key_norms, largest_norms(keys, head_count))
        key_buf[:, lower : lower + reach] = keys.T.astype(BF16)
        value_buf[lower : lower + reach] = dot(normed, w_value_ref[...]).astype(BF16)

    bound = jnp.max(norm_ref[0, 0:1, :] * key_norms) * 1.05
    safe = bound <= SAFE_SCORE * SAFE_SCORE

    lane_head = iota((1, LANES), 1) // head_size
    head_masks = [(lane_head == head).astype(F32).astype(BF16) for head in range(group_heads)]

    def scores_of(start, count, group):
        lanes = slice(group * LANES, (group + 1) * LANES)
        queries = query_ref[0, pl.ds(start, count), lanes]
        stacked = jnp.concatenate([queries * mask for mask in head_masks], axis=0)
        return dot(stacked, key_buf[lanes, pl.ds(start, count + 2 * reach)])

    def mix_values(start, count, group, weights, totals):
        lanes = slice(group * LANES, (group + 1) * LANES)
        mixed_all = dot(jnp.concatenate(weights, axis=0), value_buf[pl.ds(start, count + 2 * reach), lanes])
        mixed = mixed_all[:count] * (1.0 / totals[0])
        for head in range(1, group_heads):
            part = mixed_all[head * count : (head + 1) * count] * (1.0 / totals[head])
            mixed = jnp.where(lane_head == head, part, mixed)
        mixed_buf[pl.ds(start, count), lanes] = mixed.astype(BF16)

    groups = head_count // group_heads

    @pl.when(safe)
    def _():
        pair = 2 * Q_ROWS
        corner = jnp.zeros((Q_ROWS, Q_ROWS), BF16)
        units = [(start, group) for start in range(0, rows, pair) for group in range(groups)]
        scores = scores_of(units[0][0], pair, units[0][1])
        for at, (start, group) in enumerate(units):
            following = scores_of(units[at + 1][0], pair, units[at + 1][1]) if at + 1 < len(units) else None
            weights, totals = [], []
            for head in range(group_heads):
                top = head * pair
                bias = [bias_buf[start // Q_ROWS + part, group * group_heads + head] for part in range(2)]
                upper = jnp.exp2(scores[top : top + Q_ROWS, :key_count] + bias[0])
                lower = jnp.exp2(scores[top + Q_ROWS : top + pair, Q_ROWS:] + bias[1])
                totals.append(
                    jnp.concatenate([jnp.sum(v, axis=-1, keepdims=True) for v in (upper, lower)], axis=0)
                )
                weights.append(jnp.concatenate([upper.astype(BF16), corner], axis=1))
                weights.append(jnp.concatenate([corner, lower.astype(BF16)], axis=1))
            mix_values(start, pair, group, weights, totals)
            scores = following

    @pl.when(jnp.logical_not(safe))
    def _():
        for block in range(blocks):
            start = block * Q_ROWS
            for group in range(groups):
                scores = scores_of(start, Q_ROWS, group)
                weights, totals = [], []
                for head in range(group_heads):
                    score_matrix = scores[head * Q_ROWS : (head + 1) * Q_ROWS]
                    score_matrix = score_matrix + bias_buf[block, group * group_heads + head]
                    expo = jnp.exp2(score_matrix - jnp.max(score_matrix, axis=-1, keepdims=True))
                    totals.append(jnp.sum(expo, axis=-1, keepdims=True))
                    weights.append(expo.astype(BF16))
                mix_values(start, Q_ROWS, group, weights, totals)

    after = (state_ref[0].astype(F32) + dot(mixed_buf[...], w_out_ref[...])).astype(BF16)
    normed_mid = rms_scaled(after.astype(F32), ffn_gain_ref[...]).astype(BF16)
    forecast = after.astype(F32)
    for lower in range(0, w_gate_ref.shape[1], HIDDEN_CHUNK):
        part = slice(lower, lower + HIDDEN_CHUNK)
        gate = 0.5 * dot(normed_mid, w_gate_ref[:, part])
        hidden = (gate * (1.0 + jnp.tanh(gate)) * dot(normed_mid, w_up_ref[:, part])).astype(BF16)
        forecast += dot(hidden, down_weight_ref[part, :])
    forecast = forecast.astype(BF16)
    shares, _, share_rows, _ = out_ref.shape
    for share in range(shares):
        out_ref[share, 0] = forecast[share * share_rows : (share + 1) * share_rows]


def forward(place, head_window, own, projected, left, right, gains, weights, shares):
    members, row_count, feat_width = own.shape
    reach = left.shape[1]
    key_count = Q_ROWS + 2 * reach
    hidden_width = weights[3].shape[1]
    macs = members * row_count * feat_width * (3 * feat_width + 3 * hidden_width + 8 * key_count)
    edge_block = pl.BlockSpec((1, reach, feat_width), lambda m: (m, 0, 0))
    return pl.pallas_call(
        forward_kernel,
        grid=(members,),
        out_shape=jax.ShapeDtypeStruct((shares, members, row_count // shares, feat_width), BF16),
        in_specs=[smem_spec()] * 2
        + [pl.BlockSpec((1, *v.shape[1:]), lambda m: (m, 0, 0)) for v in (own, *projected)]
        + [edge_block] * 2
        + [vmem_spec()] * (len(gains) + len(weights)),
        out_specs=pl.BlockSpec((shares, 1, row_count // shares, feat_width), lambda m: (0, m, 0, 0)),
        scratch_shapes=[
            pltpu.VMEM((feat_width, row_count + 2 * reach), BF16),
            pltpu.VMEM((row_count + 2 * reach, feat_width), BF16),
            pltpu.VMEM((row_count // Q_ROWS, head_window.shape[0], Q_ROWS, key_count), F32),
            pltpu.VMEM((row_count, feat_width), BF16),
        ],
        compiler_params=pltpu.CompilerParams(vmem_limit_bytes=VMEM_LIMIT),
        cost_estimate=pl.CostEstimate(flops=2 * macs, bytes_accessed=10 * own.size, transcendentals=0),
        name="forward",
    )(place, head_window, own, *projected, left, right, *gains, *weights)


def gram_kernel(share_ref, grid_ref, out_ref):
    members, rows, feat_width = share_ref.shape
    stack = members * GROUP
    total = jnp.zeros((stack, stack), F32)
    proj = jnp.zeros((members, GROUP, feat_width), F32)
    for lower in range(0, rows, GROUP):
        part = slice(lower, lower + GROUP)
        fields = share_ref[:, part, :].astype(F32)
        mean = jnp.sum(fields, axis=0) * (1.0 / members)
        spread = fields - mean[None]
        weight = grid_ref[0, part, :]
        proj += spread * (grid_ref[1, part, :] - weight * mean)[None]
        high, low = halves(spread.reshape(stack, feat_width))
        w_high, w_low = halves((spread * weight[None]).reshape(stack, feat_width))
        last = ((1,), (1,))
        total += dot(w_high, high, last) + dot(w_high, low, last) + dot(w_low, high, last)
    same = iota((stack, stack), 0) % GROUP == iota((stack, stack), 1) % GROUP
    by_row = jnp.sum(jnp.where(same, total, 0.0).reshape(members, GROUP, stack), axis=1)
    folded = (iota((stack, LANES), 0) // GROUP == iota((stack, LANES), 1) % members).astype(F32)
    tiled = exact_dot(by_row, folded)
    per_row = LANES // members
    keep = iota((members, LANES), 0) % per_row == iota((members, LANES), 1) // members
    packed = jnp.sum(jnp.where(keep, tiled, 0.0).reshape(members // per_row, per_row, LANES), axis=1)
    proj_col = jnp.sum(jnp.sum(proj, axis=1), axis=1, keepdims=True)
    proj_row = jnp.sum(
        jnp.where(iota((members, LANES), 0) == iota((members, LANES), 1), proj_col, 0.0), axis=0, keepdims=True
    )
    filled = members // per_row + 1
    blank = jnp.zeros((out_ref.shape[0] - filled, LANES), F32)
    out_ref[...] = jnp.concatenate([packed, proj_row, blank], axis=0)


def gram_partial(share, grid):
    members = share.shape[0]
    filled = members * members // LANES + 1
    return pl.pallas_call(
        gram_kernel,
        out_shape=jax.ShapeDtypeStruct((-(-filled // 8) * 8, LANES), F32),
        in_specs=[vmem_spec()] * 2,
        out_specs=vmem_spec(),
        compiler_params=pltpu.CompilerParams(vmem_limit_bytes=VMEM_LIMIT),
        cost_estimate=pl.CostEstimate(
            flops=6 * GROUP * members * share.size, bytes_accessed=2 * share.size, transcendentals=0
        ),
        name="gram",
    )(share, grid)


def ensemble_transform(gram, proj):
    members = gram.shape[0]
    row, column = iota((members, members), 0), iota((members, members), 1)
    identity = (row == column).astype(F32)
    system = gram + (members - 1.0) * identity
    left, right = system, proj
    for pivot in range(members):
        is_pivot = iota((members, 1), 0) == pivot
        scale = 1.0 / left[pivot : pivot + 1, pivot : pivot + 1]
        pivot_row = left[pivot : pivot + 1, :] * scale
        pivot_right = right[pivot : pivot + 1, :] * scale
        factor = left[:, pivot : pivot + 1]
        left = jnp.where(is_pivot, pivot_row, left - factor * pivot_row)
        right = jnp.where(is_pivot, pivot_right, right - factor * pivot_right)
    mean_weights = right
    mean_level = jnp.sum(jnp.sum(system * identity, axis=1, keepdims=True), axis=0, keepdims=True) / members
    lifted = system + (mean_level - (members - 1.0)) * (1.0 / members)
    frobenius = jnp.sqrt(jnp.sum(jnp.sum(lifted * lifted, axis=1, keepdims=True), axis=0, keepdims=True))
    root_iter = lifted / frobenius
    inv_iter = identity
    for sweep in range(NS_STEPS):
        product = root_iter if sweep == 0 else exact_dot(inv_iter, root_iter)
        correction = 1.5 * identity - 0.5 * product
        inv_iter = correction if sweep == 0 else exact_dot(correction, inv_iter)
        if sweep < NS_STEPS - 1:
            root_iter = exact_dot(root_iter, correction)
    inv_root = inv_iter / jnp.sqrt(frobenius) + (1.0 / math.sqrt(members - 1.0) - 1.0 / jnp.sqrt(mean_level)) * (
        1.0 / members
    )
    moved = mean_weights + math.sqrt(members - 1.0) * inv_root
    return 1.0 / members + moved - jnp.sum(moved, axis=0, keepdims=True) * (1.0 / members)


def combine_kernel(partial_ref, share_ref, out_ref):
    members, rows, feat_width = share_ref.shape
    stack = members * GROUP
    per_row = LANES // members
    sums = jnp.sum(partial_ref[...], axis=0)
    spread_rows = jnp.concatenate(
        [jnp.broadcast_to(sums[r : r + 1], (per_row, LANES)) for r in range(members // per_row)], axis=0
    )
    keep = iota((members, LANES), 0) % per_row == iota((members, LANES), 1) // members
    folded = (iota((LANES, members), 0) % members == iota((LANES, members), 1)).astype(F32)
    gram = exact_dot(jnp.where(keep, spread_rows, 0.0), folded)
    proj_row = jnp.broadcast_to(sums[members // per_row : members // per_row + 1], (members, LANES))
    on_diagonal = iota((members, LANES), 0) == iota((members, LANES), 1)
    proj = jnp.sum(jnp.where(on_diagonal, proj_row, 0.0), axis=1, keepdims=True)
    transform = ensemble_transform(gram, proj)
    pick = (iota((stack, members), 0) // GROUP == iota((stack, members), 1)).astype(F32).astype(BF16)
    same = iota((stack, stack), 0) % GROUP == iota((stack, stack), 1) % GROUP
    mixers = []
    for piece in halves(transform):
        rows_of = dot(pick, piece, ((1,), (1,))).astype(BF16)
        mixers.append(jnp.where(same, dot(rows_of, pick, ((1,), (1,))), 0.0).astype(BF16))
    for lower in range(0, rows, GROUP):
        fields = share_ref[:, lower : lower + GROUP, :].reshape(stack, feat_width)
        mixed = dot(mixers[0], fields) + dot(mixers[1], fields)
        out_ref[:, lower : lower + GROUP, :] = mixed.astype(BF16).reshape(members, GROUP, feat_width)


def combine(partials, share):
    members = share.shape[0]
    return pl.pallas_call(
        combine_kernel,
        out_shape=jax.ShapeDtypeStruct(share.shape, BF16),
        in_specs=[vmem_spec()] * 2,
        out_specs=vmem_spec(),
        compiler_params=pltpu.CompilerParams(vmem_limit_bytes=VMEM_LIMIT),
        cost_estimate=pl.CostEstimate(
            flops=4 * GROUP * members * share.size, bytes_accessed=4 * share.size, transcendentals=0
        ),
        name="combine",
    )(partials, share)


def local(
    ens_state,
    attn_gain,
    ffn_gain,
    w_query,
    w_key,
    w_value,
    w_out,
    w_gate,
    w_up,
    down_weight,
    head_window,
    obs_token,
    obs_channel,
    obs_value,
    obs_var,
):
    own_members, row_count, feat_width = ens_state.shape
    mem_count = lax.axis_size("mem")
    tok_count = lax.axis_size("tok")
    device_count = mem_count * tok_count
    members = own_members * mem_count
    share_rows = row_count // mem_count
    first_pos = lax.axis_index("tok") * row_count
    up = [(i, i + 1) for i in range(tok_count - 1)]
    down = [(i + 1, i) for i in range(tok_count - 1)]
    left = lax.ppermute(ens_state[:, row_count - WIN :], "tok", up)
    right = lax.ppermute(ens_state[:, :WIN], "tok", down)
    share_start = first_pos + lax.axis_index("mem") * share_rows
    grid = sample_grid(
        share_start.astype(jnp.int32).reshape(1), obs_token, obs_channel, obs_value, obs_var, share_rows, feat_width
    )
    place = jnp.stack([first_pos, row_count * tok_count]).astype(jnp.int32)
    gains = [attn_gain.reshape(1, -1), ffn_gain.reshape(1, -1)]
    projected = project(ens_state, head_window.shape[0], gains[0], w_query, w_key, w_value)
    weights = [w_key, w_value, w_out, w_gate, w_up, down_weight]
    forecast = forward(place, head_window, ens_state, projected, left, right, gains, weights, mem_count)
    share = lax.all_to_all(forecast, "mem", split_axis=0, concat_axis=0, tiled=True)
    share = share.reshape(members, share_rows, feat_width)
    partial = gram_partial(share, grid)
    partials = lax.all_to_all(
        jnp.broadcast_to(partial[None], (device_count, *partial.shape)),
        ("mem", "tok"),
        split_axis=0,
        concat_axis=0,
        tiled=True,
    )
    mixed = combine(partials, share).reshape(mem_count, own_members, share_rows, feat_width)
    mixed = lax.all_to_all(mixed, "mem", split_axis=0, concat_axis=0, tiled=True)
    return jnp.moveaxis(mixed, 0, 1).reshape(own_members, row_count, feat_width)


def solution(mesh):
    in_specs = (P("mem", "tok", None), *[P()] * 10, *[P("tok")] * 4)
    return jax.shard_map(local, mesh=mesh, in_specs=in_specs, out_specs=P("mem", "tok", None), check_vma=False)
```

```python
import functools
import math

import jax
import jax.numpy as jnp
from jax import lax
from jax.experimental import pallas as pl
from jax.experimental.pallas import tpu as pltpu
from jax.sharding import PartitionSpec as P

WIN = 256
NS_STEPS = 8
EPS = 1e-05
Q_ROWS = 128
GROUP = 16
LANES = 128
VMEM_LIMIT = 32 * 1024 * 1024
SAFE_SCORE = 56.0
HIDDEN_CHUNK = 256

F32 = jnp.float32
BF16 = jnp.bfloat16


def dot(a, b, contract=((1,), (0,)), precision=None):
    return lax.dot_general(a, b, (contract, ((), ())), precision=precision, preferred_element_type=F32)


def exact_dot(a, b, contract=((1,), (0,))):
    return dot(a, b, contract, lax.Precision.HIGHEST)


def iota(shape, axis):
    return lax.broadcasted_iota(jnp.int32, shape, axis)


def halves(values):
    high = values.astype(BF16)
    return high, (values - high.astype(F32)).astype(BF16)


def rms_scaled(values, gain):
    return values * lax.rsqrt(jnp.mean(values * values, axis=-1, keepdims=True) + EPS) * gain


def vmem_spec():
    return pl.BlockSpec(memory_space=pltpu.VMEM)


def smem_spec():
    return pl.BlockSpec(memory_space=pltpu.SMEM)


def sample_grid_kernel(start_ref, token_ref, channel_ref, value_ref, var_ref, out_ref):
    rows, feat_width = out_ref.shape[1:]
    count = token_ref.shape[1]
    chunk = min(1024, count)
    total = jnp.zeros((4 * rows, feat_width), F32)
    for lower in range(0, count, chunk):
        part = slice(lower, lower + chunk)
        inv_var = 1.0 / var_ref[:, part]
        weighted = value_ref[:, part] * inv_var
        here = iota((rows, chunk), 0) == token_ref[:, part] - start_ref[0]
        pieces = []
        for row in (inv_var, weighted):
            high = row.astype(BF16).astype(F32)
            pieces.append(jnp.where(here, high, 0.0).astype(BF16))
            pieces.append(jnp.where(here, row - high, 0.0).astype(BF16))
        channel_hot = jnp.where(iota((feat_width, chunk), 0) == channel_ref[:, part], 1.0, 0.0).astype(BF16)
        total += dot(jnp.concatenate(pieces, axis=0), channel_hot, ((1,), (1,)))
    out_ref[0] = total[:rows] + total[rows : 2 * rows]
    out_ref[1] = total[2 * rows : 3 * rows] + total[3 * rows :]


def sample_grid(start, obs_token, obs_channel, obs_value, obs_var, rows, feat_width):
    count = obs_token.shape[0]
    return pl.pallas_call(
        sample_grid_kernel,
        out_shape=jax.ShapeDtypeStruct((2, rows, feat_width), F32),
        in_specs=[smem_spec()] + [vmem_spec()] * 4,
        out_specs=vmem_spec(),
        compiler_params=pltpu.CompilerParams(vmem_limit_bytes=VMEM_LIMIT),
        cost_estimate=pl.CostEstimate(flops=8 * rows * count * feat_width, bytes_accessed=16 * count, transcendentals=0),
        name="sample_grid",
    )(start, *(v.reshape(1, count) for v in (obs_token, obs_channel, obs_value, obs_var)))


def head_lanes(feat_width, heads):
    lane_head = iota((feat_width, LANES), 0) // (feat_width // heads)
    return (lane_head == iota((feat_width, LANES), 1)).astype(F32).astype(BF16)


def largest_norms(values, heads):
    squares = dot((values * values).astype(BF16), head_lanes(values.shape[1], heads))
    return jnp.max(squares, axis=0, keepdims=True)


def band_bias(window, lower, upper, reach):
    apart = jnp.abs(iota((Q_ROWS, upper - lower), 1) + (lower - reach) - iota((Q_ROWS, upper - lower), 0))
    return jnp.where(apart <= window, 0.0, -1e30)


def head_masks(head_size):
    lane_head = iota((1, LANES), 1) // head_size
    return [(lane_head == head).astype(F32).astype(BF16) for head in range(LANES // head_size)]


def stacked_heads(queries, head_size):
    return jnp.concatenate([queries * mask for mask in head_masks(head_size)], axis=0)


def by_lane_head(parts, head_size):
    lane_head = iota((1, LANES), 1) // head_size
    joined = parts[0]
    for head in range(1, len(parts)):
        joined = jnp.where(lane_head == head, parts[head], joined)
    return joined


def row_sums(values):
    return jnp.sum(values, axis=-1, keepdims=True)


def padded_lanes(values, before, after):
    pieces = [jnp.zeros((values.shape[0], before), BF16)] if before else []
    pieces.append(values.astype(BF16))
    if after:
        pieces.append(jnp.zeros((values.shape[0], after), BF16))
    return jnp.concatenate(pieces, axis=1) if len(pieces) > 1 else pieces[0]


def unit_weights(scores, count, spans, bias_of):
    width = scores.shape[1]
    weights, totals = [], []
    for head in range(scores.shape[0] // count):
        sums = []
        for block, (lower, upper) in enumerate(spans):
            top = head * count + block * Q_ROWS
            expo = jnp.exp2(scores[top : top + Q_ROWS, lower:upper] + bias_of(head, block))
            sums.append(row_sums(expo))
            weights.append(padded_lanes(expo, lower, width - upper))
        totals.append(jnp.concatenate(sums, axis=0))
    return jnp.concatenate(weights, axis=0), totals


def inner_kernel(
    window_ref,
    own_ref,
    gain_ref,
    w_query_ref,
    w_key_ref,
    w_value_ref,
    query_ref,
    key_ref,
    value_ref,
    norm_ref,
    mixed_ref,
    total_ref,
    bias_buf,
):
    rows, feat_width = own_ref.shape[1:]
    heads = window_ref.shape[0]
    head_size = feat_width // heads
    group_heads = LANES // head_size
    reach = (bias_buf.shape[2] - Q_ROWS) // 2
    reach_blocks = reach // Q_ROWS
    blocks = rows // Q_ROWS

    @pl.when(pl.program_id(0) == 0)
    def _():
        for head in range(heads):
            bias_buf[head] = band_bias(window_ref[head], 0, Q_ROWS + 2 * reach, reach)

    normed = rms_scaled(own_ref[0].astype(F32), gain_ref[...]).astype(BF16)
    query_rows = dot(normed, w_query_ref[...]) * (math.log2(math.e) / math.sqrt(head_size))
    key_rows = dot(normed, w_key_ref[...])
    query_ref[0] = query_rows.astype(BF16)
    key_ref[0] = key_rows.T.astype(BF16)
    value_ref[0] = dot(normed, w_value_ref[...]).astype(BF16)
    query_norms, key_norms = largest_norms(query_rows, heads), largest_norms(key_rows, heads)
    blank = jnp.zeros((norm_ref.shape[1] - 2, LANES), F32)
    norm_ref[0] = jnp.concatenate([query_norms, key_norms, blank], axis=0)

    @pl.when(is_safe(query_norms, key_norms))
    def _():
        count = 2 * Q_ROWS
        units = [(first, group) for first in range(0, blocks, 2) for group in range(heads // group_heads)]

        def scores_of(first, group):
            lanes = slice(group * LANES, (group + 1) * LANES)
            queries = query_ref[0, first * Q_ROWS : first * Q_ROWS + count, lanes]
            return dot(stacked_heads(queries, head_size), key_ref[0, lanes, :])

        scores = scores_of(*units[0])
        totals_by_lane = jnp.zeros((count, LANES), F32)
        for at, (first, group) in enumerate(units):
            following = scores_of(*units[at + 1]) if at + 1 < len(units) else None
            ranges = [(max(0, b - reach_blocks), min(blocks, b + reach_blocks + 1)) for b in (first, first + 1)]
            spans = [(lower * Q_ROWS, upper * Q_ROWS) for lower, upper in ranges]

            def bias_of(head, block):
                shift = (reach_blocks - first - block) * Q_ROWS
                lower, upper = spans[block]
                return bias_buf[group * group_heads + head, :, lower + shift : upper + shift]

            weights, totals = unit_weights(scores, count, spans, bias_of)
            lanes = slice(group * LANES, (group + 1) * LANES)
            mixed = dot(weights, value_ref[0, :, lanes])
            start = first * Q_ROWS
            parts = [mixed[head * count : (head + 1) * count] for head in range(group_heads)]
            mixed_ref[0, start : start + count, lanes] = by_lane_head(parts, head_size)
            for head, total in enumerate(totals):
                here = iota((1, LANES), 1) == group * group_heads + head
                totals_by_lane = jnp.where(here, total, totals_by_lane)
            total_ref[0, start : start + count, :] = totals_by_lane
            scores = following


def is_safe(query_norms, key_norms):
    return jnp.max(query_norms * key_norms) * 1.05 <= SAFE_SCORE * SAFE_SCORE


def inner(head_window, own, gain, w_query, w_key, w_value, reach):
    members, rows, feat_width = own.shape
    heads = head_window.shape[0]
    upright = (members, rows, feat_width)
    shapes = [
        (upright, BF16),
        ((members, feat_width, rows), BF16),
        (upright, BF16),
        ((members, 8, LANES), F32),
        (upright, F32),
        ((members, rows, LANES), F32),
    ]

    def spec(shape):
        return pl.BlockSpec((1, *shape[1:]), lambda m: (m, 0, 0))

    return pl.pallas_call(
        inner_kernel,
        grid=(members,),
        out_shape=[jax.ShapeDtypeStruct(*v) for v in shapes],
        in_specs=[smem_spec(), spec(upright)] + [vmem_spec()] * 4,
        out_specs=[spec(shape) for shape, _ in shapes],
        scratch_shapes=[pltpu.VMEM((heads, Q_ROWS, Q_ROWS + 2 * reach), F32)],
        compiler_params=pltpu.CompilerParams(vmem_limit_bytes=VMEM_LIMIT),
        cost_estimate=pl.CostEstimate(
            flops=own.size * (6 * feat_width + 16 * rows), bytes_accessed=14 * own.size, transcendentals=0
        ),
        name="inner",
    )(head_window, own, gain, w_query, w_key, w_value)


def forward_kernel(
    place_ref,
    window_ref,
    state_ref,
    query_ref,
    key_ref,
    value_ref,
    norm_ref,
    inner_mixed_ref,
    inner_total_ref,
    left_ref,
    right_ref,
    attn_gain_ref,
    ffn_gain_ref,
    w_key_ref,
    w_value_ref,
    w_out_ref,
    w_gate_ref,
    w_up_ref,
    down_weight_ref,
    out_ref,
    halo_key_buf,
    halo_value_buf,
    bias_buf,
    mixed_buf,
    key_buf,
    value_buf,
):
    rows, feat_width = state_ref.shape[1:]
    reach = left_ref.shape[1]
    heads = window_ref.shape[0]
    head_size = feat_width // heads
    group_heads = LANES // head_size
    blocks = rows // Q_ROWS
    key_count = Q_ROWS + 2 * reach
    count = 2 * Q_ROWS
    first_valid = place_ref[0] - reach >= 0
    last_valid = place_ref[0] + rows + reach <= place_ref[1]

    @pl.when(pl.program_id(0) == 0)
    def _():
        for head in range(heads):
            left_bias = band_bias(window_ref[head], 0, reach, reach)
            right_bias = band_bias(window_ref[head], key_count - reach, key_count, reach)
            bias_buf[0, head] = jnp.where(first_valid, left_bias, -1e30)
            bias_buf[1, head] = jnp.where(last_valid, right_bias, -1e30)

    key_norms = norm_ref[0, 1:2, :]
    for side, ref in enumerate((left_ref, right_ref)):
        normed = rms_scaled(ref[0].astype(F32), attn_gain_ref[...]).astype(BF16)
        keys = dot(normed, w_key_ref[...])
        key_norms = jnp.maximum(key_norms, largest_norms(keys, heads))
        halo_key_buf[side] = keys.T.astype(BF16)
        halo_value_buf[side] = dot(normed, w_value_ref[...]).astype(BF16)
    safe = is_safe(norm_ref[0, 0:1, :], key_norms)

    @pl.when(safe)
    def _():
        units = [(side, group) for side in range(2) for group in range(heads // group_heads)]

        def scores_of(side, group):
            lanes = slice(group * LANES, (group + 1) * LANES)
            start = side * (rows - count)
            queries = query_ref[0, start : start + count, lanes]
            return dot(stacked_heads(queries, head_size), halo_key_buf[side, lanes, :])

        scores = scores_of(*units[0])
        for at, (side, group) in enumerate(units):
            following = scores_of(*units[at + 1]) if at + 1 < len(units) else None
            spans = [(0, reach), (Q_ROWS, reach)] if side == 0 else [(0, reach - Q_ROWS), (0, reach)]

            def bias_of(head, block):
                lower, upper = spans[block]
                shift = -block * Q_ROWS if side == 0 else (1 - block) * Q_ROWS
                return bias_buf[side, group * group_heads + head, :, lower + shift : upper + shift]

            weights, totals = unit_weights(scores, count, spans, bias_of)
            lanes = slice(group * LANES, (group + 1) * LANES)
            mixed = dot(weights, halo_value_buf[side, :, lanes])
            start = side * (rows - count)
            parts = []
            for head, total in enumerate(totals):
                at_lane = group * group_heads + head
                total = total + inner_total_ref[0, start : start + count, at_lane : at_lane + 1]
                part = mixed[head * count : (head + 1) * count] + inner_mixed_ref[0, start : start + count, lanes]
                parts.append(part * (1.0 / total))
            mixed_buf[start : start + count, lanes] = by_lane_head(parts, head_size).astype(BF16)
            scores = following

    @pl.when(jnp.logical_not(safe))
    def _():
        key_buf[:, :reach] = halo_key_buf[0]
        key_buf[:, reach : reach + rows] = key_ref[0]
        key_buf[:, reach + rows :] = halo_key_buf[1]
        value_buf[:reach] = halo_value_buf[0]
        value_buf[reach : reach + rows] = value_ref[0]
        value_buf[reach + rows :] = halo_value_buf[1]
        for block in range(blocks):
            start = block * Q_ROWS
            k_pos = place_ref[0] - reach + start + iota((Q_ROWS, key_count), 1)
            inside = (k_pos >= 0) & (k_pos < place_ref[1])
            for group in range(heads // group_heads):
                lanes = slice(group * LANES, (group + 1) * LANES)
                queries = query_ref[0, start : start + Q_ROWS, lanes]
                scores = dot(stacked_heads(queries, head_size), key_buf[lanes, start : start + key_count])
                weights, totals = [], []
                for head in range(group_heads):
                    bias = band_bias(window_ref[group * group_heads + head], 0, key_count, reach)
                    score_matrix = scores[head * Q_ROWS : (head + 1) * Q_ROWS] + jnp.where(inside, bias, -1e30)
                    expo = jnp.exp2(score_matrix - jnp.max(score_matrix, axis=-1, keepdims=True))
                    totals.append(row_sums(expo))
                    weights.append(expo.astype(BF16))
                mixed = dot(jnp.concatenate(weights, axis=0), value_buf[start : start + key_count, lanes])
                parts = [mixed[head * Q_ROWS : (head + 1) * Q_ROWS] * (1.0 / v) for head, v in enumerate(totals)]
                mixed_buf[start : start + Q_ROWS, lanes] = by_lane_head(parts, head_size).astype(BF16)

    after = (state_ref[0].astype(F32) + dot(mixed_buf[...], w_out_ref[...])).astype(BF16)
    normed_mid = rms_scaled(after.astype(F32), ffn_gain_ref[...]).astype(BF16)
    forecast = after.astype(F32)
    for lower in range(0, w_gate_ref.shape[1], HIDDEN_CHUNK):
        part = slice(lower, lower + HIDDEN_CHUNK)
        gate = 0.5 * dot(normed_mid, w_gate_ref[:, part])
        hidden = (gate * (1.0 + jnp.tanh(gate)) * dot(normed_mid, w_up_ref[:, part])).astype(BF16)
        forecast += dot(hidden, down_weight_ref[part, :])
    forecast = forecast.astype(BF16)
    shares, _, share_rows, _ = out_ref.shape
    for share in range(shares):
        out_ref[share, 0] = forecast[share * share_rows : (share + 1) * share_rows]


def forward(place, head_window, own, inner_parts, left, right, gains, weights, shares):
    members, row_count, feat_width = own.shape
    reach = left.shape[1]
    heads = head_window.shape[0]
    hidden_width = weights[3].shape[1]
    macs = members * row_count * feat_width * (3 * feat_width + 3 * hidden_width + 4 * reach)

    def spec(array):
        return pl.BlockSpec((1, *array.shape[1:]), lambda m: (m, 0, 0))

    return pl.pallas_call(
        forward_kernel,
        grid=(members,),
        out_shape=jax.ShapeDtypeStruct((shares, members, row_count // shares, feat_width), BF16),
        in_specs=[smem_spec()] * 2
        + [spec(v) for v in (own, *inner_parts, left, right)]
        + [vmem_spec()] * (len(gains) + len(weights)),
        out_specs=pl.BlockSpec((shares, 1, row_count // shares, feat_width), lambda m: (0, m, 0, 0)),
        scratch_shapes=[
            pltpu.VMEM((2, feat_width, reach), BF16),
            pltpu.VMEM((2, reach, feat_width), BF16),
            pltpu.VMEM((2, heads, Q_ROWS, reach), F32),
            pltpu.VMEM((row_count, feat_width), BF16),
            pltpu.VMEM((feat_width, row_count + 2 * reach), BF16),
            pltpu.VMEM((row_count + 2 * reach, feat_width), BF16),
        ],
        compiler_params=pltpu.CompilerParams(vmem_limit_bytes=VMEM_LIMIT),
        cost_estimate=pl.CostEstimate(flops=2 * macs, bytes_accessed=10 * own.size, transcendentals=0),
        name="forward",
    )(place, head_window, own, *inner_parts, left, right, *gains, *weights)


def gram_kernel(share_ref, grid_ref, out_ref):
    members, rows, feat_width = share_ref.shape
    stack = members * GROUP
    total = jnp.zeros((stack, stack), F32)
    proj = jnp.zeros((members, GROUP, feat_width), F32)
    for lower in range(0, rows, GROUP):
        part = slice(lower, lower + GROUP)
        fields = share_ref[:, part, :].astype(F32)
        mean = jnp.sum(fields, axis=0) * (1.0 / members)
        spread = fields - mean[None]
        weight = grid_ref[0, part, :]
        proj += spread * (grid_ref[1, part, :] - weight * mean)[None]
        high, low = halves(spread.reshape(stack, feat_width))
        w_high, w_low = halves((spread * weight[None]).reshape(stack, feat_width))
        last = ((1,), (1,))
        total += dot(w_high, high, last) + dot(w_high, low, last) + dot(w_low, high, last)
    same = iota((stack, stack), 0) % GROUP == iota((stack, stack), 1) % GROUP
    by_row = jnp.sum(jnp.where(same, total, 0.0).reshape(members, GROUP, stack), axis=1)
    folded = (iota((stack, LANES), 0) // GROUP == iota((stack, LANES), 1) % members).astype(F32)
    tiled = exact_dot(by_row, folded)
    per_row = LANES // members
    keep = iota((members, LANES), 0) % per_row == iota((members, LANES), 1) // members
    packed = jnp.sum(jnp.where(keep, tiled, 0.0).reshape(members // per_row, per_row, LANES), axis=1)
    proj_col = jnp.sum(jnp.sum(proj, axis=1), axis=1, keepdims=True)
    proj_row = jnp.sum(
        jnp.where(iota((members, LANES), 0) == iota((members, LANES), 1), proj_col, 0.0), axis=0, keepdims=True
    )
    filled = members // per_row + 1
    blank = jnp.zeros((out_ref.shape[0] - filled, LANES), F32)
    out_ref[...] = jnp.concatenate([packed, proj_row, blank], axis=0)


def gram_partial(share, grid):
    members = share.shape[0]
    filled = members * members // LANES + 1
    return pl.pallas_call(
        gram_kernel,
        out_shape=jax.ShapeDtypeStruct((-(-filled // 8) * 8, LANES), F32),
        in_specs=[vmem_spec()] * 2,
        out_specs=vmem_spec(),
        compiler_params=pltpu.CompilerParams(vmem_limit_bytes=VMEM_LIMIT),
        cost_estimate=pl.CostEstimate(
            flops=6 * GROUP * members * share.size, bytes_accessed=2 * share.size, transcendentals=0
        ),
        name="gram",
    )(share, grid)


def ensemble_transform(gram, proj):
    members = gram.shape[0]
    row, column = iota((members, members), 0), iota((members, members), 1)
    identity = (row == column).astype(F32)
    system = gram + (members - 1.0) * identity
    left, right = system, proj
    for pivot in range(members):
        is_pivot = iota((members, 1), 0) == pivot
        scale = 1.0 / left[pivot : pivot + 1, pivot : pivot + 1]
        pivot_row = left[pivot : pivot + 1, :] * scale
        pivot_right = right[pivot : pivot + 1, :] * scale
        factor = left[:, pivot : pivot + 1]
        left = jnp.where(is_pivot, pivot_row, left - factor * pivot_row)
        right = jnp.where(is_pivot, pivot_right, right - factor * pivot_right)
    mean_weights = right
    mean_level = jnp.sum(jnp.sum(system * identity, axis=1, keepdims=True), axis=0, keepdims=True) / members
    lifted = system + (mean_level - (members - 1.0)) * (1.0 / members)
    frobenius = jnp.sqrt(jnp.sum(jnp.sum(lifted * lifted, axis=1, keepdims=True), axis=0, keepdims=True))
    root_iter = lifted / frobenius
    inv_iter = identity
    for sweep in range(NS_STEPS):
        product = root_iter if sweep == 0 else exact_dot(inv_iter, root_iter)
        correction = 1.5 * identity - 0.5 * product
        inv_iter = correction if sweep == 0 else exact_dot(correction, inv_iter)
        if sweep < NS_STEPS - 1:
            root_iter = exact_dot(root_iter, correction)
    inv_root = inv_iter / jnp.sqrt(frobenius) + (1.0 / math.sqrt(members - 1.0) - 1.0 / jnp.sqrt(mean_level)) * (
        1.0 / members
    )
    moved = mean_weights + math.sqrt(members - 1.0) * inv_root
    return 1.0 / members + moved - jnp.sum(moved, axis=0, keepdims=True) * (1.0 / members)


def combine_kernel(partial_ref, share_ref, out_ref):
    members, rows, feat_width = share_ref.shape
    stack = members * GROUP
    per_row = LANES // members
    sums = jnp.sum(partial_ref[...], axis=0)
    spread_rows = jnp.concatenate(
        [jnp.broadcast_to(sums[r : r + 1], (per_row, LANES)) for r in range(members // per_row)], axis=0
    )
    keep = iota((members, LANES), 0) % per_row == iota((members, LANES), 1) // members
    folded = (iota((LANES, members), 0) % members == iota((LANES, members), 1)).astype(F32)
    gram = exact_dot(jnp.where(keep, spread_rows, 0.0), folded)
    proj_row = jnp.broadcast_to(sums[members // per_row : members // per_row + 1], (members, LANES))
    on_diagonal = iota((members, LANES), 0) == iota((members, LANES), 1)
    proj = jnp.sum(jnp.where(on_diagonal, proj_row, 0.0), axis=1, keepdims=True)
    transform = ensemble_transform(gram, proj)
    pick = (iota((stack, members), 0) // GROUP == iota((stack, members), 1)).astype(F32).astype(BF16)
    same = iota((stack, stack), 0) % GROUP == iota((stack, stack), 1) % GROUP
    mixers = []
    for piece in halves(transform):
        rows_of = dot(pick, piece, ((1,), (1,))).astype(BF16)
        mixers.append(jnp.where(same, dot(rows_of, pick, ((1,), (1,))), 0.0).astype(BF16))
    for lower in range(0, rows, GROUP):
        fields = share_ref[:, lower : lower + GROUP, :].reshape(stack, feat_width)
        mixed = dot(mixers[0], fields) + dot(mixers[1], fields)
        out_ref[:, lower : lower + GROUP, :] = mixed.astype(BF16).reshape(members, GROUP, feat_width)


def combine(partials, share):
    members = share.shape[0]
    return pl.pallas_call(
        combine_kernel,
        out_shape=jax.ShapeDtypeStruct(share.shape, BF16),
        in_specs=[vmem_spec()] * 2,
        out_specs=vmem_spec(),
        compiler_params=pltpu.CompilerParams(vmem_limit_bytes=VMEM_LIMIT),
        cost_estimate=pl.CostEstimate(
            flops=4 * GROUP * members * share.size, bytes_accessed=4 * share.size, transcendentals=0
        ),
        name="combine",
    )(partials, share)


def local(
    ens_state,
    attn_gain,
    ffn_gain,
    w_query,
    w_key,
    w_value,
    w_out,
    w_gate,
    w_up,
    down_weight,
    head_window,
    obs_token,
    obs_channel,
    obs_value,
    obs_var,
):
    own_members, row_count, feat_width = ens_state.shape
    mem_count = lax.axis_size("mem")
    tok_count = lax.axis_size("tok")
    device_count = mem_count * tok_count
    members = own_members * mem_count
    share_rows = row_count // mem_count
    first_pos = lax.axis_index("tok") * row_count
    up = [(i, i + 1) for i in range(tok_count - 1)]
    down = [(i + 1, i) for i in range(tok_count - 1)]
    left = lax.ppermute(ens_state[:, row_count - WIN :], "tok", up)
    right = lax.ppermute(ens_state[:, :WIN], "tok", down)
    share_start = first_pos + lax.axis_index("mem") * share_rows
    grid = sample_grid(
        share_start.astype(jnp.int32).reshape(1), obs_token, obs_channel, obs_value, obs_var, share_rows, feat_width
    )
    place = jnp.stack([first_pos, row_count * tok_count]).astype(jnp.int32)
    gains = [attn_gain.reshape(1, -1), ffn_gain.reshape(1, -1)]
    inner_parts = inner(head_window, ens_state, gains[0], w_query, w_key, w_value, WIN)
    weights = [w_key, w_value, w_out, w_gate, w_up, down_weight]
    forecast = forward(place, head_window, ens_state, inner_parts, left, right, gains, weights, mem_count)
    share = lax.all_to_all(forecast, "mem", split_axis=0, concat_axis=0, tiled=True)
    share = share.reshape(members, share_rows, feat_width)
    partial = gram_partial(share, grid)
    partials = lax.all_to_all(
        jnp.broadcast_to(partial[None], (device_count, *partial.shape)),
        ("mem", "tok"),
        split_axis=0,
        concat_axis=0,
        tiled=True,
    )
    mixed = combine(partials, share).reshape(mem_count, own_members, share_rows, feat_width)
    mixed = lax.all_to_all(mixed, "mem", split_axis=0, concat_axis=0, tiled=True)
    return jnp.moveaxis(mixed, 0, 1).reshape(own_members, row_count, feat_width)


def solution(mesh):
    in_specs = (P("mem", "tok", None), *[P()] * 10, *[P("tok")] * 4)
    return jax.shard_map(local, mesh=mesh, in_specs=in_specs, out_specs=P("mem", "tok", None), check_vma=False)
```

```python
import functools
import math

import jax
import jax.numpy as jnp
from jax import lax
from jax.experimental import pallas as pl
from jax.experimental.pallas import tpu as pltpu
from jax.sharding import PartitionSpec as P

WIN = 256
NS_STEPS = 8
EPS = 1e-05
Q_ROWS = 128
GROUP = 16
LANES = 128
VMEM_LIMIT = 32 * 1024 * 1024
SAFE_SCORE = 56.0
HIDDEN_CHUNK = 256

F32 = jnp.float32
BF16 = jnp.bfloat16


def dot(a, b, contract=((1,), (0,)), precision=None):
    return lax.dot_general(a, b, (contract, ((), ())), precision=precision, preferred_element_type=F32)


def exact_dot(a, b, contract=((1,), (0,))):
    return dot(a, b, contract, lax.Precision.HIGHEST)


def iota(shape, axis):
    return lax.broadcasted_iota(jnp.int32, shape, axis)


def halves(values):
    high = values.astype(BF16)
    return high, (values - high.astype(F32)).astype(BF16)


def rms_scaled(values, gain):
    rows, width = values.shape
    ones = jnp.ones((width, LANES), BF16)
    means = dot((values * values).astype(BF16), ones) * (1.0 / width)
    scale = lax.rsqrt(means + EPS)
    return values * jnp.concatenate([scale] * (width // LANES), axis=1) * gain


def vmem_spec():
    return pl.BlockSpec(memory_space=pltpu.VMEM)


def smem_spec():
    return pl.BlockSpec(memory_space=pltpu.SMEM)


def sample_grid_kernel(start_ref, token_ref, channel_ref, value_ref, var_ref, out_ref):
    rows, feat_width = out_ref.shape[1:]
    count = token_ref.shape[1]
    chunk = min(1024, count)
    total = jnp.zeros((4 * rows, feat_width), F32)
    for lower in range(0, count, chunk):
        part = slice(lower, lower + chunk)
        inv_var = 1.0 / var_ref[:, part]
        weighted = value_ref[:, part] * inv_var
        here = iota((rows, chunk), 0) == token_ref[:, part] - start_ref[0]
        pieces = []
        for row in (inv_var, weighted):
            high = row.astype(BF16).astype(F32)
            pieces.append(jnp.where(here, high, 0.0).astype(BF16))
            pieces.append(jnp.where(here, row - high, 0.0).astype(BF16))
        channel_hot = jnp.where(iota((feat_width, chunk), 0) == channel_ref[:, part], 1.0, 0.0).astype(BF16)
        total += dot(jnp.concatenate(pieces, axis=0), channel_hot, ((1,), (1,)))
    out_ref[0] = total[:rows] + total[rows : 2 * rows]
    out_ref[1] = total[2 * rows : 3 * rows] + total[3 * rows :]


def sample_grid(start, obs_token, obs_channel, obs_value, obs_var, rows, feat_width):
    count = obs_token.shape[0]
    return pl.pallas_call(
        sample_grid_kernel,
        out_shape=jax.ShapeDtypeStruct((2, rows, feat_width), F32),
        in_specs=[smem_spec()] + [vmem_spec()] * 4,
        out_specs=vmem_spec(),
        compiler_params=pltpu.CompilerParams(vmem_limit_bytes=VMEM_LIMIT),
        cost_estimate=pl.CostEstimate(flops=8 * rows * count * feat_width, bytes_accessed=16 * count, transcendentals=0),
        name="sample_grid",
    )(start, *(v.reshape(1, count) for v in (obs_token, obs_channel, obs_value, obs_var)))


def head_lanes(feat_width, heads):
    lane_head = iota((feat_width, LANES), 0) // (feat_width // heads)
    return (lane_head == iota((feat_width, LANES), 1)).astype(F32).astype(BF16)


def largest_norms(values, heads):
    squares = dot((values * values).astype(BF16), head_lanes(values.shape[1], heads))
    return jnp.max(squares, axis=0, keepdims=True)


def project_kernel(
    heads, own_ref, gain_ref, w_query_ref, w_key_ref, w_value_ref, query_ref, key_ref, value_ref, norm_ref
):
    scale = math.log2(math.e) / math.sqrt(own_ref.shape[2] // heads)
    normed = rms_scaled(own_ref[0].astype(F32), gain_ref[...]).astype(BF16)
    queries = dot(normed, w_query_ref[...]) * scale
    keys = dot(normed, w_key_ref[...])
    query_ref[0] = queries.astype(BF16)
    key_ref[0] = keys.T.astype(BF16)
    value_ref[0] = dot(normed, w_value_ref[...]).astype(BF16)
    blank = jnp.zeros((norm_ref.shape[1] - 2, LANES), F32)
    norm_ref[0] = jnp.concatenate([largest_norms(queries, heads), largest_norms(keys, heads), blank], axis=0)


def project(own, heads, gain, w_query, w_key, w_value):
    members, rows, feat_width = own.shape
    upright = (members, rows, feat_width)
    shapes = [upright, (members, feat_width, rows), upright]
    norm_shape = (members, 8, LANES)

    def spec(shape):
        return pl.BlockSpec((1, *shape[1:]), lambda m: (m, 0, 0))

    return pl.pallas_call(
        functools.partial(project_kernel, heads),
        grid=(members,),
        out_shape=[jax.ShapeDtypeStruct(v, BF16) for v in shapes] + [jax.ShapeDtypeStruct(norm_shape, F32)],
        in_specs=[spec(upright)] + [vmem_spec()] * 4,
        out_specs=[spec(v) for v in (*shapes, norm_shape)],
        compiler_params=pltpu.CompilerParams(vmem_limit_bytes=VMEM_LIMIT),
        cost_estimate=pl.CostEstimate(
            flops=6 * own.size * feat_width, bytes_accessed=8 * own.size, transcendentals=0
        ),
        name="project",
    )(own, gain, w_query, w_key, w_value)


def forward_kernel(
    place_ref,
    window_ref,
    state_ref,
    query_ref,
    key_ref,
    value_ref,
    norm_ref,
    left_ref,
    right_ref,
    attn_gain_ref,
    ffn_gain_ref,
    w_key_ref,
    w_value_ref,
    w_out_ref,
    w_gate_ref,
    w_up_ref,
    down_weight_ref,
    out_ref,
    key_buf,
    value_buf,
    bias_buf,
    mixed_buf,
):
    rows, feat_width = state_ref.shape[1:]
    reach = left_ref.shape[1]
    head_count = window_ref.shape[0]
    head_size = feat_width // head_count
    group_heads = LANES // head_size
    blocks = rows // Q_ROWS
    key_count = Q_ROWS + 2 * reach

    @pl.when(pl.program_id(0) == 0)
    def _():
        apart = jnp.abs(iota((Q_ROWS, key_count), 1) - reach - iota((Q_ROWS, key_count), 0))
        for block in range(blocks):
            k_pos = place_ref[0] - reach + block * Q_ROWS + iota((Q_ROWS, key_count), 1)
            inside = (k_pos >= 0) & (k_pos < place_ref[1])
            for head in range(head_count):
                bias_buf[block, head] = jnp.where(inside & (apart <= window_ref[head]), 0.0, -1e30)
        value_buf[...] = jnp.ones(value_buf.shape, BF16)

    key_buf[:, reach : reach + rows] = key_ref[0]
    groups = head_count // group_heads

    def put_values(lower, values):
        for group in range(groups):
            lanes = slice(2 * group * LANES, (2 * group + 1) * LANES)
            value_buf[lower : lower + values.shape[0], lanes] = values[:, group * LANES : (group + 1) * LANES]

    put_values(reach, value_ref[0])
    key_norms = norm_ref[0, 1:2, :]
    for ref, lower in ((left_ref, 0), (right_ref, reach + rows)):
        normed = rms_scaled(ref[0].astype(F32), attn_gain_ref[...]).astype(BF16)
        keys = dot(normed, w_key_ref[...])
        key_norms = jnp.maximum(key_norms, largest_norms(keys, head_count))
        key_buf[:, lower : lower + reach] = keys.T.astype(BF16)
        put_values(lower, dot(normed, w_value_ref[...]).astype(BF16))

    bound = jnp.max(norm_ref[0, 0:1, :] * key_norms) * 1.05
    safe = bound <= SAFE_SCORE * SAFE_SCORE

    lane_head = iota((1, LANES), 1) // head_size
    head_masks = [(lane_head == head).astype(F32).astype(BF16) for head in range(group_heads)]

    def scores_of(start, count, group):
        lanes = slice(group * LANES, (group + 1) * LANES)
        queries = query_ref[0, pl.ds(start, count), lanes]
        stacked = jnp.concatenate([queries * mask for mask in head_masks], axis=0)
        return dot(stacked, key_buf[lanes, pl.ds(start, count + 2 * reach)])

    def mix_values(start, count, group, weights):
        lanes = slice(2 * group * LANES, 2 * (group + 1) * LANES)
        mixed_all = dot(jnp.concatenate(weights, axis=0), value_buf[pl.ds(start, count + 2 * reach), lanes])
        mixed, totals = mixed_all[:count, :LANES], mixed_all[:count, LANES:]
        for head in range(1, group_heads):
            part = mixed_all[head * count : (head + 1) * count]
            mixed = jnp.where(lane_head == head, part[:, :LANES], mixed)
            totals = jnp.where(lane_head == head, part[:, LANES:], totals)
        mixed_buf[pl.ds(start, count), group * LANES : (group + 1) * LANES] = (mixed / totals).astype(BF16)

    @pl.when(safe)
    def _():
        pair = 2 * Q_ROWS
        corner = jnp.zeros((Q_ROWS, Q_ROWS), BF16)
        units = [(start, group) for start in range(0, rows, pair) for group in range(groups)]
        scores = scores_of(units[0][0], pair, units[0][1])
        for at, (start, group) in enumerate(units):
            following = scores_of(units[at + 1][0], pair, units[at + 1][1]) if at + 1 < len(units) else None
            weights = []
            for head in range(group_heads):
                top = head * pair
                bias = [bias_buf[start // Q_ROWS + part, group * group_heads + head] for part in range(2)]
                upper = jnp.exp2(scores[top : top + Q_ROWS, :key_count] + bias[0])
                lower = jnp.exp2(scores[top + Q_ROWS : top + pair, Q_ROWS:] + bias[1])
                weights.append(jnp.concatenate([upper.astype(BF16), corner], axis=1))
                weights.append(jnp.concatenate([corner, lower.astype(BF16)], axis=1))
            mix_values(start, pair, group, weights)
            scores = following

    @pl.when(jnp.logical_not(safe))
    def _():
        for block in range(blocks):
            start = block * Q_ROWS
            for group in range(groups):
                scores = scores_of(start, Q_ROWS, group)
                weights = []
                for head in range(group_heads):
                    score_matrix = scores[head * Q_ROWS : (head + 1) * Q_ROWS]
                    score_matrix = score_matrix + bias_buf[block, group * group_heads + head]
                    expo = jnp.exp2(score_matrix - jnp.max(score_matrix, axis=-1, keepdims=True))
                    weights.append(expo.astype(BF16))
                mix_values(start, Q_ROWS, group, weights)

    after = (state_ref[0].astype(F32) + dot(mixed_buf[...], w_out_ref[...])).astype(BF16)
    normed_mid = rms_scaled(after.astype(F32), ffn_gain_ref[...]).astype(BF16)
    forecast = after.astype(F32)
    for lower in range(0, w_gate_ref.shape[1], HIDDEN_CHUNK):
        part = slice(lower, lower + HIDDEN_CHUNK)
        gate = 0.5 * dot(normed_mid, w_gate_ref[:, part])
        hidden = (gate * (1.0 + jnp.tanh(gate)) * dot(normed_mid, w_up_ref[:, part])).astype(BF16)
        forecast += dot(hidden, down_weight_ref[part, :])
    forecast = forecast.astype(BF16)
    shares, _, share_rows, _ = out_ref.shape
    for share in range(shares):
        out_ref[share, 0] = forecast[share * share_rows : (share + 1) * share_rows]


def forward(place, head_window, own, projected, left, right, gains, weights, shares):
    members, row_count, feat_width = own.shape
    reach = left.shape[1]
    key_count = Q_ROWS + 2 * reach
    hidden_width = weights[3].shape[1]
    macs = members * row_count * feat_width * (3 * feat_width + 3 * hidden_width + 8 * key_count)
    edge_block = pl.BlockSpec((1, reach, feat_width), lambda m: (m, 0, 0))
    return pl.pallas_call(
        forward_kernel,
        grid=(members,),
        out_shape=jax.ShapeDtypeStruct((shares, members, row_count // shares, feat_width), BF16),
        in_specs=[smem_spec()] * 2
        + [pl.BlockSpec((1, *v.shape[1:]), lambda m: (m, 0, 0)) for v in (own, *projected)]
        + [edge_block] * 2
        + [vmem_spec()] * (len(gains) + len(weights)),
        out_specs=pl.BlockSpec((shares, 1, row_count // shares, feat_width), lambda m: (0, m, 0, 0)),
        scratch_shapes=[
            pltpu.VMEM((feat_width, row_count + 2 * reach), BF16),
            pltpu.VMEM((row_count + 2 * reach, 2 * feat_width), BF16),
            pltpu.VMEM((row_count // Q_ROWS, head_window.shape[0], Q_ROWS, key_count), F32),
            pltpu.VMEM((row_count, feat_width), BF16),
        ],
        compiler_params=pltpu.CompilerParams(vmem_limit_bytes=VMEM_LIMIT),
        cost_estimate=pl.CostEstimate(flops=2 * macs, bytes_accessed=10 * own.size, transcendentals=0),
        name="forward",
    )(place, head_window, own, *projected, left, right, *gains, *weights)


def gram_kernel(share_ref, grid_ref, out_ref):
    members, rows, feat_width = share_ref.shape
    stack = members * GROUP
    total = jnp.zeros((stack, stack), F32)
    proj = jnp.zeros((members, GROUP, feat_width), F32)
    for lower in range(0, rows, GROUP):
        part = slice(lower, lower + GROUP)
        fields = share_ref[:, part, :].astype(F32)
        mean = jnp.sum(fields, axis=0) * (1.0 / members)
        spread = fields - mean[None]
        weight = grid_ref[0, part, :]
        proj += spread * (grid_ref[1, part, :] - weight * mean)[None]
        high, low = halves(spread.reshape(stack, feat_width))
        w_high, w_low = halves((spread * weight[None]).reshape(stack, feat_width))
        last = ((1,), (1,))
        total += dot(w_high, high, last) + dot(w_high, low, last) + dot(w_low, high, last)
    same = iota((stack, stack), 0) % GROUP == iota((stack, stack), 1) % GROUP
    by_row = jnp.sum(jnp.where(same, total, 0.0).reshape(members, GROUP, stack), axis=1)
    folded = (iota((stack, LANES), 0) // GROUP == iota((stack, LANES), 1) % members).astype(F32)
    tiled = exact_dot(by_row, folded)
    per_row = LANES // members
    keep = iota((members, LANES), 0) % per_row == iota((members, LANES), 1) // members
    packed = jnp.sum(jnp.where(keep, tiled, 0.0).reshape(members // per_row, per_row, LANES), axis=1)
    proj_col = jnp.sum(jnp.sum(proj, axis=1), axis=1, keepdims=True)
    proj_row = jnp.sum(
        jnp.where(iota((members, LANES), 0) == iota((members, LANES), 1), proj_col, 0.0), axis=0, keepdims=True
    )
    filled = members // per_row + 1
    blank = jnp.zeros((out_ref.shape[0] - filled, LANES), F32)
    out_ref[...] = jnp.concatenate([packed, proj_row, blank], axis=0)


def gram_partial(share, grid):
    members = share.shape[0]
    filled = members * members // LANES + 1
    return pl.pallas_call(
        gram_kernel,
        out_shape=jax.ShapeDtypeStruct((-(-filled // 8) * 8, LANES), F32),
        in_specs=[vmem_spec()] * 2,
        out_specs=vmem_spec(),
        compiler_params=pltpu.CompilerParams(vmem_limit_bytes=VMEM_LIMIT),
        cost_estimate=pl.CostEstimate(
            flops=6 * GROUP * members * share.size, bytes_accessed=2 * share.size, transcendentals=0
        ),
        name="gram",
    )(share, grid)


def ensemble_transform(gram, proj):
    members = gram.shape[0]
    row, column = iota((members, members), 0), iota((members, members), 1)
    identity = (row == column).astype(F32)
    system = gram + (members - 1.0) * identity
    left, right = system, proj
    for pivot in range(members):
        is_pivot = iota((members, 1), 0) == pivot
        scale = 1.0 / left[pivot : pivot + 1, pivot : pivot + 1]
        pivot_row = left[pivot : pivot + 1, :] * scale
        pivot_right = right[pivot : pivot + 1, :] * scale
        factor = left[:, pivot : pivot + 1]
        left = jnp.where(is_pivot, pivot_row, left - factor * pivot_row)
        right = jnp.where(is_pivot, pivot_right, right - factor * pivot_right)
    mean_weights = right
    mean_level = jnp.sum(jnp.sum(system * identity, axis=1, keepdims=True), axis=0, keepdims=True) / members
    lifted = system + (mean_level - (members - 1.0)) * (1.0 / members)
    frobenius = jnp.sqrt(jnp.sum(jnp.sum(lifted * lifted, axis=1, keepdims=True), axis=0, keepdims=True))
    root_iter = lifted / frobenius
    inv_iter = identity
    for sweep in range(NS_STEPS):
        product = root_iter if sweep == 0 else exact_dot(inv_iter, root_iter)
        correction = 1.5 * identity - 0.5 * product
        inv_iter = correction if sweep == 0 else exact_dot(correction, inv_iter)
        if sweep < NS_STEPS - 1:
            root_iter = exact_dot(root_iter, correction)
    inv_root = inv_iter / jnp.sqrt(frobenius) + (1.0 / math.sqrt(members - 1.0) - 1.0 / jnp.sqrt(mean_level)) * (
        1.0 / members
    )
    moved = mean_weights + math.sqrt(members - 1.0) * inv_root
    return 1.0 / members + moved - jnp.sum(moved, axis=0, keepdims=True) * (1.0 / members)


def combine_kernel(partial_ref, share_ref, out_ref):
    members, rows, feat_width = share_ref.shape
    stack = members * GROUP
    per_row = LANES // members
    sums = jnp.sum(partial_ref[...], axis=0)
    spread_rows = jnp.concatenate(
        [jnp.broadcast_to(sums[r : r + 1], (per_row, LANES)) for r in range(members // per_row)], axis=0
    )
    keep = iota((members, LANES), 0) % per_row == iota((members, LANES), 1) // members
    folded = (iota((LANES, members), 0) % members == iota((LANES, members), 1)).astype(F32)
    gram = exact_dot(jnp.where(keep, spread_rows, 0.0), folded)
    proj_row = jnp.broadcast_to(sums[members // per_row : members // per_row + 1], (members, LANES))
    on_diagonal = iota((members, LANES), 0) == iota((members, LANES), 1)
    proj = jnp.sum(jnp.where(on_diagonal, proj_row, 0.0), axis=1, keepdims=True)
    transform = ensemble_transform(gram, proj)
    pick = (iota((stack, members), 0) // GROUP == iota((stack, members), 1)).astype(F32).astype(BF16)
    same = iota((stack, stack), 0) % GROUP == iota((stack, stack), 1) % GROUP
    mixers = []
    for piece in halves(transform):
        rows_of = dot(pick, piece, ((1,), (1,))).astype(BF16)
        mixers.append(jnp.where(same, dot(rows_of, pick, ((1,), (1,))), 0.0).astype(BF16))
    for lower in range(0, rows, GROUP):
        fields = share_ref[:, lower : lower + GROUP, :].reshape(stack, feat_width)
        mixed = dot(mixers[0], fields) + dot(mixers[1], fields)
        out_ref[:, lower : lower + GROUP, :] = mixed.astype(BF16).reshape(members, GROUP, feat_width)


def combine(partials, share):
    members = share.shape[0]
    return pl.pallas_call(
        combine_kernel,
        out_shape=jax.ShapeDtypeStruct(share.shape, BF16),
        in_specs=[vmem_spec()] * 2,
        out_specs=vmem_spec(),
        compiler_params=pltpu.CompilerParams(vmem_limit_bytes=VMEM_LIMIT),
        cost_estimate=pl.CostEstimate(
            flops=4 * GROUP * members * share.size, bytes_accessed=4 * share.size, transcendentals=0
        ),
        name="combine",
    )(partials, share)


def local(
    ens_state,
    attn_gain,
    ffn_gain,
    w_query,
    w_key,
    w_value,
    w_out,
    w_gate,
    w_up,
    down_weight,
    head_window,
    obs_token,
    obs_channel,
    obs_value,
    obs_var,
):
    own_members, row_count, feat_width = ens_state.shape
    mem_count = lax.axis_size("mem")
    tok_count = lax.axis_size("tok")
    device_count = mem_count * tok_count
    members = own_members * mem_count
    share_rows = row_count // mem_count
    first_pos = lax.axis_index("tok") * row_count
    up = [(i, i + 1) for i in range(tok_count - 1)]
    down = [(i + 1, i) for i in range(tok_count - 1)]
    left = lax.ppermute(ens_state[:, row_count - WIN :], "tok", up)
    right = lax.ppermute(ens_state[:, :WIN], "tok", down)
    share_start = first_pos + lax.axis_index("mem") * share_rows
    grid = sample_grid(
        share_start.astype(jnp.int32).reshape(1), obs_token, obs_channel, obs_value, obs_var, share_rows, feat_width
    )
    place = jnp.stack([first_pos, row_count * tok_count]).astype(jnp.int32)
    gains = [attn_gain.reshape(1, -1), ffn_gain.reshape(1, -1)]
    projected = project(ens_state, head_window.shape[0], gains[0], w_query, w_key, w_value)
    weights = [w_key, w_value, w_out, w_gate, w_up, down_weight]
    forecast = forward(place, head_window, ens_state, projected, left, right, gains, weights, mem_count)
    share = lax.all_to_all(forecast, "mem", split_axis=0, concat_axis=0, tiled=True)
    share = share.reshape(members, share_rows, feat_width)
    partial = gram_partial(share, grid)
    partials = lax.all_to_all(
        jnp.broadcast_to(partial[None], (device_count, *partial.shape)),
        ("mem", "tok"),
        split_axis=0,
        concat_axis=0,
        tiled=True,
    )
    mixed = combine(partials, share).reshape(mem_count, own_members, share_rows, feat_width)
    mixed = lax.all_to_all(mixed, "mem", split_axis=0, concat_axis=0, tiled=True)
    return jnp.moveaxis(mixed, 0, 1).reshape(own_members, row_count, feat_width)


def solution(mesh):
    in_specs = (P("mem", "tok", None), *[P()] * 10, *[P("tok")] * 4)
    return jax.shard_map(local, mesh=mesh, in_specs=in_specs, out_specs=P("mem", "tok", None), check_vma=False)
```

```python
import functools
import math

import jax
import jax.numpy as jnp
from jax import lax
from jax.experimental import pallas as pl
from jax.experimental.pallas import tpu as pltpu
from jax.sharding import PartitionSpec as P

WIN = 256
NS_STEPS = 8
EPS = 1e-05
Q_ROWS = 128
GROUP = 16
LANES = 128
VMEM_LIMIT = 32 * 1024 * 1024
SAFE_SCORE = 56.0
HIDDEN_CHUNK = 256

F32 = jnp.float32
BF16 = jnp.bfloat16


def dot(a, b, contract=((1,), (0,)), precision=None):
    return lax.dot_general(a, b, (contract, ((), ())), precision=precision, preferred_element_type=F32)


def exact_dot(a, b, contract=((1,), (0,))):
    return dot(a, b, contract, lax.Precision.HIGHEST)


def iota(shape, axis):
    return lax.broadcasted_iota(jnp.int32, shape, axis)


def halves(values):
    high = values.astype(BF16)
    return high, (values - high.astype(F32)).astype(BF16)


def rms_scaled(values, gain):
    rows, width = values.shape
    ones = jnp.ones((width, LANES), BF16)
    means = dot((values * values).astype(BF16), ones) * (1.0 / width)
    scale = lax.rsqrt(means + EPS)
    return values * jnp.concatenate([scale] * (width // LANES), axis=1) * gain


def vmem_spec():
    return pl.BlockSpec(memory_space=pltpu.VMEM)


def smem_spec():
    return pl.BlockSpec(memory_space=pltpu.SMEM)


def sample_grid_kernel(start_ref, token_ref, channel_ref, value_ref, var_ref, out_ref):
    rows, feat_width = out_ref.shape[1:]
    count = token_ref.shape[1]
    chunk = min(1024, count)
    total = jnp.zeros((4 * rows, feat_width), F32)
    for lower in range(0, count, chunk):
        part = slice(lower, lower + chunk)
        inv_var = 1.0 / var_ref[:, part]
        weighted = value_ref[:, part] * inv_var
        here = iota((rows, chunk), 0) == token_ref[:, part] - start_ref[0]
        pieces = []
        for row in (inv_var, weighted):
            high = row.astype(BF16).astype(F32)
            pieces.append(jnp.where(here, high, 0.0).astype(BF16))
            pieces.append(jnp.where(here, row - high, 0.0).astype(BF16))
        channel_hot = jnp.where(iota((feat_width, chunk), 0) == channel_ref[:, part], 1.0, 0.0).astype(BF16)
        total += dot(jnp.concatenate(pieces, axis=0), channel_hot, ((1,), (1,)))
    out_ref[0] = total[:rows] + total[rows : 2 * rows]
    out_ref[1] = total[2 * rows : 3 * rows] + total[3 * rows :]


def sample_grid(start, obs_token, obs_channel, obs_value, obs_var, rows, feat_width):
    count = obs_token.shape[0]
    return pl.pallas_call(
        sample_grid_kernel,
        out_shape=jax.ShapeDtypeStruct((2, rows, feat_width), F32),
        in_specs=[smem_spec()] + [vmem_spec()] * 4,
        out_specs=vmem_spec(),
        compiler_params=pltpu.CompilerParams(vmem_limit_bytes=VMEM_LIMIT),
        cost_estimate=pl.CostEstimate(flops=8 * rows * count * feat_width, bytes_accessed=16 * count, transcendentals=0),
        name="sample_grid",
    )(start, *(v.reshape(1, count) for v in (obs_token, obs_channel, obs_value, obs_var)))


def head_lanes(feat_width, heads):
    lane_head = iota((feat_width, LANES), 0) // (feat_width // heads)
    return (lane_head == iota((feat_width, LANES), 1)).astype(F32).astype(BF16)


def largest_norms(values, heads):
    squares = dot((values * values).astype(BF16), head_lanes(values.shape[1], heads))
    return jnp.max(squares, axis=0, keepdims=True)


def project_kernel(
    heads, own_ref, gain_ref, w_query_ref, w_key_ref, w_value_ref, query_ref, key_ref, value_ref, norm_ref
):
    scale = math.log2(math.e) / math.sqrt(own_ref.shape[2] // heads)
    normed = rms_scaled(own_ref[0].astype(F32), gain_ref[...]).astype(BF16)
    queries = dot(normed, w_query_ref[...]) * scale
    keys = dot(normed, w_key_ref[...])
    query_ref[0] = queries.astype(BF16)
    key_ref[0] = keys.T.astype(BF16)
    value_ref[0] = dot(normed, w_value_ref[...]).astype(BF16)
    blank = jnp.zeros((norm_ref.shape[1] - 2, LANES), F32)
    norm_ref[0] = jnp.concatenate([largest_norms(queries, heads), largest_norms(keys, heads), blank], axis=0)


def project(own, heads, gain, w_query, w_key, w_value):
    members, rows, feat_width = own.shape
    upright = (members, rows, feat_width)
    shapes = [upright, (members, feat_width, rows), upright]
    norm_shape = (members, 8, LANES)

    def spec(shape):
        return pl.BlockSpec((1, *shape[1:]), lambda m: (m, 0, 0))

    return pl.pallas_call(
        functools.partial(project_kernel, heads),
        grid=(members,),
        out_shape=[jax.ShapeDtypeStruct(v, BF16) for v in shapes] + [jax.ShapeDtypeStruct(norm_shape, F32)],
        in_specs=[spec(upright)] + [vmem_spec()] * 4,
        out_specs=[spec(v) for v in (*shapes, norm_shape)],
        compiler_params=pltpu.CompilerParams(vmem_limit_bytes=VMEM_LIMIT),
        cost_estimate=pl.CostEstimate(
            flops=6 * own.size * feat_width, bytes_accessed=8 * own.size, transcendentals=0
        ),
        name="project",
    )(own, gain, w_query, w_key, w_value)


def forward_kernel(
    place_ref,
    window_ref,
    state_ref,
    query_ref,
    key_ref,
    value_ref,
    norm_ref,
    left_ref,
    right_ref,
    attn_gain_ref,
    ffn_gain_ref,
    w_key_ref,
    w_value_ref,
    w_out_ref,
    w_gate_ref,
    w_up_ref,
    down_weight_ref,
    *refs,
):
    out_refs, (key_buf, value_buf, bias_buf, mixed_buf, forecast_buf) = refs[:-5], refs[-5:]
    rows, feat_width = state_ref.shape[1:]
    reach = left_ref.shape[1]
    head_count = window_ref.shape[0]
    head_size = feat_width // head_count
    group_heads = LANES // head_size
    blocks = rows // Q_ROWS
    key_count = Q_ROWS + 2 * reach

    @pl.when(pl.program_id(0) == 0)
    def _():
        apart = jnp.abs(iota((Q_ROWS, key_count), 1) - reach - iota((Q_ROWS, key_count), 0))
        for block in range(blocks):
            k_pos = place_ref[0] - reach + block * Q_ROWS + iota((Q_ROWS, key_count), 1)
            inside = (k_pos >= 0) & (k_pos < place_ref[1])
            for head in range(head_count):
                bias_buf[block, head] = jnp.where(inside & (apart <= window_ref[head]), 0.0, -1e30)
        value_buf[...] = jnp.ones(value_buf.shape, BF16)

    key_buf[:, reach : reach + rows] = key_ref[0]
    groups = head_count // group_heads

    def put_values(lower, values):
        for group in range(groups):
            lanes = slice(2 * group * LANES, (2 * group + 1) * LANES)
            value_buf[lower : lower + values.shape[0], lanes] = values[:, group * LANES : (group + 1) * LANES]

    put_values(reach, value_ref[0])
    key_norms = norm_ref[0, 1:2, :]
    for ref, lower in ((left_ref, 0), (right_ref, reach + rows)):
        normed = rms_scaled(ref[0].astype(F32), attn_gain_ref[...]).astype(BF16)
        keys = dot(normed, w_key_ref[...])
        key_norms = jnp.maximum(key_norms, largest_norms(keys, head_count))
        key_buf[:, lower : lower + reach] = keys.T.astype(BF16)
        put_values(lower, dot(normed, w_value_ref[...]).astype(BF16))

    bound = jnp.max(norm_ref[0, 0:1, :] * key_norms) * 1.05
    safe = bound <= SAFE_SCORE * SAFE_SCORE

    lane_head = iota((1, LANES), 1) // head_size
    head_masks = [(lane_head == head).astype(F32).astype(BF16) for head in range(group_heads)]

    def scores_of(start, count, group):
        lanes = slice(group * LANES, (group + 1) * LANES)
        queries = query_ref[0, pl.ds(start, count), lanes]
        stacked = jnp.concatenate([queries * mask for mask in head_masks], axis=0)
        return dot(stacked, key_buf[lanes, pl.ds(start, count + 2 * reach)])

    def mix_values(start, count, group, weights):
        lanes = slice(2 * group * LANES, 2 * (group + 1) * LANES)
        mixed_all = dot(jnp.concatenate(weights, axis=0), value_buf[pl.ds(start, count + 2 * reach), lanes])
        mixed, totals = mixed_all[:count, :LANES], mixed_all[:count, LANES:]
        for head in range(1, group_heads):
            part = mixed_all[head * count : (head + 1) * count]
            mixed = jnp.where(lane_head == head, part[:, :LANES], mixed)
            totals = jnp.where(lane_head == head, part[:, LANES:], totals)
        mixed_buf[pl.ds(start, count), group * LANES : (group + 1) * LANES] = (mixed / totals).astype(BF16)

    @pl.when(safe)
    def _():
        pair = 2 * Q_ROWS
        corner = jnp.zeros((Q_ROWS, Q_ROWS), BF16)
        units = [(start, group) for start in range(0, rows, pair) for group in range(groups)]
        scores = scores_of(units[0][0], pair, units[0][1])
        for at, (start, group) in enumerate(units):
            following = scores_of(units[at + 1][0], pair, units[at + 1][1]) if at + 1 < len(units) else None
            weights = []
            for head in range(group_heads):
                top = head * pair
                bias = [bias_buf[start // Q_ROWS + part, group * group_heads + head] for part in range(2)]
                upper = jnp.exp2(scores[top : top + Q_ROWS, :key_count] + bias[0])
                lower = jnp.exp2(scores[top + Q_ROWS : top + pair, Q_ROWS:] + bias[1])
                weights.append(jnp.concatenate([upper.astype(BF16), corner], axis=1))
                weights.append(jnp.concatenate([corner, lower.astype(BF16)], axis=1))
            mix_values(start, pair, group, weights)
            scores = following

    @pl.when(jnp.logical_not(safe))
    def _():
        for block in range(blocks):
            start = block * Q_ROWS
            for group in range(groups):
                scores = scores_of(start, Q_ROWS, group)
                weights = []
                for head in range(group_heads):
                    score_matrix = scores[head * Q_ROWS : (head + 1) * Q_ROWS]
                    score_matrix = score_matrix + bias_buf[block, group * group_heads + head]
                    expo = jnp.exp2(score_matrix - jnp.max(score_matrix, axis=-1, keepdims=True))
                    weights.append(expo.astype(BF16))
                mix_values(start, Q_ROWS, group, weights)

    after = (state_ref[0].astype(F32) + dot(mixed_buf[...], w_out_ref[...])).astype(BF16)
    normed_mid = rms_scaled(after.astype(F32), ffn_gain_ref[...]).astype(BF16)
    forecast = after.astype(F32)
    for lower in range(0, w_gate_ref.shape[1], HIDDEN_CHUNK):
        part = slice(lower, lower + HIDDEN_CHUNK)
        gate = 0.5 * dot(normed_mid, w_gate_ref[:, part])
        hidden = (gate * (1.0 + jnp.tanh(gate)) * dot(normed_mid, w_up_ref[:, part])).astype(BF16)
        forecast += dot(hidden, down_weight_ref[part, :])
    forecast_buf[...] = forecast.astype(BF16)
    share_rows = out_refs[0].shape[1]
    for part, out_ref in enumerate(out_refs):
        lower = pl.multiple_of((place_ref[2] ^ part) * share_rows, share_rows)
        out_ref[0] = forecast_buf[pl.ds(lower, share_rows), :]


def forward(place, head_window, own, projected, left, right, gains, weights, shares):
    members, row_count, feat_width = own.shape
    reach = left.shape[1]
    key_count = Q_ROWS + 2 * reach
    hidden_width = weights[3].shape[1]
    macs = members * row_count * feat_width * (3 * feat_width + 3 * hidden_width + 8 * key_count)
    edge_block = pl.BlockSpec((1, reach, feat_width), lambda m: (m, 0, 0))
    return pl.pallas_call(
        forward_kernel,
        grid=(members,),
        out_shape=[jax.ShapeDtypeStruct((members, row_count // shares, feat_width), BF16)] * shares,
        in_specs=[smem_spec()] * 2
        + [pl.BlockSpec((1, *v.shape[1:]), lambda m: (m, 0, 0)) for v in (own, *projected)]
        + [edge_block] * 2
        + [vmem_spec()] * (len(gains) + len(weights)),
        out_specs=[pl.BlockSpec((1, row_count // shares, feat_width), lambda m: (m, 0, 0))] * shares,
        scratch_shapes=[
            pltpu.VMEM((feat_width, row_count + 2 * reach), BF16),
            pltpu.VMEM((row_count + 2 * reach, 2 * feat_width), BF16),
            pltpu.VMEM((row_count // Q_ROWS, head_window.shape[0], Q_ROWS, key_count), F32),
            pltpu.VMEM((row_count, feat_width), BF16),
            pltpu.VMEM((row_count, feat_width), BF16),
        ],
        compiler_params=pltpu.CompilerParams(vmem_limit_bytes=VMEM_LIMIT),
        cost_estimate=pl.CostEstimate(flops=2 * macs, bytes_accessed=10 * own.size, transcendentals=0),
        name="forward",
    )(place, head_window, own, *projected, left, right, *gains, *weights)


def global_member(held, index, own_members):
    return ((held // own_members) ^ index) * own_members + held % own_members


def gram_kernel(index_ref, *refs):
    share_refs, grid_ref, out_ref = refs[:-2], refs[-2], refs[-1]
    own_members, rows, feat_width = share_refs[0].shape
    members = own_members * len(share_refs)
    index = index_ref[0]
    stack = members * GROUP
    total = jnp.zeros((stack, stack), F32)
    proj = jnp.zeros((members, GROUP, feat_width), F32)
    for lower in range(0, rows, GROUP):
        part = slice(lower, lower + GROUP)
        fields = jnp.concatenate([ref[:, part, :] for ref in share_refs], axis=0).astype(F32)
        mean = jnp.sum(fields, axis=0) * (1.0 / members)
        spread = fields - mean[None]
        weight = grid_ref[0, part, :]
        proj += spread * (grid_ref[1, part, :] - weight * mean)[None]
        high, low = halves(spread.reshape(stack, feat_width))
        w_high, w_low = halves((spread * weight[None]).reshape(stack, feat_width))
        last = ((1,), (1,))
        total += dot(w_high, high, last) + dot(w_high, low, last) + dot(w_low, high, last)
    same = iota((stack, stack), 0) % GROUP == iota((stack, stack), 1) % GROUP
    by_row = jnp.sum(jnp.where(same, total, 0.0).reshape(members, GROUP, stack), axis=1)
    column = global_member(iota((stack, LANES), 0) // GROUP, index, own_members)
    folded = (column == iota((stack, LANES), 1) % members).astype(F32)
    held = global_member(iota((members, members), 1), index, own_members)
    in_order = (held == iota((members, members), 0)).astype(F32)
    tiled = exact_dot(in_order, exact_dot(by_row, folded))
    per_row = LANES // members
    keep = iota((members, LANES), 0) % per_row == iota((members, LANES), 1) // members
    packed = jnp.sum(jnp.where(keep, tiled, 0.0).reshape(members // per_row, per_row, LANES), axis=1)
    proj_col = jnp.sum(jnp.sum(proj, axis=1), axis=1, keepdims=True)
    at_lane = global_member(iota((members, LANES), 0), index, own_members) == iota((members, LANES), 1)
    proj_row = jnp.sum(jnp.where(at_lane, proj_col, 0.0), axis=0, keepdims=True)
    filled = members // per_row + 1
    blank = jnp.zeros((out_ref.shape[0] - filled, LANES), F32)
    out_ref[...] = jnp.concatenate([packed, proj_row, blank], axis=0)


def gram_partial(index, shares, grid):
    members = shares[0].shape[0] * len(shares)
    filled = members * members // LANES + 1
    return pl.pallas_call(
        gram_kernel,
        out_shape=jax.ShapeDtypeStruct((-(-filled // 8) * 8, LANES), F32),
        in_specs=[smem_spec()] + [vmem_spec()] * (len(shares) + 1),
        out_specs=vmem_spec(),
        compiler_params=pltpu.CompilerParams(vmem_limit_bytes=VMEM_LIMIT),
        cost_estimate=pl.CostEstimate(
            flops=3 * GROUP * members * members * grid.size, bytes_accessed=members * grid.size, transcendentals=0
        ),
        name="gram",
    )(index, *shares, grid)


def ensemble_transform(gram, proj):
    members = gram.shape[0]
    row, column = iota((members, members), 0), iota((members, members), 1)
    identity = (row == column).astype(F32)
    system = gram + (members - 1.0) * identity
    left, right = system, proj
    for pivot in range(members):
        is_pivot = iota((members, 1), 0) == pivot
        scale = 1.0 / left[pivot : pivot + 1, pivot : pivot + 1]
        pivot_row = left[pivot : pivot + 1, :] * scale
        pivot_right = right[pivot : pivot + 1, :] * scale
        factor = left[:, pivot : pivot + 1]
        left = jnp.where(is_pivot, pivot_row, left - factor * pivot_row)
        right = jnp.where(is_pivot, pivot_right, right - factor * pivot_right)
    mean_weights = right
    mean_level = jnp.sum(jnp.sum(system * identity, axis=1, keepdims=True), axis=0, keepdims=True) / members
    lifted = system + (mean_level - (members - 1.0)) * (1.0 / members)
    frobenius = jnp.sqrt(jnp.sum(jnp.sum(lifted * lifted, axis=1, keepdims=True), axis=0, keepdims=True))
    root_iter = lifted / frobenius
    inv_iter = identity
    for sweep in range(NS_STEPS):
        product = root_iter if sweep == 0 else exact_dot(inv_iter, root_iter)
        correction = 1.5 * identity - 0.5 * product
        inv_iter = correction if sweep == 0 else exact_dot(correction, inv_iter)
        if sweep < NS_STEPS - 1:
            root_iter = exact_dot(root_iter, correction)
    inv_root = inv_iter / jnp.sqrt(frobenius) + (1.0 / math.sqrt(members - 1.0) - 1.0 / jnp.sqrt(mean_level)) * (
        1.0 / members
    )
    moved = mean_weights + math.sqrt(members - 1.0) * inv_root
    return 1.0 / members + moved - jnp.sum(moved, axis=0, keepdims=True) * (1.0 / members)


def combine_kernel(index_ref, partial_ref, *refs):
    share_refs, out_refs = refs[: len(refs) // 2], refs[len(refs) // 2 :]
    own_members, rows, feat_width = share_refs[0].shape
    members = own_members * len(share_refs)
    stack = members * GROUP
    per_row = LANES // members
    sums = jnp.sum(partial_ref[...], axis=0)
    spread_rows = jnp.concatenate(
        [jnp.broadcast_to(sums[r : r + 1], (per_row, LANES)) for r in range(members // per_row)], axis=0
    )
    keep = iota((members, LANES), 0) % per_row == iota((members, LANES), 1) // members
    folded = (iota((LANES, members), 0) % members == iota((LANES, members), 1)).astype(F32)
    gram = exact_dot(jnp.where(keep, spread_rows, 0.0), folded)
    proj_row = jnp.broadcast_to(sums[members // per_row : members // per_row + 1], (members, LANES))
    on_diagonal = iota((members, LANES), 0) == iota((members, LANES), 1)
    proj = jnp.sum(jnp.where(on_diagonal, proj_row, 0.0), axis=1, keepdims=True)
    transform = ensemble_transform(gram, proj)
    held = global_member(iota((stack, members), 0) // GROUP, index_ref[0], own_members)
    pick = (held == iota((stack, members), 1)).astype(F32).astype(BF16)
    same = iota((stack, stack), 0) % GROUP == iota((stack, stack), 1) % GROUP
    mixers = []
    for piece in halves(transform):
        rows_of = dot(pick, piece, ((1,), (1,))).astype(BF16)
        mixers.append(jnp.where(same, dot(rows_of, pick, ((1,), (1,))), 0.0).astype(BF16))
    for lower in range(0, rows, GROUP):
        part = slice(lower, lower + GROUP)
        fields = jnp.concatenate([ref[:, part, :].reshape(-1, feat_width) for ref in share_refs], axis=0)
        mixed = (dot(mixers[0], fields) + dot(mixers[1], fields)).astype(BF16)
        own_stack = own_members * GROUP
        for at, out_ref in enumerate(out_refs):
            piece = mixed[at * own_stack : (at + 1) * own_stack]
            out_ref[:, part, :] = piece.reshape(own_members, GROUP, feat_width)


def combine(index, partials, shares):
    size = shares[0].size * len(shares)
    members = shares[0].shape[0] * len(shares)
    return pl.pallas_call(
        combine_kernel,
        out_shape=[jax.ShapeDtypeStruct(v.shape, BF16) for v in shares],
        in_specs=[smem_spec()] + [vmem_spec()] * (1 + len(shares)),
        out_specs=[vmem_spec()] * len(shares),
        compiler_params=pltpu.CompilerParams(vmem_limit_bytes=VMEM_LIMIT),
        cost_estimate=pl.CostEstimate(flops=4 * GROUP * members * size, bytes_accessed=4 * size, transcendentals=0),
        name="combine",
    )(index, partials, *shares)


def assemble_kernel(index_ref, *refs):
    part_refs, out_ref = refs[:-1], refs[-1]
    rows = part_refs[0].shape[1]
    for part, ref in enumerate(part_refs):
        lower = pl.multiple_of((index_ref[0] ^ part) * rows, rows)
        out_ref[0, pl.ds(lower, rows), :] = ref[0]


def assemble(index, parts):
    members, rows, feat_width = parts[0].shape
    return pl.pallas_call(
        assemble_kernel,
        grid=(members,),
        out_shape=jax.ShapeDtypeStruct((members, len(parts) * rows, feat_width), BF16),
        in_specs=[smem_spec()] + [pl.BlockSpec((1, rows, feat_width), lambda m: (m, 0, 0))] * len(parts),
        out_specs=pl.BlockSpec((1, len(parts) * rows, feat_width), lambda m: (m, 0, 0)),
        compiler_params=pltpu.CompilerParams(vmem_limit_bytes=VMEM_LIMIT),
        cost_estimate=pl.CostEstimate(flops=0, bytes_accessed=4 * len(parts) * parts[0].size, transcendentals=0),
        name="assemble",
    )(index, *parts)


def exchanged(parts):
    count = lax.axis_size("mem")
    return [
        lax.ppermute(v, "mem", [(i, i ^ part) for i in range(count)]) if part else v for part, v in enumerate(parts)
    ]


def local(
    ens_state,
    attn_gain,
    ffn_gain,
    w_query,
    w_key,
    w_value,
    w_out,
    w_gate,
    w_up,
    down_weight,
    head_window,
    obs_token,
    obs_channel,
    obs_value,
    obs_var,
):
    own_members, row_count, feat_width = ens_state.shape
    mem_count = lax.axis_size("mem")
    tok_count = lax.axis_size("tok")
    device_count = mem_count * tok_count
    share_rows = row_count // mem_count
    first_pos = lax.axis_index("tok") * row_count
    up = [(i, i + 1) for i in range(tok_count - 1)]
    down = [(i + 1, i) for i in range(tok_count - 1)]
    left = lax.ppermute(ens_state[:, row_count - WIN :], "tok", up)
    right = lax.ppermute(ens_state[:, :WIN], "tok", down)
    share_start = first_pos + lax.axis_index("mem") * share_rows
    grid = sample_grid(
        share_start.astype(jnp.int32).reshape(1), obs_token, obs_channel, obs_value, obs_var, share_rows, feat_width
    )
    index = lax.axis_index("mem")
    place = jnp.stack([first_pos, row_count * tok_count, index]).astype(jnp.int32)
    index = index.astype(jnp.int32).reshape(1)
    gains = [attn_gain.reshape(1, -1), ffn_gain.reshape(1, -1)]
    projected = project(ens_state, head_window.shape[0], gains[0], w_query, w_key, w_value)
    weights = [w_key, w_value, w_out, w_gate, w_up, down_weight]
    forecast = forward(place, head_window, ens_state, projected, left, right, gains, weights, mem_count)
    shares = exchanged(forecast)
    partial = gram_partial(index, shares, grid)
    partials = lax.all_to_all(
        jnp.broadcast_to(partial[None], (device_count, *partial.shape)),
        ("mem", "tok"),
        split_axis=0,
        concat_axis=0,
        tiled=True,
    )
    return assemble(index, exchanged(combine(index, partials, shares)))


def solution(mesh):
    in_specs = (P("mem", "tok", None), *[P()] * 10, *[P("tok")] * 4)
    return jax.shard_map(local, mesh=mesh, in_specs=in_specs, out_specs=P("mem", "tok", None), check_vma=False)
```

```python
import functools
import math

import jax
import jax.numpy as jnp
from jax import lax
from jax.experimental import pallas as pl
from jax.experimental.pallas import tpu as pltpu
from jax.sharding import PartitionSpec as P

WIN = 256
NS_STEPS = 8
EPS = 1e-05
Q_ROWS = 128
GROUP = 16
LANES = 128
VMEM_LIMIT = 32 * 1024 * 1024
SAFE_SCORE = 56.0
HIDDEN_CHUNK = 256

F32 = jnp.float32
BF16 = jnp.bfloat16


def dot(a, b, contract=((1,), (0,)), precision=None):
    return lax.dot_general(a, b, (contract, ((), ())), precision=precision, preferred_element_type=F32)


def exact_dot(a, b, contract=((1,), (0,))):
    return dot(a, b, contract, lax.Precision.HIGHEST)


def iota(shape, axis):
    return lax.broadcasted_iota(jnp.int32, shape, axis)


def halves(values):
    high = values.astype(BF16)
    return high, (values - high.astype(F32)).astype(BF16)


def rms_scaled(values, gain):
    rows, width = values.shape
    ones = jnp.ones((width, LANES), BF16)
    means = dot((values * values).astype(BF16), ones) * (1.0 / width)
    scale = lax.rsqrt(means + EPS)
    return values * jnp.concatenate([scale] * (width // LANES), axis=1) * gain


def vmem_spec():
    return pl.BlockSpec(memory_space=pltpu.VMEM)


def smem_spec():
    return pl.BlockSpec(memory_space=pltpu.SMEM)


def sample_grid_kernel(start_ref, token_ref, channel_ref, value_ref, var_ref, out_ref):
    rows, feat_width = out_ref.shape[1:]
    count = token_ref.shape[1]
    chunk = min(1024, count)
    total = jnp.zeros((4 * rows, feat_width), F32)
    for lower in range(0, count, chunk):
        part = slice(lower, lower + chunk)
        inv_var = 1.0 / var_ref[:, part]
        weighted = value_ref[:, part] * inv_var
        here = iota((rows, chunk), 0) == token_ref[:, part] - start_ref[0]
        pieces = []
        for row in (inv_var, weighted):
            high = row.astype(BF16).astype(F32)
            pieces.append(jnp.where(here, high, 0.0).astype(BF16))
            pieces.append(jnp.where(here, row - high, 0.0).astype(BF16))
        channel_hot = jnp.where(iota((feat_width, chunk), 0) == channel_ref[:, part], 1.0, 0.0).astype(BF16)
        total += dot(jnp.concatenate(pieces, axis=0), channel_hot, ((1,), (1,)))
    out_ref[0] = total[:rows] + total[rows : 2 * rows]
    out_ref[1] = total[2 * rows : 3 * rows] + total[3 * rows :]


def sample_grid(start, obs_token, obs_channel, obs_value, obs_var, rows, feat_width):
    count = obs_token.shape[0]
    return pl.pallas_call(
        sample_grid_kernel,
        out_shape=jax.ShapeDtypeStruct((2, rows, feat_width), F32),
        in_specs=[smem_spec()] + [vmem_spec()] * 4,
        out_specs=vmem_spec(),
        compiler_params=pltpu.CompilerParams(vmem_limit_bytes=VMEM_LIMIT),
        cost_estimate=pl.CostEstimate(flops=8 * rows * count * feat_width, bytes_accessed=16 * count, transcendentals=0),
        name="sample_grid",
    )(start, *(v.reshape(1, count) for v in (obs_token, obs_channel, obs_value, obs_var)))


def head_lanes(feat_width, heads):
    lane_head = iota((feat_width, LANES), 0) // (feat_width // heads)
    return (lane_head == iota((feat_width, LANES), 1)).astype(F32).astype(BF16)


def largest_norms(values, heads):
    squares = dot((values * values).astype(BF16), head_lanes(values.shape[1], heads))
    return jnp.max(squares, axis=0, keepdims=True)


def project_kernel(
    heads, own_ref, gain_ref, w_query_ref, w_key_ref, w_value_ref, query_ref, key_ref, value_ref, norm_ref
):
    scale = math.log2(math.e) / math.sqrt(own_ref.shape[2] // heads)
    normed = rms_scaled(own_ref[0].astype(F32), gain_ref[...]).astype(BF16)
    queries = dot(normed, w_query_ref[...]) * scale
    keys = dot(normed, w_key_ref[...])
    query_ref[0] = queries.astype(BF16)
    key_ref[0] = keys.T.astype(BF16)
    value_ref[0] = dot(normed, w_value_ref[...]).astype(BF16)
    blank = jnp.zeros((norm_ref.shape[1] - 2, LANES), F32)
    norm_ref[0] = jnp.concatenate([largest_norms(queries, heads), largest_norms(keys, heads), blank], axis=0)


def project(own, heads, gain, w_query, w_key, w_value):
    members, rows, feat_width = own.shape
    upright = (members, rows, feat_width)
    shapes = [upright, (members, feat_width, rows), upright]
    norm_shape = (members, 8, LANES)

    def spec(shape):
        return pl.BlockSpec((1, *shape[1:]), lambda m: (m, 0, 0))

    return pl.pallas_call(
        functools.partial(project_kernel, heads),
        grid=(members,),
        out_shape=[jax.ShapeDtypeStruct(v, BF16) for v in shapes] + [jax.ShapeDtypeStruct(norm_shape, F32)],
        in_specs=[spec(upright)] + [vmem_spec()] * 4,
        out_specs=[spec(v) for v in (*shapes, norm_shape)],
        compiler_params=pltpu.CompilerParams(vmem_limit_bytes=VMEM_LIMIT),
        cost_estimate=pl.CostEstimate(
            flops=6 * own.size * feat_width, bytes_accessed=8 * own.size, transcendentals=0
        ),
        name="project",
    )(own, gain, w_query, w_key, w_value)


def forward_kernel(
    earlier,
    place_ref,
    window_ref,
    state_ref,
    query_ref,
    key_ref,
    value_ref,
    norm_ref,
    left_ref,
    right_ref,
    attn_gain_ref,
    ffn_gain_ref,
    w_key_ref,
    w_value_ref,
    w_out_ref,
    w_gate_ref,
    w_up_ref,
    down_weight_ref,
    *refs,
):
    refs = refs[earlier:]
    out_refs, (key_buf, value_buf, bias_buf, mixed_buf, forecast_buf) = refs[:-5], refs[-5:]
    rows, feat_width = state_ref.shape[1:]
    reach = left_ref.shape[1]
    head_count = window_ref.shape[0]
    head_size = feat_width // head_count
    group_heads = LANES // head_size
    blocks = rows // Q_ROWS
    key_count = Q_ROWS + 2 * reach

    @pl.when(pl.program_id(0) == 0)
    def _():
        apart = jnp.abs(iota((Q_ROWS, key_count), 1) - reach - iota((Q_ROWS, key_count), 0))
        for block in range(blocks):
            k_pos = place_ref[0] - reach + block * Q_ROWS + iota((Q_ROWS, key_count), 1)
            inside = (k_pos >= 0) & (k_pos < place_ref[1])
            for head in range(head_count):
                bias_buf[block, head] = jnp.where(inside & (apart <= window_ref[head]), 0.0, -1e30)
        value_buf[...] = jnp.ones(value_buf.shape, BF16)

    key_buf[:, reach : reach + rows] = key_ref[0]
    groups = head_count // group_heads

    def put_values(lower, values):
        for group in range(groups):
            lanes = slice(2 * group * LANES, (2 * group + 1) * LANES)
            value_buf[lower : lower + values.shape[0], lanes] = values[:, group * LANES : (group + 1) * LANES]

    put_values(reach, value_ref[0])
    key_norms = norm_ref[0, 1:2, :]
    for ref, lower in ((left_ref, 0), (right_ref, reach + rows)):
        normed = rms_scaled(ref[0].astype(F32), attn_gain_ref[...]).astype(BF16)
        keys = dot(normed, w_key_ref[...])
        key_norms = jnp.maximum(key_norms, largest_norms(keys, head_count))
        key_buf[:, lower : lower + reach] = keys.T.astype(BF16)
        put_values(lower, dot(normed, w_value_ref[...]).astype(BF16))

    bound = jnp.max(norm_ref[0, 0:1, :] * key_norms) * 1.05
    safe = bound <= SAFE_SCORE * SAFE_SCORE

    lane_head = iota((1, LANES), 1) // head_size
    head_masks = [(lane_head == head).astype(F32).astype(BF16) for head in range(group_heads)]

    def scores_of(start, count, group):
        lanes = slice(group * LANES, (group + 1) * LANES)
        queries = query_ref[0, pl.ds(start, count), lanes]
        stacked = jnp.concatenate([queries * mask for mask in head_masks], axis=0)
        return dot(stacked, key_buf[lanes, pl.ds(start, count + 2 * reach)])

    def mix_values(start, count, group, weights):
        lanes = slice(2 * group * LANES, 2 * (group + 1) * LANES)
        mixed_all = dot(jnp.concatenate(weights, axis=0), value_buf[pl.ds(start, count + 2 * reach), lanes])
        mixed, totals = mixed_all[:count, :LANES], mixed_all[:count, LANES:]
        for head in range(1, group_heads):
            part = mixed_all[head * count : (head + 1) * count]
            mixed = jnp.where(lane_head == head, part[:, :LANES], mixed)
            totals = jnp.where(lane_head == head, part[:, LANES:], totals)
        mixed_buf[pl.ds(start, count), group * LANES : (group + 1) * LANES] = (mixed / totals).astype(BF16)

    @pl.when(safe)
    def _():
        pair = 2 * Q_ROWS
        corner = jnp.zeros((Q_ROWS, Q_ROWS), BF16)
        units = [(start, group) for start in range(0, rows, pair) for group in range(groups)]
        scores = scores_of(units[0][0], pair, units[0][1])
        for at, (start, group) in enumerate(units):
            following = scores_of(units[at + 1][0], pair, units[at + 1][1]) if at + 1 < len(units) else None
            weights = []
            for head in range(group_heads):
                top = head * pair
                bias = [bias_buf[start // Q_ROWS + part, group * group_heads + head] for part in range(2)]
                upper = jnp.exp2(scores[top : top + Q_ROWS, :key_count] + bias[0])
                lower = jnp.exp2(scores[top + Q_ROWS : top + pair, Q_ROWS:] + bias[1])
                weights.append(jnp.concatenate([upper.astype(BF16), corner], axis=1))
                weights.append(jnp.concatenate([corner, lower.astype(BF16)], axis=1))
            mix_values(start, pair, group, weights)
            scores = following

    @pl.when(jnp.logical_not(safe))
    def _():
        for block in range(blocks):
            start = block * Q_ROWS
            for group in range(groups):
                scores = scores_of(start, Q_ROWS, group)
                weights = []
                for head in range(group_heads):
                    score_matrix = scores[head * Q_ROWS : (head + 1) * Q_ROWS]
                    score_matrix = score_matrix + bias_buf[block, group * group_heads + head]
                    expo = jnp.exp2(score_matrix - jnp.max(score_matrix, axis=-1, keepdims=True))
                    weights.append(expo.astype(BF16))
                mix_values(start, Q_ROWS, group, weights)

    after = (state_ref[0].astype(F32) + dot(mixed_buf[...], w_out_ref[...])).astype(BF16)
    normed_mid = rms_scaled(after.astype(F32), ffn_gain_ref[...]).astype(BF16)
    forecast = after.astype(F32)
    for lower in range(0, w_gate_ref.shape[1], HIDDEN_CHUNK):
        part = slice(lower, lower + HIDDEN_CHUNK)
        gate = 0.5 * dot(normed_mid, w_gate_ref[:, part])
        hidden = (gate * (1.0 + jnp.tanh(gate)) * dot(normed_mid, w_up_ref[:, part])).astype(BF16)
        forecast += dot(hidden, down_weight_ref[part, :])
    forecast_buf[...] = forecast.astype(BF16)
    share_rows = out_refs[0].shape[1]
    for part, out_ref in enumerate(out_refs):
        lower = pl.multiple_of((place_ref[2] ^ part) * share_rows, share_rows)
        out_ref[0] = forecast_buf[pl.ds(lower, share_rows), :]


def forward(place, head_window, own, projected, left, right, gains, weights, shares, first, earlier):
    _, row_count, feat_width = own.shape
    members, reach, _ = left.shape
    key_count = Q_ROWS + 2 * reach
    hidden_width = weights[3].shape[1]
    macs = members * row_count * feat_width * (3 * feat_width + 3 * hidden_width + 8 * key_count)

    def spec(array, offset):
        return pl.BlockSpec((1, *array.shape[1:]), lambda m: (m + offset, 0, 0))

    return pl.pallas_call(
        functools.partial(forward_kernel, len(earlier)),
        grid=(members,),
        out_shape=[jax.ShapeDtypeStruct((members, row_count // shares, feat_width), BF16)] * shares,
        in_specs=[smem_spec()] * 2
        + [spec(v, first) for v in (own, *projected)]
        + [spec(v, 0) for v in (left, right)]
        + [vmem_spec()] * (len(gains) + len(weights))
        + [pl.BlockSpec(memory_space=pl.ANY)] * len(earlier),
        out_specs=[pl.BlockSpec((1, row_count // shares, feat_width), lambda m: (m, 0, 0))] * shares,
        scratch_shapes=[
            pltpu.VMEM((feat_width, row_count + 2 * reach), BF16),
            pltpu.VMEM((row_count + 2 * reach, 2 * feat_width), BF16),
            pltpu.VMEM((row_count // Q_ROWS, head_window.shape[0], Q_ROWS, key_count), F32),
            pltpu.VMEM((row_count, feat_width), BF16),
            pltpu.VMEM((row_count, feat_width), BF16),
        ],
        compiler_params=pltpu.CompilerParams(vmem_limit_bytes=VMEM_LIMIT),
        cost_estimate=pl.CostEstimate(
            flops=2 * macs, bytes_accessed=10 * members * row_count * feat_width, transcendentals=0
        ),
        name="forward",
    )(place, head_window, own, *projected, left, right, *gains, *weights, *earlier)


def global_member(held, index, own_members):
    return ((held // own_members) ^ index) * own_members + held % own_members


def gram_kernel(parts, index_ref, *refs):
    share_refs, grid_ref, out_ref = refs[:-2], refs[-2], refs[-1]
    rows, feat_width = share_refs[0].shape[1:]
    members = sum(ref.shape[0] for ref in share_refs)
    own_members = members // parts
    index = index_ref[0]
    stack = members * GROUP
    total = jnp.zeros((stack, stack), F32)
    proj = jnp.zeros((members, GROUP, feat_width), F32)
    for lower in range(0, rows, GROUP):
        part = slice(lower, lower + GROUP)
        fields = jnp.concatenate([ref[:, part, :] for ref in share_refs], axis=0).astype(F32)
        mean = jnp.sum(fields, axis=0) * (1.0 / members)
        spread = fields - mean[None]
        weight = grid_ref[0, part, :]
        proj += spread * (grid_ref[1, part, :] - weight * mean)[None]
        high, low = halves(spread.reshape(stack, feat_width))
        w_high, w_low = halves((spread * weight[None]).reshape(stack, feat_width))
        last = ((1,), (1,))
        total += dot(w_high, high, last) + dot(w_high, low, last) + dot(w_low, high, last)
    same = iota((stack, stack), 0) % GROUP == iota((stack, stack), 1) % GROUP
    by_row = jnp.sum(jnp.where(same, total, 0.0).reshape(members, GROUP, stack), axis=1)
    column = global_member(iota((stack, LANES), 0) // GROUP, index, own_members)
    folded = (column == iota((stack, LANES), 1) % members).astype(F32)
    held = global_member(iota((members, members), 1), index, own_members)
    in_order = (held == iota((members, members), 0)).astype(F32)
    tiled = exact_dot(in_order, exact_dot(by_row, folded))
    per_row = LANES // members
    keep = iota((members, LANES), 0) % per_row == iota((members, LANES), 1) // members
    packed = jnp.sum(jnp.where(keep, tiled, 0.0).reshape(members // per_row, per_row, LANES), axis=1)
    proj_col = jnp.sum(jnp.sum(proj, axis=1), axis=1, keepdims=True)
    at_lane = global_member(iota((members, LANES), 0), index, own_members) == iota((members, LANES), 1)
    proj_row = jnp.sum(jnp.where(at_lane, proj_col, 0.0), axis=0, keepdims=True)
    filled = members // per_row + 1
    blank = jnp.zeros((out_ref.shape[0] - filled, LANES), F32)
    out_ref[...] = jnp.concatenate([packed, proj_row, blank], axis=0)


def gram_partial(index, shares, grid):
    flat = [v for part in shares for v in part]
    members = sum(v.shape[0] for v in flat)
    filled = members * members // LANES + 1
    return pl.pallas_call(
        functools.partial(gram_kernel, len(shares)),
        out_shape=jax.ShapeDtypeStruct((-(-filled // 8) * 8, LANES), F32),
        in_specs=[smem_spec()] + [vmem_spec()] * (len(flat) + 1),
        out_specs=vmem_spec(),
        compiler_params=pltpu.CompilerParams(vmem_limit_bytes=VMEM_LIMIT),
        cost_estimate=pl.CostEstimate(
            flops=3 * GROUP * members * members * grid.size, bytes_accessed=members * grid.size, transcendentals=0
        ),
        name="gram",
    )(index, *flat, grid)


def ensemble_transform(gram, proj):
    members = gram.shape[0]
    row, column = iota((members, members), 0), iota((members, members), 1)
    identity = (row == column).astype(F32)
    system = gram + (members - 1.0) * identity
    left, right = system, proj
    for pivot in range(members):
        is_pivot = iota((members, 1), 0) == pivot
        scale = 1.0 / left[pivot : pivot + 1, pivot : pivot + 1]
        pivot_row = left[pivot : pivot + 1, :] * scale
        pivot_right = right[pivot : pivot + 1, :] * scale
        factor = left[:, pivot : pivot + 1]
        left = jnp.where(is_pivot, pivot_row, left - factor * pivot_row)
        right = jnp.where(is_pivot, pivot_right, right - factor * pivot_right)
    mean_weights = right
    mean_level = jnp.sum(jnp.sum(system * identity, axis=1, keepdims=True), axis=0, keepdims=True) / members
    lifted = system + (mean_level - (members - 1.0)) * (1.0 / members)
    frobenius = jnp.sqrt(jnp.sum(jnp.sum(lifted * lifted, axis=1, keepdims=True), axis=0, keepdims=True))
    root_iter = lifted / frobenius
    inv_iter = identity
    for sweep in range(NS_STEPS):
        product = root_iter if sweep == 0 else exact_dot(inv_iter, root_iter)
        correction = 1.5 * identity - 0.5 * product
        inv_iter = correction if sweep == 0 else exact_dot(correction, inv_iter)
        if sweep < NS_STEPS - 1:
            root_iter = exact_dot(root_iter, correction)
    inv_root = inv_iter / jnp.sqrt(frobenius) + (1.0 / math.sqrt(members - 1.0) - 1.0 / jnp.sqrt(mean_level)) * (
        1.0 / members
    )
    moved = mean_weights + math.sqrt(members - 1.0) * inv_root
    return 1.0 / members + moved - jnp.sum(moved, axis=0, keepdims=True) * (1.0 / members)


def combine_kernel(parts, index_ref, partial_ref, *refs):
    share_refs, out_refs = refs[:-parts], refs[-parts:]
    own_members, rows, feat_width = out_refs[0].shape
    members = own_members * parts
    stack = members * GROUP
    per_row = LANES // members
    sums = jnp.sum(partial_ref[...], axis=0)
    spread_rows = jnp.concatenate(
        [jnp.broadcast_to(sums[r : r + 1], (per_row, LANES)) for r in range(members // per_row)], axis=0
    )
    keep = iota((members, LANES), 0) % per_row == iota((members, LANES), 1) // members
    folded = (iota((LANES, members), 0) % members == iota((LANES, members), 1)).astype(F32)
    gram = exact_dot(jnp.where(keep, spread_rows, 0.0), folded)
    proj_row = jnp.broadcast_to(sums[members // per_row : members // per_row + 1], (members, LANES))
    on_diagonal = iota((members, LANES), 0) == iota((members, LANES), 1)
    proj = jnp.sum(jnp.where(on_diagonal, proj_row, 0.0), axis=1, keepdims=True)
    transform = ensemble_transform(gram, proj)
    held = global_member(iota((stack, members), 0) // GROUP, index_ref[0], own_members)
    pick = (held == iota((stack, members), 1)).astype(F32).astype(BF16)
    same = iota((stack, stack), 0) % GROUP == iota((stack, stack), 1) % GROUP
    mixers = []
    for piece in halves(transform):
        rows_of = dot(pick, piece, ((1,), (1,))).astype(BF16)
        mixers.append(jnp.where(same, dot(rows_of, pick, ((1,), (1,))), 0.0).astype(BF16))
    for lower in range(0, rows, GROUP):
        part = slice(lower, lower + GROUP)
        fields = jnp.concatenate([ref[:, part, :].reshape(-1, feat_width) for ref in share_refs], axis=0)
        mixed = (dot(mixers[0], fields) + dot(mixers[1], fields)).astype(BF16)
        own_stack = own_members * GROUP
        for at, out_ref in enumerate(out_refs):
            piece = mixed[at * own_stack : (at + 1) * own_stack]
            out_ref[:, part, :] = piece.reshape(own_members, GROUP, feat_width)


def combine(index, partials, shares):
    flat = [v for part in shares for v in part]
    own_members = sum(v.shape[0] for v in shares[0])
    shape = (own_members, *flat[0].shape[1:])
    size = len(shares) * math.prod(shape)
    return pl.pallas_call(
        functools.partial(combine_kernel, len(shares)),
        out_shape=[jax.ShapeDtypeStruct(shape, BF16)] * len(shares),
        in_specs=[smem_spec()] + [vmem_spec()] * (1 + len(flat)),
        out_specs=[vmem_spec()] * len(shares),
        compiler_params=pltpu.CompilerParams(vmem_limit_bytes=VMEM_LIMIT),
        cost_estimate=pl.CostEstimate(
            flops=4 * GROUP * own_members * len(shares) * size, bytes_accessed=4 * size, transcendentals=0
        ),
        name="combine",
    )(index, partials, *flat)


def assemble_kernel(index_ref, *refs):
    part_refs, out_ref = refs[:-1], refs[-1]
    rows = part_refs[0].shape[1]
    for part, ref in enumerate(part_refs):
        lower = pl.multiple_of((index_ref[0] ^ part) * rows, rows)
        out_ref[0, pl.ds(lower, rows), :] = ref[0]


def assemble(index, parts):
    members, rows, feat_width = parts[0].shape
    return pl.pallas_call(
        assemble_kernel,
        grid=(members,),
        out_shape=jax.ShapeDtypeStruct((members, len(parts) * rows, feat_width), BF16),
        in_specs=[smem_spec()] + [pl.BlockSpec((1, rows, feat_width), lambda m: (m, 0, 0))] * len(parts),
        out_specs=pl.BlockSpec((1, len(parts) * rows, feat_width), lambda m: (m, 0, 0)),
        compiler_params=pltpu.CompilerParams(vmem_limit_bytes=VMEM_LIMIT),
        cost_estimate=pl.CostEstimate(flops=0, bytes_accessed=4 * len(parts) * parts[0].size, transcendentals=0),
        name="assemble",
    )(index, *parts)


def exchanged(parts):
    count = lax.axis_size("mem")
    return [
        lax.ppermute(v, "mem", [(i, i ^ part) for i in range(count)]) if part else v for part, v in enumerate(parts)
    ]


def local(
    ens_state,
    attn_gain,
    ffn_gain,
    w_query,
    w_key,
    w_value,
    w_out,
    w_gate,
    w_up,
    down_weight,
    head_window,
    obs_token,
    obs_channel,
    obs_value,
    obs_var,
):
    own_members, row_count, feat_width = ens_state.shape
    mem_count = lax.axis_size("mem")
    tok_count = lax.axis_size("tok")
    device_count = mem_count * tok_count
    share_rows = row_count // mem_count
    first_pos = lax.axis_index("tok") * row_count
    up = [(i, i + 1) for i in range(tok_count - 1)]
    down = [(i + 1, i) for i in range(tok_count - 1)]
    half = own_members // 2
    bounds = [(0, half), (half, own_members)]
    halos = [
        (
            lax.ppermute(ens_state[lower:upper, row_count - WIN :], "tok", up),
            lax.ppermute(ens_state[lower:upper, :WIN], "tok", down),
        )
        for lower, upper in bounds
    ]
    share_start = first_pos + lax.axis_index("mem") * share_rows
    grid = sample_grid(
        share_start.astype(jnp.int32).reshape(1), obs_token, obs_channel, obs_value, obs_var, share_rows, feat_width
    )
    index = lax.axis_index("mem")
    place = jnp.stack([first_pos, row_count * tok_count, index]).astype(jnp.int32)
    index = index.astype(jnp.int32).reshape(1)
    gains = [attn_gain.reshape(1, -1), ffn_gain.reshape(1, -1)]
    projected = project(ens_state, head_window.shape[0], gains[0], w_query, w_key, w_value)
    weights = [w_key, w_value, w_out, w_gate, w_up, down_weight]
    by_half, earlier = [], []
    for (lower, _), (left, right) in zip(bounds, halos):
        forecast = forward(
            place, head_window, ens_state, projected, left, right, gains, weights, mem_count, lower, earlier
        )
        earlier = forecast[:1]
        by_half.append(exchanged(forecast))
    shares = list(zip(*by_half))
    partial = gram_partial(index, shares, grid)
    partials = lax.all_to_all(
        jnp.broadcast_to(partial[None], (device_count, *partial.shape)),
        ("mem", "tok"),
        split_axis=0,
        concat_axis=0,
        tiled=True,
    )
    return assemble(index, exchanged(combine(index, partials, shares)))


def solution(mesh):
    in_specs = (P("mem", "tok", None), *[P()] * 10, *[P("tok")] * 4)
    return jax.shard_map(local, mesh=mesh, in_specs=in_specs, out_specs=P("mem", "tok", None), check_vma=False)
```

```python
import functools
import math

import jax
import jax.numpy as jnp
from jax import lax
from jax.experimental import pallas as pl
from jax.experimental.pallas import tpu as pltpu
from jax.sharding import PartitionSpec as P

WIN = 256
NS_STEPS = 8
EPS = 1e-05
Q_ROWS = 128
GROUP = 16
LANES = 128
VMEM_LIMIT = 32 * 1024 * 1024
SAFE_SCORE = 56.0
HIDDEN_CHUNK = 256

F32 = jnp.float32
BF16 = jnp.bfloat16


def dot(a, b, contract=((1,), (0,)), precision=None):
    return lax.dot_general(a, b, (contract, ((), ())), precision=precision, preferred_element_type=F32)


def exact_dot(a, b, contract=((1,), (0,))):
    return dot(a, b, contract, lax.Precision.HIGHEST)


def iota(shape, axis):
    return lax.broadcasted_iota(jnp.int32, shape, axis)


def halves(values):
    high = values.astype(BF16)
    return high, (values - high.astype(F32)).astype(BF16)


def rms_scaled(values, gain):
    rows, width = values.shape
    ones = jnp.ones((width, LANES), BF16)
    means = dot((values * values).astype(BF16), ones) * (1.0 / width)
    scale = lax.rsqrt(means + EPS)
    return values * jnp.concatenate([scale] * (width // LANES), axis=1) * gain


def vmem_spec():
    return pl.BlockSpec(memory_space=pltpu.VMEM)


def smem_spec():
    return pl.BlockSpec(memory_space=pltpu.SMEM)


def sample_grid_kernel(start_ref, token_ref, channel_ref, value_ref, var_ref, out_ref):
    rows, feat_width = out_ref.shape[1:]
    count = token_ref.shape[1]
    chunk = min(1024, count)
    total = jnp.zeros((4 * rows, feat_width), F32)
    for lower in range(0, count, chunk):
        part = slice(lower, lower + chunk)
        inv_var = 1.0 / var_ref[:, part]
        weighted = value_ref[:, part] * inv_var
        here = iota((rows, chunk), 0) == token_ref[:, part] - start_ref[0]
        pieces = []
        for row in (inv_var, weighted):
            high = row.astype(BF16).astype(F32)
            pieces.append(jnp.where(here, high, 0.0).astype(BF16))
            pieces.append(jnp.where(here, row - high, 0.0).astype(BF16))
        channel_hot = jnp.where(iota((feat_width, chunk), 0) == channel_ref[:, part], 1.0, 0.0).astype(BF16)
        total += dot(jnp.concatenate(pieces, axis=0), channel_hot, ((1,), (1,)))
    out_ref[0] = total[:rows] + total[rows : 2 * rows]
    out_ref[1] = total[2 * rows : 3 * rows] + total[3 * rows :]


def sample_grid(start, obs_token, obs_channel, obs_value, obs_var, rows, feat_width):
    count = obs_token.shape[0]
    return pl.pallas_call(
        sample_grid_kernel,
        out_shape=jax.ShapeDtypeStruct((2, rows, feat_width), F32),
        in_specs=[smem_spec()] + [vmem_spec()] * 4,
        out_specs=vmem_spec(),
        compiler_params=pltpu.CompilerParams(vmem_limit_bytes=VMEM_LIMIT),
        cost_estimate=pl.CostEstimate(flops=8 * rows * count * feat_width, bytes_accessed=16 * count, transcendentals=0),
        name="sample_grid",
    )(start, *(v.reshape(1, count) for v in (obs_token, obs_channel, obs_value, obs_var)))


def head_lanes(feat_width, heads):
    lane_head = iota((feat_width, LANES), 0) // (feat_width // heads)
    return (lane_head == iota((feat_width, LANES), 1)).astype(F32).astype(BF16)


def largest_norms(values, heads):
    squares = dot((values * values).astype(BF16), head_lanes(values.shape[1], heads))
    return jnp.max(squares, axis=0, keepdims=True)


def is_safe(query_norms, key_norms):
    return jnp.max(query_norms * key_norms) * 1.05 <= SAFE_SCORE * SAFE_SCORE


def query_scale(head_size):
    return math.log2(math.e) / math.sqrt(head_size)


def band_bias(window, lower, upper, reach):
    apart = jnp.abs(iota((Q_ROWS, upper - lower), 1) + (lower - reach) - iota((Q_ROWS, upper - lower), 0))
    return jnp.where(apart <= window, 0.0, -1e30)


def group_lanes(group):
    return slice(group * LANES, (group + 1) * LANES)


def stacked_heads(queries, head_size):
    lane_head = iota((1, LANES), 1) // head_size
    masks = [(lane_head == head).astype(F32).astype(BF16) for head in range(LANES // head_size)]
    return jnp.concatenate([queries * mask for mask in masks], axis=0)


def put_values(buf, lower, values):
    for group in range(values.shape[1] // LANES):
        lanes = slice(2 * group * LANES, (2 * group + 1) * LANES)
        buf[lower : lower + values.shape[0], lanes] = values[:, group_lanes(group)]


def weighted_sums(weights, values, head_size):
    mixed_all = dot(weights, values)
    heads = LANES // head_size
    count = mixed_all.shape[0] // heads
    lane_head = iota((1, LANES), 1) // head_size
    mixed, totals = mixed_all[:count, :LANES], mixed_all[:count, LANES:]
    for head in range(1, heads):
        part = mixed_all[head * count : (head + 1) * count]
        mixed = jnp.where(lane_head == head, part[:, :LANES], mixed)
        totals = jnp.where(lane_head == head, part[:, LANES:], totals)
    return mixed, totals


def padded_lanes(values, before, after):
    pieces = [jnp.zeros((values.shape[0], before), BF16)] if before else []
    pieces.append(values.astype(BF16))
    if after:
        pieces.append(jnp.zeros((values.shape[0], after), BF16))
    return jnp.concatenate(pieces, axis=1) if len(pieces) > 1 else pieces[0]


def unit_weights(scores, spans, bias_of):
    width = scores.shape[1]
    count = len(spans) * Q_ROWS
    weights = []
    for head in range(scores.shape[0] // count):
        for block, (lower, upper) in enumerate(spans):
            top = head * count + block * Q_ROWS
            expo = jnp.exp2(scores[top : top + Q_ROWS, lower:upper] + bias_of(head, block))
            weights.append(padded_lanes(expo, lower, width - upper))
    return jnp.concatenate(weights, axis=0)


def inner_kernel(
    window_ref,
    own_ref,
    gain_ref,
    w_query_ref,
    w_key_ref,
    w_value_ref,
    query_ref,
    norm_ref,
    mixed_ref,
    total_ref,
    key_buf,
    value_buf,
    bias_buf,
):
    rows, feat_width = own_ref.shape[1:]
    heads = window_ref.shape[0]
    head_size = feat_width // heads
    group_heads = LANES // head_size
    key_count = bias_buf.shape[2]
    reach = (key_count - Q_ROWS) // 2
    reach_blocks = reach // Q_ROWS
    blocks = rows // Q_ROWS

    @pl.when(pl.program_id(0) == 0)
    def _():
        for head in range(heads):
            bias_buf[head] = band_bias(window_ref[head], 0, key_count, reach)
        value_buf[...] = jnp.ones(value_buf.shape, BF16)

    normed = rms_scaled(own_ref[0].astype(F32), gain_ref[...]).astype(BF16)
    query_rows = dot(normed, w_query_ref[...]) * query_scale(head_size)
    key_rows = dot(normed, w_key_ref[...])
    query_ref[0] = query_rows.astype(BF16)
    key_buf[...] = key_rows.T.astype(BF16)
    put_values(value_buf, 0, dot(normed, w_value_ref[...]).astype(BF16))
    query_norms, key_norms = largest_norms(query_rows, heads), largest_norms(key_rows, heads)
    blank = jnp.zeros((norm_ref.shape[1] - 2, LANES), F32)
    norm_ref[0] = jnp.concatenate([query_norms, key_norms, blank], axis=0)

    @pl.when(is_safe(query_norms, key_norms))
    def _():
        units = [(first, group) for first in range(0, blocks, 2) for group in range(heads // group_heads)]

        def scores_of(first, group):
            queries = query_ref[0, first * Q_ROWS : (first + 2) * Q_ROWS, group_lanes(group)]
            return dot(stacked_heads(queries, head_size), key_buf[group_lanes(group), :])

        scores = scores_of(*units[0])
        for at, (first, group) in enumerate(units):
            following = scores_of(*units[at + 1]) if at + 1 < len(units) else None
            ranges = [(max(0, b - reach_blocks), min(blocks, b + reach_blocks + 1)) for b in (first, first + 1)]
            spans = [(lower * Q_ROWS, upper * Q_ROWS) for lower, upper in ranges]

            def bias_of(head, block):
                shift = (reach_blocks - first - block) * Q_ROWS
                lower, upper = spans[block]
                return bias_buf[group * group_heads + head, :, lower + shift : upper + shift]

            values = value_buf[:, 2 * group * LANES : 2 * (group + 1) * LANES]
            mixed, totals = weighted_sums(unit_weights(scores, spans, bias_of), values, head_size)
            here = slice(first * Q_ROWS, (first + 2) * Q_ROWS)
            mixed_ref[0, here, group_lanes(group)] = mixed
            total_ref[0, here, group_lanes(group)] = totals
            scores = following


def inner(head_window, own, gain, w_query, w_key, w_value, reach):
    members, rows, feat_width = own.shape
    heads = head_window.shape[0]
    key_count = Q_ROWS + 2 * reach
    shapes = [(own.shape, BF16), ((members, 8, LANES), F32), (own.shape, F32), (own.shape, F32)]

    def spec(shape):
        return pl.BlockSpec((1, *shape[1:]), lambda m: (m, 0, 0))

    return pl.pallas_call(
        inner_kernel,
        grid=(members,),
        out_shape=[jax.ShapeDtypeStruct(*v) for v in shapes],
        in_specs=[smem_spec(), spec(own.shape)] + [vmem_spec()] * 4,
        out_specs=[spec(shape) for shape, _ in shapes],
        scratch_shapes=[
            pltpu.VMEM((feat_width, rows), BF16),
            pltpu.VMEM((rows, 2 * feat_width), BF16),
            pltpu.VMEM((heads, Q_ROWS, key_count), F32),
        ],
        compiler_params=pltpu.CompilerParams(vmem_limit_bytes=VMEM_LIMIT),
        cost_estimate=pl.CostEstimate(
            flops=own.size * (6 * feat_width + 16 * rows), bytes_accessed=14 * own.size, transcendentals=0
        ),
        name="inner",
    )(head_window, own, gain, w_query, w_key, w_value)


def forward_kernel(
    place_ref,
    window_ref,
    state_ref,
    query_ref,
    norm_ref,
    inner_mixed_ref,
    inner_total_ref,
    left_ref,
    right_ref,
    attn_gain_ref,
    ffn_gain_ref,
    w_key_ref,
    w_value_ref,
    w_out_ref,
    w_gate_ref,
    w_up_ref,
    down_weight_ref,
    *refs,
):
    out_refs, (halo_key_buf, halo_value_buf, bias_buf, mixed_buf, key_buf, value_buf, forecast_buf) = (
        refs[:-7],
        refs[-7:],
    )
    rows, feat_width = state_ref.shape[1:]
    reach = left_ref.shape[1]
    heads = window_ref.shape[0]
    head_size = feat_width // heads
    group_heads = LANES // head_size
    groups = heads // group_heads
    blocks = rows // Q_ROWS
    key_count = Q_ROWS + 2 * reach
    count = 2 * Q_ROWS

    @pl.when(pl.program_id(0) == 0)
    def _():
        first_valid = place_ref[0] - reach >= 0
        last_valid = place_ref[0] + rows + reach <= place_ref[1]
        for head in range(heads):
            left_bias = band_bias(window_ref[head], 0, reach, reach)
            right_bias = band_bias(window_ref[head], key_count - reach, key_count, reach)
            bias_buf[0, head] = jnp.where(first_valid, left_bias, -1e30)
            bias_buf[1, head] = jnp.where(last_valid, right_bias, -1e30)
        halo_value_buf[...] = jnp.ones(halo_value_buf.shape, BF16)

    def keys_of(normed):
        return dot(normed, w_key_ref[...])

    def values_of(normed):
        return dot(normed, w_value_ref[...]).astype(BF16)

    key_norms = norm_ref[0, 1:2, :]
    for side, ref in enumerate((left_ref, right_ref)):
        normed = rms_scaled(ref[0].astype(F32), attn_gain_ref[...]).astype(BF16)
        keys = keys_of(normed)
        key_norms = jnp.maximum(key_norms, largest_norms(keys, heads))
        halo_key_buf[side] = keys.T.astype(BF16)
        put_values(halo_value_buf.at[side], 0, values_of(normed))
    safe = is_safe(norm_ref[0, 0:1, :], key_norms)

    @pl.when(safe)
    def _():
        units = [(side, group) for side in range(2) for group in range(groups)]

        def scores_of(side, group):
            start = side * (rows - count)
            queries = query_ref[0, start : start + count, group_lanes(group)]
            return dot(stacked_heads(queries, head_size), halo_key_buf[side, group_lanes(group), :])

        scores = scores_of(*units[0])
        for at, (side, group) in enumerate(units):
            following = scores_of(*units[at + 1]) if at + 1 < len(units) else None
            spans = [(0, reach), (Q_ROWS, reach)] if side == 0 else [(0, reach - Q_ROWS), (0, reach)]

            def bias_of(head, block):
                lower, upper = spans[block]
                shift = -block * Q_ROWS if side == 0 else (1 - block) * Q_ROWS
                return bias_buf[side, group * group_heads + head, :, lower + shift : upper + shift]

            values = halo_value_buf[side, :, 2 * group * LANES : 2 * (group + 1) * LANES]
            mixed, totals = weighted_sums(unit_weights(scores, spans, bias_of), values, head_size)
            here = slice(side * (rows - count), side * (rows - count) + count)
            mixed = mixed + inner_mixed_ref[0, here, group_lanes(group)]
            totals = totals + inner_total_ref[0, here, group_lanes(group)]
            mixed_buf[here, group_lanes(group)] = (mixed / totals).astype(BF16)
            scores = following

    @pl.when(jnp.logical_not(safe))
    def _():
        normed = rms_scaled(state_ref[0].astype(F32), attn_gain_ref[...]).astype(BF16)
        key_buf[:, :reach] = halo_key_buf[0]
        key_buf[:, reach : reach + rows] = keys_of(normed).T.astype(BF16)
        key_buf[:, reach + rows :] = halo_key_buf[1]
        value_buf[...] = jnp.ones(value_buf.shape, BF16)
        put_values(value_buf, reach, values_of(normed))
        value_buf[:reach] = halo_value_buf[0]
        value_buf[reach + rows :] = halo_value_buf[1]
        for block in range(blocks):
            start = block * Q_ROWS
            k_pos = place_ref[0] - reach + start + iota((Q_ROWS, key_count), 1)
            inside = (k_pos >= 0) & (k_pos < place_ref[1])
            for group in range(groups):
                queries = query_ref[0, start : start + Q_ROWS, group_lanes(group)]
                keys = key_buf[group_lanes(group), start : start + key_count]
                scores = dot(stacked_heads(queries, head_size), keys)
                weights = []
                for head in range(group_heads):
                    bias = band_bias(window_ref[group * group_heads + head], 0, key_count, reach)
                    score_matrix = scores[head * Q_ROWS : (head + 1) * Q_ROWS] + jnp.where(inside, bias, -1e30)
                    row_top = jnp.max(score_matrix, axis=-1, keepdims=True)
                    weights.append(jnp.exp2(score_matrix - row_top).astype(BF16))
                values = value_buf[start : start + key_count, 2 * group * LANES : 2 * (group + 1) * LANES]
                mixed, totals = weighted_sums(jnp.concatenate(weights, axis=0), values, head_size)
                mixed_buf[start : start + Q_ROWS, group_lanes(group)] = (mixed / totals).astype(BF16)

    after = (state_ref[0].astype(F32) + dot(mixed_buf[...], w_out_ref[...])).astype(BF16)
    normed_mid = rms_scaled(after.astype(F32), ffn_gain_ref[...]).astype(BF16)
    forecast = after.astype(F32)
    for lower in range(0, w_gate_ref.shape[1], HIDDEN_CHUNK):
        part = slice(lower, lower + HIDDEN_CHUNK)
        gate = 0.5 * dot(normed_mid, w_gate_ref[:, part])
        hidden = (gate * (1.0 + jnp.tanh(gate)) * dot(normed_mid, w_up_ref[:, part])).astype(BF16)
        forecast += dot(hidden, down_weight_ref[part, :])
    forecast_buf[...] = forecast.astype(BF16)
    share_rows = out_refs[0].shape[1]
    for part, out_ref in enumerate(out_refs):
        lower = pl.multiple_of((place_ref[2] ^ part) * share_rows, share_rows)
        out_ref[0] = forecast_buf[pl.ds(lower, share_rows), :]


def forward(place, head_window, own, inner_parts, left, right, gains, weights, shares):
    members, row_count, feat_width = own.shape
    reach = left.shape[1]
    heads = head_window.shape[0]
    hidden_width = weights[3].shape[1]
    macs = members * row_count * feat_width * (3 * feat_width + 3 * hidden_width + 4 * reach)

    def spec(array):
        return pl.BlockSpec((1, *array.shape[1:]), lambda m: (m, 0, 0))

    return pl.pallas_call(
        forward_kernel,
        grid=(members,),
        out_shape=[jax.ShapeDtypeStruct((members, row_count // shares, feat_width), BF16)] * shares,
        in_specs=[smem_spec()] * 2
        + [spec(v) for v in (own, *inner_parts, left, right)]
        + [vmem_spec()] * (len(gains) + len(weights)),
        out_specs=[pl.BlockSpec((1, row_count // shares, feat_width), lambda m: (m, 0, 0))] * shares,
        scratch_shapes=[
            pltpu.VMEM((2, feat_width, reach), BF16),
            pltpu.VMEM((2, reach, 2 * feat_width), BF16),
            pltpu.VMEM((2, heads, Q_ROWS, reach), F32),
            pltpu.VMEM((row_count, feat_width), BF16),
            pltpu.VMEM((feat_width, row_count + 2 * reach), BF16),
            pltpu.VMEM((row_count + 2 * reach, 2 * feat_width), BF16),
            pltpu.VMEM((row_count, feat_width), BF16),
        ],
        compiler_params=pltpu.CompilerParams(vmem_limit_bytes=VMEM_LIMIT),
        cost_estimate=pl.CostEstimate(flops=2 * macs, bytes_accessed=10 * own.size, transcendentals=0),
        name="forward",
    )(place, head_window, own, *inner_parts, left, right, *gains, *weights)


def global_member(held, index, own_members):
    return ((held // own_members) ^ index) * own_members + held % own_members


def gram_kernel(index_ref, *refs):
    share_refs, grid_ref, out_ref = refs[:-2], refs[-2], refs[-1]
    own_members, rows, feat_width = share_refs[0].shape
    members = own_members * len(share_refs)
    index = index_ref[0]
    stack = members * GROUP
    total = jnp.zeros((stack, stack), F32)
    proj = jnp.zeros((members, GROUP, feat_width), F32)
    for lower in range(0, rows, GROUP):
        part = slice(lower, lower + GROUP)
        fields = jnp.concatenate([ref[:, part, :] for ref in share_refs], axis=0).astype(F32)
        mean = jnp.sum(fields, axis=0) * (1.0 / members)
        spread = fields - mean[None]
        weight = grid_ref[0, part, :]
        proj += spread * (grid_ref[1, part, :] - weight * mean)[None]
        high, low = halves(spread.reshape(stack, feat_width))
        w_high, w_low = halves((spread * weight[None]).reshape(stack, feat_width))
        last = ((1,), (1,))
        total += dot(w_high, high, last) + dot(w_high, low, last) + dot(w_low, high, last)
    same = iota((stack, stack), 0) % GROUP == iota((stack, stack), 1) % GROUP
    by_row = jnp.sum(jnp.where(same, total, 0.0).reshape(members, GROUP, stack), axis=1)
    column = global_member(iota((stack, LANES), 0) // GROUP, index, own_members)
    folded = (column == iota((stack, LANES), 1) % members).astype(F32)
    held = global_member(iota((members, members), 1), index, own_members)
    in_order = (held == iota((members, members), 0)).astype(F32)
    tiled = exact_dot(in_order, exact_dot(by_row, folded))
    per_row = LANES // members
    keep = iota((members, LANES), 0) % per_row == iota((members, LANES), 1) // members
    packed = jnp.sum(jnp.where(keep, tiled, 0.0).reshape(members // per_row, per_row, LANES), axis=1)
    proj_col = jnp.sum(jnp.sum(proj, axis=1), axis=1, keepdims=True)
    at_lane = global_member(iota((members, LANES), 0), index, own_members) == iota((members, LANES), 1)
    proj_row = jnp.sum(jnp.where(at_lane, proj_col, 0.0), axis=0, keepdims=True)
    filled = members // per_row + 1
    blank = jnp.zeros((out_ref.shape[0] - filled, LANES), F32)
    out_ref[...] = jnp.concatenate([packed, proj_row, blank], axis=0)


def gram_partial(index, shares, grid):
    members = shares[0].shape[0] * len(shares)
    filled = members * members // LANES + 1
    return pl.pallas_call(
        gram_kernel,
        out_shape=jax.ShapeDtypeStruct((-(-filled // 8) * 8, LANES), F32),
        in_specs=[smem_spec()] + [vmem_spec()] * (len(shares) + 1),
        out_specs=vmem_spec(),
        compiler_params=pltpu.CompilerParams(vmem_limit_bytes=VMEM_LIMIT),
        cost_estimate=pl.CostEstimate(
            flops=3 * GROUP * members * members * grid.size, bytes_accessed=members * grid.size, transcendentals=0
        ),
        name="gram",
    )(index, *shares, grid)


def ensemble_transform(gram, proj):
    members = gram.shape[0]
    row, column = iota((members, members), 0), iota((members, members), 1)
    identity = (row == column).astype(F32)
    system = gram + (members - 1.0) * identity
    left, right = system, proj
    for pivot in range(members):
        is_pivot = iota((members, 1), 0) == pivot
        scale = 1.0 / left[pivot : pivot + 1, pivot : pivot + 1]
        pivot_row = left[pivot : pivot + 1, :] * scale
        pivot_right = right[pivot : pivot + 1, :] * scale
        factor = left[:, pivot : pivot + 1]
        left = jnp.where(is_pivot, pivot_row, left - factor * pivot_row)
        right = jnp.where(is_pivot, pivot_right, right - factor * pivot_right)
    mean_weights = right
    mean_level = jnp.sum(jnp.sum(system * identity, axis=1, keepdims=True), axis=0, keepdims=True) / members
    lifted = system + (mean_level - (members - 1.0)) * (1.0 / members)
    frobenius = jnp.sqrt(jnp.sum(jnp.sum(lifted * lifted, axis=1, keepdims=True), axis=0, keepdims=True))
    root_iter = lifted / frobenius
    inv_iter = identity
    for sweep in range(NS_STEPS):
        product = root_iter if sweep == 0 else exact_dot(inv_iter, root_iter)
        correction = 1.5 * identity - 0.5 * product
        inv_iter = correction if sweep == 0 else exact_dot(correction, inv_iter)
        if sweep < NS_STEPS - 1:
            root_iter = exact_dot(root_iter, correction)
    inv_root = inv_iter / jnp.sqrt(frobenius) + (1.0 / math.sqrt(members - 1.0) - 1.0 / jnp.sqrt(mean_level)) * (
        1.0 / members
    )
    moved = mean_weights + math.sqrt(members - 1.0) * inv_root
    return 1.0 / members + moved - jnp.sum(moved, axis=0, keepdims=True) * (1.0 / members)


def combine_kernel(index_ref, partial_ref, *refs):
    share_refs, out_refs = refs[: len(refs) // 2], refs[len(refs) // 2 :]
    own_members, rows, feat_width = share_refs[0].shape
    members = own_members * len(share_refs)
    stack = members * GROUP
    per_row = LANES // members
    sums = jnp.sum(partial_ref[...], axis=0)
    spread_rows = jnp.concatenate(
        [jnp.broadcast_to(sums[r : r + 1], (per_row, LANES)) for r in range(members // per_row)], axis=0
    )
    keep = iota((members, LANES), 0) % per_row == iota((members, LANES), 1) // members
    folded = (iota((LANES, members), 0) % members == iota((LANES, members), 1)).astype(F32)
    gram = exact_dot(jnp.where(keep, spread_rows, 0.0), folded)
    proj_row = jnp.broadcast_to(sums[members // per_row : members // per_row + 1], (members, LANES))
    on_diagonal = iota((members, LANES), 0) == iota((members, LANES), 1)
    proj = jnp.sum(jnp.where(on_diagonal, proj_row, 0.0), axis=1, keepdims=True)
    transform = ensemble_transform(gram, proj)
    held = global_member(iota((stack, members), 0) // GROUP, index_ref[0], own_members)
    pick = (held == iota((stack, members), 1)).astype(F32).astype(BF16)
    same = iota((stack, stack), 0) % GROUP == iota((stack, stack), 1) % GROUP
    mixers = []
    for piece in halves(transform):
        rows_of = dot(pick, piece, ((1,), (1,))).astype(BF16)
        mixers.append(jnp.where(same, dot(rows_of, pick, ((1,), (1,))), 0.0).astype(BF16))
    for lower in range(0, rows, GROUP):
        part = slice(lower, lower + GROUP)
        fields = jnp.concatenate([ref[:, part, :].reshape(-1, feat_width) for ref in share_refs], axis=0)
        mixed = (dot(mixers[0], fields) + dot(mixers[1], fields)).astype(BF16)
        own_stack = own_members * GROUP
        for at, out_ref in enumerate(out_refs):
            piece = mixed[at * own_stack : (at + 1) * own_stack]
            out_ref[:, part, :] = piece.reshape(own_members, GROUP, feat_width)


def combine(index, partials, shares):
    size = shares[0].size * len(shares)
    members = shares[0].shape[0] * len(shares)
    return pl.pallas_call(
        combine_kernel,
        out_shape=[jax.ShapeDtypeStruct(v.shape, BF16) for v in shares],
        in_specs=[smem_spec()] + [vmem_spec()] * (1 + len(shares)),
        out_specs=[vmem_spec()] * len(shares),
        compiler_params=pltpu.CompilerParams(vmem_limit_bytes=VMEM_LIMIT),
        cost_estimate=pl.CostEstimate(flops=4 * GROUP * members * size, bytes_accessed=4 * size, transcendentals=0),
        name="combine",
    )(index, partials, *shares)


def assemble_kernel(index_ref, *refs):
    part_refs, out_ref = refs[:-1], refs[-1]
    rows = part_refs[0].shape[1]
    for part, ref in enumerate(part_refs):
        lower = pl.multiple_of((index_ref[0] ^ part) * rows, rows)
        out_ref[0, pl.ds(lower, rows), :] = ref[0]


def assemble(index, parts):
    members, rows, feat_width = parts[0].shape
    return pl.pallas_call(
        assemble_kernel,
        grid=(members,),
        out_shape=jax.ShapeDtypeStruct((members, len(parts) * rows, feat_width), BF16),
        in_specs=[smem_spec()] + [pl.BlockSpec((1, rows, feat_width), lambda m: (m, 0, 0))] * len(parts),
        out_specs=pl.BlockSpec((1, len(parts) * rows, feat_width), lambda m: (m, 0, 0)),
        compiler_params=pltpu.CompilerParams(vmem_limit_bytes=VMEM_LIMIT),
        cost_estimate=pl.CostEstimate(flops=0, bytes_accessed=4 * len(parts) * parts[0].size, transcendentals=0),
        name="assemble",
    )(index, *parts)


def exchanged(parts):
    count = lax.axis_size("mem")
    return [
        lax.ppermute(v, "mem", [(i, i ^ part) for i in range(count)]) if part else v for part, v in enumerate(parts)
    ]


def local(
    ens_state,
    attn_gain,
    ffn_gain,
    w_query,
    w_key,
    w_value,
    w_out,
    w_gate,
    w_up,
    down_weight,
    head_window,
    obs_token,
    obs_channel,
    obs_value,
    obs_var,
):
    own_members, row_count, feat_width = ens_state.shape
    mem_count = lax.axis_size("mem")
    tok_count = lax.axis_size("tok")
    device_count = mem_count * tok_count
    share_rows = row_count // mem_count
    first_pos = lax.axis_index("tok") * row_count
    up = [(i, i + 1) for i in range(tok_count - 1)]
    down = [(i + 1, i) for i in range(tok_count - 1)]
    left = lax.ppermute(ens_state[:, row_count - WIN :], "tok", up)
    right = lax.ppermute(ens_state[:, :WIN], "tok", down)
    share_start = first_pos + lax.axis_index("mem") * share_rows
    grid = sample_grid(
        share_start.astype(jnp.int32).reshape(1), obs_token, obs_channel, obs_value, obs_var, share_rows, feat_width
    )
    index = lax.axis_index("mem")
    place = jnp.stack([first_pos, row_count * tok_count, index]).astype(jnp.int32)
    index = index.astype(jnp.int32).reshape(1)
    gains = [attn_gain.reshape(1, -1), ffn_gain.reshape(1, -1)]
    inner_parts = inner(head_window, ens_state, gains[0], w_query, w_key, w_value, WIN)
    weights = [w_key, w_value, w_out, w_gate, w_up, down_weight]
    forecast = forward(place, head_window, ens_state, inner_parts, left, right, gains, weights, mem_count)
    shares = exchanged(forecast)
    partial = gram_partial(index, shares, grid)
    partials = lax.all_to_all(
        jnp.broadcast_to(partial[None], (device_count, *partial.shape)),
        ("mem", "tok"),
        split_axis=0,
        concat_axis=0,
        tiled=True,
    )
    return assemble(index, exchanged(combine(index, partials, shares)))


def solution(mesh):
    in_specs = (P("mem", "tok", None), *[P()] * 10, *[P("tok")] * 4)
    return jax.shard_map(local, mesh=mesh, in_specs=in_specs, out_specs=P("mem", "tok", None), check_vma=False)
```

```python
import functools
import math

import jax
import jax.numpy as jnp
from jax import lax
from jax.experimental import pallas as pl
from jax.experimental.pallas import tpu as pltpu
from jax.sharding import PartitionSpec as P

WIN = 256
NS_STEPS = 8
EPS = 1e-05
Q_ROWS = 128
GROUP = 16
LANES = 128
VMEM_LIMIT = 32 * 1024 * 1024
SAFE_SCORE = 56.0
HIDDEN_CHUNK = 256

F32 = jnp.float32
BF16 = jnp.bfloat16


def dot(a, b, contract=((1,), (0,)), precision=None):
    return lax.dot_general(a, b, (contract, ((), ())), precision=precision, preferred_element_type=F32)


def exact_dot(a, b, contract=((1,), (0,))):
    return dot(a, b, contract, lax.Precision.HIGHEST)


def iota(shape, axis):
    return lax.broadcasted_iota(jnp.int32, shape, axis)


def halves(values):
    high = values.astype(BF16)
    return high, (values - high.astype(F32)).astype(BF16)


def rms_scaled(values, gain):
    rows, width = values.shape
    ones = jnp.ones((width, LANES), BF16)
    means = dot((values * values).astype(BF16), ones) * (1.0 / width)
    scale = lax.rsqrt(means + EPS)
    return values * jnp.concatenate([scale] * (width // LANES), axis=1) * gain


def vmem_spec():
    return pl.BlockSpec(memory_space=pltpu.VMEM)


def smem_spec():
    return pl.BlockSpec(memory_space=pltpu.SMEM)


def sample_grid_kernel(start_ref, token_ref, channel_ref, value_ref, var_ref, out_ref):
    rows, feat_width = out_ref.shape[1:]
    count = token_ref.shape[1]
    chunk = min(1024, count)
    total = jnp.zeros((4 * rows, feat_width), F32)
    for lower in range(0, count, chunk):
        part = slice(lower, lower + chunk)
        inv_var = 1.0 / var_ref[:, part]
        weighted = value_ref[:, part] * inv_var
        here = iota((rows, chunk), 0) == token_ref[:, part] - start_ref[0]
        pieces = []
        for row in (inv_var, weighted):
            high = row.astype(BF16).astype(F32)
            pieces.append(jnp.where(here, high, 0.0).astype(BF16))
            pieces.append(jnp.where(here, row - high, 0.0).astype(BF16))
        channel_hot = jnp.where(iota((feat_width, chunk), 0) == channel_ref[:, part], 1.0, 0.0).astype(BF16)
        total += dot(jnp.concatenate(pieces, axis=0), channel_hot, ((1,), (1,)))
    out_ref[0] = total[:rows] + total[rows : 2 * rows]
    out_ref[1] = total[2 * rows : 3 * rows] + total[3 * rows :]


def sample_grid(start, obs_token, obs_channel, obs_value, obs_var, rows, feat_width):
    count = obs_token.shape[0]
    return pl.pallas_call(
        sample_grid_kernel,
        out_shape=jax.ShapeDtypeStruct((2, rows, feat_width), F32),
        in_specs=[smem_spec()] + [vmem_spec()] * 4,
        out_specs=vmem_spec(),
        compiler_params=pltpu.CompilerParams(vmem_limit_bytes=VMEM_LIMIT),
        cost_estimate=pl.CostEstimate(flops=8 * rows * count * feat_width, bytes_accessed=16 * count, transcendentals=0),
        name="sample_grid",
    )(start, *(v.reshape(1, count) for v in (obs_token, obs_channel, obs_value, obs_var)))


def head_lanes(feat_width, heads):
    lane_head = iota((feat_width, LANES), 0) // (feat_width // heads)
    return (lane_head == iota((feat_width, LANES), 1)).astype(F32).astype(BF16)


def largest_norms(values, heads):
    squares = dot((values * values).astype(BF16), head_lanes(values.shape[1], heads))
    return jnp.max(squares, axis=0, keepdims=True)


def is_safe(query_norms, key_norms):
    return jnp.max(query_norms * key_norms) * 1.05 <= SAFE_SCORE * SAFE_SCORE


def query_scale(head_size):
    return math.log2(math.e) / math.sqrt(head_size)


def band_bias(window, lower, upper, reach):
    apart = jnp.abs(iota((Q_ROWS, upper - lower), 1) + (lower - reach) - iota((Q_ROWS, upper - lower), 0))
    return jnp.where(apart <= window, 0.0, -1e30)


def group_lanes(group):
    return slice(group * LANES, (group + 1) * LANES)


def stacked_heads(queries, head_size):
    lane_head = iota((1, LANES), 1) // head_size
    masks = [(lane_head == head).astype(F32).astype(BF16) for head in range(LANES // head_size)]
    return jnp.concatenate([queries * mask for mask in masks], axis=0)


def put_values(buf, lower, values):
    for group in range(values.shape[1] // LANES):
        lanes = slice(2 * group * LANES, (2 * group + 1) * LANES)
        buf[lower : lower + values.shape[0], lanes] = values[:, group_lanes(group)]


def weighted_sums(weights, values, head_size):
    mixed_all = dot(weights, values)
    heads = LANES // head_size
    count = mixed_all.shape[0] // heads
    lane_head = iota((1, LANES), 1) // head_size
    mixed, totals = mixed_all[:count, :LANES], mixed_all[:count, LANES:]
    for head in range(1, heads):
        part = mixed_all[head * count : (head + 1) * count]
        mixed = jnp.where(lane_head == head, part[:, :LANES], mixed)
        totals = jnp.where(lane_head == head, part[:, LANES:], totals)
    return mixed, totals


def padded_lanes(values, before, after):
    pieces = [jnp.zeros((values.shape[0], before), BF16)] if before else []
    pieces.append(values.astype(BF16))
    if after:
        pieces.append(jnp.zeros((values.shape[0], after), BF16))
    return jnp.concatenate(pieces, axis=1) if len(pieces) > 1 else pieces[0]


def unit_weights(scores, spans, bias_of):
    width = scores.shape[1]
    count = len(spans) * Q_ROWS
    weights = []
    for head in range(scores.shape[0] // count):
        for block, (lower, upper) in enumerate(spans):
            top = head * count + block * Q_ROWS
            expo = jnp.exp2(scores[top : top + Q_ROWS, lower:upper] + bias_of(head, block))
            weights.append(padded_lanes(expo, lower, width - upper))
    return jnp.concatenate(weights, axis=0)


def inner_kernel(
    window_ref,
    own_ref,
    gain_ref,
    w_query_ref,
    w_key_ref,
    w_value_ref,
    query_ref,
    norm_ref,
    mixed_ref,
    total_ref,
    key_buf,
    value_buf,
    bias_buf,
):
    rows, feat_width = own_ref.shape[1:]
    heads = window_ref.shape[0]
    head_size = feat_width // heads
    group_heads = LANES // head_size
    key_count = bias_buf.shape[2]
    reach = (key_count - Q_ROWS) // 2
    reach_blocks = reach // Q_ROWS
    blocks = rows // Q_ROWS

    @pl.when(pl.program_id(0) == 0)
    def _():
        for head in range(heads):
            bias_buf[head] = band_bias(window_ref[head], 0, key_count, reach)
        value_buf[...] = jnp.ones(value_buf.shape, BF16)

    normed = rms_scaled(own_ref[0].astype(F32), gain_ref[...]).astype(BF16)
    query_rows = dot(normed, w_query_ref[...]) * query_scale(head_size)
    key_rows = dot(normed, w_key_ref[...])
    query_ref[0] = query_rows.astype(BF16)
    key_buf[...] = key_rows.T.astype(BF16)
    put_values(value_buf, 0, dot(normed, w_value_ref[...]).astype(BF16))
    query_norms, key_norms = largest_norms(query_rows, heads), largest_norms(key_rows, heads)
    blank = jnp.zeros((norm_ref.shape[1] - 2, LANES), F32)
    norm_ref[0] = jnp.concatenate([query_norms, key_norms, blank], axis=0)

    @pl.when(is_safe(query_norms, key_norms))
    def _():
        units = [(first, group) for first in range(0, blocks, 2) for group in range(heads // group_heads)]

        def scores_of(first, group):
            queries = query_ref[0, first * Q_ROWS : (first + 2) * Q_ROWS, group_lanes(group)]
            return dot(stacked_heads(queries, head_size), key_buf[group_lanes(group), :])

        scores = scores_of(*units[0])
        for at, (first, group) in enumerate(units):
            following = scores_of(*units[at + 1]) if at + 1 < len(units) else None
            ranges = [(max(0, b - reach_blocks), min(blocks, b + reach_blocks + 1)) for b in (first, first + 1)]
            spans = [(lower * Q_ROWS, upper * Q_ROWS) for lower, upper in ranges]

            def bias_of(head, block):
                shift = (reach_blocks - first - block) * Q_ROWS
                lower, upper = spans[block]
                return bias_buf[group * group_heads + head, :, lower + shift : upper + shift]

            values = value_buf[:, 2 * group * LANES : 2 * (group + 1) * LANES]
            mixed, totals = weighted_sums(unit_weights(scores, spans, bias_of), values, head_size)
            here = slice(first * Q_ROWS, (first + 2) * Q_ROWS)
            mixed_ref[0, here, group_lanes(group)] = mixed
            total_ref[0, here, group_lanes(group)] = totals
            scores = following


def inner(head_window, own, gain, w_query, w_key, w_value, reach):
    members, rows, feat_width = own.shape
    heads = head_window.shape[0]
    key_count = Q_ROWS + 2 * reach
    shapes = [(own.shape, BF16), ((members, 8, LANES), F32), (own.shape, F32), (own.shape, F32)]

    def spec(shape):
        return pl.BlockSpec((1, *shape[1:]), lambda m: (m, 0, 0))

    return pl.pallas_call(
        inner_kernel,
        grid=(members,),
        out_shape=[jax.ShapeDtypeStruct(*v) for v in shapes],
        in_specs=[smem_spec(), spec(own.shape)] + [vmem_spec()] * 4,
        out_specs=[spec(shape) for shape, _ in shapes],
        scratch_shapes=[
            pltpu.VMEM((feat_width, rows), BF16),
            pltpu.VMEM((rows, 2 * feat_width), BF16),
            pltpu.VMEM((heads, Q_ROWS, key_count), F32),
        ],
        compiler_params=pltpu.CompilerParams(vmem_limit_bytes=VMEM_LIMIT),
        cost_estimate=pl.CostEstimate(
            flops=own.size * (6 * feat_width + 16 * rows), bytes_accessed=14 * own.size, transcendentals=0
        ),
        name="inner",
    )(head_window, own, gain, w_query, w_key, w_value)


def forward_kernel(
    place_ref,
    window_ref,
    state_ref,
    query_ref,
    norm_ref,
    inner_mixed_ref,
    inner_total_ref,
    left_ref,
    right_ref,
    attn_gain_ref,
    ffn_gain_ref,
    w_key_ref,
    w_value_ref,
    w_out_ref,
    w_gate_ref,
    w_up_ref,
    down_weight_ref,
    *refs,
):
    out_refs, (halo_key_buf, halo_value_buf, bias_buf, mixed_buf, key_buf, value_buf, forecast_buf) = (
        refs[:-7],
        refs[-7:],
    )
    rows, feat_width = state_ref.shape[1:]
    reach = left_ref.shape[1]
    heads = window_ref.shape[0]
    head_size = feat_width // heads
    group_heads = LANES // head_size
    groups = heads // group_heads
    blocks = rows // Q_ROWS
    key_count = Q_ROWS + 2 * reach
    count = 2 * Q_ROWS

    @pl.when(pl.program_id(0) == 0)
    def _():
        first_valid = place_ref[0] - reach >= 0
        last_valid = place_ref[0] + rows + reach <= place_ref[1]
        for head in range(heads):
            left_bias = band_bias(window_ref[head], 0, reach, reach)
            right_bias = band_bias(window_ref[head], key_count - reach, key_count, reach)
            bias_buf[0, head] = jnp.where(first_valid, left_bias, -1e30)
            bias_buf[1, head] = jnp.where(last_valid, right_bias, -1e30)
        halo_value_buf[...] = jnp.ones(halo_value_buf.shape, BF16)

    def keys_of(normed):
        return dot(normed, w_key_ref[...])

    def values_of(normed):
        return dot(normed, w_value_ref[...]).astype(BF16)

    key_norms = norm_ref[0, 1:2, :]
    for side, ref in enumerate((left_ref, right_ref)):
        normed = rms_scaled(ref[0].astype(F32), attn_gain_ref[...]).astype(BF16)
        keys = keys_of(normed)
        key_norms = jnp.maximum(key_norms, largest_norms(keys, heads))
        halo_key_buf[side] = keys.T.astype(BF16)
        put_values(halo_value_buf.at[side], 0, values_of(normed))
    safe = is_safe(norm_ref[0, 0:1, :], key_norms)

    @pl.when(safe)
    def _():
        units = [(side, group) for side in range(2) for group in range(groups)]

        def scores_of(side, group):
            start = side * (rows - count)
            queries = query_ref[0, start : start + count, group_lanes(group)]
            return dot(stacked_heads(queries, head_size), halo_key_buf[side, group_lanes(group), :])

        scores = scores_of(*units[0])
        for at, (side, group) in enumerate(units):
            following = scores_of(*units[at + 1]) if at + 1 < len(units) else None
            spans = [(0, reach), (Q_ROWS, reach)] if side == 0 else [(0, reach - Q_ROWS), (0, reach)]

            def bias_of(head, block):
                lower, upper = spans[block]
                shift = -block * Q_ROWS if side == 0 else (1 - block) * Q_ROWS
                return bias_buf[side, group * group_heads + head, :, lower + shift : upper + shift]

            values = halo_value_buf[side, :, 2 * group * LANES : 2 * (group + 1) * LANES]
            mixed, totals = weighted_sums(unit_weights(scores, spans, bias_of), values, head_size)
            here = slice(side * (rows - count), side * (rows - count) + count)
            mixed = mixed + inner_mixed_ref[0, here, group_lanes(group)]
            totals = totals + inner_total_ref[0, here, group_lanes(group)]
            mixed_buf[here, group_lanes(group)] = (mixed / totals).astype(BF16)
            scores = following

    @pl.when(jnp.logical_not(safe))
    def _():
        normed = rms_scaled(state_ref[0].astype(F32), attn_gain_ref[...]).astype(BF16)
        key_buf[:, :reach] = halo_key_buf[0]
        key_buf[:, reach : reach + rows] = keys_of(normed).T.astype(BF16)
        key_buf[:, reach + rows :] = halo_key_buf[1]
        value_buf[...] = jnp.ones(value_buf.shape, BF16)
        put_values(value_buf, reach, values_of(normed))
        value_buf[:reach] = halo_value_buf[0]
        value_buf[reach + rows :] = halo_value_buf[1]
        for block in range(blocks):
            start = block * Q_ROWS
            k_pos = place_ref[0] - reach + start + iota((Q_ROWS, key_count), 1)
            inside = (k_pos >= 0) & (k_pos < place_ref[1])
            for group in range(groups):
                queries = query_ref[0, start : start + Q_ROWS, group_lanes(group)]
                keys = key_buf[group_lanes(group), start : start + key_count]
                scores = dot(stacked_heads(queries, head_size), keys)
                weights = []
                for head in range(group_heads):
                    bias = band_bias(window_ref[group * group_heads + head], 0, key_count, reach)
                    score_matrix = scores[head * Q_ROWS : (head + 1) * Q_ROWS] + jnp.where(inside, bias, -1e30)
                    row_top = jnp.max(score_matrix, axis=-1, keepdims=True)
                    weights.append(jnp.exp2(score_matrix - row_top).astype(BF16))
                values = value_buf[start : start + key_count, 2 * group * LANES : 2 * (group + 1) * LANES]
                mixed, totals = weighted_sums(jnp.concatenate(weights, axis=0), values, head_size)
                mixed_buf[start : start + Q_ROWS, group_lanes(group)] = (mixed / totals).astype(BF16)

    after = (state_ref[0].astype(F32) + dot(mixed_buf[...], w_out_ref[...])).astype(BF16)
    normed_mid = rms_scaled(after.astype(F32), ffn_gain_ref[...]).astype(BF16)
    forecast = after.astype(F32)
    for lower in range(0, w_gate_ref.shape[1], HIDDEN_CHUNK):
        part = slice(lower, lower + HIDDEN_CHUNK)
        gate = 0.5 * dot(normed_mid, w_gate_ref[:, part])
        hidden = (gate * (1.0 + jnp.tanh(gate)) * dot(normed_mid, w_up_ref[:, part])).astype(BF16)
        forecast += dot(hidden, down_weight_ref[part, :])
    forecast_buf[...] = forecast.astype(BF16)
    share_rows = out_refs[0].shape[1]
    for part, out_ref in enumerate(out_refs):
        partner = partner_bits(part, place_ref[3] == 1, len(out_refs)) ^ place_ref[2]
        lower = pl.multiple_of(partner * share_rows, share_rows)
        out_ref[0] = forecast_buf[pl.ds(lower, share_rows), :]


def forward(place, head_window, own, inner_parts, left, right, gains, weights, shares):
    members, row_count, feat_width = own.shape
    reach = left.shape[1]
    heads = head_window.shape[0]
    hidden_width = weights[3].shape[1]
    macs = members * row_count * feat_width * (3 * feat_width + 3 * hidden_width + 4 * reach)

    def spec(array):
        return pl.BlockSpec((1, *array.shape[1:]), lambda m: (m, 0, 0))

    return pl.pallas_call(
        forward_kernel,
        grid=(members,),
        out_shape=[jax.ShapeDtypeStruct((members, row_count // shares, feat_width), BF16)] * shares,
        in_specs=[smem_spec()] * 2
        + [spec(v) for v in (own, *inner_parts, left, right)]
        + [vmem_spec()] * (len(gains) + len(weights)),
        out_specs=[pl.BlockSpec((1, row_count // shares, feat_width), lambda m: (m, 0, 0))] * shares,
        scratch_shapes=[
            pltpu.VMEM((2, feat_width, reach), BF16),
            pltpu.VMEM((2, reach, 2 * feat_width), BF16),
            pltpu.VMEM((2, heads, Q_ROWS, reach), F32),
            pltpu.VMEM((row_count, feat_width), BF16),
            pltpu.VMEM((feat_width, row_count + 2 * reach), BF16),
            pltpu.VMEM((row_count + 2 * reach, 2 * feat_width), BF16),
            pltpu.VMEM((row_count, feat_width), BF16),
        ],
        compiler_params=pltpu.CompilerParams(vmem_limit_bytes=VMEM_LIMIT),
        cost_estimate=pl.CostEstimate(flops=2 * macs, bytes_accessed=10 * own.size, transcendentals=0),
        name="forward",
    )(place, head_window, own, *inner_parts, left, right, *gains, *weights)


def partner_bits(part, odd, count):
    fine = math.isqrt(count)
    if fine * fine != count:
        return part
    turned = (part % fine) * fine + part // fine
    return jnp.where(odd, turned, part) if isinstance(odd, jax.Array) else (turned if odd else part)


def global_member(held, place_ref, own_members, parts):
    bits = partner_bits(held // own_members, place_ref[1] == 1, parts)
    return (bits ^ place_ref[0]) * own_members + held % own_members


def gram_kernel(index_ref, *refs):
    share_refs, grid_ref, out_ref = refs[:-2], refs[-2], refs[-1]
    own_members, rows, feat_width = share_refs[0].shape
    members = own_members * len(share_refs)
    parts = len(share_refs)
    stack = members * GROUP
    total = jnp.zeros((stack, stack), F32)
    proj = jnp.zeros((members, GROUP, feat_width), F32)
    for lower in range(0, rows, GROUP):
        part = slice(lower, lower + GROUP)
        fields = jnp.concatenate([ref[:, part, :] for ref in share_refs], axis=0).astype(F32)
        mean = jnp.sum(fields, axis=0) * (1.0 / members)
        spread = fields - mean[None]
        weight = grid_ref[0, part, :]
        proj += spread * (grid_ref[1, part, :] - weight * mean)[None]
        high, low = halves(spread.reshape(stack, feat_width))
        w_high, w_low = halves((spread * weight[None]).reshape(stack, feat_width))
        last = ((1,), (1,))
        total += dot(w_high, high, last) + dot(w_high, low, last) + dot(w_low, high, last)
    same = iota((stack, stack), 0) % GROUP == iota((stack, stack), 1) % GROUP
    by_row = jnp.sum(jnp.where(same, total, 0.0).reshape(members, GROUP, stack), axis=1)
    column = global_member(iota((stack, LANES), 0) // GROUP, index_ref, own_members, parts)
    folded = (column == iota((stack, LANES), 1) % members).astype(F32)
    held = global_member(iota((members, members), 1), index_ref, own_members, parts)
    in_order = (held == iota((members, members), 0)).astype(F32)
    tiled = exact_dot(in_order, exact_dot(by_row, folded))
    per_row = LANES // members
    keep = iota((members, LANES), 0) % per_row == iota((members, LANES), 1) // members
    packed = jnp.sum(jnp.where(keep, tiled, 0.0).reshape(members // per_row, per_row, LANES), axis=1)
    proj_col = jnp.sum(jnp.sum(proj, axis=1), axis=1, keepdims=True)
    at_lane = global_member(iota((members, LANES), 0), index_ref, own_members, parts) == iota((members, LANES), 1)
    proj_row = jnp.sum(jnp.where(at_lane, proj_col, 0.0), axis=0, keepdims=True)
    filled = members // per_row + 1
    blank = jnp.zeros((out_ref.shape[0] - filled, LANES), F32)
    out_ref[...] = jnp.concatenate([packed, proj_row, blank], axis=0)


def gram_partial(index, shares, grid):
    members = shares[0].shape[0] * len(shares)
    filled = members * members // LANES + 1
    return pl.pallas_call(
        gram_kernel,
        out_shape=jax.ShapeDtypeStruct((-(-filled // 8) * 8, LANES), F32),
        in_specs=[smem_spec()] + [vmem_spec()] * (len(shares) + 1),
        out_specs=vmem_spec(),
        compiler_params=pltpu.CompilerParams(vmem_limit_bytes=VMEM_LIMIT),
        cost_estimate=pl.CostEstimate(
            flops=3 * GROUP * members * members * grid.size, bytes_accessed=members * grid.size, transcendentals=0
        ),
        name="gram",
    )(index, *shares, grid)


def ensemble_transform(gram, proj):
    members = gram.shape[0]
    row, column = iota((members, members), 0), iota((members, members), 1)
    identity = (row == column).astype(F32)
    system = gram + (members - 1.0) * identity
    left, right = system, proj
    for pivot in range(members):
        is_pivot = iota((members, 1), 0) == pivot
        scale = 1.0 / left[pivot : pivot + 1, pivot : pivot + 1]
        pivot_row = left[pivot : pivot + 1, :] * scale
        pivot_right = right[pivot : pivot + 1, :] * scale
        factor = left[:, pivot : pivot + 1]
        left = jnp.where(is_pivot, pivot_row, left - factor * pivot_row)
        right = jnp.where(is_pivot, pivot_right, right - factor * pivot_right)
    mean_weights = right
    mean_level = jnp.sum(jnp.sum(system * identity, axis=1, keepdims=True), axis=0, keepdims=True) / members
    lifted = system + (mean_level - (members - 1.0)) * (1.0 / members)
    frobenius = jnp.sqrt(jnp.sum(jnp.sum(lifted * lifted, axis=1, keepdims=True), axis=0, keepdims=True))
    root_iter = lifted / frobenius
    inv_iter = identity
    for sweep in range(NS_STEPS):
        product = root_iter if sweep == 0 else exact_dot(inv_iter, root_iter)
        correction = 1.5 * identity - 0.5 * product
        inv_iter = correction if sweep == 0 else exact_dot(correction, inv_iter)
        if sweep < NS_STEPS - 1:
            root_iter = exact_dot(root_iter, correction)
    inv_root = inv_iter / jnp.sqrt(frobenius) + (1.0 / math.sqrt(members - 1.0) - 1.0 / jnp.sqrt(mean_level)) * (
        1.0 / members
    )
    moved = mean_weights + math.sqrt(members - 1.0) * inv_root
    return 1.0 / members + moved - jnp.sum(moved, axis=0, keepdims=True) * (1.0 / members)


def combine_kernel(index_ref, partial_ref, *refs):
    share_refs, out_refs = refs[: len(refs) // 2], refs[len(refs) // 2 :]
    own_members, rows, feat_width = share_refs[0].shape
    members = own_members * len(share_refs)
    stack = members * GROUP
    per_row = LANES // members
    sums = jnp.sum(partial_ref[...], axis=0)
    spread_rows = jnp.concatenate(
        [jnp.broadcast_to(sums[r : r + 1], (per_row, LANES)) for r in range(members // per_row)], axis=0
    )
    keep = iota((members, LANES), 0) % per_row == iota((members, LANES), 1) // members
    folded = (iota((LANES, members), 0) % members == iota((LANES, members), 1)).astype(F32)
    gram = exact_dot(jnp.where(keep, spread_rows, 0.0), folded)
    proj_row = jnp.broadcast_to(sums[members // per_row : members // per_row + 1], (members, LANES))
    on_diagonal = iota((members, LANES), 0) == iota((members, LANES), 1)
    proj = jnp.sum(jnp.where(on_diagonal, proj_row, 0.0), axis=1, keepdims=True)
    transform = ensemble_transform(gram, proj)
    held = global_member(iota((stack, members), 0) // GROUP, index_ref, own_members, len(share_refs))
    pick = (held == iota((stack, members), 1)).astype(F32).astype(BF16)
    same = iota((stack, stack), 0) % GROUP == iota((stack, stack), 1) % GROUP
    mixers = []
    for piece in halves(transform):
        rows_of = dot(pick, piece, ((1,), (1,))).astype(BF16)
        mixers.append(jnp.where(same, dot(rows_of, pick, ((1,), (1,))), 0.0).astype(BF16))
    for lower in range(0, rows, GROUP):
        part = slice(lower, lower + GROUP)
        fields = jnp.concatenate([ref[:, part, :].reshape(-1, feat_width) for ref in share_refs], axis=0)
        mixed = (dot(mixers[0], fields) + dot(mixers[1], fields)).astype(BF16)
        own_stack = own_members * GROUP
        for at, out_ref in enumerate(out_refs):
            piece = mixed[at * own_stack : (at + 1) * own_stack]
            out_ref[:, part, :] = piece.reshape(own_members, GROUP, feat_width)


def combine(index, partials, shares):
    size = shares[0].size * len(shares)
    members = shares[0].shape[0] * len(shares)
    return pl.pallas_call(
        combine_kernel,
        out_shape=[jax.ShapeDtypeStruct(v.shape, BF16) for v in shares],
        in_specs=[smem_spec()] + [vmem_spec()] * (1 + len(shares)),
        out_specs=[vmem_spec()] * len(shares),
        compiler_params=pltpu.CompilerParams(vmem_limit_bytes=VMEM_LIMIT),
        cost_estimate=pl.CostEstimate(flops=4 * GROUP * members * size, bytes_accessed=4 * size, transcendentals=0),
        name="combine",
    )(index, partials, *shares)


def assemble_kernel(index_ref, *refs):
    part_refs, out_ref = refs[:-1], refs[-1]
    rows = part_refs[0].shape[1]
    for part, ref in enumerate(part_refs):
        partner = partner_bits(part, index_ref[1] == 1, len(part_refs)) ^ index_ref[0]
        lower = pl.multiple_of(partner * rows, rows)
        out_ref[0, pl.ds(lower, rows), :] = ref[0]


def assemble(index, parts):
    members, rows, feat_width = parts[0].shape
    return pl.pallas_call(
        assemble_kernel,
        grid=(members,),
        out_shape=jax.ShapeDtypeStruct((members, len(parts) * rows, feat_width), BF16),
        in_specs=[smem_spec()] + [pl.BlockSpec((1, rows, feat_width), lambda m: (m, 0, 0))] * len(parts),
        out_specs=pl.BlockSpec((1, len(parts) * rows, feat_width), lambda m: (m, 0, 0)),
        compiler_params=pltpu.CompilerParams(vmem_limit_bytes=VMEM_LIMIT),
        cost_estimate=pl.CostEstimate(flops=0, bytes_accessed=4 * len(parts) * parts[0].size, transcendentals=0),
        name="assemble",
    )(index, *parts)


def exchanged(parts):
    mem_count, tok_count = lax.axis_size("mem"), lax.axis_size("tok")

    def pairs(part):
        for mem in range(mem_count):
            for tok in range(tok_count):
                target = mem ^ partner_bits(part, tok % 2 == 1, mem_count)
                yield mem * tok_count + tok, target * tok_count + tok

    return [lax.ppermute(v, ("mem", "tok"), list(pairs(part))) if part else v for part, v in enumerate(parts)]


def local(
    ens_state,
    attn_gain,
    ffn_gain,
    w_query,
    w_key,
    w_value,
    w_out,
    w_gate,
    w_up,
    down_weight,
    head_window,
    obs_token,
    obs_channel,
    obs_value,
    obs_var,
):
    own_members, row_count, feat_width = ens_state.shape
    mem_count = lax.axis_size("mem")
    tok_count = lax.axis_size("tok")
    device_count = mem_count * tok_count
    share_rows = row_count // mem_count
    first_pos = lax.axis_index("tok") * row_count
    up = [(i, i + 1) for i in range(tok_count - 1)]
    down = [(i + 1, i) for i in range(tok_count - 1)]
    left = lax.ppermute(ens_state[:, row_count - WIN :], "tok", up)
    right = lax.ppermute(ens_state[:, :WIN], "tok", down)
    share_start = first_pos + lax.axis_index("mem") * share_rows
    grid = sample_grid(
        share_start.astype(jnp.int32).reshape(1), obs_token, obs_channel, obs_value, obs_var, share_rows, feat_width
    )
    index = jnp.stack([lax.axis_index("mem"), lax.axis_index("tok") % 2]).astype(jnp.int32)
    place = jnp.concatenate([jnp.stack([first_pos, row_count * tok_count]).astype(jnp.int32), index])
    gains = [attn_gain.reshape(1, -1), ffn_gain.reshape(1, -1)]
    inner_parts = inner(head_window, ens_state, gains[0], w_query, w_key, w_value, WIN)
    weights = [w_key, w_value, w_out, w_gate, w_up, down_weight]
    forecast = forward(place, head_window, ens_state, inner_parts, left, right, gains, weights, mem_count)
    shares = exchanged(forecast)
    partial = gram_partial(index, shares, grid)
    partials = lax.all_to_all(
        jnp.broadcast_to(partial[None], (device_count, *partial.shape)),
        ("mem", "tok"),
        split_axis=0,
        concat_axis=0,
        tiled=True,
    )
    return assemble(index, exchanged(combine(index, partials, shares)))


def solution(mesh):
    in_specs = (P("mem", "tok", None), *[P()] * 10, *[P("tok")] * 4)
    return jax.shard_map(local, mesh=mesh, in_specs=in_specs, out_specs=P("mem", "tok", None), check_vma=False)
```

```python
import functools
import math

import jax
import jax.numpy as jnp
from jax import lax
from jax.experimental import pallas as pl
from jax.experimental.pallas import tpu as pltpu
from jax.sharding import PartitionSpec as P

WIN = 256
NS_STEPS = 8
EPS = 1e-05
Q_ROWS = 128
GROUP = 16
LANES = 128
VMEM_LIMIT = 32 * 1024 * 1024
SAFE_SCORE = 56.0
HIDDEN_CHUNK = 256

F32 = jnp.float32
BF16 = jnp.bfloat16


def dot(a, b, contract=((1,), (0,)), precision=None):
    return lax.dot_general(a, b, (contract, ((), ())), precision=precision, preferred_element_type=F32)


def exact_dot(a, b, contract=((1,), (0,))):
    return dot(a, b, contract, lax.Precision.HIGHEST)


def iota(shape, axis):
    return lax.broadcasted_iota(jnp.int32, shape, axis)


def halves(values):
    high = values.astype(BF16)
    return high, (values - high.astype(F32)).astype(BF16)


def rms_scaled(values, gain):
    rows, width = values.shape
    ones = jnp.ones((width, LANES), BF16)
    means = dot((values * values).astype(BF16), ones) * (1.0 / width)
    scale = lax.rsqrt(means + EPS)
    return values * jnp.concatenate([scale] * (width // LANES), axis=1) * gain


def vmem_spec():
    return pl.BlockSpec(memory_space=pltpu.VMEM)


def smem_spec():
    return pl.BlockSpec(memory_space=pltpu.SMEM)


def sample_grid_kernel(start_ref, token_ref, channel_ref, value_ref, var_ref, out_ref):
    rows, feat_width = out_ref.shape[1:]
    count = token_ref.shape[1]
    chunk = min(1024, count)
    total = jnp.zeros((4 * rows, feat_width), F32)
    for lower in range(0, count, chunk):
        part = slice(lower, lower + chunk)
        inv_var = 1.0 / var_ref[:, part]
        weighted = value_ref[:, part] * inv_var
        here = iota((rows, chunk), 0) == token_ref[:, part] - start_ref[0]
        pieces = []
        for row in (inv_var, weighted):
            high = row.astype(BF16).astype(F32)
            pieces.append(jnp.where(here, high, 0.0).astype(BF16))
            pieces.append(jnp.where(here, row - high, 0.0).astype(BF16))
        channel_hot = jnp.where(iota((feat_width, chunk), 0) == channel_ref[:, part], 1.0, 0.0).astype(BF16)
        total += dot(jnp.concatenate(pieces, axis=0), channel_hot, ((1,), (1,)))
    out_ref[0] = total[:rows] + total[rows : 2 * rows]
    out_ref[1] = total[2 * rows : 3 * rows] + total[3 * rows :]


def sample_grid(start, obs_token, obs_channel, obs_value, obs_var, rows, feat_width):
    count = obs_token.shape[0]
    return pl.pallas_call(
        sample_grid_kernel,
        out_shape=jax.ShapeDtypeStruct((2, rows, feat_width), F32),
        in_specs=[smem_spec()] + [vmem_spec()] * 4,
        out_specs=vmem_spec(),
        compiler_params=pltpu.CompilerParams(vmem_limit_bytes=VMEM_LIMIT),
        cost_estimate=pl.CostEstimate(flops=8 * rows * count * feat_width, bytes_accessed=16 * count, transcendentals=0),
        name="sample_grid",
    )(start, *(v.reshape(1, count) for v in (obs_token, obs_channel, obs_value, obs_var)))


def head_lanes(feat_width, heads):
    lane_head = iota((feat_width, LANES), 0) // (feat_width // heads)
    return (lane_head == iota((feat_width, LANES), 1)).astype(F32).astype(BF16)


def largest_norms(values, heads):
    squares = dot((values * values).astype(BF16), head_lanes(values.shape[1], heads))
    return jnp.max(squares, axis=0, keepdims=True)


def is_safe(query_norms, key_norms):
    return jnp.max(query_norms * key_norms) * 1.05 <= SAFE_SCORE * SAFE_SCORE


def query_scale(head_size):
    return math.log2(math.e) / math.sqrt(head_size)


def band_bias(window, lower, upper, reach):
    apart = jnp.abs(iota((Q_ROWS, upper - lower), 1) + (lower - reach) - iota((Q_ROWS, upper - lower), 0))
    return jnp.where(apart <= window, 0.0, -1e30)


def group_lanes(group):
    return slice(group * LANES, (group + 1) * LANES)


def stacked_heads(queries, head_size):
    lane_head = iota((1, LANES), 1) // head_size
    masks = [(lane_head == head).astype(F32).astype(BF16) for head in range(LANES // head_size)]
    return jnp.concatenate([queries * mask for mask in masks], axis=0)


def put_values(buf, lower, values):
    for group in range(values.shape[1] // LANES):
        lanes = slice(2 * group * LANES, (2 * group + 1) * LANES)
        buf[lower : lower + values.shape[0], lanes] = values[:, group_lanes(group)]


def weighted_sums(weights, values, head_size):
    mixed_all = dot(weights, values)
    heads = LANES // head_size
    count = mixed_all.shape[0] // heads
    lane_head = iota((1, LANES), 1) // head_size
    mixed, totals = mixed_all[:count, :LANES], mixed_all[:count, LANES:]
    for head in range(1, heads):
        part = mixed_all[head * count : (head + 1) * count]
        mixed = jnp.where(lane_head == head, part[:, :LANES], mixed)
        totals = jnp.where(lane_head == head, part[:, LANES:], totals)
    return mixed, totals


def padded_lanes(values, before, after):
    pieces = [jnp.zeros((values.shape[0], before), BF16)] if before else []
    pieces.append(values.astype(BF16))
    if after:
        pieces.append(jnp.zeros((values.shape[0], after), BF16))
    return jnp.concatenate(pieces, axis=1) if len(pieces) > 1 else pieces[0]


def unit_weights(scores, spans, bias_of):
    width = scores.shape[1]
    count = len(spans) * Q_ROWS
    weights = []
    for head in range(scores.shape[0] // count):
        for block, (lower, upper) in enumerate(spans):
            top = head * count + block * Q_ROWS
            expo = jnp.exp2(scores[top : top + Q_ROWS, lower:upper] + bias_of(head, block))
            weights.append(padded_lanes(expo, lower, width - upper))
    return jnp.concatenate(weights, axis=0)


def inner_kernel(
    window_ref,
    own_ref,
    gain_ref,
    w_query_ref,
    w_key_ref,
    w_value_ref,
    query_ref,
    norm_ref,
    mixed_ref,
    total_ref,
    key_buf,
    value_buf,
    bias_buf,
):
    rows, feat_width = own_ref.shape[1:]
    heads = window_ref.shape[0]
    head_size = feat_width // heads
    group_heads = LANES // head_size
    key_count = bias_buf.shape[2]
    reach = (key_count - Q_ROWS) // 2
    reach_blocks = reach // Q_ROWS
    blocks = rows // Q_ROWS

    @pl.when(pl.program_id(0) == 0)
    def _():
        for head in range(heads):
            bias_buf[head] = band_bias(window_ref[head], 0, key_count, reach)
        value_buf[...] = jnp.ones(value_buf.shape, BF16)

    normed = rms_scaled(own_ref[0].astype(F32), gain_ref[...]).astype(BF16)
    query_rows = dot(normed, w_query_ref[...]) * query_scale(head_size)
    key_rows = dot(normed, w_key_ref[...])
    query_ref[0] = query_rows.astype(BF16)
    key_buf[...] = key_rows.T.astype(BF16)
    put_values(value_buf, 0, dot(normed, w_value_ref[...]).astype(BF16))
    query_norms, key_norms = largest_norms(query_rows, heads), largest_norms(key_rows, heads)
    blank = jnp.zeros((norm_ref.shape[1] - 2, LANES), F32)
    norm_ref[0] = jnp.concatenate([query_norms, key_norms, blank], axis=0)

    @pl.when(is_safe(query_norms, key_norms))
    def _():
        groups = heads // group_heads
        ranges = [(max(0, b - reach_blocks), min(blocks, b + reach_blocks + 1)) for b in range(blocks)]
        spans = [(lower * Q_ROWS, upper * Q_ROWS) for lower, upper in ranges]

        def scores_of(group):
            queries = query_ref[0, :, group_lanes(group)]
            return dot(stacked_heads(queries, head_size), key_buf[group_lanes(group), :])

        scores = scores_of(0)
        for group in range(groups):
            following = scores_of(group + 1) if group + 1 < groups else None

            def bias_of(head, block):
                shift = (reach_blocks - block) * Q_ROWS
                lower, upper = spans[block]
                return bias_buf[group * group_heads + head, :, lower + shift : upper + shift]

            values = value_buf[:, 2 * group * LANES : 2 * (group + 1) * LANES]
            mixed, totals = weighted_sums(unit_weights(scores, spans, bias_of), values, head_size)
            mixed_ref[0, :, group_lanes(group)] = mixed
            total_ref[0, :, group_lanes(group)] = totals
            scores = following


def inner(head_window, own, gain, w_query, w_key, w_value, reach):
    members, rows, feat_width = own.shape
    heads = head_window.shape[0]
    key_count = Q_ROWS + 2 * reach
    shapes = [(own.shape, BF16), ((members, 8, LANES), F32), (own.shape, F32), (own.shape, F32)]

    def spec(shape):
        return pl.BlockSpec((1, *shape[1:]), lambda m: (m, 0, 0))

    return pl.pallas_call(
        inner_kernel,
        grid=(members,),
        out_shape=[jax.ShapeDtypeStruct(*v) for v in shapes],
        in_specs=[smem_spec(), spec(own.shape)] + [vmem_spec()] * 4,
        out_specs=[spec(shape) for shape, _ in shapes],
        scratch_shapes=[
            pltpu.VMEM((feat_width, rows), BF16),
            pltpu.VMEM((rows, 2 * feat_width), BF16),
            pltpu.VMEM((heads, Q_ROWS, key_count), F32),
        ],
        compiler_params=pltpu.CompilerParams(vmem_limit_bytes=VMEM_LIMIT),
        cost_estimate=pl.CostEstimate(
            flops=own.size * (6 * feat_width + 16 * rows), bytes_accessed=14 * own.size, transcendentals=0
        ),
        name="inner",
    )(head_window, own, gain, w_query, w_key, w_value)


def forward_kernel(
    total_len,
    tok_ref,
    mem_ref,
    window_ref,
    state_ref,
    query_ref,
    norm_ref,
    inner_mixed_ref,
    inner_total_ref,
    left_ref,
    right_ref,
    attn_gain_ref,
    ffn_gain_ref,
    w_key_ref,
    w_value_ref,
    w_out_ref,
    w_gate_ref,
    w_up_ref,
    down_weight_ref,
    *refs,
):
    out_refs, (halo_key_buf, halo_value_buf, bias_buf, mixed_buf, key_buf, value_buf, forecast_buf) = (
        refs[:-7],
        refs[-7:],
    )
    rows, feat_width = state_ref.shape[1:]
    reach = left_ref.shape[1]
    heads = window_ref.shape[0]
    head_size = feat_width // heads
    group_heads = LANES // head_size
    groups = heads // group_heads
    blocks = rows // Q_ROWS
    key_count = Q_ROWS + 2 * reach
    count = 2 * Q_ROWS
    first_pos = tok_ref[0] * rows

    @pl.when(pl.program_id(0) == 0)
    def _():
        first_valid = first_pos - reach >= 0
        last_valid = first_pos + rows + reach <= total_len
        for head in range(heads):
            left_bias = band_bias(window_ref[head], 0, reach, reach)
            right_bias = band_bias(window_ref[head], key_count - reach, key_count, reach)
            bias_buf[0, head] = jnp.where(first_valid, left_bias, -1e30)
            bias_buf[1, head] = jnp.where(last_valid, right_bias, -1e30)
        halo_value_buf[...] = jnp.ones(halo_value_buf.shape, BF16)

    def keys_of(normed):
        return dot(normed, w_key_ref[...])

    def values_of(normed):
        return dot(normed, w_value_ref[...]).astype(BF16)

    key_norms = norm_ref[0, 1:2, :]
    for side, ref in enumerate((left_ref, right_ref)):
        normed = rms_scaled(ref[0].astype(F32), attn_gain_ref[...]).astype(BF16)
        keys = keys_of(normed)
        key_norms = jnp.maximum(key_norms, largest_norms(keys, heads))
        halo_key_buf[side] = keys.T.astype(BF16)
        put_values(halo_value_buf.at[side], 0, values_of(normed))
    safe = is_safe(norm_ref[0, 0:1, :], key_norms)

    @pl.when(safe)
    def _():
        units = [(side, group) for side in range(2) for group in range(groups)]

        def scores_of(side, group):
            start = side * (rows - count)
            queries = query_ref[0, start : start + count, group_lanes(group)]
            return dot(stacked_heads(queries, head_size), halo_key_buf[side, group_lanes(group), :])

        scores = scores_of(*units[0])
        for at, (side, group) in enumerate(units):
            following = scores_of(*units[at + 1]) if at + 1 < len(units) else None
            spans = [(0, reach), (Q_ROWS, reach)] if side == 0 else [(0, reach - Q_ROWS), (0, reach)]

            def bias_of(head, block):
                lower, upper = spans[block]
                shift = -block * Q_ROWS if side == 0 else (1 - block) * Q_ROWS
                return bias_buf[side, group * group_heads + head, :, lower + shift : upper + shift]

            values = halo_value_buf[side, :, 2 * group * LANES : 2 * (group + 1) * LANES]
            mixed, totals = weighted_sums(unit_weights(scores, spans, bias_of), values, head_size)
            here = slice(side * (rows - count), side * (rows - count) + count)
            mixed = mixed + inner_mixed_ref[0, here, group_lanes(group)]
            totals = totals + inner_total_ref[0, here, group_lanes(group)]
            mixed_buf[here, group_lanes(group)] = (mixed / totals).astype(BF16)
            scores = following

    @pl.when(jnp.logical_not(safe))
    def _():
        normed = rms_scaled(state_ref[0].astype(F32), attn_gain_ref[...]).astype(BF16)
        key_buf[:, :reach] = halo_key_buf[0]
        key_buf[:, reach : reach + rows] = keys_of(normed).T.astype(BF16)
        key_buf[:, reach + rows :] = halo_key_buf[1]
        value_buf[...] = jnp.ones(value_buf.shape, BF16)
        put_values(value_buf, reach, values_of(normed))
        value_buf[:reach] = halo_value_buf[0]
        value_buf[reach + rows :] = halo_value_buf[1]
        for block in range(blocks):
            start = block * Q_ROWS
            k_pos = first_pos - reach + start + iota((Q_ROWS, key_count), 1)
            inside = (k_pos >= 0) & (k_pos < total_len)
            for group in range(groups):
                queries = query_ref[0, start : start + Q_ROWS, group_lanes(group)]
                keys = key_buf[group_lanes(group), start : start + key_count]
                scores = dot(stacked_heads(queries, head_size), keys)
                weights = []
                for head in range(group_heads):
                    bias = band_bias(window_ref[group * group_heads + head], 0, key_count, reach)
                    score_matrix = scores[head * Q_ROWS : (head + 1) * Q_ROWS] + jnp.where(inside, bias, -1e30)
                    row_top = jnp.max(score_matrix, axis=-1, keepdims=True)
                    weights.append(jnp.exp2(score_matrix - row_top).astype(BF16))
                values = value_buf[start : start + key_count, 2 * group * LANES : 2 * (group + 1) * LANES]
                mixed, totals = weighted_sums(jnp.concatenate(weights, axis=0), values, head_size)
                mixed_buf[start : start + Q_ROWS, group_lanes(group)] = (mixed / totals).astype(BF16)

    after = (state_ref[0].astype(F32) + dot(mixed_buf[...], w_out_ref[...])).astype(BF16)
    normed_mid = rms_scaled(after.astype(F32), ffn_gain_ref[...]).astype(BF16)
    hidden = []
    for lower in range(0, w_gate_ref.shape[1], HIDDEN_CHUNK):
        part = slice(lower, lower + HIDDEN_CHUNK)
        gate = 0.5 * dot(normed_mid, w_gate_ref[:, part])
        hidden.append((gate * (1.0 + jnp.tanh(gate)) * dot(normed_mid, w_up_ref[:, part])).astype(BF16))
    forecast = after.astype(F32) + dot(jnp.concatenate(hidden, axis=1), down_weight_ref[...])
    forecast_buf[...] = forecast.astype(BF16)
    share_rows = out_refs[0].shape[1]
    for part, out_ref in enumerate(out_refs):
        lower = pl.multiple_of((mem_ref[0] ^ part) * share_rows, share_rows)
        out_ref[0] = forecast_buf[pl.ds(lower, share_rows), :]


def forward(total_len, tok_index, mem_index, head_window, own, inner_parts, left, right, gains, weights, shares):
    members, row_count, feat_width = own.shape
    reach = left.shape[1]
    heads = head_window.shape[0]
    hidden_width = weights[3].shape[1]
    macs = members * row_count * feat_width * (3 * feat_width + 3 * hidden_width + 4 * reach)

    def spec(array):
        return pl.BlockSpec((1, *array.shape[1:]), lambda m: (m, 0, 0))

    return pl.pallas_call(
        functools.partial(forward_kernel, total_len),
        grid=(members,),
        out_shape=[jax.ShapeDtypeStruct((members, row_count // shares, feat_width), BF16)] * shares,
        in_specs=[smem_spec()] * 3
        + [spec(v) for v in (own, *inner_parts, left, right)]
        + [vmem_spec()] * (len(gains) + len(weights)),
        out_specs=[pl.BlockSpec((1, row_count // shares, feat_width), lambda m: (m, 0, 0))] * shares,
        scratch_shapes=[
            pltpu.VMEM((2, feat_width, reach), BF16),
            pltpu.VMEM((2, reach, 2 * feat_width), BF16),
            pltpu.VMEM((2, heads, Q_ROWS, reach), F32),
            pltpu.VMEM((row_count, feat_width), BF16),
            pltpu.VMEM((feat_width, row_count + 2 * reach), BF16),
            pltpu.VMEM((row_count + 2 * reach, 2 * feat_width), BF16),
            pltpu.VMEM((row_count, feat_width), BF16),
        ],
        compiler_params=pltpu.CompilerParams(vmem_limit_bytes=VMEM_LIMIT),
        cost_estimate=pl.CostEstimate(flops=2 * macs, bytes_accessed=10 * own.size, transcendentals=0),
        name="forward",
    )(tok_index, mem_index, head_window, own, *inner_parts, left, right, *gains, *weights)


def global_member(held, index, own_members):
    return ((held // own_members) ^ index) * own_members + held % own_members


def gram_kernel(index_ref, *refs):
    share_refs, grid_ref, out_ref = refs[:-2], refs[-2], refs[-1]
    own_members, rows, feat_width = share_refs[0].shape
    members = own_members * len(share_refs)
    index = index_ref[0]
    stack = members * GROUP
    total = jnp.zeros((stack, stack), F32)
    proj = jnp.zeros((members, GROUP, feat_width), F32)
    for lower in range(0, rows, GROUP):
        part = slice(lower, lower + GROUP)
        fields = jnp.concatenate([ref[:, part, :] for ref in share_refs], axis=0).astype(F32)
        mean = jnp.sum(fields, axis=0) * (1.0 / members)
        spread = fields - mean[None]
        weight = grid_ref[0, part, :]
        proj += spread * (grid_ref[1, part, :] - weight * mean)[None]
        high, low = halves(spread.reshape(stack, feat_width))
        w_high, w_low = halves((spread * weight[None]).reshape(stack, feat_width))
        last = ((1,), (1,))
        total += dot(w_high, high, last) + dot(w_high, low, last) + dot(w_low, high, last)
    same = iota((stack, stack), 0) % GROUP == iota((stack, stack), 1) % GROUP
    by_row = jnp.sum(jnp.where(same, total, 0.0).reshape(members, GROUP, stack), axis=1)
    column = global_member(iota((stack, LANES), 0) // GROUP, index, own_members)
    folded = (column == iota((stack, LANES), 1) % members).astype(F32)
    held = global_member(iota((members, members), 1), index, own_members)
    in_order = (held == iota((members, members), 0)).astype(F32)
    tiled = exact_dot(in_order, exact_dot(by_row, folded))
    per_row = LANES // members
    keep = iota((members, LANES), 0) % per_row == iota((members, LANES), 1) // members
    packed = jnp.sum(jnp.where(keep, tiled, 0.0).reshape(members // per_row, per_row, LANES), axis=1)
    proj_col = jnp.sum(jnp.sum(proj, axis=1), axis=1, keepdims=True)
    at_lane = global_member(iota((members, LANES), 0), index, own_members) == iota((members, LANES), 1)
    proj_row = jnp.sum(jnp.where(at_lane, proj_col, 0.0), axis=0, keepdims=True)
    filled = members // per_row + 1
    blank = jnp.zeros((out_ref.shape[0] - filled, LANES), F32)
    out_ref[...] = jnp.concatenate([packed, proj_row, blank], axis=0)


def gram_partial(index, shares, grid):
    members = shares[0].shape[0] * len(shares)
    filled = members * members // LANES + 1
    return pl.pallas_call(
        gram_kernel,
        out_shape=jax.ShapeDtypeStruct((-(-filled // 8) * 8, LANES), F32),
        in_specs=[smem_spec()] + [vmem_spec()] * (len(shares) + 1),
        out_specs=vmem_spec(),
        compiler_params=pltpu.CompilerParams(vmem_limit_bytes=VMEM_LIMIT),
        cost_estimate=pl.CostEstimate(
            flops=3 * GROUP * members * members * grid.size, bytes_accessed=members * grid.size, transcendentals=0
        ),
        name="gram",
    )(index, *shares, grid)


def ensemble_transform(gram, proj):
    members = gram.shape[0]
    row, column = iota((members, members), 0), iota((members, members), 1)
    identity = (row == column).astype(F32)
    system = gram + (members - 1.0) * identity
    left, right = system, proj
    for pivot in range(members):
        is_pivot = iota((members, 1), 0) == pivot
        scale = 1.0 / left[pivot : pivot + 1, pivot : pivot + 1]
        pivot_row = left[pivot : pivot + 1, :] * scale
        pivot_right = right[pivot : pivot + 1, :] * scale
        factor = left[:, pivot : pivot + 1]
        left = jnp.where(is_pivot, pivot_row, left - factor * pivot_row)
        right = jnp.where(is_pivot, pivot_right, right - factor * pivot_right)
    mean_weights = right
    mean_level = jnp.sum(jnp.sum(system * identity, axis=1, keepdims=True), axis=0, keepdims=True) / members
    lifted = system + (mean_level - (members - 1.0)) * (1.0 / members)
    frobenius = jnp.sqrt(jnp.sum(jnp.sum(lifted * lifted, axis=1, keepdims=True), axis=0, keepdims=True))
    root_iter = lifted / frobenius
    inv_iter = identity
    for sweep in range(NS_STEPS):
        product = root_iter if sweep == 0 else exact_dot(inv_iter, root_iter)
        correction = 1.5 * identity - 0.5 * product
        inv_iter = correction if sweep == 0 else exact_dot(correction, inv_iter)
        if sweep < NS_STEPS - 1:
            root_iter = exact_dot(root_iter, correction)
    inv_root = inv_iter / jnp.sqrt(frobenius) + (1.0 / math.sqrt(members - 1.0) - 1.0 / jnp.sqrt(mean_level)) * (
        1.0 / members
    )
    moved = mean_weights + math.sqrt(members - 1.0) * inv_root
    return 1.0 / members + moved - jnp.sum(moved, axis=0, keepdims=True) * (1.0 / members)


def combine_kernel(index_ref, partial_ref, *refs):
    share_refs, out_refs = refs[: len(refs) // 2], refs[len(refs) // 2 :]
    own_members, rows, feat_width = share_refs[0].shape
    members = own_members * len(share_refs)
    stack = members * GROUP
    per_row = LANES // members
    sums = jnp.sum(partial_ref[...], axis=0)
    spread_rows = jnp.concatenate(
        [jnp.broadcast_to(sums[r : r + 1], (per_row, LANES)) for r in range(members // per_row)], axis=0
    )
    keep = iota((members, LANES), 0) % per_row == iota((members, LANES), 1) // members
    folded = (iota((LANES, members), 0) % members == iota((LANES, members), 1)).astype(F32)
    gram = exact_dot(jnp.where(keep, spread_rows, 0.0), folded)
    proj_row = jnp.broadcast_to(sums[members // per_row : members // per_row + 1], (members, LANES))
    on_diagonal = iota((members, LANES), 0) == iota((members, LANES), 1)
    proj = jnp.sum(jnp.where(on_diagonal, proj_row, 0.0), axis=1, keepdims=True)
    transform = ensemble_transform(gram, proj)
    held = global_member(iota((stack, members), 0) // GROUP, index_ref[0], own_members)
    pick = (held == iota((stack, members), 1)).astype(F32).astype(BF16)
    same = iota((stack, stack), 0) % GROUP == iota((stack, stack), 1) % GROUP
    mixers = []
    for piece in halves(transform):
        rows_of = dot(pick, piece, ((1,), (1,))).astype(BF16)
        mixers.append(jnp.where(same, dot(rows_of, pick, ((1,), (1,))), 0.0).astype(BF16))
    for lower in range(0, rows, GROUP):
        part = slice(lower, lower + GROUP)
        fields = jnp.concatenate([ref[:, part, :].reshape(-1, feat_width) for ref in share_refs], axis=0)
        mixed = (dot(mixers[0], fields) + dot(mixers[1], fields)).astype(BF16)
        own_stack = own_members * GROUP
        for at, out_ref in enumerate(out_refs):
            piece = mixed[at * own_stack : (at + 1) * own_stack]
            out_ref[:, part, :] = piece.reshape(own_members, GROUP, feat_width)


def combine(index, partials, shares):
    size = shares[0].size * len(shares)
    members = shares[0].shape[0] * len(shares)
    return pl.pallas_call(
        combine_kernel,
        out_shape=[jax.ShapeDtypeStruct(v.shape, BF16) for v in shares],
        in_specs=[smem_spec()] + [vmem_spec()] * (1 + len(shares)),
        out_specs=[vmem_spec()] * len(shares),
        compiler_params=pltpu.CompilerParams(vmem_limit_bytes=VMEM_LIMIT),
        cost_estimate=pl.CostEstimate(flops=4 * GROUP * members * size, bytes_accessed=4 * size, transcendentals=0),
        name="combine",
    )(index, partials, *shares)


def assemble_kernel(index_ref, *refs):
    part_refs, out_ref, sems = refs[:-2], refs[-2], refs[-1]
    rows = part_refs[0].shape[1]
    copies = []
    for part, ref in enumerate(part_refs):
        lower = pl.multiple_of((index_ref[0] ^ part) * rows, rows)
        copies.append(pltpu.make_async_copy(ref, out_ref.at[:, pl.ds(lower, rows), :], sems.at[part]))
    for copy in copies:
        copy.start()
    for copy in copies:
        copy.wait()


def assemble(index, parts):
    members, rows, feat_width = parts[0].shape
    return pl.pallas_call(
        assemble_kernel,
        out_shape=jax.ShapeDtypeStruct((members, len(parts) * rows, feat_width), BF16),
        in_specs=[smem_spec()] + [vmem_spec()] * len(parts),
        out_specs=pl.BlockSpec(memory_space=pl.ANY),
        scratch_shapes=[pltpu.SemaphoreType.DMA((len(parts),))],
        compiler_params=pltpu.CompilerParams(vmem_limit_bytes=VMEM_LIMIT),
        cost_estimate=pl.CostEstimate(flops=0, bytes_accessed=4 * len(parts) * parts[0].size, transcendentals=0),
        name="assemble",
    )(index, *parts)


def exchanged(parts):
    count = lax.axis_size("mem")
    return [
        lax.ppermute(v, "mem", [(i, i ^ part) for i in range(count)]) if part else v for part, v in enumerate(parts)
    ]


def local(
    ens_state,
    attn_gain,
    ffn_gain,
    w_query,
    w_key,
    w_value,
    w_out,
    w_gate,
    w_up,
    down_weight,
    head_window,
    obs_token,
    obs_channel,
    obs_value,
    obs_var,
):
    own_members, row_count, feat_width = ens_state.shape
    mem_count = lax.axis_size("mem")
    tok_count = lax.axis_size("tok")
    device_count = mem_count * tok_count
    share_rows = row_count // mem_count
    first_pos = lax.axis_index("tok") * row_count
    up = [(i, i + 1) for i in range(tok_count - 1)]
    down = [(i + 1, i) for i in range(tok_count - 1)]
    left = lax.ppermute(ens_state[:, row_count - WIN :], "tok", up)
    right = lax.ppermute(ens_state[:, :WIN], "tok", down)
    share_start = first_pos + lax.axis_index("mem") * share_rows
    grid = sample_grid(
        share_start.astype(jnp.int32).reshape(1), obs_token, obs_channel, obs_value, obs_var, share_rows, feat_width
    )
    mem_index = lax.axis_index("mem").astype(jnp.int32).reshape(1)
    tok_index = lax.axis_index("tok").astype(jnp.int32).reshape(1)
    gains = [attn_gain.reshape(1, -1), ffn_gain.reshape(1, -1)]
    inner_parts = inner(head_window, ens_state, gains[0], w_query, w_key, w_value, WIN)
    weights = [w_key, w_value, w_out, w_gate, w_up, down_weight]
    total_len = row_count * tok_count
    forecast = forward(
        total_len, tok_index, mem_index, head_window, ens_state, inner_parts, left, right, gains, weights, mem_count
    )
    shares = exchanged(forecast)
    partial = gram_partial(mem_index, shares, grid)
    partials = lax.all_to_all(
        jnp.broadcast_to(partial[None], (device_count, *partial.shape)),
        ("mem", "tok"),
        split_axis=0,
        concat_axis=0,
        tiled=True,
    )
    return assemble(mem_index, exchanged(combine(mem_index, partials, shares)))


def solution(mesh):
    in_specs = (P("mem", "tok", None), *[P()] * 10, *[P("tok")] * 4)
    return jax.shard_map(local, mesh=mesh, in_specs=in_specs, out_specs=P("mem", "tok", None), check_vma=False)
```

```python
import functools
import math

import jax
import jax.numpy as jnp
from jax import lax
from jax.experimental import pallas as pl
from jax.experimental.pallas import tpu as pltpu
from jax.sharding import PartitionSpec as P

WIN = 256
NS_STEPS = 8
EPS = 1e-05
Q_ROWS = 128
GROUP = 16
LANES = 128
VMEM_LIMIT = 32 * 1024 * 1024
SAFE_SCORE = 56.0
HIDDEN_CHUNK = 256

F32 = jnp.float32
BF16 = jnp.bfloat16


def dot(a, b, contract=((1,), (0,)), precision=None):
    return lax.dot_general(a, b, (contract, ((), ())), precision=precision, preferred_element_type=F32)


def exact_dot(a, b, contract=((1,), (0,))):
    return dot(a, b, contract, lax.Precision.HIGHEST)


def iota(shape, axis):
    return lax.broadcasted_iota(jnp.int32, shape, axis)


def halves(values):
    high = values.astype(BF16)
    return high, (values - high.astype(F32)).astype(BF16)


def rms_scaled(values, gain):
    rows, width = values.shape
    ones = jnp.ones((width, LANES), BF16)
    means = dot((values * values).astype(BF16), ones) * (1.0 / width)
    scale = lax.rsqrt(means + EPS)
    return values * jnp.concatenate([scale] * (width // LANES), axis=1) * gain


def vmem_spec():
    return pl.BlockSpec(memory_space=pltpu.VMEM)


def smem_spec():
    return pl.BlockSpec(memory_space=pltpu.SMEM)


def edges_kernel(own_ref, head_ref, tail_ref, sems):
    reach = head_ref.shape[1]
    rows = own_ref.shape[1]
    copies = [
        pltpu.make_async_copy(own_ref.at[:, pl.ds(lower, reach), :], ref, sems.at[which])
        for which, (lower, ref) in enumerate(((rows - reach, tail_ref), (0, head_ref)))
    ]
    for copy in copies:
        copy.start()
    for copy in copies:
        copy.wait()


def edges(own, reach):
    members, _, feat_width = own.shape
    return pl.pallas_call(
        edges_kernel,
        out_shape=[jax.ShapeDtypeStruct((members, reach, feat_width), own.dtype)] * 2,
        in_specs=[pl.BlockSpec(memory_space=pl.ANY)],
        out_specs=[vmem_spec()] * 2,
        scratch_shapes=[pltpu.SemaphoreType.DMA((2,))],
        compiler_params=pltpu.CompilerParams(vmem_limit_bytes=VMEM_LIMIT),
        cost_estimate=pl.CostEstimate(flops=0, bytes_accessed=8 * members * reach * feat_width, transcendentals=0),
        name="edges",
    )(own)


def sample_grid_kernel(start_ref, token_ref, channel_ref, value_ref, var_ref, out_ref):
    rows, feat_width = out_ref.shape[1:]
    count = token_ref.shape[1]
    chunk = min(1024, count)
    total = jnp.zeros((4 * rows, feat_width), F32)
    for lower in range(0, count, chunk):
        part = slice(lower, lower + chunk)
        inv_var = 1.0 / var_ref[:, part]
        weighted = value_ref[:, part] * inv_var
        here = iota((rows, chunk), 0) == token_ref[:, part] - start_ref[0]
        pieces = []
        for row in (inv_var, weighted):
            high = row.astype(BF16).astype(F32)
            pieces.append(jnp.where(here, high, 0.0).astype(BF16))
            pieces.append(jnp.where(here, row - high, 0.0).astype(BF16))
        channel_hot = jnp.where(iota((feat_width, chunk), 0) == channel_ref[:, part], 1.0, 0.0).astype(BF16)
        total += dot(jnp.concatenate(pieces, axis=0), channel_hot, ((1,), (1,)))
    out_ref[0] = total[:rows] + total[rows : 2 * rows]
    out_ref[1] = total[2 * rows : 3 * rows] + total[3 * rows :]


def sample_grid(start, obs_token, obs_channel, obs_value, obs_var, rows, feat_width):
    count = obs_token.shape[0]
    return pl.pallas_call(
        sample_grid_kernel,
        out_shape=jax.ShapeDtypeStruct((2, rows, feat_width), F32),
        in_specs=[smem_spec()] + [vmem_spec()] * 4,
        out_specs=vmem_spec(),
        compiler_params=pltpu.CompilerParams(vmem_limit_bytes=VMEM_LIMIT),
        cost_estimate=pl.CostEstimate(flops=8 * rows * count * feat_width, bytes_accessed=16 * count, transcendentals=0),
        name="sample_grid",
    )(start, *(v.reshape(1, count) for v in (obs_token, obs_channel, obs_value, obs_var)))


def head_lanes(feat_width, heads):
    lane_head = iota((feat_width, LANES), 0) // (feat_width // heads)
    return (lane_head == iota((feat_width, LANES), 1)).astype(F32).astype(BF16)


def largest_norms(values, heads):
    squares = dot((values * values).astype(BF16), head_lanes(values.shape[1], heads))
    return jnp.max(squares, axis=0, keepdims=True)


def is_safe(query_norms, key_norms):
    return jnp.max(query_norms * key_norms) * 1.05 <= SAFE_SCORE * SAFE_SCORE


def query_scale(head_size):
    return math.log2(math.e) / math.sqrt(head_size)


def in_band(window, lower, upper, reach):
    apart = jnp.abs(iota((Q_ROWS, upper - lower), 1) + (lower - reach) - iota((Q_ROWS, upper - lower), 0))
    return apart <= window


def factor(mask):
    return jnp.where(mask, 1.0, 0.0).astype(BF16)


def group_lanes(group):
    return slice(group * LANES, (group + 1) * LANES)


def stacked_heads(queries, head_size):
    lane_head = iota((1, LANES), 1) // head_size
    masks = [(lane_head == head).astype(F32).astype(BF16) for head in range(LANES // head_size)]
    return jnp.concatenate([queries * mask for mask in masks], axis=0)


def put_values(buf, lower, values):
    for group in range(values.shape[1] // LANES):
        lanes = slice(2 * group * LANES, (2 * group + 1) * LANES)
        buf[lower : lower + values.shape[0], lanes] = values[:, group_lanes(group)]


def weighted_sums(weights, values, head_size):
    mixed_all = dot(weights, values)
    heads = LANES // head_size
    count = mixed_all.shape[0] // heads
    lane_head = iota((1, LANES), 1) // head_size
    mixed, totals = mixed_all[:count, :LANES], mixed_all[:count, LANES:]
    for head in range(1, heads):
        part = mixed_all[head * count : (head + 1) * count]
        mixed = jnp.where(lane_head == head, part[:, :LANES], mixed)
        totals = jnp.where(lane_head == head, part[:, LANES:], totals)
    return mixed, totals


def padded_lanes(values, before, after):
    pieces = [jnp.zeros((values.shape[0], before), BF16)] if before else []
    pieces.append(values)
    if after:
        pieces.append(jnp.zeros((values.shape[0], after), BF16))
    return jnp.concatenate(pieces, axis=1) if len(pieces) > 1 else pieces[0]


def unit_weights(scores, spans, band_of):
    width = scores.shape[1]
    count = len(spans) * Q_ROWS
    weights = []
    for head in range(scores.shape[0] // count):
        for block, (lower, upper) in enumerate(spans):
            top = head * count + block * Q_ROWS
            expo = jnp.exp2(scores[top : top + Q_ROWS, lower:upper]).astype(BF16)
            weights.append(padded_lanes(expo * band_of(head, block), lower, width - upper))
    return jnp.concatenate(weights, axis=0)


def inner_kernel(
    window_ref,
    own_ref,
    gain_ref,
    w_query_ref,
    w_key_ref,
    w_value_ref,
    query_ref,
    norm_ref,
    mixed_ref,
    total_ref,
    key_buf,
    value_buf,
    band_buf,
):
    rows, feat_width = own_ref.shape[1:]
    heads = window_ref.shape[0]
    head_size = feat_width // heads
    group_heads = LANES // head_size
    key_count = band_buf.shape[2]
    reach = (key_count - Q_ROWS) // 2
    reach_blocks = reach // Q_ROWS
    blocks = rows // Q_ROWS

    @pl.when(pl.program_id(0) == 0)
    def _():
        for head in range(heads):
            band_buf[head] = factor(in_band(window_ref[head], 0, key_count, reach))
        value_buf[...] = jnp.ones(value_buf.shape, BF16)

    normed = rms_scaled(own_ref[0].astype(F32), gain_ref[...]).astype(BF16)
    query_rows = dot(normed, w_query_ref[...]) * query_scale(head_size)
    key_rows = dot(normed, w_key_ref[...])
    query_ref[0] = query_rows.astype(BF16)
    key_buf[...] = key_rows.astype(BF16).T
    put_values(value_buf, 0, dot(normed, w_value_ref[...]).astype(BF16))
    query_norms, key_norms = largest_norms(query_rows, heads), largest_norms(key_rows, heads)
    blank = jnp.zeros((norm_ref.shape[1] - 2, LANES), F32)
    norm_ref[0] = jnp.concatenate([query_norms, key_norms, blank], axis=0)

    @pl.when(is_safe(query_norms, key_norms))
    def _():
        units = [(first, group) for first in range(0, blocks, 2) for group in range(heads // group_heads)]

        def scores_of(first, group):
            queries = query_ref[0, first * Q_ROWS : (first + 2) * Q_ROWS, group_lanes(group)]
            return dot(stacked_heads(queries, head_size), key_buf[group_lanes(group), :])

        scores = scores_of(*units[0])
        for at, (first, group) in enumerate(units):
            following = scores_of(*units[at + 1]) if at + 1 < len(units) else None
            ranges = [(max(0, b - reach_blocks), min(blocks, b + reach_blocks + 1)) for b in (first, first + 1)]
            spans = [(lower * Q_ROWS, upper * Q_ROWS) for lower, upper in ranges]

            def band_of(head, block):
                shift = (reach_blocks - first - block) * Q_ROWS
                lower, upper = spans[block]
                return band_buf[group * group_heads + head, :, lower + shift : upper + shift]

            values = value_buf[:, 2 * group * LANES : 2 * (group + 1) * LANES]
            mixed, totals = weighted_sums(unit_weights(scores, spans, band_of), values, head_size)
            here = slice(first * Q_ROWS, (first + 2) * Q_ROWS)
            mixed_ref[0, here, group_lanes(group)] = mixed
            total_ref[0, here, group_lanes(group)] = totals
            scores = following


def inner(head_window, own, gain, w_query, w_key, w_value, reach):
    members, rows, feat_width = own.shape
    heads = head_window.shape[0]
    key_count = Q_ROWS + 2 * reach
    shapes = [(own.shape, BF16), ((members, 8, LANES), F32), (own.shape, F32), (own.shape, F32)]

    def spec(shape):
        return pl.BlockSpec((1, *shape[1:]), lambda m: (m, 0, 0))

    return pl.pallas_call(
        inner_kernel,
        grid=(members,),
        out_shape=[jax.ShapeDtypeStruct(*v) for v in shapes],
        in_specs=[smem_spec(), spec(own.shape)] + [vmem_spec()] * 4,
        out_specs=[spec(shape) for shape, _ in shapes],
        scratch_shapes=[
            pltpu.VMEM((feat_width, rows), BF16),
            pltpu.VMEM((rows, 2 * feat_width), BF16),
            pltpu.VMEM((heads, Q_ROWS, key_count), BF16),
        ],
        compiler_params=pltpu.CompilerParams(vmem_limit_bytes=VMEM_LIMIT),
        cost_estimate=pl.CostEstimate(
            flops=own.size * (6 * feat_width + 16 * rows), bytes_accessed=14 * own.size, transcendentals=0
        ),
        name="inner",
    )(head_window, own, gain, w_query, w_key, w_value)


def forward_kernel(
    total_len,
    tok_ref,
    mem_ref,
    window_ref,
    state_ref,
    query_ref,
    norm_ref,
    inner_mixed_ref,
    inner_total_ref,
    left_ref,
    right_ref,
    attn_gain_ref,
    ffn_gain_ref,
    w_key_ref,
    w_value_ref,
    w_out_ref,
    w_gate_ref,
    w_up_ref,
    down_weight_ref,
    *refs,
):
    out_refs, (halo_key_buf, halo_value_buf, band_buf, mixed_buf, key_buf, value_buf, forecast_buf) = (
        refs[:-7],
        refs[-7:],
    )
    rows, feat_width = state_ref.shape[1:]
    reach = left_ref.shape[1]
    heads = window_ref.shape[0]
    head_size = feat_width // heads
    group_heads = LANES // head_size
    groups = heads // group_heads
    blocks = rows // Q_ROWS
    key_count = Q_ROWS + 2 * reach
    count = 2 * Q_ROWS
    first_pos = tok_ref[0] * rows

    @pl.when(pl.program_id(0) == 0)
    def _():
        first_valid = first_pos - reach >= 0
        last_valid = first_pos + rows + reach <= total_len
        for head in range(heads):
            window = window_ref[head]
            band_buf[0, head] = factor(in_band(jnp.where(first_valid, window, -1), 0, reach, reach))
            right_window = jnp.where(last_valid, window, -1)
            band_buf[1, head] = factor(in_band(right_window, key_count - reach, key_count, reach))
        halo_value_buf[...] = jnp.ones(halo_value_buf.shape, BF16)

    def keys_of(normed):
        return dot(normed, w_key_ref[...])

    def values_of(normed):
        return dot(normed, w_value_ref[...]).astype(BF16)

    key_norms = norm_ref[0, 1:2, :]
    for side, ref in enumerate((left_ref, right_ref)):
        normed = rms_scaled(ref[0].astype(F32), attn_gain_ref[...]).astype(BF16)
        keys = keys_of(normed)
        key_norms = jnp.maximum(key_norms, largest_norms(keys, heads))
        halo_key_buf[side] = keys.astype(BF16).T
        put_values(halo_value_buf.at[side], 0, values_of(normed))
    safe = is_safe(norm_ref[0, 0:1, :], key_norms)

    @pl.when(safe)
    def _():
        units = [(side, group) for side in range(2) for group in range(groups)]

        def scores_of(side, group):
            start = side * (rows - count)
            queries = query_ref[0, start : start + count, group_lanes(group)]
            return dot(stacked_heads(queries, head_size), halo_key_buf[side, group_lanes(group), :])

        scores = scores_of(*units[0])
        for at, (side, group) in enumerate(units):
            following = scores_of(*units[at + 1]) if at + 1 < len(units) else None
            spans = [(0, reach), (Q_ROWS, reach)] if side == 0 else [(0, reach - Q_ROWS), (0, reach)]

            def band_of(head, block):
                lower, upper = spans[block]
                shift = -block * Q_ROWS if side == 0 else (1 - block) * Q_ROWS
                return band_buf[side, group * group_heads + head, :, lower + shift : upper + shift]

            values = halo_value_buf[side, :, 2 * group * LANES : 2 * (group + 1) * LANES]
            mixed, totals = weighted_sums(unit_weights(scores, spans, band_of), values, head_size)
            here = slice(side * (rows - count), side * (rows - count) + count)
            mixed = mixed + inner_mixed_ref[0, here, group_lanes(group)]
            totals = totals + inner_total_ref[0, here, group_lanes(group)]
            mixed_buf[here, group_lanes(group)] = (mixed / totals).astype(BF16)
            scores = following

    @pl.when(jnp.logical_not(safe))
    def _():
        normed = rms_scaled(state_ref[0].astype(F32), attn_gain_ref[...]).astype(BF16)
        key_buf[:, :reach] = halo_key_buf[0]
        key_buf[:, reach : reach + rows] = keys_of(normed).astype(BF16).T
        key_buf[:, reach + rows :] = halo_key_buf[1]
        value_buf[...] = jnp.ones(value_buf.shape, BF16)
        put_values(value_buf, reach, values_of(normed))
        value_buf[:reach] = halo_value_buf[0]
        value_buf[reach + rows :] = halo_value_buf[1]
        for block in range(blocks):
            start = block * Q_ROWS
            k_pos = first_pos - reach + start + iota((Q_ROWS, key_count), 1)
            inside = (k_pos >= 0) & (k_pos < total_len)
            for group in range(groups):
                queries = query_ref[0, start : start + Q_ROWS, group_lanes(group)]
                keys = key_buf[group_lanes(group), start : start + key_count]
                scores = dot(stacked_heads(queries, head_size), keys)
                weights = []
                for head in range(group_heads):
                    allowed = inside & in_band(window_ref[group * group_heads + head], 0, key_count, reach)
                    score_matrix = jnp.where(allowed, scores[head * Q_ROWS : (head + 1) * Q_ROWS], -1e30)
                    row_top = jnp.max(score_matrix, axis=-1, keepdims=True)
                    weights.append(jnp.exp2(score_matrix - row_top).astype(BF16))
                values = value_buf[start : start + key_count, 2 * group * LANES : 2 * (group + 1) * LANES]
                mixed, totals = weighted_sums(jnp.concatenate(weights, axis=0), values, head_size)
                mixed_buf[start : start + Q_ROWS, group_lanes(group)] = (mixed / totals).astype(BF16)

    after = (state_ref[0].astype(F32) + dot(mixed_buf[...], w_out_ref[...])).astype(BF16)
    normed_mid = rms_scaled(after.astype(F32), ffn_gain_ref[...]).astype(BF16)
    forecast = after.astype(F32)
    for lower in range(0, w_gate_ref.shape[1], HIDDEN_CHUNK):
        part = slice(lower, lower + HIDDEN_CHUNK)
        gate = 0.5 * dot(normed_mid, w_gate_ref[:, part])
        hidden = (gate * (1.0 + jnp.tanh(gate)) * dot(normed_mid, w_up_ref[:, part])).astype(BF16)
        forecast += dot(hidden, down_weight_ref[part, :])
    forecast_buf[...] = forecast.astype(BF16)
    share_rows = out_refs[0].shape[1]
    for part, out_ref in enumerate(out_refs):
        lower = pl.multiple_of((mem_ref[0] ^ part) * share_rows, share_rows)
        out_ref[0] = forecast_buf[pl.ds(lower, share_rows), :]


def forward(total_len, tok_index, mem_index, head_window, own, inner_parts, left, right, gains, weights, shares):
    members, row_count, feat_width = own.shape
    reach = left.shape[1]
    heads = head_window.shape[0]
    hidden_width = weights[3].shape[1]
    macs = members * row_count * feat_width * (3 * feat_width + 3 * hidden_width + 4 * reach)

    def spec(array):
        return pl.BlockSpec((1, *array.shape[1:]), lambda m: (m, 0, 0))

    return pl.pallas_call(
        functools.partial(forward_kernel, total_len),
        grid=(members,),
        out_shape=[jax.ShapeDtypeStruct((members, row_count // shares, feat_width), BF16)] * shares,
        in_specs=[smem_spec()] * 3
        + [spec(v) for v in (own, *inner_parts, left, right)]
        + [vmem_spec()] * (len(gains) + len(weights)),
        out_specs=[pl.BlockSpec((1, row_count // shares, feat_width), lambda m: (m, 0, 0))] * shares,
        scratch_shapes=[
            pltpu.VMEM((2, feat_width, reach), BF16),
            pltpu.VMEM((2, reach, 2 * feat_width), BF16),
            pltpu.VMEM((2, heads, Q_ROWS, reach), BF16),
            pltpu.VMEM((row_count, feat_width), BF16),
            pltpu.VMEM((feat_width, row_count + 2 * reach), BF16),
            pltpu.VMEM((row_count + 2 * reach, 2 * feat_width), BF16),
            pltpu.VMEM((row_count, feat_width), BF16),
        ],
        compiler_params=pltpu.CompilerParams(vmem_limit_bytes=VMEM_LIMIT),
        cost_estimate=pl.CostEstimate(flops=2 * macs, bytes_accessed=10 * own.size, transcendentals=0),
        name="forward",
    )(tok_index, mem_index, head_window, own, *inner_parts, left, right, *gains, *weights)


def global_member(held, index, own_members):
    return ((held // own_members) ^ index) * own_members + held % own_members


def gram_kernel(index_ref, *refs):
    share_refs, grid_ref, out_ref = refs[:-2], refs[-2], refs[-1]
    own_members, rows, feat_width = share_refs[0].shape
    members = own_members * len(share_refs)
    index = index_ref[0]
    stack = members * GROUP
    total = jnp.zeros((stack, stack), F32)
    proj = jnp.zeros((members, GROUP, feat_width), F32)
    for lower in range(0, rows, GROUP):
        part = slice(lower, lower + GROUP)
        fields = jnp.concatenate([ref[:, part, :] for ref in share_refs], axis=0).astype(F32)
        mean = jnp.sum(fields, axis=0) * (1.0 / members)
        spread = fields - mean[None]
        weight = grid_ref[0, part, :]
        proj += spread * (grid_ref[1, part, :] - weight * mean)[None]
        high, low = halves(spread.reshape(stack, feat_width))
        w_high, w_low = halves((spread * weight[None]).reshape(stack, feat_width))
        last = ((1,), (1,))
        total += dot(w_high, high, last) + dot(w_high, low, last) + dot(w_low, high, last)
    same = iota((stack, stack), 0) % GROUP == iota((stack, stack), 1) % GROUP
    by_row = jnp.sum(jnp.where(same, total, 0.0).reshape(members, GROUP, stack), axis=1)
    column = global_member(iota((stack, LANES), 0) // GROUP, index, own_members)
    folded = (column == iota((stack, LANES), 1) % members).astype(F32)
    held = global_member(iota((members, members), 1), index, own_members)
    in_order = (held == iota((members, members), 0)).astype(F32)
    tiled = exact_dot(in_order, exact_dot(by_row, folded))
    per_row = LANES // members
    keep = iota((members, LANES), 0) % per_row == iota((members, LANES), 1) // members
    packed = jnp.sum(jnp.where(keep, tiled, 0.0).reshape(members // per_row, per_row, LANES), axis=1)
    proj_col = jnp.sum(jnp.sum(proj, axis=1), axis=1, keepdims=True)
    at_lane = global_member(iota((members, LANES), 0), index, own_members) == iota((members, LANES), 1)
    proj_row = jnp.sum(jnp.where(at_lane, proj_col, 0.0), axis=0, keepdims=True)
    filled = members // per_row + 1
    blank = jnp.zeros((out_ref.shape[0] - filled, LANES), F32)
    out_ref[...] = jnp.concatenate([packed, proj_row, blank], axis=0)


def gram_partial(index, shares, grid):
    members = shares[0].shape[0] * len(shares)
    filled = members * members // LANES + 1
    return pl.pallas_call(
        gram_kernel,
        out_shape=jax.ShapeDtypeStruct((-(-filled // 8) * 8, LANES), F32),
        in_specs=[smem_spec()] + [vmem_spec()] * (len(shares) + 1),
        out_specs=vmem_spec(),
        compiler_params=pltpu.CompilerParams(vmem_limit_bytes=VMEM_LIMIT),
        cost_estimate=pl.CostEstimate(
            flops=3 * GROUP * members * members * grid.size, bytes_accessed=members * grid.size, transcendentals=0
        ),
        name="gram",
    )(index, *shares, grid)


def ensemble_transform(gram, proj):
    members = gram.shape[0]
    row, column = iota((members, members), 0), iota((members, members), 1)
    identity = (row == column).astype(F32)
    system = gram + (members - 1.0) * identity
    left, right = system, proj
    for pivot in range(members):
        is_pivot = iota((members, 1), 0) == pivot
        scale = 1.0 / left[pivot : pivot + 1, pivot : pivot + 1]
        pivot_row = left[pivot : pivot + 1, :] * scale
        pivot_right = right[pivot : pivot + 1, :] * scale
        factor = left[:, pivot : pivot + 1]
        left = jnp.where(is_pivot, pivot_row, left - factor * pivot_row)
        right = jnp.where(is_pivot, pivot_right, right - factor * pivot_right)
    mean_weights = right
    mean_level = jnp.sum(jnp.sum(system * identity, axis=1, keepdims=True), axis=0, keepdims=True) / members
    lifted = system + (mean_level - (members - 1.0)) * (1.0 / members)
    frobenius = jnp.sqrt(jnp.sum(jnp.sum(lifted * lifted, axis=1, keepdims=True), axis=0, keepdims=True))
    root_iter = lifted / frobenius
    inv_iter = identity
    for sweep in range(NS_STEPS):
        product = root_iter if sweep == 0 else exact_dot(inv_iter, root_iter)
        correction = 1.5 * identity - 0.5 * product
        inv_iter = correction if sweep == 0 else exact_dot(correction, inv_iter)
        if sweep < NS_STEPS - 1:
            root_iter = exact_dot(root_iter, correction)
    inv_root = inv_iter / jnp.sqrt(frobenius) + (1.0 / math.sqrt(members - 1.0) - 1.0 / jnp.sqrt(mean_level)) * (
        1.0 / members
    )
    moved = mean_weights + math.sqrt(members - 1.0) * inv_root
    return 1.0 / members + moved - jnp.sum(moved, axis=0, keepdims=True) * (1.0 / members)


def combine_kernel(index_ref, partial_ref, *refs):
    share_refs, out_refs = refs[: len(refs) // 2], refs[len(refs) // 2 :]
    own_members, rows, feat_width = share_refs[0].shape
    members = own_members * len(share_refs)
    stack = members * GROUP
    per_row = LANES // members
    sums = jnp.sum(partial_ref[...], axis=0)
    spread_rows = jnp.concatenate(
        [jnp.broadcast_to(sums[r : r + 1], (per_row, LANES)) for r in range(members // per_row)], axis=0
    )
    keep = iota((members, LANES), 0) % per_row == iota((members, LANES), 1) // members
    folded = (iota((LANES, members), 0) % members == iota((LANES, members), 1)).astype(F32)
    gram = exact_dot(jnp.where(keep, spread_rows, 0.0), folded)
    proj_row = jnp.broadcast_to(sums[members // per_row : members // per_row + 1], (members, LANES))
    on_diagonal = iota((members, LANES), 0) == iota((members, LANES), 1)
    proj = jnp.sum(jnp.where(on_diagonal, proj_row, 0.0), axis=1, keepdims=True)
    transform = ensemble_transform(gram, proj)
    held = global_member(iota((stack, members), 0) // GROUP, index_ref[0], own_members)
    pick = (held == iota((stack, members), 1)).astype(F32).astype(BF16)
    same = iota((stack, stack), 0) % GROUP == iota((stack, stack), 1) % GROUP
    mixers = []
    for piece in halves(transform):
        rows_of = dot(pick, piece, ((1,), (1,))).astype(BF16)
        mixers.append(jnp.where(same, dot(rows_of, pick, ((1,), (1,))), 0.0).astype(BF16))
    for lower in range(0, rows, GROUP):
        part = slice(lower, lower + GROUP)
        fields = jnp.concatenate([ref[:, part, :].reshape(-1, feat_width) for ref in share_refs], axis=0)
        mixed = (dot(mixers[0], fields) + dot(mixers[1], fields)).astype(BF16)
        own_stack = own_members * GROUP
        for at, out_ref in enumerate(out_refs):
            piece = mixed[at * own_stack : (at + 1) * own_stack]
            out_ref[:, part, :] = piece.reshape(own_members, GROUP, feat_width)


def combine(index, partials, shares):
    size = shares[0].size * len(shares)
    members = shares[0].shape[0] * len(shares)
    return pl.pallas_call(
        combine_kernel,
        out_shape=[jax.ShapeDtypeStruct(v.shape, BF16) for v in shares],
        in_specs=[smem_spec()] + [vmem_spec()] * (1 + len(shares)),
        out_specs=[vmem_spec()] * len(shares),
        compiler_params=pltpu.CompilerParams(vmem_limit_bytes=VMEM_LIMIT),
        cost_estimate=pl.CostEstimate(flops=4 * GROUP * members * size, bytes_accessed=4 * size, transcendentals=0),
        name="combine",
    )(index, partials, *shares)


def assemble_kernel(index_ref, *refs):
    part_refs, out_ref, sems = refs[:-2], refs[-2], refs[-1]
    rows = part_refs[0].shape[1]
    copies = []
    for part, ref in enumerate(part_refs):
        lower = pl.multiple_of((index_ref[0] ^ part) * rows, rows)
        copies.append(pltpu.make_async_copy(ref, out_ref.at[:, pl.ds(lower, rows), :], sems.at[part]))
    for copy in copies:
        copy.start()
    for copy in copies:
        copy.wait()


def assemble(index, parts):
    members, rows, feat_width = parts[0].shape
    return pl.pallas_call(
        assemble_kernel,
        out_shape=jax.ShapeDtypeStruct((members, len(parts) * rows, feat_width), BF16),
        in_specs=[smem_spec()] + [vmem_spec()] * len(parts),
        out_specs=pl.BlockSpec(memory_space=pl.ANY),
        scratch_shapes=[pltpu.SemaphoreType.DMA((len(parts),))],
        compiler_params=pltpu.CompilerParams(vmem_limit_bytes=VMEM_LIMIT),
        cost_estimate=pl.CostEstimate(flops=0, bytes_accessed=4 * len(parts) * parts[0].size, transcendentals=0),
        name="assemble",
    )(index, *parts)


def exchanged(parts):
    count = lax.axis_size("mem")
    return [
        lax.ppermute(v, "mem", [(i, i ^ part) for i in range(count)]) if part else v for part, v in enumerate(parts)
    ]


def local(
    ens_state,
    attn_gain,
    ffn_gain,
    w_query,
    w_key,
    w_value,
    w_out,
    w_gate,
    w_up,
    down_weight,
    head_window,
    obs_token,
    obs_channel,
    obs_value,
    obs_var,
):
    own_members, row_count, feat_width = ens_state.shape
    mem_count = lax.axis_size("mem")
    tok_count = lax.axis_size("tok")
    device_count = mem_count * tok_count
    share_rows = row_count // mem_count
    first_pos = lax.axis_index("tok") * row_count
    up = [(i, i + 1) for i in range(tok_count - 1)]
    down = [(i + 1, i) for i in range(tok_count - 1)]
    head, tail = edges(ens_state, WIN)
    left = lax.ppermute(tail, "tok", up)
    right = lax.ppermute(head, "tok", down)
    share_start = first_pos + lax.axis_index("mem") * share_rows
    grid = sample_grid(
        share_start.astype(jnp.int32).reshape(1), obs_token, obs_channel, obs_value, obs_var, share_rows, feat_width
    )
    mem_index = lax.axis_index("mem").astype(jnp.int32).reshape(1)
    tok_index = lax.axis_index("tok").astype(jnp.int32).reshape(1)
    gains = [attn_gain.reshape(1, -1), ffn_gain.reshape(1, -1)]
    inner_parts = inner(head_window, ens_state, gains[0], w_query, w_key, w_value, WIN)
    weights = [w_key, w_value, w_out, w_gate, w_up, down_weight]
    total_len = row_count * tok_count
    forecast = forward(
        total_len, tok_index, mem_index, head_window, ens_state, inner_parts, left, right, gains, weights, mem_count
    )
    shares = exchanged(forecast)
    partial = gram_partial(mem_index, shares, grid)
    partials = lax.all_to_all(
        jnp.broadcast_to(partial[None], (device_count, *partial.shape)),
        ("mem", "tok"),
        split_axis=0,
        concat_axis=0,
        tiled=True,
    )
    return assemble(mem_index, exchanged(combine(mem_index, partials, shares)))


def solution(mesh):
    in_specs = (P("mem", "tok", None), *[P()] * 10, *[P("tok")] * 4)
    return jax.shard_map(local, mesh=mesh, in_specs=in_specs, out_specs=P("mem", "tok", None), check_vma=False)
```

```python
import functools
import math

import jax
import jax.numpy as jnp
from jax import lax
from jax.experimental import pallas as pl
from jax.experimental.pallas import tpu as pltpu
from jax.sharding import PartitionSpec as P

WIN = 256
NS_STEPS = 8
EPS = 1e-05
Q_ROWS = 128
GROUP = 16
LANES = 128
VMEM_LIMIT = 32 * 1024 * 1024
SAFE_SCORE = 56.0
HIDDEN_CHUNK = 256

F32 = jnp.float32
BF16 = jnp.bfloat16


def dot(a, b, contract=((1,), (0,)), precision=None):
    return lax.dot_general(a, b, (contract, ((), ())), precision=precision, preferred_element_type=F32)


def exact_dot(a, b, contract=((1,), (0,))):
    return dot(a, b, contract, lax.Precision.HIGHEST)


def iota(shape, axis):
    return lax.broadcasted_iota(jnp.int32, shape, axis)


def halves(values):
    high = values.astype(BF16)
    return high, (values - high.astype(F32)).astype(BF16)


def rms_scaled(values, gain):
    rows, width = values.shape
    ones = jnp.ones((width, LANES), BF16)
    means = dot((values * values).astype(BF16), ones) * (1.0 / width)
    scale = lax.rsqrt(means + EPS)
    return values * jnp.concatenate([scale] * (width // LANES), axis=1) * gain


def vmem_spec():
    return pl.BlockSpec(memory_space=pltpu.VMEM)


def smem_spec():
    return pl.BlockSpec(memory_space=pltpu.SMEM)


def sample_grid_kernel(start_ref, token_ref, channel_ref, value_ref, var_ref, out_ref):
    rows, feat_width = out_ref.shape[1:]
    count = token_ref.shape[1]
    chunk = min(1024, count)
    total = jnp.zeros((4 * rows, feat_width), F32)
    for lower in range(0, count, chunk):
        part = slice(lower, lower + chunk)
        inv_var = 1.0 / var_ref[:, part]
        weighted = value_ref[:, part] * inv_var
        here = iota((rows, chunk), 0) == token_ref[:, part] - start_ref[0]
        pieces = []
        for row in (inv_var, weighted):
            high = row.astype(BF16).astype(F32)
            pieces.append(jnp.where(here, high, 0.0).astype(BF16))
            pieces.append(jnp.where(here, row - high, 0.0).astype(BF16))
        channel_hot = jnp.where(iota((feat_width, chunk), 0) == channel_ref[:, part], 1.0, 0.0).astype(BF16)
        total += dot(jnp.concatenate(pieces, axis=0), channel_hot, ((1,), (1,)))
    out_ref[0] = total[:rows] + total[rows : 2 * rows]
    out_ref[1] = total[2 * rows : 3 * rows] + total[3 * rows :]


def sample_grid(start, obs_token, obs_channel, obs_value, obs_var, rows, feat_width):
    count = obs_token.shape[0]
    return pl.pallas_call(
        sample_grid_kernel,
        out_shape=jax.ShapeDtypeStruct((2, rows, feat_width), F32),
        in_specs=[smem_spec()] + [vmem_spec()] * 4,
        out_specs=vmem_spec(),
        compiler_params=pltpu.CompilerParams(vmem_limit_bytes=VMEM_LIMIT),
        cost_estimate=pl.CostEstimate(flops=8 * rows * count * feat_width, bytes_accessed=16 * count, transcendentals=0),
        name="sample_grid",
    )(start, *(v.reshape(1, count) for v in (obs_token, obs_channel, obs_value, obs_var)))


def head_lanes(feat_width, heads):
    lane_head = iota((feat_width, LANES), 0) // (feat_width // heads)
    return (lane_head == iota((feat_width, LANES), 1)).astype(F32).astype(BF16)


def largest_norms(values, heads):
    squares = dot((values * values).astype(BF16), head_lanes(values.shape[1], heads))
    return jnp.max(squares, axis=0, keepdims=True)


def is_safe(query_norms, key_norms):
    return jnp.max(query_norms * key_norms) * 1.05 <= SAFE_SCORE * SAFE_SCORE


def query_scale(head_size):
    return math.log2(math.e) / math.sqrt(head_size)


def in_band(window, lower, upper, reach):
    apart = jnp.abs(iota((Q_ROWS, upper - lower), 1) + (lower - reach) - iota((Q_ROWS, upper - lower), 0))
    return apart <= window


def factor(mask):
    return jnp.where(mask, 1.0, 0.0).astype(BF16)


def group_lanes(group):
    return slice(group * LANES, (group + 1) * LANES)


def stacked_heads(queries, head_size):
    lane_head = iota((1, LANES), 1) // head_size
    masks = [(lane_head == head).astype(F32).astype(BF16) for head in range(LANES // head_size)]
    return jnp.concatenate([queries * mask for mask in masks], axis=0)


def put_values(buf, lower, values):
    for group in range(values.shape[1] // LANES):
        lanes = slice(2 * group * LANES, (2 * group + 1) * LANES)
        buf[lower : lower + values.shape[0], lanes] = values[:, group_lanes(group)]


def weighted_sums(weights, values, head_size):
    mixed_all = dot(weights, values)
    heads = LANES // head_size
    count = mixed_all.shape[0] // heads
    lane_head = iota((1, LANES), 1) // head_size
    mixed, totals = mixed_all[:count, :LANES], mixed_all[:count, LANES:]
    for head in range(1, heads):
        part = mixed_all[head * count : (head + 1) * count]
        mixed = jnp.where(lane_head == head, part[:, :LANES], mixed)
        totals = jnp.where(lane_head == head, part[:, LANES:], totals)
    return mixed, totals


def padded_lanes(values, before, after):
    pieces = [jnp.zeros((values.shape[0], before), BF16)] if before else []
    pieces.append(values)
    if after:
        pieces.append(jnp.zeros((values.shape[0], after), BF16))
    return jnp.concatenate(pieces, axis=1) if len(pieces) > 1 else pieces[0]


def unit_weights(scores, spans, band_of):
    width = scores.shape[1]
    count = len(spans) * Q_ROWS
    weights = []
    for head in range(scores.shape[0] // count):
        for block, (lower, upper) in enumerate(spans):
            top = head * count + block * Q_ROWS
            expo = jnp.exp2(scores[top : top + Q_ROWS, lower:upper]).astype(BF16)
            weights.append(padded_lanes(expo * band_of(head, block), lower, width - upper))
    return jnp.concatenate(weights, axis=0)


def inner_kernel(
    window_ref,
    own_ref,
    gain_ref,
    w_query_ref,
    w_key_ref,
    w_value_ref,
    query_ref,
    norm_ref,
    mixed_ref,
    total_ref,
    key_buf,
    value_buf,
    band_buf,
):
    rows, feat_width = own_ref.shape[1:]
    heads = window_ref.shape[0]
    head_size = feat_width // heads
    group_heads = LANES // head_size
    key_count = band_buf.shape[2]
    reach = (key_count - Q_ROWS) // 2
    reach_blocks = reach // Q_ROWS
    blocks = rows // Q_ROWS

    @pl.when(pl.program_id(0) == 0)
    def _():
        for head in range(heads):
            band_buf[head] = factor(in_band(window_ref[head], 0, key_count, reach))
        value_buf[...] = jnp.ones(value_buf.shape, BF16)

    normed = rms_scaled(own_ref[0].astype(F32), gain_ref[...]).astype(BF16)
    query_rows = dot(normed, w_query_ref[...]) * query_scale(head_size)
    key_rows = dot(normed, w_key_ref[...])
    query_ref[0] = query_rows.astype(BF16)
    key_buf[...] = key_rows.astype(BF16).T
    put_values(value_buf, 0, dot(normed, w_value_ref[...]).astype(BF16))
    query_norms, key_norms = largest_norms(query_rows, heads), largest_norms(key_rows, heads)
    blank = jnp.zeros((norm_ref.shape[1] - 2, LANES), F32)
    norm_ref[0] = jnp.concatenate([query_norms, key_norms, blank], axis=0)

    @pl.when(is_safe(query_norms, key_norms))
    def _():
        units = [(first, group) for first in range(0, blocks, 2) for group in range(heads // group_heads)]

        def scores_of(first, group):
            queries = query_ref[0, first * Q_ROWS : (first + 2) * Q_ROWS, group_lanes(group)]
            return dot(stacked_heads(queries, head_size), key_buf[group_lanes(group), :])

        scores = scores_of(*units[0])
        for at, (first, group) in enumerate(units):
            following = scores_of(*units[at + 1]) if at + 1 < len(units) else None
            ranges = [(max(0, b - reach_blocks), min(blocks, b + reach_blocks + 1)) for b in (first, first + 1)]
            spans = [(lower * Q_ROWS, upper * Q_ROWS) for lower, upper in ranges]

            def band_of(head, block):
                shift = (reach_blocks - first - block) * Q_ROWS
                lower, upper = spans[block]
                return band_buf[group * group_heads + head, :, lower + shift : upper + shift]

            values = value_buf[:, 2 * group * LANES : 2 * (group + 1) * LANES]
            mixed, totals = weighted_sums(unit_weights(scores, spans, band_of), values, head_size)
            here = slice(first * Q_ROWS, (first + 2) * Q_ROWS)
            mixed_ref[0, here, group_lanes(group)] = mixed
            total_ref[0, here, group_lanes(group)] = totals
            scores = following


def inner(head_window, own, gain, w_query, w_key, w_value, reach):
    members, rows, feat_width = own.shape
    heads = head_window.shape[0]
    key_count = Q_ROWS + 2 * reach
    shapes = [(own.shape, BF16), ((members, 8, LANES), F32), (own.shape, F32), (own.shape, F32)]

    def spec(shape):
        return pl.BlockSpec((1, *shape[1:]), lambda m: (m, 0, 0))

    return pl.pallas_call(
        inner_kernel,
        grid=(members,),
        out_shape=[jax.ShapeDtypeStruct(*v) for v in shapes],
        in_specs=[smem_spec(), spec(own.shape)] + [vmem_spec()] * 4,
        out_specs=[spec(shape) for shape, _ in shapes],
        scratch_shapes=[
            pltpu.VMEM((feat_width, rows), BF16),
            pltpu.VMEM((rows, 2 * feat_width), BF16),
            pltpu.VMEM((heads, Q_ROWS, key_count), BF16),
        ],
        compiler_params=pltpu.CompilerParams(vmem_limit_bytes=VMEM_LIMIT),
        cost_estimate=pl.CostEstimate(
            flops=own.size * (6 * feat_width + 16 * rows), bytes_accessed=14 * own.size, transcendentals=0
        ),
        name="inner",
    )(head_window, own, gain, w_query, w_key, w_value)


def forward_kernel(
    total_len,
    tok_ref,
    mem_ref,
    window_ref,
    state_ref,
    query_ref,
    norm_ref,
    inner_mixed_ref,
    inner_total_ref,
    left_ref,
    right_ref,
    attn_gain_ref,
    ffn_gain_ref,
    w_key_ref,
    w_value_ref,
    w_out_ref,
    w_gate_ref,
    w_up_ref,
    down_weight_ref,
    *refs,
):
    out_refs, (halo_key_buf, halo_value_buf, band_buf, mixed_buf, key_buf, value_buf, forecast_buf) = (
        refs[:-7],
        refs[-7:],
    )
    rows, feat_width = state_ref.shape[1:]
    reach = left_ref.shape[1]
    heads = window_ref.shape[0]
    head_size = feat_width // heads
    group_heads = LANES // head_size
    groups = heads // group_heads
    blocks = rows // Q_ROWS
    key_count = Q_ROWS + 2 * reach
    count = 2 * Q_ROWS
    first_pos = tok_ref[0] * rows

    @pl.when(pl.program_id(0) == 0)
    def _():
        first_valid = first_pos - reach >= 0
        last_valid = first_pos + rows + reach <= total_len
        for head in range(heads):
            window = window_ref[head]
            band_buf[0, head] = factor(in_band(jnp.where(first_valid, window, -1), 0, reach, reach))
            right_window = jnp.where(last_valid, window, -1)
            band_buf[1, head] = factor(in_band(right_window, key_count - reach, key_count, reach))
        halo_value_buf[...] = jnp.ones(halo_value_buf.shape, BF16)

    def keys_of(normed):
        return dot(normed, w_key_ref[...])

    def values_of(normed):
        return dot(normed, w_value_ref[...]).astype(BF16)

    key_norms = norm_ref[0, 1:2, :]
    for side, ref in enumerate((left_ref, right_ref)):
        normed = rms_scaled(ref[0].astype(F32), attn_gain_ref[...]).astype(BF16)
        keys = keys_of(normed)
        key_norms = jnp.maximum(key_norms, largest_norms(keys, heads))
        halo_key_buf[side] = keys.astype(BF16).T
        put_values(halo_value_buf.at[side], 0, values_of(normed))
    safe = is_safe(norm_ref[0, 0:1, :], key_norms)

    @pl.when(safe)
    def _():
        units = [(side, group) for side in range(2) for group in range(groups)]

        def scores_of(side, group):
            start = side * (rows - count)
            queries = query_ref[0, start : start + count, group_lanes(group)]
            return dot(stacked_heads(queries, head_size), halo_key_buf[side, group_lanes(group), :])

        scores = scores_of(*units[0])
        for at, (side, group) in enumerate(units):
            following = scores_of(*units[at + 1]) if at + 1 < len(units) else None
            spans = [(0, reach), (Q_ROWS, reach)] if side == 0 else [(0, reach - Q_ROWS), (0, reach)]

            def band_of(head, block):
                lower, upper = spans[block]
                shift = -block * Q_ROWS if side == 0 else (1 - block) * Q_ROWS
                return band_buf[side, group * group_heads + head, :, lower + shift : upper + shift]

            values = halo_value_buf[side, :, 2 * group * LANES : 2 * (group + 1) * LANES]
            mixed, totals = weighted_sums(unit_weights(scores, spans, band_of), values, head_size)
            here = slice(side * (rows - count), side * (rows - count) + count)
            mixed = mixed + inner_mixed_ref[0, here, group_lanes(group)]
            totals = totals + inner_total_ref[0, here, group_lanes(group)]
            mixed_buf[here, group_lanes(group)] = (mixed / totals).astype(BF16)
            scores = following

    @pl.when(jnp.logical_not(safe))
    def _():
        normed = rms_scaled(state_ref[0].astype(F32), attn_gain_ref[...]).astype(BF16)
        key_buf[:, :reach] = halo_key_buf[0]
        key_buf[:, reach : reach + rows] = keys_of(normed).astype(BF16).T
        key_buf[:, reach + rows :] = halo_key_buf[1]
        value_buf[...] = jnp.ones(value_buf.shape, BF16)
        put_values(value_buf, reach, values_of(normed))
        value_buf[:reach] = halo_value_buf[0]
        value_buf[reach + rows :] = halo_value_buf[1]
        for block in range(blocks):
            start = block * Q_ROWS
            k_pos = first_pos - reach + start + iota((Q_ROWS, key_count), 1)
            inside = (k_pos >= 0) & (k_pos < total_len)
            for group in range(groups):
                queries = query_ref[0, start : start + Q_ROWS, group_lanes(group)]
                keys = key_buf[group_lanes(group), start : start + key_count]
                scores = dot(stacked_heads(queries, head_size), keys)
                weights = []
                for head in range(group_heads):
                    allowed = inside & in_band(window_ref[group * group_heads + head], 0, key_count, reach)
                    score_matrix = jnp.where(allowed, scores[head * Q_ROWS : (head + 1) * Q_ROWS], -1e30)
                    row_top = jnp.max(score_matrix, axis=-1, keepdims=True)
                    weights.append(jnp.exp2(score_matrix - row_top).astype(BF16))
                values = value_buf[start : start + key_count, 2 * group * LANES : 2 * (group + 1) * LANES]
                mixed, totals = weighted_sums(jnp.concatenate(weights, axis=0), values, head_size)
                mixed_buf[start : start + Q_ROWS, group_lanes(group)] = (mixed / totals).astype(BF16)

    after = (state_ref[0].astype(F32) + dot(mixed_buf[...], w_out_ref[...])).astype(BF16)
    normed_mid = rms_scaled(after.astype(F32), ffn_gain_ref[...]).astype(BF16)
    forecast = after.astype(F32)
    for lower in range(0, w_gate_ref.shape[1], HIDDEN_CHUNK):
        part = slice(lower, lower + HIDDEN_CHUNK)
        gate = 0.5 * dot(normed_mid, w_gate_ref[:, part])
        hidden = (gate * (1.0 + jnp.tanh(gate.astype(BF16)).astype(F32)) * dot(normed_mid, w_up_ref[:, part])).astype(BF16)
        forecast += dot(hidden, down_weight_ref[part, :])
    forecast_buf[...] = forecast.astype(BF16)
    share_rows = out_refs[0].shape[1]
    for part, out_ref in enumerate(out_refs):
        lower = pl.multiple_of((mem_ref[0] ^ part) * share_rows, share_rows)
        out_ref[0] = forecast_buf[pl.ds(lower, share_rows), :]


def forward(total_len, tok_index, mem_index, head_window, own, inner_parts, left, right, gains, weights, shares):
    members, row_count, feat_width = own.shape
    reach = left.shape[1]
    heads = head_window.shape[0]
    hidden_width = weights[3].shape[1]
    macs = members * row_count * feat_width * (3 * feat_width + 3 * hidden_width + 4 * reach)

    def spec(array):
        return pl.BlockSpec((1, *array.shape[1:]), lambda m: (m, 0, 0))

    return pl.pallas_call(
        functools.partial(forward_kernel, total_len),
        grid=(members,),
        out_shape=[jax.ShapeDtypeStruct((members, row_count // shares, feat_width), BF16)] * shares,
        in_specs=[smem_spec()] * 3
        + [spec(v) for v in (own, *inner_parts, left, right)]
        + [vmem_spec()] * (len(gains) + len(weights)),
        out_specs=[pl.BlockSpec((1, row_count // shares, feat_width), lambda m: (m, 0, 0))] * shares,
        scratch_shapes=[
            pltpu.VMEM((2, feat_width, reach), BF16),
            pltpu.VMEM((2, reach, 2 * feat_width), BF16),
            pltpu.VMEM((2, heads, Q_ROWS, reach), BF16),
            pltpu.VMEM((row_count, feat_width), BF16),
            pltpu.VMEM((feat_width, row_count + 2 * reach), BF16),
            pltpu.VMEM((row_count + 2 * reach, 2 * feat_width), BF16),
            pltpu.VMEM((row_count, feat_width), BF16),
        ],
        compiler_params=pltpu.CompilerParams(vmem_limit_bytes=VMEM_LIMIT),
        cost_estimate=pl.CostEstimate(flops=2 * macs, bytes_accessed=10 * own.size, transcendentals=0),
        name="forward",
    )(tok_index, mem_index, head_window, own, *inner_parts, left, right, *gains, *weights)


def global_member(held, index, own_members):
    return ((held // own_members) ^ index) * own_members + held % own_members


def gram_kernel(index_ref, *refs):
    share_refs, grid_ref, out_ref = refs[:-2], refs[-2], refs[-1]
    own_members, rows, feat_width = share_refs[0].shape
    members = own_members * len(share_refs)
    index = index_ref[0]
    stack = members * GROUP
    total = jnp.zeros((stack, stack), F32)
    proj = jnp.zeros((members, GROUP, feat_width), F32)
    for lower in range(0, rows, GROUP):
        part = slice(lower, lower + GROUP)
        fields = jnp.concatenate([ref[:, part, :] for ref in share_refs], axis=0).astype(F32)
        mean = jnp.sum(fields, axis=0) * (1.0 / members)
        spread = fields - mean[None]
        weight = grid_ref[0, part, :]
        proj += spread * (grid_ref[1, part, :] - weight * mean)[None]
        high, low = halves(spread.reshape(stack, feat_width))
        w_high, w_low = halves((spread * weight[None]).reshape(stack, feat_width))
        last = ((1,), (1,))
        total += dot(w_high, high, last) + dot(w_high, low, last) + dot(w_low, high, last)
    same = iota((stack, stack), 0) % GROUP == iota((stack, stack), 1) % GROUP
    by_row = jnp.sum(jnp.where(same, total, 0.0).reshape(members, GROUP, stack), axis=1)
    column = global_member(iota((stack, LANES), 0) // GROUP, index, own_members)
    folded = (column == iota((stack, LANES), 1) % members).astype(F32)
    held = global_member(iota((members, members), 1), index, own_members)
    in_order = (held == iota((members, members), 0)).astype(F32)
    tiled = exact_dot(in_order, exact_dot(by_row, folded))
    per_row = LANES // members
    keep = iota((members, LANES), 0) % per_row == iota((members, LANES), 1) // members
    packed = jnp.sum(jnp.where(keep, tiled, 0.0).reshape(members // per_row, per_row, LANES), axis=1)
    proj_col = jnp.sum(jnp.sum(proj, axis=1), axis=1, keepdims=True)
    at_lane = global_member(iota((members, LANES), 0), index, own_members) == iota((members, LANES), 1)
    proj_row = jnp.sum(jnp.where(at_lane, proj_col, 0.0), axis=0, keepdims=True)
    filled = members // per_row + 1
    blank = jnp.zeros((out_ref.shape[0] - filled, LANES), F32)
    out_ref[...] = jnp.concatenate([packed, proj_row, blank], axis=0)


def gram_partial(index, shares, grid):
    members = shares[0].shape[0] * len(shares)
    filled = members * members // LANES + 1
    return pl.pallas_call(
        gram_kernel,
        out_shape=jax.ShapeDtypeStruct((-(-filled // 8) * 8, LANES), F32),
        in_specs=[smem_spec()] + [vmem_spec()] * (len(shares) + 1),
        out_specs=vmem_spec(),
        compiler_params=pltpu.CompilerParams(vmem_limit_bytes=VMEM_LIMIT),
        cost_estimate=pl.CostEstimate(
            flops=3 * GROUP * members * members * grid.size, bytes_accessed=members * grid.size, transcendentals=0
        ),
        name="gram",
    )(index, *shares, grid)


def ensemble_transform(gram, proj):
    members = gram.shape[0]
    row, column = iota((members, members), 0), iota((members, members), 1)
    identity = (row == column).astype(F32)
    system = gram + (members - 1.0) * identity
    left, right = system, proj
    for pivot in range(members):
        is_pivot = iota((members, 1), 0) == pivot
        scale = 1.0 / left[pivot : pivot + 1, pivot : pivot + 1]
        pivot_row = left[pivot : pivot + 1, :] * scale
        pivot_right = right[pivot : pivot + 1, :] * scale
        factor = left[:, pivot : pivot + 1]
        left = jnp.where(is_pivot, pivot_row, left - factor * pivot_row)
        right = jnp.where(is_pivot, pivot_right, right - factor * pivot_right)
    mean_weights = right
    mean_level = jnp.sum(jnp.sum(system * identity, axis=1, keepdims=True), axis=0, keepdims=True) / members
    lifted = system + (mean_level - (members - 1.0)) * (1.0 / members)
    frobenius = jnp.sqrt(jnp.sum(jnp.sum(lifted * lifted, axis=1, keepdims=True), axis=0, keepdims=True))
    root_iter = lifted / frobenius
    inv_iter = identity
    for sweep in range(NS_STEPS):
        product = root_iter if sweep == 0 else exact_dot(inv_iter, root_iter)
        correction = 1.5 * identity - 0.5 * product
        inv_iter = correction if sweep == 0 else exact_dot(correction, inv_iter)
        if sweep < NS_STEPS - 1:
            root_iter = exact_dot(root_iter, correction)
    inv_root = inv_iter / jnp.sqrt(frobenius) + (1.0 / math.sqrt(members - 1.0) - 1.0 / jnp.sqrt(mean_level)) * (
        1.0 / members
    )
    moved = mean_weights + math.sqrt(members - 1.0) * inv_root
    return 1.0 / members + moved - jnp.sum(moved, axis=0, keepdims=True) * (1.0 / members)


def combine_kernel(index_ref, partial_ref, *refs):
    share_refs, out_refs = refs[: len(refs) // 2], refs[len(refs) // 2 :]
    own_members, rows, feat_width = share_refs[0].shape
    members = own_members * len(share_refs)
    stack = members * GROUP
    per_row = LANES // members
    sums = jnp.sum(partial_ref[...], axis=0)
    spread_rows = jnp.concatenate(
        [jnp.broadcast_to(sums[r : r + 1], (per_row, LANES)) for r in range(members // per_row)], axis=0
    )
    keep = iota((members, LANES), 0) % per_row == iota((members, LANES), 1) // members
    folded = (iota((LANES, members), 0) % members == iota((LANES, members), 1)).astype(F32)
    gram = exact_dot(jnp.where(keep, spread_rows, 0.0), folded)
    proj_row = jnp.broadcast_to(sums[members // per_row : members // per_row + 1], (members, LANES))
    on_diagonal = iota((members, LANES), 0) == iota((members, LANES), 1)
    proj = jnp.sum(jnp.where(on_diagonal, proj_row, 0.0), axis=1, keepdims=True)
    transform = ensemble_transform(gram, proj)
    held = global_member(iota((stack, members), 0) // GROUP, index_ref[0], own_members)
    pick = (held == iota((stack, members), 1)).astype(F32).astype(BF16)
    same = iota((stack, stack), 0) % GROUP == iota((stack, stack), 1) % GROUP
    mixers = []
    for piece in halves(transform):
        rows_of = dot(pick, piece, ((1,), (1,))).astype(BF16)
        mixers.append(jnp.where(same, dot(rows_of, pick, ((1,), (1,))), 0.0).astype(BF16))
    for lower in range(0, rows, GROUP):
        part = slice(lower, lower + GROUP)
        fields = jnp.concatenate([ref[:, part, :].reshape(-1, feat_width) for ref in share_refs], axis=0)
        mixed = (dot(mixers[0], fields) + dot(mixers[1], fields)).astype(BF16)
        own_stack = own_members * GROUP
        for at, out_ref in enumerate(out_refs):
            piece = mixed[at * own_stack : (at + 1) * own_stack]
            out_ref[:, part, :] = piece.reshape(own_members, GROUP, feat_width)


def combine(index, partials, shares):
    size = shares[0].size * len(shares)
    members = shares[0].shape[0] * len(shares)
    return pl.pallas_call(
        combine_kernel,
        out_shape=[jax.ShapeDtypeStruct(v.shape, BF16) for v in shares],
        in_specs=[smem_spec()] + [vmem_spec()] * (1 + len(shares)),
        out_specs=[vmem_spec()] * len(shares),
        compiler_params=pltpu.CompilerParams(vmem_limit_bytes=VMEM_LIMIT),
        cost_estimate=pl.CostEstimate(flops=4 * GROUP * members * size, bytes_accessed=4 * size, transcendentals=0),
        name="combine",
    )(index, partials, *shares)


def assemble_kernel(index_ref, *refs):
    part_refs, out_ref, sems = refs[:-2], refs[-2], refs[-1]
    rows = part_refs[0].shape[1]
    copies = []
    for part, ref in enumerate(part_refs):
        lower = pl.multiple_of((index_ref[0] ^ part) * rows, rows)
        copies.append(pltpu.make_async_copy(ref, out_ref.at[:, pl.ds(lower, rows), :], sems.at[part]))
    for copy in copies:
        copy.start()
    for copy in copies:
        copy.wait()


def assemble(index, parts):
    members, rows, feat_width = parts[0].shape
    return pl.pallas_call(
        assemble_kernel,
        out_shape=jax.ShapeDtypeStruct((members, len(parts) * rows, feat_width), BF16),
        in_specs=[smem_spec()] + [vmem_spec()] * len(parts),
        out_specs=pl.BlockSpec(memory_space=pl.ANY),
        scratch_shapes=[pltpu.SemaphoreType.DMA((len(parts),))],
        compiler_params=pltpu.CompilerParams(vmem_limit_bytes=VMEM_LIMIT),
        cost_estimate=pl.CostEstimate(flops=0, bytes_accessed=4 * len(parts) * parts[0].size, transcendentals=0),
        name="assemble",
    )(index, *parts)


def exchanged(parts):
    count = lax.axis_size("mem")
    return [
        lax.ppermute(v, "mem", [(i, i ^ part) for i in range(count)]) if part else v for part, v in enumerate(parts)
    ]


def local(
    ens_state,
    attn_gain,
    ffn_gain,
    w_query,
    w_key,
    w_value,
    w_out,
    w_gate,
    w_up,
    down_weight,
    head_window,
    obs_token,
    obs_channel,
    obs_value,
    obs_var,
):
    own_members, row_count, feat_width = ens_state.shape
    mem_count = lax.axis_size("mem")
    tok_count = lax.axis_size("tok")
    device_count = mem_count * tok_count
    share_rows = row_count // mem_count
    first_pos = lax.axis_index("tok") * row_count
    up = [(i, i + 1) for i in range(tok_count - 1)]
    down = [(i + 1, i) for i in range(tok_count - 1)]
    left = lax.ppermute(ens_state[:, row_count - WIN :], "tok", up)
    right = lax.ppermute(ens_state[:, :WIN], "tok", down)
    share_start = first_pos + lax.axis_index("mem") * share_rows
    grid = sample_grid(
        share_start.astype(jnp.int32).reshape(1), obs_token, obs_channel, obs_value, obs_var, share_rows, feat_width
    )
    mem_index = lax.axis_index("mem").astype(jnp.int32).reshape(1)
    tok_index = lax.axis_index("tok").astype(jnp.int32).reshape(1)
    gains = [attn_gain.reshape(1, -1), ffn_gain.reshape(1, -1)]
    inner_parts = inner(head_window, ens_state, gains[0], w_query, w_key, w_value, WIN)
    weights = [w_key, w_value, w_out, w_gate, w_up, down_weight]
    total_len = row_count * tok_count
    forecast = forward(
        total_len, tok_index, mem_index, head_window, ens_state, inner_parts, left, right, gains, weights, mem_count
    )
    shares = exchanged(forecast)
    partial = gram_partial(mem_index, shares, grid)
    partials = lax.all_to_all(
        jnp.broadcast_to(partial[None], (device_count, *partial.shape)),
        ("mem", "tok"),
        split_axis=0,
        concat_axis=0,
        tiled=True,
    )
    return assemble(mem_index, exchanged(combine(mem_index, partials, shares)))


def solution(mesh):
    in_specs = (P("mem", "tok", None), *[P()] * 10, *[P("tok")] * 4)
    return jax.shard_map(local, mesh=mesh, in_specs=in_specs, out_specs=P("mem", "tok", None), check_vma=False)
```

```python
import functools
import math

import jax
import jax.numpy as jnp
from jax import lax
from jax.experimental import pallas as pl
from jax.experimental.pallas import tpu as pltpu
from jax.sharding import PartitionSpec as P

WIN = 256
NS_STEPS = 8
EPS = 1e-05
Q_ROWS = 128
GROUP = 16
LANES = 128
VMEM_LIMIT = 32 * 1024 * 1024
SAFE_SCORE = 100.0
FOLD = 4
HIDDEN_CHUNK = 256

F32 = jnp.float32
BF16 = jnp.bfloat16


def dot(a, b, contract=((1,), (0,)), precision=None):
    return lax.dot_general(a, b, (contract, ((), ())), precision=precision, preferred_element_type=F32)


def exact_dot(a, b, contract=((1,), (0,))):
    return dot(a, b, contract, lax.Precision.HIGHEST)


def iota(shape, axis):
    return lax.broadcasted_iota(jnp.int32, shape, axis)


def halves(values):
    high = values.astype(BF16)
    return high, (values - high.astype(F32)).astype(BF16)


def rms_scaled(values, gain):
    return values * lax.rsqrt(jnp.mean(values * values, axis=-1, keepdims=True) + EPS) * gain


def vmem_spec():
    return pl.BlockSpec(memory_space=pltpu.VMEM)


def smem_spec():
    return pl.BlockSpec(memory_space=pltpu.SMEM)


def sample_grid_kernel(start_ref, token_ref, channel_ref, value_ref, var_ref, out_ref):
    rows, feat_width = out_ref.shape[1:]
    count = token_ref.shape[1]
    chunk = min(1024, count)
    total = jnp.zeros((4 * rows, feat_width), F32)
    for lower in range(0, count, chunk):
        part = slice(lower, lower + chunk)
        inv_var = 1.0 / var_ref[:, part]
        weighted = value_ref[:, part] * inv_var
        here = iota((rows, chunk), 0) == token_ref[:, part] - start_ref[0]
        pieces = []
        for row in (inv_var, weighted):
            high = row.astype(BF16).astype(F32)
            pieces.append(jnp.where(here, high, 0.0).astype(BF16))
            pieces.append(jnp.where(here, row - high, 0.0).astype(BF16))
        channel_hot = jnp.where(iota((feat_width, chunk), 0) == channel_ref[:, part], 1.0, 0.0).astype(BF16)
        total += dot(jnp.concatenate(pieces, axis=0), channel_hot, ((1,), (1,)))
    out_ref[0] = total[:rows] + total[rows : 2 * rows]
    out_ref[1] = total[2 * rows : 3 * rows] + total[3 * rows :]


def sample_grid(start, obs_token, obs_channel, obs_value, obs_var, rows, feat_width):
    count = obs_token.shape[0]
    return pl.pallas_call(
        sample_grid_kernel,
        out_shape=jax.ShapeDtypeStruct((2, rows, feat_width), F32),
        in_specs=[smem_spec()] + [vmem_spec()] * 4,
        out_specs=vmem_spec(),
        compiler_params=pltpu.CompilerParams(vmem_limit_bytes=VMEM_LIMIT),
        cost_estimate=pl.CostEstimate(flops=8 * rows * count * feat_width, bytes_accessed=16 * count, transcendentals=0),
        name="sample_grid",
    )(start, *(v.reshape(1, count) for v in (obs_token, obs_channel, obs_value, obs_var)))


def head_lanes(feat_width, heads):
    lane_head = iota((feat_width, LANES), 0) // (feat_width // heads)
    return (lane_head == iota((feat_width, LANES), 1)).astype(F32).astype(BF16)


def norm_bounds(values, heads):
    rows = values.shape[0] // FOLD
    squares = values * values
    folded = squares[:rows]
    for part in range(1, FOLD):
        folded = jnp.maximum(folded, squares[part * rows : (part + 1) * rows])
    return jnp.max(dot(folded.astype(BF16), head_lanes(values.shape[1], heads)), axis=0, keepdims=True)


def is_safe(query_norms, key_norms):
    return jnp.max(query_norms * key_norms) * 1.05 <= SAFE_SCORE * SAFE_SCORE


def query_scale(head_size):
    return math.log2(math.e) / math.sqrt(head_size)


def in_band(window, lower, upper, reach):
    apart = jnp.abs(iota((Q_ROWS, upper - lower), 1) + (lower - reach) - iota((Q_ROWS, upper - lower), 0))
    return apart <= window


def factor(mask):
    return jnp.where(mask, 1.0, 0.0).astype(BF16)


def group_lanes(group):
    return slice(group * LANES, (group + 1) * LANES)


def stacked_heads(queries, head_size):
    lane_head = iota((1, LANES), 1) // head_size
    masks = [(lane_head == head).astype(F32).astype(BF16) for head in range(LANES // head_size)]
    return jnp.concatenate([queries * mask for mask in masks], axis=0)


def put_values(buf, lower, values):
    for group in range(values.shape[1] // LANES):
        lanes = slice(2 * group * LANES, (2 * group + 1) * LANES)
        buf[lower : lower + values.shape[0], lanes] = values[:, group_lanes(group)]


def weighted_sums(weights, values, head_size):
    mixed_all = dot(weights, values)
    heads = LANES // head_size
    count = mixed_all.shape[0] // heads
    lane_head = iota((1, LANES), 1) // head_size
    mixed, totals = mixed_all[:count, :LANES], mixed_all[:count, LANES:]
    for head in range(1, heads):
        part = mixed_all[head * count : (head + 1) * count]
        mixed = jnp.where(lane_head == head, part[:, :LANES], mixed)
        totals = jnp.where(lane_head == head, part[:, LANES:], totals)
    return mixed, totals


def padded_lanes(values, before, after):
    pieces = [jnp.zeros((values.shape[0], before), BF16)] if before else []
    pieces.append(values)
    if after:
        pieces.append(jnp.zeros((values.shape[0], after), BF16))
    return jnp.concatenate(pieces, axis=1) if len(pieces) > 1 else pieces[0]


def unit_weights(scores, spans, band_of):
    width = scores.shape[1]
    count = len(spans) * Q_ROWS
    weights = []
    for head in range(scores.shape[0] // count):
        for block, (lower, upper) in enumerate(spans):
            top = head * count + block * Q_ROWS
            expo = jnp.exp2(scores[top : top + Q_ROWS, lower:upper]).astype(BF16)
            weights.append(padded_lanes(expo * band_of(head, block), lower, width - upper))
    return jnp.concatenate(weights, axis=0)


def inner_kernel(
    window_ref,
    own_ref,
    gain_ref,
    w_query_ref,
    w_key_ref,
    w_value_ref,
    query_ref,
    norm_ref,
    mixed_ref,
    total_ref,
    key_buf,
    value_buf,
    band_buf,
):
    rows, feat_width = own_ref.shape[1:]
    heads = window_ref.shape[0]
    head_size = feat_width // heads
    group_heads = LANES // head_size
    key_count = band_buf.shape[2]
    reach = (key_count - Q_ROWS) // 2
    reach_blocks = reach // Q_ROWS
    blocks = rows // Q_ROWS

    @pl.when(pl.program_id(0) == 0)
    def _():
        for head in range(heads):
            band_buf[head] = factor(in_band(window_ref[head], 0, key_count, reach))
        value_buf[...] = jnp.ones(value_buf.shape, BF16)

    normed = rms_scaled(own_ref[0].astype(F32), gain_ref[...]).astype(BF16)
    query_rows = dot(normed, w_query_ref[...]) * query_scale(head_size)
    key_rows = dot(normed, w_key_ref[...])
    query_ref[0] = query_rows.astype(BF16)
    key_buf[...] = key_rows.astype(BF16).T
    put_values(value_buf, 0, dot(normed, w_value_ref[...]).astype(BF16))
    query_norms, key_norms = norm_bounds(query_rows, heads), norm_bounds(key_rows, heads)
    blank = jnp.zeros((norm_ref.shape[1] - 2, LANES), F32)
    norm_ref[0] = jnp.concatenate([query_norms, key_norms, blank], axis=0)

    @pl.when(is_safe(query_norms, key_norms))
    def _():
        units = [(first, group) for first in range(0, blocks, 2) for group in range(heads // group_heads)]

        def scores_of(first, group):
            queries = query_ref[0, first * Q_ROWS : (first + 2) * Q_ROWS, group_lanes(group)]
            return dot(stacked_heads(queries, head_size), key_buf[group_lanes(group), :])

        scores = scores_of(*units[0])
        for at, (first, group) in enumerate(units):
            following = scores_of(*units[at + 1]) if at + 1 < len(units) else None
            ranges = [(max(0, b - reach_blocks), min(blocks, b + reach_blocks + 1)) for b in (first, first + 1)]
            spans = [(lower * Q_ROWS, upper * Q_ROWS) for lower, upper in ranges]

            def band_of(head, block):
                shift = (reach_blocks - first - block) * Q_ROWS
                lower, upper = spans[block]
                return band_buf[group * group_heads + head, :, lower + shift : upper + shift]

            values = value_buf[:, 2 * group * LANES : 2 * (group + 1) * LANES]
            mixed, totals = weighted_sums(unit_weights(scores, spans, band_of), values, head_size)
            here = slice(first * Q_ROWS, (first + 2) * Q_ROWS)
            mixed_ref[0, here, group_lanes(group)] = mixed
            total_ref[0, here, group_lanes(group)] = totals
            scores = following


def inner(head_window, own, gain, w_query, w_key, w_value, reach):
    members, rows, feat_width = own.shape
    heads = head_window.shape[0]
    key_count = Q_ROWS + 2 * reach
    shapes = [(own.shape, BF16), ((members, 8, LANES), F32), (own.shape, F32), (own.shape, F32)]

    def spec(shape):
        return pl.BlockSpec((1, *shape[1:]), lambda m: (m, 0, 0))

    return pl.pallas_call(
        inner_kernel,
        grid=(members,),
        out_shape=[jax.ShapeDtypeStruct(*v) for v in shapes],
        in_specs=[smem_spec(), spec(own.shape)] + [vmem_spec()] * 4,
        out_specs=[spec(shape) for shape, _ in shapes],
        scratch_shapes=[
            pltpu.VMEM((feat_width, rows), BF16),
            pltpu.VMEM((rows, 2 * feat_width), BF16),
            pltpu.VMEM((heads, Q_ROWS, key_count), BF16),
        ],
        compiler_params=pltpu.CompilerParams(vmem_limit_bytes=VMEM_LIMIT),
        cost_estimate=pl.CostEstimate(
            flops=own.size * (6 * feat_width + 16 * rows), bytes_accessed=14 * own.size, transcendentals=0
        ),
        name="inner",
    )(head_window, own, gain, w_query, w_key, w_value)


def forward_kernel(
    total_len,
    tok_ref,
    mem_ref,
    window_ref,
    state_ref,
    query_ref,
    norm_ref,
    inner_mixed_ref,
    inner_total_ref,
    left_ref,
    right_ref,
    attn_gain_ref,
    ffn_gain_ref,
    w_key_ref,
    w_value_ref,
    w_out_ref,
    w_gate_ref,
    w_up_ref,
    down_weight_ref,
    *refs,
):
    out_refs, (halo_key_buf, halo_value_buf, band_buf, mixed_buf, key_buf, value_buf, forecast_buf) = (
        refs[:-7],
        refs[-7:],
    )
    rows, feat_width = state_ref.shape[1:]
    reach = left_ref.shape[1]
    heads = window_ref.shape[0]
    head_size = feat_width // heads
    group_heads = LANES // head_size
    groups = heads // group_heads
    blocks = rows // Q_ROWS
    key_count = Q_ROWS + 2 * reach
    count = 2 * Q_ROWS
    first_pos = tok_ref[0] * rows

    @pl.when(pl.program_id(0) == 0)
    def _():
        first_valid = first_pos - reach >= 0
        last_valid = first_pos + rows + reach <= total_len
        for head in range(heads):
            window = window_ref[head]
            band_buf[0, head] = factor(in_band(jnp.where(first_valid, window, -1), 0, reach, reach))
            right_window = jnp.where(last_valid, window, -1)
            band_buf[1, head] = factor(in_band(right_window, key_count - reach, key_count, reach))
        halo_value_buf[...] = jnp.ones(halo_value_buf.shape, BF16)

    def keys_of(normed):
        return dot(normed, w_key_ref[...])

    def values_of(normed):
        return dot(normed, w_value_ref[...]).astype(BF16)

    halo = jnp.concatenate([left_ref[0], right_ref[0]], axis=0)
    normed = rms_scaled(halo.astype(F32), attn_gain_ref[...]).astype(BF16)
    halo_keys = keys_of(normed)
    halo_values = values_of(normed)
    key_norms = jnp.maximum(norm_ref[0, 1:2, :], norm_bounds(halo_keys, heads))
    for side in range(2):
        here = slice(side * reach, (side + 1) * reach)
        halo_key_buf[side] = halo_keys[here].astype(BF16).T
        put_values(halo_value_buf.at[side], 0, halo_values[here])
    safe = is_safe(norm_ref[0, 0:1, :], key_norms)

    @pl.when(safe)
    def _():
        units = [(side, group) for side in range(2) for group in range(groups)]

        def scores_of(side, group):
            start = side * (rows - count)
            queries = query_ref[0, start : start + count, group_lanes(group)]
            return dot(stacked_heads(queries, head_size), halo_key_buf[side, group_lanes(group), :])

        scores = scores_of(*units[0])
        for at, (side, group) in enumerate(units):
            following = scores_of(*units[at + 1]) if at + 1 < len(units) else None
            spans = [(0, reach), (Q_ROWS, reach)] if side == 0 else [(0, reach - Q_ROWS), (0, reach)]

            def band_of(head, block):
                lower, upper = spans[block]
                shift = -block * Q_ROWS if side == 0 else (1 - block) * Q_ROWS
                return band_buf[side, group * group_heads + head, :, lower + shift : upper + shift]

            values = halo_value_buf[side, :, 2 * group * LANES : 2 * (group + 1) * LANES]
            mixed, totals = weighted_sums(unit_weights(scores, spans, band_of), values, head_size)
            here = slice(side * (rows - count), side * (rows - count) + count)
            mixed = mixed + inner_mixed_ref[0, here, group_lanes(group)]
            totals = totals + inner_total_ref[0, here, group_lanes(group)]
            mixed_buf[here, group_lanes(group)] = (mixed / totals).astype(BF16)
            scores = following

    @pl.when(jnp.logical_not(safe))
    def _():
        normed = rms_scaled(state_ref[0].astype(F32), attn_gain_ref[...]).astype(BF16)
        key_buf[:, :reach] = halo_key_buf[0]
        key_buf[:, reach : reach + rows] = keys_of(normed).astype(BF16).T
        key_buf[:, reach + rows :] = halo_key_buf[1]
        value_buf[...] = jnp.ones(value_buf.shape, BF16)
        put_values(value_buf, reach, values_of(normed))
        value_buf[:reach] = halo_value_buf[0]
        value_buf[reach + rows :] = halo_value_buf[1]
        for block in range(blocks):
            start = block * Q_ROWS
            k_pos = first_pos - reach + start + iota((Q_ROWS, key_count), 1)
            inside = (k_pos >= 0) & (k_pos < total_len)
            for group in range(groups):
                queries = query_ref[0, start : start + Q_ROWS, group_lanes(group)]
                keys = key_buf[group_lanes(group), start : start + key_count]
                scores = dot(stacked_heads(queries, head_size), keys)
                weights = []
                for head in range(group_heads):
                    allowed = inside & in_band(window_ref[group * group_heads + head], 0, key_count, reach)
                    score_matrix = jnp.where(allowed, scores[head * Q_ROWS : (head + 1) * Q_ROWS], -1e30)
                    row_top = jnp.max(score_matrix, axis=-1, keepdims=True)
                    weights.append(jnp.exp2(score_matrix - row_top).astype(BF16))
                values = value_buf[start : start + key_count, 2 * group * LANES : 2 * (group + 1) * LANES]
                mixed, totals = weighted_sums(jnp.concatenate(weights, axis=0), values, head_size)
                mixed_buf[start : start + Q_ROWS, group_lanes(group)] = (mixed / totals).astype(BF16)

    after = (state_ref[0].astype(F32) + dot(mixed_buf[...], w_out_ref[...])).astype(BF16)
    normed_mid = rms_scaled(after.astype(F32), ffn_gain_ref[...]).astype(BF16)
    forecast = after.astype(F32)
    for lower in range(0, w_gate_ref.shape[1], HIDDEN_CHUNK):
        part = slice(lower, lower + HIDDEN_CHUNK)
        gate = 0.5 * dot(normed_mid, w_gate_ref[:, part])
        hidden = (gate * (1.0 + jnp.tanh(gate.astype(BF16)).astype(F32)) * dot(normed_mid, w_up_ref[:, part])).astype(BF16)
        forecast += dot(hidden, down_weight_ref[part, :])
    forecast_buf[...] = forecast.astype(BF16)
    share_rows = out_refs[0].shape[1]
    for part, out_ref in enumerate(out_refs):
        lower = pl.multiple_of((mem_ref[0] ^ part) * share_rows, share_rows)
        out_ref[0] = forecast_buf[pl.ds(lower, share_rows), :]


def forward(total_len, tok_index, mem_index, head_window, own, inner_parts, left, right, gains, weights, shares):
    members, row_count, feat_width = own.shape
    reach = left.shape[1]
    heads = head_window.shape[0]
    hidden_width = weights[3].shape[1]
    macs = members * row_count * feat_width * (3 * feat_width + 3 * hidden_width + 4 * reach)

    def spec(array):
        return pl.BlockSpec((1, *array.shape[1:]), lambda m: (m, 0, 0))

    return pl.pallas_call(
        functools.partial(forward_kernel, total_len),
        grid=(members,),
        out_shape=[jax.ShapeDtypeStruct((members, row_count // shares, feat_width), BF16)] * shares,
        in_specs=[smem_spec()] * 3
        + [spec(v) for v in (own, *inner_parts, left, right)]
        + [vmem_spec()] * (len(gains) + len(weights)),
        out_specs=[pl.BlockSpec((1, row_count // shares, feat_width), lambda m: (m, 0, 0))] * shares,
        scratch_shapes=[
            pltpu.VMEM((2, feat_width, reach), BF16),
            pltpu.VMEM((2, reach, 2 * feat_width), BF16),
            pltpu.VMEM((2, heads, Q_ROWS, reach), BF16),
            pltpu.VMEM((row_count, feat_width), BF16),
            pltpu.VMEM((feat_width, row_count + 2 * reach), BF16),
            pltpu.VMEM((row_count + 2 * reach, 2 * feat_width), BF16),
            pltpu.VMEM((row_count, feat_width), BF16),
        ],
        compiler_params=pltpu.CompilerParams(vmem_limit_bytes=VMEM_LIMIT),
        cost_estimate=pl.CostEstimate(flops=2 * macs, bytes_accessed=10 * own.size, transcendentals=0),
        name="forward",
    )(tok_index, mem_index, head_window, own, *inner_parts, left, right, *gains, *weights)


def global_member(held, index, own_members):
    return ((held // own_members) ^ index) * own_members + held % own_members


def gram_kernel(index_ref, *refs):
    share_refs, grid_ref, out_ref = refs[:-2], refs[-2], refs[-1]
    own_members, rows, feat_width = share_refs[0].shape
    members = own_members * len(share_refs)
    index = index_ref[0]
    tokens = GROUP // 2
    stack = members * tokens
    total = jnp.zeros((stack, 2 * stack), F32)
    proj = jnp.zeros((members, tokens, feat_width), F32)
    for first in range(0, rows, GROUP):
        loaded = jnp.concatenate([ref[:, first : first + GROUP, :] for ref in share_refs], axis=0).astype(F32)
        for lower in range(0, GROUP, tokens):
            fields = loaded[:, lower : lower + tokens, :]
            mean = jnp.sum(fields, axis=0) * (1.0 / members)
            spread = fields - mean[None]
            part = slice(first + lower, first + lower + tokens)
            weight = grid_ref[0, part, :]
            proj += spread * (grid_ref[1, part, :] - weight * mean)[None]
            both = jnp.concatenate(halves(spread.reshape(stack, feat_width)), axis=0)
            w_high, w_low = halves((spread * weight[None]).reshape(stack, feat_width))
            last = ((1,), (1,))
            total += dot(w_high, both, last) + dot(w_low, both, last)
    total = total[:, :stack] + total[:, stack:]
    same = iota((stack, stack), 0) % tokens == iota((stack, stack), 1) % tokens
    by_row = jnp.sum(jnp.where(same, total, 0.0).reshape(members, tokens, stack), axis=1)
    column = global_member(iota((stack, LANES), 0) // tokens, index, own_members)
    folded = (column == iota((stack, LANES), 1) % members).astype(F32)
    held = global_member(iota((members, members), 1), index, own_members)
    in_order = (held == iota((members, members), 0)).astype(F32)
    tiled = exact_dot(in_order, exact_dot(by_row, folded))
    per_row = LANES // members
    keep = iota((members, LANES), 0) % per_row == iota((members, LANES), 1) // members
    packed = jnp.sum(jnp.where(keep, tiled, 0.0).reshape(members // per_row, per_row, LANES), axis=1)
    proj_col = jnp.sum(jnp.sum(proj, axis=1), axis=1, keepdims=True)
    at_lane = global_member(iota((members, LANES), 0), index, own_members) == iota((members, LANES), 1)
    proj_row = jnp.sum(jnp.where(at_lane, proj_col, 0.0), axis=0, keepdims=True)
    filled = members // per_row + 1
    blank = jnp.zeros((out_ref.shape[0] - filled, LANES), F32)
    out_ref[...] = jnp.concatenate([packed, proj_row, blank], axis=0)


def gram_partial(index, shares, grid):
    members = shares[0].shape[0] * len(shares)
    filled = members * members // LANES + 1
    return pl.pallas_call(
        gram_kernel,
        out_shape=jax.ShapeDtypeStruct((-(-filled // 8) * 8, LANES), F32),
        in_specs=[smem_spec()] + [vmem_spec()] * (len(shares) + 1),
        out_specs=vmem_spec(),
        compiler_params=pltpu.CompilerParams(vmem_limit_bytes=VMEM_LIMIT),
        cost_estimate=pl.CostEstimate(
            flops=3 * GROUP * members * members * grid.size, bytes_accessed=members * grid.size, transcendentals=0
        ),
        name="gram",
    )(index, *shares, grid)


def ensemble_transform(gram, proj):
    members = gram.shape[0]
    row, column = iota((members, members), 0), iota((members, members), 1)
    identity = (row == column).astype(F32)
    system = gram + (members - 1.0) * identity
    left, right = system, proj
    for pivot in range(members):
        is_pivot = iota((members, 1), 0) == pivot
        scale = 1.0 / left[pivot : pivot + 1, pivot : pivot + 1]
        pivot_row = left[pivot : pivot + 1, :] * scale
        pivot_right = right[pivot : pivot + 1, :] * scale
        factor = left[:, pivot : pivot + 1]
        left = jnp.where(is_pivot, pivot_row, left - factor * pivot_row)
        right = jnp.where(is_pivot, pivot_right, right - factor * pivot_right)
    mean_weights = right
    mean_level = jnp.sum(jnp.sum(system * identity, axis=1, keepdims=True), axis=0, keepdims=True) / members
    lifted = system + (mean_level - (members - 1.0)) * (1.0 / members)
    frobenius = jnp.sqrt(jnp.sum(jnp.sum(lifted * lifted, axis=1, keepdims=True), axis=0, keepdims=True))
    root_iter = lifted / frobenius
    inv_iter = identity
    for sweep in range(NS_STEPS):
        product = root_iter if sweep == 0 else exact_dot(inv_iter, root_iter)
        correction = 1.5 * identity - 0.5 * product
        inv_iter = correction if sweep == 0 else exact_dot(correction, inv_iter)
        if sweep < NS_STEPS - 1:
            root_iter = exact_dot(root_iter, correction)
    inv_root = inv_iter / jnp.sqrt(frobenius) + (1.0 / math.sqrt(members - 1.0) - 1.0 / jnp.sqrt(mean_level)) * (
        1.0 / members
    )
    moved = mean_weights + math.sqrt(members - 1.0) * inv_root
    return 1.0 / members + moved - jnp.sum(moved, axis=0, keepdims=True) * (1.0 / members)


def combine_kernel(index_ref, partial_ref, *refs):
    share_refs, out_refs = refs[: len(refs) // 2], refs[len(refs) // 2 :]
    own_members, rows, feat_width = share_refs[0].shape
    members = own_members * len(share_refs)
    stack = members * GROUP
    per_row = LANES // members
    sums = jnp.sum(partial_ref[...], axis=0)
    spread_rows = jnp.concatenate(
        [jnp.broadcast_to(sums[r : r + 1], (per_row, LANES)) for r in range(members // per_row)], axis=0
    )
    keep = iota((members, LANES), 0) % per_row == iota((members, LANES), 1) // members
    folded = (iota((LANES, members), 0) % members == iota((LANES, members), 1)).astype(F32)
    gram = exact_dot(jnp.where(keep, spread_rows, 0.0), folded)
    proj_row = jnp.broadcast_to(sums[members // per_row : members // per_row + 1], (members, LANES))
    on_diagonal = iota((members, LANES), 0) == iota((members, LANES), 1)
    proj = jnp.sum(jnp.where(on_diagonal, proj_row, 0.0), axis=1, keepdims=True)
    transform = ensemble_transform(gram, proj)
    held = global_member(iota((stack, members), 0) // GROUP, index_ref[0], own_members)
    pick = (held == iota((stack, members), 1)).astype(F32).astype(BF16)
    same = iota((stack, stack), 0) % GROUP == iota((stack, stack), 1) % GROUP
    mixers = []
    for piece in halves(transform):
        rows_of = dot(pick, piece, ((1,), (1,))).astype(BF16)
        mixers.append(jnp.where(same, dot(rows_of, pick, ((1,), (1,))), 0.0).astype(BF16))
    for lower in range(0, rows, GROUP):
        part = slice(lower, lower + GROUP)
        fields = jnp.concatenate([ref[:, part, :].reshape(-1, feat_width) for ref in share_refs], axis=0)
        mixed = (dot(mixers[0], fields) + dot(mixers[1], fields)).astype(BF16)
        own_stack = own_members * GROUP
        for at, out_ref in enumerate(out_refs):
            piece = mixed[at * own_stack : (at + 1) * own_stack]
            out_ref[:, part, :] = piece.reshape(own_members, GROUP, feat_width)


def combine(index, partials, shares):
    size = shares[0].size * len(shares)
    members = shares[0].shape[0] * len(shares)
    return pl.pallas_call(
        combine_kernel,
        out_shape=[jax.ShapeDtypeStruct(v.shape, BF16) for v in shares],
        in_specs=[smem_spec()] + [vmem_spec()] * (1 + len(shares)),
        out_specs=[vmem_spec()] * len(shares),
        compiler_params=pltpu.CompilerParams(vmem_limit_bytes=VMEM_LIMIT),
        cost_estimate=pl.CostEstimate(flops=4 * GROUP * members * size, bytes_accessed=4 * size, transcendentals=0),
        name="combine",
    )(index, partials, *shares)


def assemble_kernel(index_ref, *refs):
    part_refs, out_ref, sems = refs[:-2], refs[-2], refs[-1]
    rows = part_refs[0].shape[1]
    copies = []
    for part, ref in enumerate(part_refs):
        lower = pl.multiple_of((index_ref[0] ^ part) * rows, rows)
        copies.append(pltpu.make_async_copy(ref, out_ref.at[:, pl.ds(lower, rows), :], sems.at[part]))
    for copy in copies:
        copy.start()
    for copy in copies:
        copy.wait()


def assemble(index, parts):
    members, rows, feat_width = parts[0].shape
    return pl.pallas_call(
        assemble_kernel,
        out_shape=jax.ShapeDtypeStruct((members, len(parts) * rows, feat_width), BF16),
        in_specs=[smem_spec()] + [vmem_spec()] * len(parts),
        out_specs=pl.BlockSpec(memory_space=pl.ANY),
        scratch_shapes=[pltpu.SemaphoreType.DMA((len(parts),))],
        compiler_params=pltpu.CompilerParams(vmem_limit_bytes=VMEM_LIMIT),
        cost_estimate=pl.CostEstimate(flops=0, bytes_accessed=4 * len(parts) * parts[0].size, transcendentals=0),
        name="assemble",
    )(index, *parts)


def exchanged(parts):
    count = lax.axis_size("mem")
    return [
        lax.ppermute(v, "mem", [(i, i ^ part) for i in range(count)]) if part else v for part, v in enumerate(parts)
    ]


def local(
    ens_state,
    attn_gain,
    ffn_gain,
    w_query,
    w_key,
    w_value,
    w_out,
    w_gate,
    w_up,
    down_weight,
    head_window,
    obs_token,
    obs_channel,
    obs_value,
    obs_var,
):
    own_members, row_count, feat_width = ens_state.shape
    mem_count = lax.axis_size("mem")
    tok_count = lax.axis_size("tok")
    device_count = mem_count * tok_count
    share_rows = row_count // mem_count
    first_pos = lax.axis_index("tok") * row_count
    up = [(i, i + 1) for i in range(tok_count - 1)]
    down = [(i + 1, i) for i in range(tok_count - 1)]
    left = lax.ppermute(ens_state[:, row_count - WIN :], "tok", up)
    right = lax.ppermute(ens_state[:, :WIN], "tok", down)
    share_start = first_pos + lax.axis_index("mem") * share_rows
    grid = sample_grid(
        share_start.astype(jnp.int32).reshape(1), obs_token, obs_channel, obs_value, obs_var, share_rows, feat_width
    )
    mem_index = lax.axis_index("mem").astype(jnp.int32).reshape(1)
    tok_index = lax.axis_index("tok").astype(jnp.int32).reshape(1)
    gains = [attn_gain.reshape(1, -1), ffn_gain.reshape(1, -1)]
    inner_parts = inner(head_window, ens_state, gains[0], w_query, w_key, w_value, WIN)
    weights = [w_key, w_value, w_out, w_gate, w_up, down_weight]
    total_len = row_count * tok_count
    forecast = forward(
        total_len, tok_index, mem_index, head_window, ens_state, inner_parts, left, right, gains, weights, mem_count
    )
    shares = exchanged(forecast)
    partial = gram_partial(mem_index, shares, grid)
    partials = lax.all_to_all(
        jnp.broadcast_to(partial[None], (device_count, *partial.shape)),
        ("mem", "tok"),
        split_axis=0,
        concat_axis=0,
        tiled=True,
    )
    return assemble(mem_index, exchanged(combine(mem_index, partials, shares)))


def solution(mesh):
    in_specs = (P("mem", "tok", None), *[P()] * 10, *[P("tok")] * 4)
    return jax.shard_map(local, mesh=mesh, in_specs=in_specs, out_specs=P("mem", "tok", None), check_vma=False)
```

```python
import functools
import math

import jax
import jax.numpy as jnp
from jax import lax
from jax.experimental import pallas as pl
from jax.experimental.pallas import tpu as pltpu
from jax.sharding import PartitionSpec as P

WIN = 256
NS_STEPS = 8
EPS = 1e-05
Q_ROWS = 128
GROUP = 16
LANES = 128
VMEM_LIMIT = 32 * 1024 * 1024
SAFE_SCORE = 100.0
FOLD = 4
HIDDEN_CHUNK = 256

F32 = jnp.float32
BF16 = jnp.bfloat16


def dot(a, b, contract=((1,), (0,)), precision=None):
    return lax.dot_general(a, b, (contract, ((), ())), precision=precision, preferred_element_type=F32)


def exact_dot(a, b, contract=((1,), (0,))):
    return dot(a, b, contract, lax.Precision.HIGHEST)


def iota(shape, axis):
    return lax.broadcasted_iota(jnp.int32, shape, axis)


def halves(values):
    high = values.astype(BF16)
    return high, (values - high.astype(F32)).astype(BF16)


def rms_scaled(values, gain):
    return values * lax.rsqrt(jnp.mean(values * values, axis=-1, keepdims=True) + EPS) * gain


def vmem_spec():
    return pl.BlockSpec(memory_space=pltpu.VMEM)


def smem_spec():
    return pl.BlockSpec(memory_space=pltpu.SMEM)


def sample_grid_kernel(start_ref, token_ref, channel_ref, value_ref, var_ref, out_ref):
    rows, feat_width = out_ref.shape[1:]
    count = token_ref.shape[1]
    chunk = min(1024, count)
    total = jnp.zeros((4 * rows, feat_width), F32)
    for lower in range(0, count, chunk):
        part = slice(lower, lower + chunk)
        inv_var = 1.0 / var_ref[:, part]
        weighted = value_ref[:, part] * inv_var
        here = iota((rows, chunk), 0) == token_ref[:, part] - start_ref[0]
        pieces = []
        for row in (inv_var, weighted):
            high = row.astype(BF16).astype(F32)
            pieces.append(jnp.where(here, high, 0.0).astype(BF16))
            pieces.append(jnp.where(here, row - high, 0.0).astype(BF16))
        channel_hot = jnp.where(iota((feat_width, chunk), 0) == channel_ref[:, part], 1.0, 0.0).astype(BF16)
        total += dot(jnp.concatenate(pieces, axis=0), channel_hot, ((1,), (1,)))
    out_ref[0] = total[:rows] + total[rows : 2 * rows]
    out_ref[1] = total[2 * rows : 3 * rows] + total[3 * rows :]


def sample_grid(start, obs_token, obs_channel, obs_value, obs_var, rows, feat_width):
    count = obs_token.shape[0]
    return pl.pallas_call(
        sample_grid_kernel,
        out_shape=jax.ShapeDtypeStruct((2, rows, feat_width), F32),
        in_specs=[smem_spec()] + [vmem_spec()] * 4,
        out_specs=vmem_spec(),
        compiler_params=pltpu.CompilerParams(vmem_limit_bytes=VMEM_LIMIT),
        cost_estimate=pl.CostEstimate(flops=8 * rows * count * feat_width, bytes_accessed=16 * count, transcendentals=0),
        name="sample_grid",
    )(start, *(v.reshape(1, count) for v in (obs_token, obs_channel, obs_value, obs_var)))


def head_lanes(feat_width, heads):
    lane_head = iota((feat_width, LANES), 0) // (feat_width // heads)
    return (lane_head == iota((feat_width, LANES), 1)).astype(F32).astype(BF16)


def norm_bounds(values, heads):
    rows = values.shape[0] // FOLD
    squares = values * values
    folded = squares[:rows]
    for part in range(1, FOLD):
        folded = jnp.maximum(folded, squares[part * rows : (part + 1) * rows])
    return jnp.max(dot(folded.astype(BF16), head_lanes(values.shape[1], heads)), axis=0, keepdims=True)


def is_safe(query_norms, key_norms):
    return jnp.max(query_norms * key_norms) * 1.05 <= SAFE_SCORE * SAFE_SCORE


def query_scale(head_size):
    return math.log2(math.e) / math.sqrt(head_size)


def in_band(window, lower, upper, reach):
    apart = jnp.abs(iota((Q_ROWS, upper - lower), 1) + (lower - reach) - iota((Q_ROWS, upper - lower), 0))
    return apart <= window


def factor(mask):
    return jnp.where(mask, 1.0, 0.0).astype(BF16)


def group_lanes(group):
    return slice(group * LANES, (group + 1) * LANES)


def stacked_heads(queries, head_size):
    lane_head = iota((1, LANES), 1) // head_size
    masks = [(lane_head == head).astype(F32).astype(BF16) for head in range(LANES // head_size)]
    return jnp.concatenate([queries * mask for mask in masks], axis=0)


def put_values(buf, lower, values):
    for group in range(values.shape[1] // LANES):
        lanes = slice(2 * group * LANES, (2 * group + 1) * LANES)
        buf[lower : lower + values.shape[0], lanes] = values[:, group_lanes(group)]


def weighted_sums(weights, values, head_size):
    mixed_all = dot(weights, values)
    heads = LANES // head_size
    count = mixed_all.shape[0] // heads
    lane_head = iota((1, LANES), 1) // head_size
    mixed, totals = mixed_all[:count, :LANES], mixed_all[:count, LANES:]
    for head in range(1, heads):
        part = mixed_all[head * count : (head + 1) * count]
        mixed = jnp.where(lane_head == head, part[:, :LANES], mixed)
        totals = jnp.where(lane_head == head, part[:, LANES:], totals)
    return mixed, totals


def padded_lanes(values, before, after):
    pieces = [jnp.zeros((values.shape[0], before), BF16)] if before else []
    pieces.append(values)
    if after:
        pieces.append(jnp.zeros((values.shape[0], after), BF16))
    return jnp.concatenate(pieces, axis=1) if len(pieces) > 1 else pieces[0]


def unit_weights(scores, spans, band_of):
    width = scores.shape[1]
    count = len(spans) * Q_ROWS
    weights = []
    for head in range(scores.shape[0] // count):
        for block, (lower, upper) in enumerate(spans):
            top = head * count + block * Q_ROWS
            expo = jnp.exp2(scores[top : top + Q_ROWS, lower:upper]).astype(BF16)
            weights.append(padded_lanes(expo * band_of(head, block), lower, width - upper))
    return jnp.concatenate(weights, axis=0)


def inner_kernel(
    window_ref,
    own_ref,
    gain_ref,
    w_query_ref,
    w_key_ref,
    w_value_ref,
    query_ref,
    norm_ref,
    mixed_ref,
    total_ref,
    key_buf,
    value_buf,
    band_buf,
):
    rows, feat_width = own_ref.shape[1:]
    heads = window_ref.shape[0]
    head_size = feat_width // heads
    group_heads = LANES // head_size
    key_count = band_buf.shape[2]
    reach = (key_count - Q_ROWS) // 2
    reach_blocks = reach // Q_ROWS
    blocks = rows // Q_ROWS

    @pl.when(pl.program_id(0) == 0)
    def _():
        for head in range(heads):
            band_buf[head] = factor(in_band(window_ref[head], 0, key_count, reach))
        value_buf[...] = jnp.ones(value_buf.shape, BF16)

    normed = rms_scaled(own_ref[0].astype(F32), gain_ref[...]).astype(BF16)
    query_rows = dot(normed, w_query_ref[...]) * query_scale(head_size)
    key_rows = dot(normed, w_key_ref[...])
    query_ref[0] = query_rows.astype(BF16)
    key_buf[...] = key_rows.astype(BF16).T
    put_values(value_buf, 0, dot(normed, w_value_ref[...]).astype(BF16))
    query_norms, key_norms = norm_bounds(query_rows, heads), norm_bounds(key_rows, heads)
    blank = jnp.zeros((norm_ref.shape[1] - 2, LANES), F32)
    norm_ref[0] = jnp.concatenate([query_norms, key_norms, blank], axis=0)

    @pl.when(is_safe(query_norms, key_norms))
    def _():
        units = [(first, group) for first in range(0, blocks, 2) for group in range(heads // group_heads)]

        def scores_of(first, group):
            queries = query_ref[0, first * Q_ROWS : (first + 2) * Q_ROWS, group_lanes(group)]
            return dot(stacked_heads(queries, head_size), key_buf[group_lanes(group), :])

        scores = scores_of(*units[0])
        for at, (first, group) in enumerate(units):
            following = scores_of(*units[at + 1]) if at + 1 < len(units) else None
            ranges = [(max(0, b - reach_blocks), min(blocks, b + reach_blocks + 1)) for b in (first, first + 1)]
            spans = [(lower * Q_ROWS, upper * Q_ROWS) for lower, upper in ranges]

            def band_of(head, block):
                shift = (reach_blocks - first - block) * Q_ROWS
                lower, upper = spans[block]
                return band_buf[group * group_heads + head, :, lower + shift : upper + shift]

            values = value_buf[:, 2 * group * LANES : 2 * (group + 1) * LANES]
            mixed, totals = weighted_sums(unit_weights(scores, spans, band_of), values, head_size)
            here = slice(first * Q_ROWS, (first + 2) * Q_ROWS)
            mixed_ref[0, here, group_lanes(group)] = mixed
            total_ref[0, here, group_lanes(group)] = totals
            scores = following


def inner(head_window, own, gain, w_query, w_key, w_value, reach):
    members, rows, feat_width = own.shape
    heads = head_window.shape[0]
    key_count = Q_ROWS + 2 * reach
    shapes = [(own.shape, BF16), ((members, 8, LANES), F32), (own.shape, F32), (own.shape, F32)]

    def spec(shape):
        return pl.BlockSpec((1, *shape[1:]), lambda m: (m, 0, 0))

    return pl.pallas_call(
        inner_kernel,
        grid=(members,),
        out_shape=[jax.ShapeDtypeStruct(*v) for v in shapes],
        in_specs=[smem_spec(), spec(own.shape)] + [vmem_spec()] * 4,
        out_specs=[spec(shape) for shape, _ in shapes],
        scratch_shapes=[
            pltpu.VMEM((feat_width, rows), BF16),
            pltpu.VMEM((rows, 2 * feat_width), BF16),
            pltpu.VMEM((heads, Q_ROWS, key_count), BF16),
        ],
        compiler_params=pltpu.CompilerParams(vmem_limit_bytes=VMEM_LIMIT),
        cost_estimate=pl.CostEstimate(
            flops=own.size * (6 * feat_width + 16 * rows), bytes_accessed=14 * own.size, transcendentals=0
        ),
        name="inner",
    )(head_window, own, gain, w_query, w_key, w_value)


def forward_kernel(
    total_len,
    tok_ref,
    mem_ref,
    window_ref,
    state_ref,
    query_ref,
    norm_ref,
    inner_mixed_ref,
    inner_total_ref,
    near_ref,
    far_ref,
    attn_gain_ref,
    ffn_gain_ref,
    w_key_ref,
    w_value_ref,
    w_out_ref,
    w_gate_ref,
    w_up_ref,
    down_weight_ref,
    *refs,
):
    out_refs, (halo_key_buf, halo_value_buf, band_buf, mixed_buf, key_buf, value_buf, forecast_buf) = (
        refs[:-7],
        refs[-7:],
    )
    rows, feat_width = state_ref.shape[1:]
    reach = near_ref.shape[1]
    heads = window_ref.shape[0]
    head_size = feat_width // heads
    group_heads = LANES // head_size
    groups = heads // group_heads
    blocks = rows // Q_ROWS
    key_count = Q_ROWS + 2 * reach
    count = 2 * Q_ROWS
    first_pos = tok_ref[0] * rows

    @pl.when(pl.program_id(0) == 0)
    def _():
        first_valid = first_pos - reach >= 0
        last_valid = first_pos + rows + reach <= total_len
        for head in range(heads):
            window = window_ref[head]
            band_buf[0, head] = factor(in_band(jnp.where(first_valid, window, -1), 0, reach, reach))
            right_window = jnp.where(last_valid, window, -1)
            band_buf[1, head] = factor(in_band(right_window, key_count - reach, key_count, reach))
        halo_value_buf[...] = jnp.ones(halo_value_buf.shape, BF16)

    def keys_of(normed):
        return dot(normed, w_key_ref[...])

    def values_of(normed):
        return dot(normed, w_value_ref[...]).astype(BF16)

    odd = tok_ref[0] % 2 == 1
    near, far = near_ref[0].astype(F32), far_ref[0].astype(F32)
    halo = jnp.concatenate([jnp.where(odd, near, far), jnp.where(odd, far, near)], axis=0)
    normed = rms_scaled(halo, attn_gain_ref[...]).astype(BF16)
    halo_keys = keys_of(normed)
    halo_values = values_of(normed)
    key_norms = jnp.maximum(norm_ref[0, 1:2, :], norm_bounds(halo_keys, heads))
    for side in range(2):
        here = slice(side * reach, (side + 1) * reach)
        halo_key_buf[side] = halo_keys[here].astype(BF16).T
        put_values(halo_value_buf.at[side], 0, halo_values[here])
    safe = is_safe(norm_ref[0, 0:1, :], key_norms)

    @pl.when(safe)
    def _():
        units = [(side, group) for side in range(2) for group in range(groups)]

        def scores_of(side, group):
            start = side * (rows - count)
            queries = query_ref[0, start : start + count, group_lanes(group)]
            return dot(stacked_heads(queries, head_size), halo_key_buf[side, group_lanes(group), :])

        scores = scores_of(*units[0])
        for at, (side, group) in enumerate(units):
            following = scores_of(*units[at + 1]) if at + 1 < len(units) else None
            spans = [(0, reach), (Q_ROWS, reach)] if side == 0 else [(0, reach - Q_ROWS), (0, reach)]

            def band_of(head, block):
                lower, upper = spans[block]
                shift = -block * Q_ROWS if side == 0 else (1 - block) * Q_ROWS
                return band_buf[side, group * group_heads + head, :, lower + shift : upper + shift]

            values = halo_value_buf[side, :, 2 * group * LANES : 2 * (group + 1) * LANES]
            mixed, totals = weighted_sums(unit_weights(scores, spans, band_of), values, head_size)
            here = slice(side * (rows - count), side * (rows - count) + count)
            mixed = mixed + inner_mixed_ref[0, here, group_lanes(group)]
            totals = totals + inner_total_ref[0, here, group_lanes(group)]
            mixed_buf[here, group_lanes(group)] = (mixed / totals).astype(BF16)
            scores = following

    @pl.when(jnp.logical_not(safe))
    def _():
        normed = rms_scaled(state_ref[0].astype(F32), attn_gain_ref[...]).astype(BF16)
        key_buf[:, :reach] = halo_key_buf[0]
        key_buf[:, reach : reach + rows] = keys_of(normed).astype(BF16).T
        key_buf[:, reach + rows :] = halo_key_buf[1]
        value_buf[...] = jnp.ones(value_buf.shape, BF16)
        put_values(value_buf, reach, values_of(normed))
        value_buf[:reach] = halo_value_buf[0]
        value_buf[reach + rows :] = halo_value_buf[1]
        for block in range(blocks):
            start = block * Q_ROWS
            k_pos = first_pos - reach + start + iota((Q_ROWS, key_count), 1)
            inside = (k_pos >= 0) & (k_pos < total_len)
            for group in range(groups):
                queries = query_ref[0, start : start + Q_ROWS, group_lanes(group)]
                keys = key_buf[group_lanes(group), start : start + key_count]
                scores = dot(stacked_heads(queries, head_size), keys)
                weights = []
                for head in range(group_heads):
                    allowed = inside & in_band(window_ref[group * group_heads + head], 0, key_count, reach)
                    score_matrix = jnp.where(allowed, scores[head * Q_ROWS : (head + 1) * Q_ROWS], -1e30)
                    row_top = jnp.max(score_matrix, axis=-1, keepdims=True)
                    weights.append(jnp.exp2(score_matrix - row_top).astype(BF16))
                values = value_buf[start : start + key_count, 2 * group * LANES : 2 * (group + 1) * LANES]
                mixed, totals = weighted_sums(jnp.concatenate(weights, axis=0), values, head_size)
                mixed_buf[start : start + Q_ROWS, group_lanes(group)] = (mixed / totals).astype(BF16)

    after = (state_ref[0].astype(F32) + dot(mixed_buf[...], w_out_ref[...])).astype(BF16)
    normed_mid = rms_scaled(after.astype(F32), ffn_gain_ref[...]).astype(BF16)
    forecast = after.astype(F32)
    for lower in range(0, w_gate_ref.shape[1], HIDDEN_CHUNK):
        part = slice(lower, lower + HIDDEN_CHUNK)
        gate = 0.5 * dot(normed_mid, w_gate_ref[:, part])
        hidden = (gate * (1.0 + jnp.tanh(gate.astype(BF16)).astype(F32)) * dot(normed_mid, w_up_ref[:, part])).astype(BF16)
        forecast += dot(hidden, down_weight_ref[part, :])
    forecast_buf[...] = forecast.astype(BF16)
    share_rows = out_refs[0].shape[1]
    for part, out_ref in enumerate(out_refs):
        lower = pl.multiple_of((mem_ref[0] ^ part) * share_rows, share_rows)
        out_ref[0] = forecast_buf[pl.ds(lower, share_rows), :]


def forward(total_len, tok_index, mem_index, head_window, own, inner_parts, near, far, gains, weights, shares):
    members, row_count, feat_width = own.shape
    reach = near.shape[1]
    heads = head_window.shape[0]
    hidden_width = weights[3].shape[1]
    macs = members * row_count * feat_width * (3 * feat_width + 3 * hidden_width + 4 * reach)

    def spec(array):
        return pl.BlockSpec((1, *array.shape[1:]), lambda m: (m, 0, 0))

    return pl.pallas_call(
        functools.partial(forward_kernel, total_len),
        grid=(members,),
        out_shape=[jax.ShapeDtypeStruct((members, row_count // shares, feat_width), BF16)] * shares,
        in_specs=[smem_spec()] * 3
        + [spec(v) for v in (own, *inner_parts, near, far)]
        + [vmem_spec()] * (len(gains) + len(weights)),
        out_specs=[pl.BlockSpec((1, row_count // shares, feat_width), lambda m: (m, 0, 0))] * shares,
        scratch_shapes=[
            pltpu.VMEM((2, feat_width, reach), BF16),
            pltpu.VMEM((2, reach, 2 * feat_width), BF16),
            pltpu.VMEM((2, heads, Q_ROWS, reach), BF16),
            pltpu.VMEM((row_count, feat_width), BF16),
            pltpu.VMEM((feat_width, row_count + 2 * reach), BF16),
            pltpu.VMEM((row_count + 2 * reach, 2 * feat_width), BF16),
            pltpu.VMEM((row_count, feat_width), BF16),
        ],
        compiler_params=pltpu.CompilerParams(vmem_limit_bytes=VMEM_LIMIT),
        cost_estimate=pl.CostEstimate(flops=2 * macs, bytes_accessed=10 * own.size, transcendentals=0),
        name="forward",
    )(tok_index, mem_index, head_window, own, *inner_parts, near, far, *gains, *weights)


def global_member(held, index, own_members):
    return ((held // own_members) ^ index) * own_members + held % own_members


def gram_kernel(index_ref, *refs):
    share_refs, grid_ref, out_ref = refs[:-2], refs[-2], refs[-1]
    own_members, rows, feat_width = share_refs[0].shape
    members = own_members * len(share_refs)
    index = index_ref[0]
    stack = members * GROUP
    total = jnp.zeros((stack, stack), F32)
    proj = jnp.zeros((members, GROUP, feat_width), F32)
    for lower in range(0, rows, GROUP):
        part = slice(lower, lower + GROUP)
        fields = jnp.concatenate([ref[:, part, :] for ref in share_refs], axis=0).astype(F32)
        mean = jnp.sum(fields, axis=0) * (1.0 / members)
        spread = fields - mean[None]
        weight = grid_ref[0, part, :]
        proj += spread * (grid_ref[1, part, :] - weight * mean)[None]
        high, low = halves(spread.reshape(stack, feat_width))
        w_high, w_low = halves((spread * weight[None]).reshape(stack, feat_width))
        last = ((1,), (1,))
        total += dot(w_high, high, last) + dot(w_high, low, last) + dot(w_low, high, last)
    same = iota((stack, stack), 0) % GROUP == iota((stack, stack), 1) % GROUP
    by_row = jnp.sum(jnp.where(same, total, 0.0).reshape(members, GROUP, stack), axis=1)
    column = global_member(iota((stack, LANES), 0) // GROUP, index, own_members)
    folded = (column == iota((stack, LANES), 1) % members).astype(F32)
    held = global_member(iota((members, members), 1), index, own_members)
    in_order = (held == iota((members, members), 0)).astype(F32)
    tiled = exact_dot(in_order, exact_dot(by_row, folded))
    per_row = LANES // members
    keep = iota((members, LANES), 0) % per_row == iota((members, LANES), 1) // members
    packed = jnp.sum(jnp.where(keep, tiled, 0.0).reshape(members // per_row, per_row, LANES), axis=1)
    proj_col = jnp.sum(jnp.sum(proj, axis=1), axis=1, keepdims=True)
    at_lane = global_member(iota((members, LANES), 0), index, own_members) == iota((members, LANES), 1)
    proj_row = jnp.sum(jnp.where(at_lane, proj_col, 0.0), axis=0, keepdims=True)
    filled = members // per_row + 1
    blank = jnp.zeros((out_ref.shape[0] - filled, LANES), F32)
    out_ref[...] = jnp.concatenate([packed, proj_row, blank], axis=0)


def gram_partial(index, shares, grid):
    members = shares[0].shape[0] * len(shares)
    filled = members * members // LANES + 1
    return pl.pallas_call(
        gram_kernel,
        out_shape=jax.ShapeDtypeStruct((-(-filled // 8) * 8, LANES), F32),
        in_specs=[smem_spec()] + [vmem_spec()] * (len(shares) + 1),
        out_specs=vmem_spec(),
        compiler_params=pltpu.CompilerParams(vmem_limit_bytes=VMEM_LIMIT),
        cost_estimate=pl.CostEstimate(
            flops=3 * GROUP * members * members * grid.size, bytes_accessed=members * grid.size, transcendentals=0
        ),
        name="gram",
    )(index, *shares, grid)


def ensemble_transform(gram, proj):
    members = gram.shape[0]
    row, column = iota((members, members), 0), iota((members, members), 1)
    identity = (row == column).astype(F32)
    system = gram + (members - 1.0) * identity
    left, right = system, proj
    for pivot in range(members):
        is_pivot = iota((members, 1), 0) == pivot
        scale = 1.0 / left[pivot : pivot + 1, pivot : pivot + 1]
        pivot_row = left[pivot : pivot + 1, :] * scale
        pivot_right = right[pivot : pivot + 1, :] * scale
        factor = left[:, pivot : pivot + 1]
        left = jnp.where(is_pivot, pivot_row, left - factor * pivot_row)
        right = jnp.where(is_pivot, pivot_right, right - factor * pivot_right)
    mean_weights = right
    mean_level = jnp.sum(jnp.sum(system * identity, axis=1, keepdims=True), axis=0, keepdims=True) / members
    lifted = system + (mean_level - (members - 1.0)) * (1.0 / members)
    frobenius = jnp.sqrt(jnp.sum(jnp.sum(lifted * lifted, axis=1, keepdims=True), axis=0, keepdims=True))
    root_iter = lifted / frobenius
    inv_iter = identity
    for sweep in range(NS_STEPS):
        product = root_iter if sweep == 0 else exact_dot(inv_iter, root_iter)
        correction = 1.5 * identity - 0.5 * product
        inv_iter = correction if sweep == 0 else exact_dot(correction, inv_iter)
        if sweep < NS_STEPS - 1:
            root_iter = exact_dot(root_iter, correction)
    inv_root = inv_iter / jnp.sqrt(frobenius) + (1.0 / math.sqrt(members - 1.0) - 1.0 / jnp.sqrt(mean_level)) * (
        1.0 / members
    )
    moved = mean_weights + math.sqrt(members - 1.0) * inv_root
    return 1.0 / members + moved - jnp.sum(moved, axis=0, keepdims=True) * (1.0 / members)


def combine_kernel(index_ref, partial_ref, *refs):
    share_refs, out_refs = refs[: len(refs) // 2], refs[len(refs) // 2 :]
    own_members, rows, feat_width = share_refs[0].shape
    members = own_members * len(share_refs)
    stack = members * GROUP
    per_row = LANES // members
    sums = jnp.sum(partial_ref[...], axis=0)
    spread_rows = jnp.concatenate(
        [jnp.broadcast_to(sums[r : r + 1], (per_row, LANES)) for r in range(members // per_row)], axis=0
    )
    keep = iota((members, LANES), 0) % per_row == iota((members, LANES), 1) // members
    folded = (iota((LANES, members), 0) % members == iota((LANES, members), 1)).astype(F32)
    gram = exact_dot(jnp.where(keep, spread_rows, 0.0), folded)
    proj_row = jnp.broadcast_to(sums[members // per_row : members // per_row + 1], (members, LANES))
    on_diagonal = iota((members, LANES), 0) == iota((members, LANES), 1)
    proj = jnp.sum(jnp.where(on_diagonal, proj_row, 0.0), axis=1, keepdims=True)
    transform = ensemble_transform(gram, proj)
    held = global_member(iota((stack, members), 0) // GROUP, index_ref[0], own_members)
    pick = (held == iota((stack, members), 1)).astype(F32).astype(BF16)
    same = iota((stack, stack), 0) % GROUP == iota((stack, stack), 1) % GROUP
    mixers = []
    for piece in halves(transform):
        rows_of = dot(pick, piece, ((1,), (1,))).astype(BF16)
        mixers.append(jnp.where(same, dot(rows_of, pick, ((1,), (1,))), 0.0).astype(BF16))
    for lower in range(0, rows, GROUP):
        part = slice(lower, lower + GROUP)
        fields = jnp.concatenate([ref[:, part, :].reshape(-1, feat_width) for ref in share_refs], axis=0)
        mixed = (dot(mixers[0], fields) + dot(mixers[1], fields)).astype(BF16)
        own_stack = own_members * GROUP
        for at, out_ref in enumerate(out_refs):
            piece = mixed[at * own_stack : (at + 1) * own_stack]
            out_ref[:, part, :] = piece.reshape(own_members, GROUP, feat_width)


def combine(index, partials, shares):
    size = shares[0].size * len(shares)
    members = shares[0].shape[0] * len(shares)
    return pl.pallas_call(
        combine_kernel,
        out_shape=[jax.ShapeDtypeStruct(v.shape, BF16) for v in shares],
        in_specs=[smem_spec()] + [vmem_spec()] * (1 + len(shares)),
        out_specs=[vmem_spec()] * len(shares),
        compiler_params=pltpu.CompilerParams(vmem_limit_bytes=VMEM_LIMIT),
        cost_estimate=pl.CostEstimate(flops=4 * GROUP * members * size, bytes_accessed=4 * size, transcendentals=0),
        name="combine",
    )(index, partials, *shares)


def assemble_kernel(index_ref, *refs):
    part_refs, out_ref, sems = refs[:-2], refs[-2], refs[-1]
    rows = part_refs[0].shape[1]
    copies = []
    for part, ref in enumerate(part_refs):
        lower = pl.multiple_of((index_ref[0] ^ part) * rows, rows)
        copies.append(pltpu.make_async_copy(ref, out_ref.at[:, pl.ds(lower, rows), :], sems.at[part]))
    for copy in copies:
        copy.start()
    for copy in copies:
        copy.wait()


def assemble(index, parts):
    members, rows, feat_width = parts[0].shape
    return pl.pallas_call(
        assemble_kernel,
        out_shape=jax.ShapeDtypeStruct((members, len(parts) * rows, feat_width), BF16),
        in_specs=[smem_spec()] + [vmem_spec()] * len(parts),
        out_specs=pl.BlockSpec(memory_space=pl.ANY),
        scratch_shapes=[pltpu.SemaphoreType.DMA((len(parts),))],
        compiler_params=pltpu.CompilerParams(vmem_limit_bytes=VMEM_LIMIT),
        cost_estimate=pl.CostEstimate(flops=0, bytes_accessed=4 * len(parts) * parts[0].size, transcendentals=0),
        name="assemble",
    )(index, *parts)


def exchanged(parts):
    count = lax.axis_size("mem")
    return [
        lax.ppermute(v, "mem", [(i, i ^ part) for i in range(count)]) if part else v for part, v in enumerate(parts)
    ]


def halos(own, reach):
    count = lax.axis_size("tok")
    odd = lax.axis_index("tok") % 2
    last = own.shape[1] - reach
    near = lax.dynamic_slice_in_dim(own, (1 - odd) * last, reach, axis=1)
    far = lax.dynamic_slice_in_dim(own, odd * last, reach, axis=1)
    near_pairs = [(i, i ^ 1) for i in range(count)]
    far_pairs = [pair for i in range(1, count - 1, 2) for pair in ((i, i + 1), (i + 1, i))]
    return lax.ppermute(near, "tok", near_pairs), lax.ppermute(far, "tok", far_pairs)


def local(
    ens_state,
    attn_gain,
    ffn_gain,
    w_query,
    w_key,
    w_value,
    w_out,
    w_gate,
    w_up,
    down_weight,
    head_window,
    obs_token,
    obs_channel,
    obs_value,
    obs_var,
):
    own_members, row_count, feat_width = ens_state.shape
    mem_count = lax.axis_size("mem")
    tok_count = lax.axis_size("tok")
    device_count = mem_count * tok_count
    share_rows = row_count // mem_count
    first_pos = lax.axis_index("tok") * row_count
    near_halo, far_halo = halos(ens_state, WIN)
    share_start = first_pos + lax.axis_index("mem") * share_rows
    grid = sample_grid(
        share_start.astype(jnp.int32).reshape(1), obs_token, obs_channel, obs_value, obs_var, share_rows, feat_width
    )
    mem_index = lax.axis_index("mem").astype(jnp.int32).reshape(1)
    tok_index = lax.axis_index("tok").astype(jnp.int32).reshape(1)
    gains = [attn_gain.reshape(1, -1), ffn_gain.reshape(1, -1)]
    inner_parts = inner(head_window, ens_state, gains[0], w_query, w_key, w_value, WIN)
    weights = [w_key, w_value, w_out, w_gate, w_up, down_weight]
    total_len = row_count * tok_count
    forecast = forward(
        total_len, tok_index, mem_index, head_window, ens_state, inner_parts, near_halo, far_halo, gains, weights, mem_count
    )
    shares = exchanged(forecast)
    partial = gram_partial(mem_index, shares, grid)
    partials = lax.all_to_all(
        jnp.broadcast_to(partial[None], (device_count, *partial.shape)),
        ("mem", "tok"),
        split_axis=0,
        concat_axis=0,
        tiled=True,
    )
    return assemble(mem_index, exchanged(combine(mem_index, partials, shares)))


def solution(mesh):
    in_specs = (P("mem", "tok", None), *[P()] * 10, *[P("tok")] * 4)
    return jax.shard_map(local, mesh=mesh, in_specs=in_specs, out_specs=P("mem", "tok", None), check_vma=False)
```

```python
import functools
import math

import jax
import jax.numpy as jnp
from jax import lax
from jax.experimental import pallas as pl
from jax.experimental.pallas import tpu as pltpu
from jax.sharding import PartitionSpec as P

WIN = 256
NS_STEPS = 8
EPS = 1e-05
Q_ROWS = 128
GROUP = 16
LANES = 128
VMEM_LIMIT = 32 * 1024 * 1024
SAFE_SCORE = 100.0
FOLD = 4
BATCH = 2
HIDDEN_CHUNK = 256

F32 = jnp.float32
BF16 = jnp.bfloat16


def dot(a, b, contract=((1,), (0,)), precision=None):
    return lax.dot_general(a, b, (contract, ((), ())), precision=precision, preferred_element_type=F32)


def exact_dot(a, b, contract=((1,), (0,))):
    return dot(a, b, contract, lax.Precision.HIGHEST)


def iota(shape, axis):
    return lax.broadcasted_iota(jnp.int32, shape, axis)


def halves(values):
    high = values.astype(BF16)
    return high, (values - high.astype(F32)).astype(BF16)


def rms_scaled(values, gain):
    return values * lax.rsqrt(jnp.mean(values * values, axis=-1, keepdims=True) + EPS) * gain


def vmem_spec():
    return pl.BlockSpec(memory_space=pltpu.VMEM)


def smem_spec():
    return pl.BlockSpec(memory_space=pltpu.SMEM)


def sample_grid_kernel(start_ref, token_ref, channel_ref, value_ref, var_ref, out_ref):
    rows, feat_width = out_ref.shape[1:]
    count = token_ref.shape[1]
    chunk = min(1024, count)
    total = jnp.zeros((4 * rows, feat_width), F32)
    for lower in range(0, count, chunk):
        part = slice(lower, lower + chunk)
        inv_var = 1.0 / var_ref[:, part]
        weighted = value_ref[:, part] * inv_var
        here = iota((rows, chunk), 0) == token_ref[:, part] - start_ref[0]
        pieces = []
        for row in (inv_var, weighted):
            high = row.astype(BF16).astype(F32)
            pieces.append(jnp.where(here, high, 0.0).astype(BF16))
            pieces.append(jnp.where(here, row - high, 0.0).astype(BF16))
        channel_hot = jnp.where(iota((feat_width, chunk), 0) == channel_ref[:, part], 1.0, 0.0).astype(BF16)
        total += dot(jnp.concatenate(pieces, axis=0), channel_hot, ((1,), (1,)))
    out_ref[0] = total[:rows] + total[rows : 2 * rows]
    out_ref[1] = total[2 * rows : 3 * rows] + total[3 * rows :]


def sample_grid(start, obs_token, obs_channel, obs_value, obs_var, rows, feat_width):
    count = obs_token.shape[0]
    return pl.pallas_call(
        sample_grid_kernel,
        out_shape=jax.ShapeDtypeStruct((2, rows, feat_width), F32),
        in_specs=[smem_spec()] + [vmem_spec()] * 4,
        out_specs=vmem_spec(),
        compiler_params=pltpu.CompilerParams(vmem_limit_bytes=VMEM_LIMIT),
        cost_estimate=pl.CostEstimate(flops=8 * rows * count * feat_width, bytes_accessed=16 * count, transcendentals=0),
        name="sample_grid",
    )(start, *(v.reshape(1, count) for v in (obs_token, obs_channel, obs_value, obs_var)))


def head_lanes(feat_width, heads):
    lane_head = iota((feat_width, LANES), 0) // (feat_width // heads)
    return (lane_head == iota((feat_width, LANES), 1)).astype(F32).astype(BF16)


def norm_bounds(values, heads):
    rows = values.shape[0] // FOLD
    squares = values * values
    folded = squares[:rows]
    for part in range(1, FOLD):
        folded = jnp.maximum(folded, squares[part * rows : (part + 1) * rows])
    return jnp.max(dot(folded.astype(BF16), head_lanes(values.shape[1], heads)), axis=0, keepdims=True)


def is_safe(query_norms, key_norms):
    return jnp.max(query_norms * key_norms) * 1.05 <= SAFE_SCORE * SAFE_SCORE


def query_scale(head_size):
    return math.log2(math.e) / math.sqrt(head_size)


def in_band(window, lower, upper, reach):
    apart = jnp.abs(iota((Q_ROWS, upper - lower), 1) + (lower - reach) - iota((Q_ROWS, upper - lower), 0))
    return apart <= window


def factor(mask):
    return jnp.where(mask, 1.0, 0.0).astype(BF16)


def group_lanes(group):
    return slice(group * LANES, (group + 1) * LANES)


def stacked_heads(queries, head_size):
    lane_head = iota((1, LANES), 1) // head_size
    masks = [(lane_head == head).astype(F32).astype(BF16) for head in range(LANES // head_size)]
    return jnp.concatenate([queries * mask for mask in masks], axis=0)


def put_values(buf, lower, values):
    for group in range(values.shape[1] // LANES):
        lanes = slice(2 * group * LANES, (2 * group + 1) * LANES)
        buf[lower : lower + values.shape[0], lanes] = values[:, group_lanes(group)]


def weighted_sums(weights, values, head_size):
    mixed_all = dot(weights, values)
    heads = LANES // head_size
    count = mixed_all.shape[0] // heads
    lane_head = iota((1, LANES), 1) // head_size
    mixed, totals = mixed_all[:count, :LANES], mixed_all[:count, LANES:]
    for head in range(1, heads):
        part = mixed_all[head * count : (head + 1) * count]
        mixed = jnp.where(lane_head == head, part[:, :LANES], mixed)
        totals = jnp.where(lane_head == head, part[:, LANES:], totals)
    return mixed, totals


def padded_lanes(values, before, after):
    pieces = [jnp.zeros((values.shape[0], before), BF16)] if before else []
    pieces.append(values)
    if after:
        pieces.append(jnp.zeros((values.shape[0], after), BF16))
    return jnp.concatenate(pieces, axis=1) if len(pieces) > 1 else pieces[0]


def unit_weights(scores, spans, band_of):
    width = scores.shape[1]
    count = len(spans) * Q_ROWS
    weights = []
    for head in range(scores.shape[0] // count):
        for block, (lower, upper) in enumerate(spans):
            top = head * count + block * Q_ROWS
            expo = jnp.exp2(scores[top : top + Q_ROWS, lower:upper]).astype(BF16)
            weights.append(padded_lanes(expo * band_of(head, block), lower, width - upper))
    return jnp.concatenate(weights, axis=0)


def inner_kernel(
    window_ref,
    own_ref,
    gain_ref,
    w_query_ref,
    w_key_ref,
    w_value_ref,
    query_ref,
    norm_ref,
    mixed_ref,
    total_ref,
    key_buf,
    value_buf,
    band_buf,
):
    rows, feat_width = own_ref.shape[1:]
    heads = window_ref.shape[0]
    head_size = feat_width // heads
    group_heads = LANES // head_size
    key_count = band_buf.shape[2]
    reach = (key_count - Q_ROWS) // 2
    reach_blocks = reach // Q_ROWS
    blocks = rows // Q_ROWS

    @pl.when(pl.program_id(0) == 0)
    def _():
        for head in range(heads):
            band_buf[head] = factor(in_band(window_ref[head], 0, key_count, reach))
        value_buf[...] = jnp.ones(value_buf.shape, BF16)

    normed = rms_scaled(own_ref[0].astype(F32), gain_ref[...]).astype(BF16)
    query_rows = dot(normed, w_query_ref[...]) * query_scale(head_size)
    key_rows = dot(normed, w_key_ref[...])
    query_ref[0] = query_rows.astype(BF16)
    key_buf[...] = key_rows.astype(BF16).T
    put_values(value_buf, 0, dot(normed, w_value_ref[...]).astype(BF16))
    query_norms, key_norms = norm_bounds(query_rows, heads), norm_bounds(key_rows, heads)
    blank = jnp.zeros((norm_ref.shape[1] - 2, LANES), F32)
    norm_ref[0] = jnp.concatenate([query_norms, key_norms, blank], axis=0)

    @pl.when(is_safe(query_norms, key_norms))
    def _():
        units = [(first, group) for first in range(0, blocks, 2) for group in range(heads // group_heads)]

        def scores_of(first, group):
            queries = query_ref[0, first * Q_ROWS : (first + 2) * Q_ROWS, group_lanes(group)]
            return dot(stacked_heads(queries, head_size), key_buf[group_lanes(group), :])

        scores = scores_of(*units[0])
        for at, (first, group) in enumerate(units):
            following = scores_of(*units[at + 1]) if at + 1 < len(units) else None
            ranges = [(max(0, b - reach_blocks), min(blocks, b + reach_blocks + 1)) for b in (first, first + 1)]
            spans = [(lower * Q_ROWS, upper * Q_ROWS) for lower, upper in ranges]

            def band_of(head, block):
                shift = (reach_blocks - first - block) * Q_ROWS
                lower, upper = spans[block]
                return band_buf[group * group_heads + head, :, lower + shift : upper + shift]

            values = value_buf[:, 2 * group * LANES : 2 * (group + 1) * LANES]
            mixed, totals = weighted_sums(unit_weights(scores, spans, band_of), values, head_size)
            here = slice(first * Q_ROWS, (first + 2) * Q_ROWS)
            mixed_ref[0, here, group_lanes(group)] = mixed
            total_ref[0, here, group_lanes(group)] = totals
            scores = following


def inner(head_window, own, gain, w_query, w_key, w_value, reach):
    members, rows, feat_width = own.shape
    heads = head_window.shape[0]
    key_count = Q_ROWS + 2 * reach
    shapes = [(own.shape, BF16), ((members, 8, LANES), F32), (own.shape, F32), (own.shape, F32)]

    def spec(shape):
        return pl.BlockSpec((1, *shape[1:]), lambda m: (m, 0, 0))

    return pl.pallas_call(
        inner_kernel,
        grid=(members,),
        out_shape=[jax.ShapeDtypeStruct(*v) for v in shapes],
        in_specs=[smem_spec(), spec(own.shape)] + [vmem_spec()] * 4,
        out_specs=[spec(shape) for shape, _ in shapes],
        scratch_shapes=[
            pltpu.VMEM((feat_width, rows), BF16),
            pltpu.VMEM((rows, 2 * feat_width), BF16),
            pltpu.VMEM((heads, Q_ROWS, key_count), BF16),
        ],
        compiler_params=pltpu.CompilerParams(vmem_limit_bytes=VMEM_LIMIT),
        cost_estimate=pl.CostEstimate(
            flops=own.size * (6 * feat_width + 16 * rows), bytes_accessed=14 * own.size, transcendentals=0
        ),
        name="inner",
    )(head_window, own, gain, w_query, w_key, w_value)


def forward_kernel(
    total_len,
    tok_ref,
    mem_ref,
    window_ref,
    state_ref,
    query_ref,
    norm_ref,
    inner_mixed_ref,
    inner_total_ref,
    near_ref,
    far_ref,
    attn_gain_ref,
    ffn_gain_ref,
    w_key_ref,
    w_value_ref,
    w_out_ref,
    w_gate_ref,
    w_up_ref,
    down_weight_ref,
    *refs,
):
    out_refs, (halo_key_buf, halo_value_buf, band_buf, mixed_buf, key_buf, value_buf, forecast_buf) = (
        refs[:-7],
        refs[-7:],
    )
    rows, feat_width = state_ref.shape[1:]
    reach = near_ref.shape[1]
    heads = window_ref.shape[0]
    head_size = feat_width // heads
    group_heads = LANES // head_size
    groups = heads // group_heads
    blocks = rows // Q_ROWS
    key_count = Q_ROWS + 2 * reach
    count = 2 * Q_ROWS
    first_pos = tok_ref[0] * rows

    @pl.when(pl.program_id(0) == 0)
    def _():
        first_valid = first_pos - reach >= 0
        last_valid = first_pos + rows + reach <= total_len
        for head in range(heads):
            window = window_ref[head]
            band_buf[0, head] = factor(in_band(jnp.where(first_valid, window, -1), 0, reach, reach))
            right_window = jnp.where(last_valid, window, -1)
            band_buf[1, head] = factor(in_band(right_window, key_count - reach, key_count, reach))
        halo_value_buf[...] = jnp.ones(halo_value_buf.shape, BF16)

    def keys_of(normed):
        return dot(normed, w_key_ref[...])

    def values_of(normed):
        return dot(normed, w_value_ref[...]).astype(BF16)

    odd = tok_ref[0] % 2 == 1
    batch = state_ref.shape[0]
    halo = []
    for member in range(batch):
        near, far = near_ref[member].astype(F32), far_ref[member].astype(F32)
        halo += [jnp.where(odd, near, far), jnp.where(odd, far, near)]
    normed = rms_scaled(jnp.concatenate(halo, axis=0), attn_gain_ref[...]).astype(BF16)
    halo_keys = keys_of(normed)
    halo_values = values_of(normed)
    query_norms = jnp.max(norm_ref[:, 0, :], axis=0, keepdims=True)
    key_norms = jnp.maximum(jnp.max(norm_ref[:, 1, :], axis=0, keepdims=True), norm_bounds(halo_keys, heads))
    for at in range(2 * batch):
        here = slice(at * reach, (at + 1) * reach)
        halo_key_buf[at] = halo_keys[here].astype(BF16).T
        put_values(halo_value_buf.at[at], 0, halo_values[here])
    safe = is_safe(query_norms, key_norms)

    @pl.when(safe)
    def _():
        units = [(member, side, group) for member in range(batch) for side in range(2) for group in range(groups)]

        def scores_of(member, side, group):
            start = side * (rows - count)
            queries = query_ref[member, start : start + count, group_lanes(group)]
            return dot(stacked_heads(queries, head_size), halo_key_buf[2 * member + side, group_lanes(group), :])

        scores = scores_of(*units[0])
        for at, (member, side, group) in enumerate(units):
            following = scores_of(*units[at + 1]) if at + 1 < len(units) else None
            spans = [(0, reach), (Q_ROWS, reach)] if side == 0 else [(0, reach - Q_ROWS), (0, reach)]

            def band_of(head, block):
                lower, upper = spans[block]
                shift = -block * Q_ROWS if side == 0 else (1 - block) * Q_ROWS
                return band_buf[side, group * group_heads + head, :, lower + shift : upper + shift]

            values = halo_value_buf[2 * member + side, :, 2 * group * LANES : 2 * (group + 1) * LANES]
            mixed, totals = weighted_sums(unit_weights(scores, spans, band_of), values, head_size)
            start = side * (rows - count)
            here = slice(start, start + count)
            mixed = mixed + inner_mixed_ref[member, here, group_lanes(group)]
            totals = totals + inner_total_ref[member, here, group_lanes(group)]
            start += member * rows
            mixed_buf[start : start + count, group_lanes(group)] = (mixed / totals).astype(BF16)
            scores = following

    @pl.when(jnp.logical_not(safe))
    def _():
        for member in range(batch):
            normed = rms_scaled(state_ref[member].astype(F32), attn_gain_ref[...]).astype(BF16)
            key_buf[:, :reach] = halo_key_buf[2 * member]
            key_buf[:, reach : reach + rows] = keys_of(normed).astype(BF16).T
            key_buf[:, reach + rows :] = halo_key_buf[2 * member + 1]
            value_buf[...] = jnp.ones(value_buf.shape, BF16)
            put_values(value_buf, reach, values_of(normed))
            value_buf[:reach] = halo_value_buf[2 * member]
            value_buf[reach + rows :] = halo_value_buf[2 * member + 1]
            for block in range(blocks):
                start = block * Q_ROWS
                k_pos = first_pos - reach + start + iota((Q_ROWS, key_count), 1)
                inside = (k_pos >= 0) & (k_pos < total_len)
                for group in range(groups):
                    queries = query_ref[member, start : start + Q_ROWS, group_lanes(group)]
                    keys = key_buf[group_lanes(group), start : start + key_count]
                    scores = dot(stacked_heads(queries, head_size), keys)
                    weights = []
                    for head in range(group_heads):
                        allowed = inside & in_band(window_ref[group * group_heads + head], 0, key_count, reach)
                        score_matrix = jnp.where(allowed, scores[head * Q_ROWS : (head + 1) * Q_ROWS], -1e30)
                        row_top = jnp.max(score_matrix, axis=-1, keepdims=True)
                        weights.append(jnp.exp2(score_matrix - row_top).astype(BF16))
                    values = value_buf[start : start + key_count, 2 * group * LANES : 2 * (group + 1) * LANES]
                    mixed, totals = weighted_sums(jnp.concatenate(weights, axis=0), values, head_size)
                    here = slice(member * rows + start, member * rows + start + Q_ROWS)
                    mixed_buf[here, group_lanes(group)] = (mixed / totals).astype(BF16)

    state = state_ref[...].reshape(batch * rows, feat_width).astype(F32)
    after = (state + dot(mixed_buf[...], w_out_ref[...])).astype(BF16)
    normed_mid = rms_scaled(after.astype(F32), ffn_gain_ref[...]).astype(BF16)
    forecast = after.astype(F32)
    for lower in range(0, w_gate_ref.shape[1], HIDDEN_CHUNK):
        part = slice(lower, lower + HIDDEN_CHUNK)
        gate = 0.5 * dot(normed_mid, w_gate_ref[:, part])
        hidden = (gate * (1.0 + jnp.tanh(gate.astype(BF16)).astype(F32)) * dot(normed_mid, w_up_ref[:, part])).astype(BF16)
        forecast += dot(hidden, down_weight_ref[part, :])
    forecast_buf[...] = forecast.astype(BF16)
    share_rows = out_refs[0].shape[1]
    for part, out_ref in enumerate(out_refs):
        lower = pl.multiple_of((mem_ref[0] ^ part) * share_rows, share_rows)
        for member in range(batch):
            out_ref[member] = forecast_buf[pl.ds(member * rows + lower, share_rows), :]


def forward(total_len, tok_index, mem_index, head_window, own, inner_parts, near, far, gains, weights, shares):
    members, row_count, feat_width = own.shape
    reach = near.shape[1]
    heads = head_window.shape[0]
    hidden_width = weights[3].shape[1]
    macs = members * row_count * feat_width * (3 * feat_width + 3 * hidden_width + 4 * reach)
    batch = BATCH if members % BATCH == 0 else 1
    share_rows = row_count // shares

    def spec(array):
        return pl.BlockSpec((batch, *array.shape[1:]), lambda m: (m, 0, 0))

    return pl.pallas_call(
        functools.partial(forward_kernel, total_len),
        grid=(members // batch,),
        out_shape=[jax.ShapeDtypeStruct((members, share_rows, feat_width), BF16)] * shares,
        in_specs=[smem_spec()] * 3
        + [spec(v) for v in (own, *inner_parts, near, far)]
        + [vmem_spec()] * (len(gains) + len(weights)),
        out_specs=[pl.BlockSpec((batch, share_rows, feat_width), lambda m: (m, 0, 0))] * shares,
        scratch_shapes=[
            pltpu.VMEM((2 * batch, feat_width, reach), BF16),
            pltpu.VMEM((2 * batch, reach, 2 * feat_width), BF16),
            pltpu.VMEM((2, heads, Q_ROWS, reach), BF16),
            pltpu.VMEM((batch * row_count, feat_width), BF16),
            pltpu.VMEM((feat_width, row_count + 2 * reach), BF16),
            pltpu.VMEM((row_count + 2 * reach, 2 * feat_width), BF16),
            pltpu.VMEM((batch * row_count, feat_width), BF16),
        ],
        compiler_params=pltpu.CompilerParams(vmem_limit_bytes=VMEM_LIMIT),
        cost_estimate=pl.CostEstimate(flops=2 * macs, bytes_accessed=10 * own.size, transcendentals=0),
        name="forward",
    )(tok_index, mem_index, head_window, own, *inner_parts, near, far, *gains, *weights)


def global_member(held, index, own_members):
    return ((held // own_members) ^ index) * own_members + held % own_members


def gram_kernel(index_ref, *refs):
    share_refs, grid_ref, out_ref = refs[:-2], refs[-2], refs[-1]
    own_members, rows, feat_width = share_refs[0].shape
    members = own_members * len(share_refs)
    index = index_ref[0]
    stack = members * GROUP
    total = jnp.zeros((stack, stack), F32)
    proj = jnp.zeros((members, GROUP, feat_width), F32)
    for lower in range(0, rows, GROUP):
        part = slice(lower, lower + GROUP)
        fields = jnp.concatenate([ref[:, part, :] for ref in share_refs], axis=0).astype(F32)
        mean = jnp.sum(fields, axis=0) * (1.0 / members)
        spread = fields - mean[None]
        weight = grid_ref[0, part, :]
        proj += spread * (grid_ref[1, part, :] - weight * mean)[None]
        high, low = halves(spread.reshape(stack, feat_width))
        w_high, w_low = halves((spread * weight[None]).reshape(stack, feat_width))
        last = ((1,), (1,))
        total += dot(w_high, high, last) + dot(w_high, low, last) + dot(w_low, high, last)
    same = iota((stack, stack), 0) % GROUP == iota((stack, stack), 1) % GROUP
    by_row = jnp.sum(jnp.where(same, total, 0.0).reshape(members, GROUP, stack), axis=1)
    column = global_member(iota((stack, LANES), 0) // GROUP, index, own_members)
    folded = (column == iota((stack, LANES), 1) % members).astype(F32)
    held = global_member(iota((members, members), 1), index, own_members)
    in_order = (held == iota((members, members), 0)).astype(F32)
    tiled = exact_dot(in_order, exact_dot(by_row, folded))
    per_row = LANES // members
    keep = iota((members, LANES), 0) % per_row == iota((members, LANES), 1) // members
    packed = jnp.sum(jnp.where(keep, tiled, 0.0).reshape(members // per_row, per_row, LANES), axis=1)
    proj_col = jnp.sum(jnp.sum(proj, axis=1), axis=1, keepdims=True)
    at_lane = global_member(iota((members, LANES), 0), index, own_members) == iota((members, LANES), 1)
    proj_row = jnp.sum(jnp.where(at_lane, proj_col, 0.0), axis=0, keepdims=True)
    filled = members // per_row + 1
    blank = jnp.zeros((out_ref.shape[0] - filled, LANES), F32)
    out_ref[...] = jnp.concatenate([packed, proj_row, blank], axis=0)


def gram_partial(index, shares, grid):
    members = shares[0].shape[0] * len(shares)
    filled = members * members // LANES + 1
    return pl.pallas_call(
        gram_kernel,
        out_shape=jax.ShapeDtypeStruct((-(-filled // 8) * 8, LANES), F32),
        in_specs=[smem_spec()] + [vmem_spec()] * (len(shares) + 1),
        out_specs=vmem_spec(),
        compiler_params=pltpu.CompilerParams(vmem_limit_bytes=VMEM_LIMIT),
        cost_estimate=pl.CostEstimate(
            flops=3 * GROUP * members * members * grid.size, bytes_accessed=members * grid.size, transcendentals=0
        ),
        name="gram",
    )(index, *shares, grid)


def ensemble_transform(gram, proj):
    members = gram.shape[0]
    row, column = iota((members, members), 0), iota((members, members), 1)
    identity = (row == column).astype(F32)
    system = gram + (members - 1.0) * identity
    left, right = system, proj
    for pivot in range(members):
        is_pivot = iota((members, 1), 0) == pivot
        scale = 1.0 / left[pivot : pivot + 1, pivot : pivot + 1]
        pivot_row = left[pivot : pivot + 1, :] * scale
        pivot_right = right[pivot : pivot + 1, :] * scale
        factor = left[:, pivot : pivot + 1]
        left = jnp.where(is_pivot, pivot_row, left - factor * pivot_row)
        right = jnp.where(is_pivot, pivot_right, right - factor * pivot_right)
    mean_weights = right
    mean_level = jnp.sum(jnp.sum(system * identity, axis=1, keepdims=True), axis=0, keepdims=True) / members
    lifted = system + (mean_level - (members - 1.0)) * (1.0 / members)
    frobenius = jnp.sqrt(jnp.sum(jnp.sum(lifted * lifted, axis=1, keepdims=True), axis=0, keepdims=True))
    root_iter = lifted / frobenius
    inv_iter = identity
    for sweep in range(NS_STEPS):
        product = root_iter if sweep == 0 else exact_dot(inv_iter, root_iter)
        correction = 1.5 * identity - 0.5 * product
        inv_iter = correction if sweep == 0 else exact_dot(correction, inv_iter)
        if sweep < NS_STEPS - 1:
            root_iter = exact_dot(root_iter, correction)
    inv_root = inv_iter / jnp.sqrt(frobenius) + (1.0 / math.sqrt(members - 1.0) - 1.0 / jnp.sqrt(mean_level)) * (
        1.0 / members
    )
    moved = mean_weights + math.sqrt(members - 1.0) * inv_root
    return 1.0 / members + moved - jnp.sum(moved, axis=0, keepdims=True) * (1.0 / members)


def combine_kernel(index_ref, partial_ref, *refs):
    share_refs, out_refs = refs[: len(refs) // 2], refs[len(refs) // 2 :]
    own_members, rows, feat_width = share_refs[0].shape
    members = own_members * len(share_refs)
    stack = members * GROUP
    per_row = LANES // members
    sums = jnp.sum(partial_ref[...], axis=0)
    spread_rows = jnp.concatenate(
        [jnp.broadcast_to(sums[r : r + 1], (per_row, LANES)) for r in range(members // per_row)], axis=0
    )
    keep = iota((members, LANES), 0) % per_row == iota((members, LANES), 1) // members
    folded = (iota((LANES, members), 0) % members == iota((LANES, members), 1)).astype(F32)
    gram = exact_dot(jnp.where(keep, spread_rows, 0.0), folded)
    proj_row = jnp.broadcast_to(sums[members // per_row : members // per_row + 1], (members, LANES))
    on_diagonal = iota((members, LANES), 0) == iota((members, LANES), 1)
    proj = jnp.sum(jnp.where(on_diagonal, proj_row, 0.0), axis=1, keepdims=True)
    transform = ensemble_transform(gram, proj)
    held = global_member(iota((stack, members), 0) // GROUP, index_ref[0], own_members)
    pick = (held == iota((stack, members), 1)).astype(F32).astype(BF16)
    same = iota((stack, stack), 0) % GROUP == iota((stack, stack), 1) % GROUP
    mixers = []
    for piece in halves(transform):
        rows_of = dot(pick, piece, ((1,), (1,))).astype(BF16)
        mixers.append(jnp.where(same, dot(rows_of, pick, ((1,), (1,))), 0.0).astype(BF16))
    for lower in range(0, rows, GROUP):
        part = slice(lower, lower + GROUP)
        fields = jnp.concatenate([ref[:, part, :].reshape(-1, feat_width) for ref in share_refs], axis=0)
        mixed = (dot(mixers[0], fields) + dot(mixers[1], fields)).astype(BF16)
        own_stack = own_members * GROUP
        for at, out_ref in enumerate(out_refs):
            piece = mixed[at * own_stack : (at + 1) * own_stack]
            out_ref[:, part, :] = piece.reshape(own_members, GROUP, feat_width)


def combine(index, partials, shares):
    size = shares[0].size * len(shares)
    members = shares[0].shape[0] * len(shares)
    return pl.pallas_call(
        combine_kernel,
        out_shape=[jax.ShapeDtypeStruct(v.shape, BF16) for v in shares],
        in_specs=[smem_spec()] + [vmem_spec()] * (1 + len(shares)),
        out_specs=[vmem_spec()] * len(shares),
        compiler_params=pltpu.CompilerParams(vmem_limit_bytes=VMEM_LIMIT),
        cost_estimate=pl.CostEstimate(flops=4 * GROUP * members * size, bytes_accessed=4 * size, transcendentals=0),
        name="combine",
    )(index, partials, *shares)


def assemble_kernel(index_ref, *refs):
    part_refs, out_ref, sems = refs[:-2], refs[-2], refs[-1]
    rows = part_refs[0].shape[1]
    copies = []
    for part, ref in enumerate(part_refs):
        lower = pl.multiple_of((index_ref[0] ^ part) * rows, rows)
        copies.append(pltpu.make_async_copy(ref, out_ref.at[:, pl.ds(lower, rows), :], sems.at[part]))
    for copy in copies:
        copy.start()
    for copy in copies:
        copy.wait()


def assemble(index, parts):
    members, rows, feat_width = parts[0].shape
    return pl.pallas_call(
        assemble_kernel,
        out_shape=jax.ShapeDtypeStruct((members, len(parts) * rows, feat_width), BF16),
        in_specs=[smem_spec()] + [vmem_spec()] * len(parts),
        out_specs=pl.BlockSpec(memory_space=pl.ANY),
        scratch_shapes=[pltpu.SemaphoreType.DMA((len(parts),))],
        compiler_params=pltpu.CompilerParams(vmem_limit_bytes=VMEM_LIMIT),
        cost_estimate=pl.CostEstimate(flops=0, bytes_accessed=4 * len(parts) * parts[0].size, transcendentals=0),
        name="assemble",
    )(index, *parts)


def exchanged(parts):
    count = lax.axis_size("mem")
    return [
        lax.ppermute(v, "mem", [(i, i ^ part) for i in range(count)]) if part else v for part, v in enumerate(parts)
    ]


def halos(own, reach):
    count = lax.axis_size("tok")
    odd = lax.axis_index("tok") % 2
    last = own.shape[1] - reach
    near = lax.dynamic_slice_in_dim(own, (1 - odd) * last, reach, axis=1)
    far = lax.dynamic_slice_in_dim(own, odd * last, reach, axis=1)
    near_pairs = [(i, i ^ 1) for i in range(count)]
    far_pairs = [pair for i in range(1, count - 1, 2) for pair in ((i, i + 1), (i + 1, i))]
    return lax.ppermute(near, "tok", near_pairs), lax.ppermute(far, "tok", far_pairs)


def local(
    ens_state,
    attn_gain,
    ffn_gain,
    w_query,
    w_key,
    w_value,
    w_out,
    w_gate,
    w_up,
    down_weight,
    head_window,
    obs_token,
    obs_channel,
    obs_value,
    obs_var,
):
    own_members, row_count, feat_width = ens_state.shape
    mem_count = lax.axis_size("mem")
    tok_count = lax.axis_size("tok")
    device_count = mem_count * tok_count
    share_rows = row_count // mem_count
    first_pos = lax.axis_index("tok") * row_count
    near_halo, far_halo = halos(ens_state, WIN)
    share_start = first_pos + lax.axis_index("mem") * share_rows
    grid = sample_grid(
        share_start.astype(jnp.int32).reshape(1), obs_token, obs_channel, obs_value, obs_var, share_rows, feat_width
    )
    mem_index = lax.axis_index("mem").astype(jnp.int32).reshape(1)
    tok_index = lax.axis_index("tok").astype(jnp.int32).reshape(1)
    gains = [attn_gain.reshape(1, -1), ffn_gain.reshape(1, -1)]
    inner_parts = inner(head_window, ens_state, gains[0], w_query, w_key, w_value, WIN)
    weights = [w_key, w_value, w_out, w_gate, w_up, down_weight]
    total_len = row_count * tok_count
    forecast = forward(
        total_len, tok_index, mem_index, head_window, ens_state, inner_parts, near_halo, far_halo, gains, weights, mem_count
    )
    shares = exchanged(forecast)
    partial = gram_partial(mem_index, shares, grid)
    partials = lax.all_to_all(
        jnp.broadcast_to(partial[None], (device_count, *partial.shape)),
        ("mem", "tok"),
        split_axis=0,
        concat_axis=0,
        tiled=True,
    )
    return assemble(mem_index, exchanged(combine(mem_index, partials, shares)))


def solution(mesh):
    in_specs = (P("mem", "tok", None), *[P()] * 10, *[P("tok")] * 4)
    return jax.shard_map(local, mesh=mesh, in_specs=in_specs, out_specs=P("mem", "tok", None), check_vma=False)
```

```python
import functools
import math

import jax
import jax.numpy as jnp
from jax import lax
from jax.experimental import pallas as pl
from jax.experimental.pallas import tpu as pltpu
from jax.sharding import PartitionSpec as P

WIN = 256
NS_STEPS = 8
EPS = 1e-05
Q_ROWS = 128
GROUP = 16
LANES = 128
VMEM_LIMIT = 32 * 1024 * 1024
SAFE_SCORE = 100.0
FOLD = 4
BATCH = 2
PASSES = 6
HIDDEN_CHUNK = 256

F32 = jnp.float32
BF16 = jnp.bfloat16


def dot(a, b, contract=((1,), (0,)), precision=None):
    return lax.dot_general(a, b, (contract, ((), ())), precision=precision, preferred_element_type=F32)


def exact_dot(a, b, contract=((1,), (0,))):
    return dot(a, b, contract, lax.Precision.HIGHEST)


def iota(shape, axis):
    return lax.broadcasted_iota(jnp.int32, shape, axis)


def halves(values):
    high = values.astype(BF16)
    return high, (values - high.astype(F32)).astype(BF16)


def rms_scaled(values, gain):
    return values * lax.rsqrt(jnp.mean(values * values, axis=-1, keepdims=True) + EPS) * gain


def vmem_spec():
    return pl.BlockSpec(memory_space=pltpu.VMEM)


def smem_spec():
    return pl.BlockSpec(memory_space=pltpu.SMEM)


def sample_grid_kernel(start_ref, token_ref, channel_ref, value_ref, var_ref, out_ref):
    rows, feat_width = out_ref.shape[1:]
    count = token_ref.shape[1]
    chunk = min(1024, count)
    total = jnp.zeros((4 * rows, feat_width), F32)
    for lower in range(0, count, chunk):
        part = slice(lower, lower + chunk)
        inv_var = 1.0 / var_ref[:, part]
        weighted = value_ref[:, part] * inv_var
        here = iota((rows, chunk), 0) == token_ref[:, part] - start_ref[0]
        pieces = []
        for row in (inv_var, weighted):
            high = row.astype(BF16).astype(F32)
            pieces.append(jnp.where(here, high, 0.0).astype(BF16))
            pieces.append(jnp.where(here, row - high, 0.0).astype(BF16))
        channel_hot = jnp.where(iota((feat_width, chunk), 0) == channel_ref[:, part], 1.0, 0.0).astype(BF16)
        total += dot(jnp.concatenate(pieces, axis=0), channel_hot, ((1,), (1,)))
    out_ref[0] = total[:rows] + total[rows : 2 * rows]
    out_ref[1] = total[2 * rows : 3 * rows] + total[3 * rows :]


def sample_grid(start, obs_token, obs_channel, obs_value, obs_var, rows, feat_width):
    count = obs_token.shape[0]
    return pl.pallas_call(
        sample_grid_kernel,
        out_shape=jax.ShapeDtypeStruct((2, rows, feat_width), F32),
        in_specs=[smem_spec()] + [vmem_spec()] * 4,
        out_specs=vmem_spec(),
        compiler_params=pltpu.CompilerParams(vmem_limit_bytes=VMEM_LIMIT),
        cost_estimate=pl.CostEstimate(flops=8 * rows * count * feat_width, bytes_accessed=16 * count, transcendentals=0),
        name="sample_grid",
    )(start, *(v.reshape(1, count) for v in (obs_token, obs_channel, obs_value, obs_var)))


def head_lanes(feat_width, heads):
    lane_head = iota((feat_width, LANES), 0) // (feat_width // heads)
    return (lane_head == iota((feat_width, LANES), 1)).astype(F32).astype(BF16)


def norm_bounds(values, heads):
    rows = values.shape[0] // FOLD
    squares = values * values
    folded = squares[:rows]
    for part in range(1, FOLD):
        folded = jnp.maximum(folded, squares[part * rows : (part + 1) * rows])
    return jnp.max(dot(folded.astype(BF16), head_lanes(values.shape[1], heads)), axis=0, keepdims=True)


def is_safe(query_norms, key_norms):
    return jnp.max(query_norms * key_norms) * 1.05 <= SAFE_SCORE * SAFE_SCORE


def query_scale(head_size):
    return math.log2(math.e) / math.sqrt(head_size)


def in_band(window, lower, upper, reach):
    apart = jnp.abs(iota((Q_ROWS, upper - lower), 1) + (lower - reach) - iota((Q_ROWS, upper - lower), 0))
    return apart <= window


def factor(mask):
    return jnp.where(mask, 1.0, 0.0).astype(BF16)


def group_lanes(group):
    return slice(group * LANES, (group + 1) * LANES)


def stacked_heads(queries, head_size):
    lane_head = iota((1, LANES), 1) // head_size
    masks = [(lane_head == head).astype(F32).astype(BF16) for head in range(LANES // head_size)]
    return jnp.concatenate([queries * mask for mask in masks], axis=0)


def put_values(buf, lower, values):
    for group in range(values.shape[1] // LANES):
        lanes = slice(2 * group * LANES, (2 * group + 1) * LANES)
        buf[lower : lower + values.shape[0], lanes] = values[:, group_lanes(group)]


def weighted_sums(weights, values, head_size):
    mixed_all = dot(weights, values)
    heads = LANES // head_size
    count = mixed_all.shape[0] // heads
    lane_head = iota((1, LANES), 1) // head_size
    mixed, totals = mixed_all[:count, :LANES], mixed_all[:count, LANES:]
    for head in range(1, heads):
        part = mixed_all[head * count : (head + 1) * count]
        mixed = jnp.where(lane_head == head, part[:, :LANES], mixed)
        totals = jnp.where(lane_head == head, part[:, LANES:], totals)
    return mixed, totals


def padded_lanes(values, before, after):
    pieces = [jnp.zeros((values.shape[0], before), BF16)] if before else []
    pieces.append(values)
    if after:
        pieces.append(jnp.zeros((values.shape[0], after), BF16))
    return jnp.concatenate(pieces, axis=1) if len(pieces) > 1 else pieces[0]


def unit_weights(scores, spans, band_of):
    width = scores.shape[1]
    count = len(spans) * Q_ROWS
    weights = []
    for head in range(scores.shape[0] // count):
        for block, (lower, upper) in enumerate(spans):
            top = head * count + block * Q_ROWS
            expo = jnp.exp2(scores[top : top + Q_ROWS, lower:upper]).astype(BF16)
            weights.append(padded_lanes(expo * band_of(head, block), lower, width - upper))
    return jnp.concatenate(weights, axis=0)


def inner_kernel(
    window_ref,
    own_ref,
    gain_ref,
    w_query_ref,
    w_key_ref,
    w_value_ref,
    query_ref,
    norm_ref,
    mixed_ref,
    total_ref,
    key_buf,
    value_buf,
    band_buf,
):
    rows, feat_width = own_ref.shape[1:]
    heads = window_ref.shape[0]
    head_size = feat_width // heads
    group_heads = LANES // head_size
    key_count = band_buf.shape[2]
    reach = (key_count - Q_ROWS) // 2
    reach_blocks = reach // Q_ROWS
    blocks = rows // Q_ROWS

    @pl.when(pl.program_id(0) == 0)
    def _():
        for head in range(heads):
            band_buf[head] = factor(in_band(window_ref[head], 0, key_count, reach))
        value_buf[...] = jnp.ones(value_buf.shape, BF16)

    batch = own_ref.shape[0]
    own = own_ref[...].reshape(batch * rows, feat_width).astype(F32)
    normed = rms_scaled(own, gain_ref[...]).astype(BF16)
    query_rows = dot(normed, w_query_ref[...]) * query_scale(head_size)
    key_rows = dot(normed, w_key_ref[...])
    value_rows = dot(normed, w_value_ref[...]).astype(BF16)
    query_norms, key_norms = norm_bounds(query_rows, heads), norm_bounds(key_rows, heads)
    blank = jnp.zeros((norm_ref.shape[1] - 2, LANES), F32)
    for member in range(batch):
        here = slice(member * rows, (member + 1) * rows)
        query_ref[member] = query_rows[here].astype(BF16)
        key_buf[member] = key_rows[here].astype(BF16).T
        put_values(value_buf.at[member], 0, value_rows[here])
        norm_ref[member] = jnp.concatenate([query_norms, key_norms, blank], axis=0)

    @pl.when(is_safe(query_norms, key_norms))
    def _():
        pairs = range(0, blocks, 2)
        groups = range(heads // group_heads)
        units = [(member, first, group) for member in range(batch) for first in pairs for group in groups]

        def scores_of(member, first, group):
            queries = query_ref[member, first * Q_ROWS : (first + 2) * Q_ROWS, group_lanes(group)]
            return dot(stacked_heads(queries, head_size), key_buf[member, group_lanes(group), :])

        scores = scores_of(*units[0])
        for at, (member, first, group) in enumerate(units):
            following = scores_of(*units[at + 1]) if at + 1 < len(units) else None
            ranges = [(max(0, b - reach_blocks), min(blocks, b + reach_blocks + 1)) for b in (first, first + 1)]
            spans = [(lower * Q_ROWS, upper * Q_ROWS) for lower, upper in ranges]

            def band_of(head, block):
                shift = (reach_blocks - first - block) * Q_ROWS
                lower, upper = spans[block]
                return band_buf[group * group_heads + head, :, lower + shift : upper + shift]

            values = value_buf[member, :, 2 * group * LANES : 2 * (group + 1) * LANES]
            mixed, totals = weighted_sums(unit_weights(scores, spans, band_of), values, head_size)
            here = slice(first * Q_ROWS, (first + 2) * Q_ROWS)
            mixed_ref[member, here, group_lanes(group)] = mixed
            total_ref[member, here, group_lanes(group)] = totals
            scores = following


def batch_of(members):
    return BATCH if members % BATCH == 0 else 1


def inner(head_window, own, gain, w_query, w_key, w_value, reach):
    members, rows, feat_width = own.shape
    heads = head_window.shape[0]
    key_count = Q_ROWS + 2 * reach
    shapes = [(own.shape, BF16), ((members, 8, LANES), F32), (own.shape, F32), (own.shape, F32)]

    batch = batch_of(members)

    def spec(shape):
        return pl.BlockSpec((batch, *shape[1:]), lambda m: (m, 0, 0))

    return pl.pallas_call(
        inner_kernel,
        grid=(members // batch,),
        out_shape=[jax.ShapeDtypeStruct(*v) for v in shapes],
        in_specs=[smem_spec(), spec(own.shape)] + [vmem_spec()] * 4,
        out_specs=[spec(shape) for shape, _ in shapes],
        scratch_shapes=[
            pltpu.VMEM((batch, feat_width, rows), BF16),
            pltpu.VMEM((batch, rows, 2 * feat_width), BF16),
            pltpu.VMEM((heads, Q_ROWS, key_count), BF16),
        ],
        compiler_params=pltpu.CompilerParams(vmem_limit_bytes=VMEM_LIMIT),
        cost_estimate=pl.CostEstimate(
            flops=own.size * (6 * feat_width + 16 * rows), bytes_accessed=14 * own.size, transcendentals=0
        ),
        name="inner",
    )(head_window, own, gain, w_query, w_key, w_value)


def forward_kernel(
    total_len,
    tok_ref,
    mem_ref,
    window_ref,
    state_ref,
    query_ref,
    norm_ref,
    inner_mixed_ref,
    inner_total_ref,
    near_ref,
    far_ref,
    attn_gain_ref,
    ffn_gain_ref,
    w_key_ref,
    w_value_ref,
    w_out_ref,
    w_gate_ref,
    w_up_ref,
    down_weight_ref,
    *refs,
):
    out_refs, (halo_key_buf, halo_value_buf, band_buf, mixed_buf, key_buf, value_buf, forecast_buf) = (
        refs[:-7],
        refs[-7:],
    )
    rows, feat_width = state_ref.shape[1:]
    reach = near_ref.shape[1]
    heads = window_ref.shape[0]
    head_size = feat_width // heads
    group_heads = LANES // head_size
    groups = heads // group_heads
    blocks = rows // Q_ROWS
    key_count = Q_ROWS + 2 * reach
    count = 2 * Q_ROWS
    first_pos = tok_ref[0] * rows

    @pl.when(pl.program_id(0) == 0)
    def _():
        first_valid = first_pos - reach >= 0
        last_valid = first_pos + rows + reach <= total_len
        for head in range(heads):
            window = window_ref[head]
            band_buf[0, head] = factor(in_band(jnp.where(first_valid, window, -1), 0, reach, reach))
            right_window = jnp.where(last_valid, window, -1)
            band_buf[1, head] = factor(in_band(right_window, key_count - reach, key_count, reach))
        halo_value_buf[...] = jnp.ones(halo_value_buf.shape, BF16)

    def keys_of(normed):
        return dot(normed, w_key_ref[...])

    def values_of(normed):
        return dot(normed, w_value_ref[...]).astype(BF16)

    odd = tok_ref[0] % 2 == 1
    batch = state_ref.shape[0]
    halo = []
    for member in range(batch):
        near, far = near_ref[member].astype(F32), far_ref[member].astype(F32)
        halo += [jnp.where(odd, near, far), jnp.where(odd, far, near)]
    normed = rms_scaled(jnp.concatenate(halo, axis=0), attn_gain_ref[...]).astype(BF16)
    halo_keys = keys_of(normed)
    halo_values = values_of(normed)
    query_norms = jnp.max(norm_ref[:, 0, :], axis=0, keepdims=True)
    key_norms = jnp.maximum(jnp.max(norm_ref[:, 1, :], axis=0, keepdims=True), norm_bounds(halo_keys, heads))
    for at in range(2 * batch):
        here = slice(at * reach, (at + 1) * reach)
        halo_key_buf[at] = halo_keys[here].astype(BF16).T
        put_values(halo_value_buf.at[at], 0, halo_values[here])
    safe = is_safe(query_norms, key_norms)

    @pl.when(safe)
    def _():
        units = [(member, side, group) for member in range(batch) for side in range(2) for group in range(groups)]

        def scores_of(member, side, group):
            start = side * (rows - count)
            queries = query_ref[member, start : start + count, group_lanes(group)]
            return dot(stacked_heads(queries, head_size), halo_key_buf[2 * member + side, group_lanes(group), :])

        scores = scores_of(*units[0])
        for at, (member, side, group) in enumerate(units):
            following = scores_of(*units[at + 1]) if at + 1 < len(units) else None
            spans = [(0, reach), (Q_ROWS, reach)] if side == 0 else [(0, reach - Q_ROWS), (0, reach)]

            def band_of(head, block):
                lower, upper = spans[block]
                shift = -block * Q_ROWS if side == 0 else (1 - block) * Q_ROWS
                return band_buf[side, group * group_heads + head, :, lower + shift : upper + shift]

            values = halo_value_buf[2 * member + side, :, 2 * group * LANES : 2 * (group + 1) * LANES]
            mixed, totals = weighted_sums(unit_weights(scores, spans, band_of), values, head_size)
            start = side * (rows - count)
            here = slice(start, start + count)
            mixed = mixed + inner_mixed_ref[member, here, group_lanes(group)]
            totals = totals + inner_total_ref[member, here, group_lanes(group)]
            start += member * rows
            mixed_buf[start : start + count, group_lanes(group)] = (mixed / totals).astype(BF16)
            scores = following

    @pl.when(jnp.logical_not(safe))
    def _():
        for member in range(batch):
            normed = rms_scaled(state_ref[member].astype(F32), attn_gain_ref[...]).astype(BF16)
            key_buf[:, :reach] = halo_key_buf[2 * member]
            key_buf[:, reach : reach + rows] = keys_of(normed).astype(BF16).T
            key_buf[:, reach + rows :] = halo_key_buf[2 * member + 1]
            value_buf[...] = jnp.ones(value_buf.shape, BF16)
            put_values(value_buf, reach, values_of(normed))
            value_buf[:reach] = halo_value_buf[2 * member]
            value_buf[reach + rows :] = halo_value_buf[2 * member + 1]
            for block in range(blocks):
                start = block * Q_ROWS
                k_pos = first_pos - reach + start + iota((Q_ROWS, key_count), 1)
                inside = (k_pos >= 0) & (k_pos < total_len)
                for group in range(groups):
                    queries = query_ref[member, start : start + Q_ROWS, group_lanes(group)]
                    keys = key_buf[group_lanes(group), start : start + key_count]
                    scores = dot(stacked_heads(queries, head_size), keys)
                    weights = []
                    for head in range(group_heads):
                        allowed = inside & in_band(window_ref[group * group_heads + head], 0, key_count, reach)
                        score_matrix = jnp.where(allowed, scores[head * Q_ROWS : (head + 1) * Q_ROWS], -1e30)
                        row_top = jnp.max(score_matrix, axis=-1, keepdims=True)
                        weights.append(jnp.exp2(score_matrix - row_top).astype(BF16))
                    values = value_buf[start : start + key_count, 2 * group * LANES : 2 * (group + 1) * LANES]
                    mixed, totals = weighted_sums(jnp.concatenate(weights, axis=0), values, head_size)
                    here = slice(member * rows + start, member * rows + start + Q_ROWS)
                    mixed_buf[here, group_lanes(group)] = (mixed / totals).astype(BF16)

    state = state_ref[...].reshape(batch * rows, feat_width).astype(F32)
    after = (state + dot(mixed_buf[...], w_out_ref[...])).astype(BF16)
    normed_mid = rms_scaled(after.astype(F32), ffn_gain_ref[...]).astype(BF16)
    forecast = after.astype(F32)
    for lower in range(0, w_gate_ref.shape[1], HIDDEN_CHUNK):
        part = slice(lower, lower + HIDDEN_CHUNK)
        gate = 0.5 * dot(normed_mid, w_gate_ref[:, part])
        hidden = (gate * (1.0 + jnp.tanh(gate.astype(BF16)).astype(F32)) * dot(normed_mid, w_up_ref[:, part])).astype(BF16)
        forecast += dot(hidden, down_weight_ref[part, :])
    forecast_buf[...] = forecast.astype(BF16)
    share_rows = out_refs[0].shape[1]
    for part, out_ref in enumerate(out_refs):
        lower = pl.multiple_of((mem_ref[0] ^ part) * share_rows, share_rows)
        for member in range(batch):
            out_ref[member] = forecast_buf[pl.ds(member * rows + lower, share_rows), :]


def forward(total_len, tok_index, mem_index, head_window, own, inner_parts, near, far, gains, weights, shares):
    members, row_count, feat_width = own.shape
    reach = near.shape[1]
    heads = head_window.shape[0]
    hidden_width = weights[3].shape[1]
    macs = members * row_count * feat_width * (3 * feat_width + 3 * hidden_width + 4 * reach)
    batch = batch_of(members)
    share_rows = row_count // shares

    def spec(array):
        return pl.BlockSpec((batch, *array.shape[1:]), lambda m: (m, 0, 0))

    return pl.pallas_call(
        functools.partial(forward_kernel, total_len),
        grid=(members // batch,),
        out_shape=[jax.ShapeDtypeStruct((members, share_rows, feat_width), BF16)] * shares,
        in_specs=[smem_spec()] * 3
        + [spec(v) for v in (own, *inner_parts, near, far)]
        + [vmem_spec()] * (len(gains) + len(weights)),
        out_specs=[pl.BlockSpec((batch, share_rows, feat_width), lambda m: (m, 0, 0))] * shares,
        scratch_shapes=[
            pltpu.VMEM((2 * batch, feat_width, reach), BF16),
            pltpu.VMEM((2 * batch, reach, 2 * feat_width), BF16),
            pltpu.VMEM((2, heads, Q_ROWS, reach), BF16),
            pltpu.VMEM((batch * row_count, feat_width), BF16),
            pltpu.VMEM((feat_width, row_count + 2 * reach), BF16),
            pltpu.VMEM((row_count + 2 * reach, 2 * feat_width), BF16),
            pltpu.VMEM((batch * row_count, feat_width), BF16),
        ],
        compiler_params=pltpu.CompilerParams(vmem_limit_bytes=VMEM_LIMIT),
        cost_estimate=pl.CostEstimate(flops=2 * macs, bytes_accessed=10 * own.size, transcendentals=0),
        name="forward",
    )(tok_index, mem_index, head_window, own, *inner_parts, near, far, *gains, *weights)


def global_member(held, index, own_members):
    return ((held // own_members) ^ index) * own_members + held % own_members


def gram_kernel(index_ref, *refs):
    share_refs, grid_ref, out_ref = refs[:-2], refs[-2], refs[-1]
    own_members, rows, feat_width = share_refs[0].shape
    members = own_members * len(share_refs)
    index = index_ref[0]
    stack = members * GROUP
    total = jnp.zeros((stack, stack), F32)
    proj = jnp.zeros((members, GROUP, feat_width), F32)
    for lower in range(0, rows, GROUP):
        part = slice(lower, lower + GROUP)
        fields = jnp.concatenate([ref[:, part, :] for ref in share_refs], axis=0).astype(F32)
        mean = jnp.sum(fields, axis=0) * (1.0 / members)
        spread = fields - mean[None]
        weight = grid_ref[0, part, :]
        proj += spread * (grid_ref[1, part, :] - weight * mean)[None]
        high, low = halves(spread.reshape(stack, feat_width))
        w_high, w_low = halves((spread * weight[None]).reshape(stack, feat_width))
        last = ((1,), (1,))
        total += dot(w_high, high, last) + dot(w_high, low, last) + dot(w_low, high, last)
    same = iota((stack, stack), 0) % GROUP == iota((stack, stack), 1) % GROUP
    by_row = jnp.sum(jnp.where(same, total, 0.0).reshape(members, GROUP, stack), axis=1)
    column = global_member(iota((stack, LANES), 0) // GROUP, index, own_members)
    folded = (column == iota((stack, LANES), 1) % members).astype(F32)
    held = global_member(iota((members, members), 1), index, own_members)
    in_order = (held == iota((members, members), 0)).astype(F32)
    tiled = exact_dot(in_order, exact_dot(by_row, folded))
    per_row = LANES // members
    keep = iota((members, LANES), 0) % per_row == iota((members, LANES), 1) // members
    packed = jnp.sum(jnp.where(keep, tiled, 0.0).reshape(members // per_row, per_row, LANES), axis=1)
    proj_col = jnp.sum(jnp.sum(proj, axis=1), axis=1, keepdims=True)
    at_lane = global_member(iota((members, LANES), 0), index, own_members) == iota((members, LANES), 1)
    proj_row = jnp.sum(jnp.where(at_lane, proj_col, 0.0), axis=0, keepdims=True)
    filled = members // per_row + 1
    blank = jnp.zeros((out_ref.shape[0] - filled, LANES), F32)
    out_ref[...] = jnp.concatenate([packed, proj_row, blank], axis=0)


def gram_partial(index, shares, grid):
    members = shares[0].shape[0] * len(shares)
    filled = members * members // LANES + 1
    return pl.pallas_call(
        gram_kernel,
        out_shape=jax.ShapeDtypeStruct((-(-filled // 8) * 8, LANES), F32),
        in_specs=[smem_spec()] + [vmem_spec()] * (len(shares) + 1),
        out_specs=vmem_spec(),
        compiler_params=pltpu.CompilerParams(vmem_limit_bytes=VMEM_LIMIT),
        cost_estimate=pl.CostEstimate(
            flops=3 * GROUP * members * members * grid.size, bytes_accessed=members * grid.size, transcendentals=0
        ),
        name="gram",
    )(index, *shares, grid)


def repeated_dot(a, b):
    size = a.shape[0]

    def pieces(values):
        first = values.astype(BF16).astype(F32)
        rest = values - first
        second = rest.astype(BF16).astype(F32)
        return first, second, rest - second

    block = iota(a.shape, 1) // size
    a_first, a_second, a_third = pieces(a)
    b_first, b_second, b_third = (piece.astype(BF16) for piece in pieces(b))
    left = jnp.where((block == 2) | (block == 4), a_second, jnp.where(block == 5, a_third, a_first))
    right = jnp.concatenate([b_first, b_second, b_first, b_third, b_second, b_first], axis=0)
    return dot(left.astype(BF16), right)


def ensemble_transform(gram, proj):
    members = gram.shape[0]
    row, column = iota((members, members), 0), iota((members, members), 1)
    identity = (row == column).astype(F32)
    system = gram + (members - 1.0) * identity
    left, right = system, proj
    for pivot in range(members):
        is_pivot = iota((members, 1), 0) == pivot
        scale = 1.0 / left[pivot : pivot + 1, pivot : pivot + 1]
        pivot_row = left[pivot : pivot + 1, :] * scale
        pivot_right = right[pivot : pivot + 1, :] * scale
        factor = left[:, pivot : pivot + 1]
        left = jnp.where(is_pivot, pivot_row, left - factor * pivot_row)
        right = jnp.where(is_pivot, pivot_right, right - factor * pivot_right)
    mean_weights = right
    mean_level = jnp.sum(jnp.sum(system * identity, axis=1, keepdims=True), axis=0, keepdims=True) / members
    lifted = system + (mean_level - (members - 1.0)) * (1.0 / members)
    frobenius = jnp.sqrt(jnp.sum(jnp.sum(lifted * lifted, axis=1, keepdims=True), axis=0, keepdims=True))
    root_iter = jnp.concatenate([lifted / frobenius] * PASSES, axis=1)
    repeated = iota((members, PASSES * members), 1) % members == iota((members, PASSES * members), 0)
    repeated = repeated.astype(F32)
    inv_iter = repeated
    for sweep in range(NS_STEPS):
        product = root_iter if sweep == 0 else repeated_dot(inv_iter, root_iter)
        correction = 1.5 * repeated - 0.5 * product
        inv_iter = correction if sweep == 0 else repeated_dot(correction, inv_iter)
        if sweep < NS_STEPS - 1:
            root_iter = repeated_dot(root_iter, correction)
    inv_iter = inv_iter[:, :members]
    inv_root = inv_iter / jnp.sqrt(frobenius) + (1.0 / math.sqrt(members - 1.0) - 1.0 / jnp.sqrt(mean_level)) * (
        1.0 / members
    )
    moved = mean_weights + math.sqrt(members - 1.0) * inv_root
    return 1.0 / members + moved - jnp.sum(moved, axis=0, keepdims=True) * (1.0 / members)


def combine_kernel(index_ref, partial_ref, *refs):
    share_refs, out_refs = refs[: len(refs) // 2], refs[len(refs) // 2 :]
    own_members, rows, feat_width = share_refs[0].shape
    members = own_members * len(share_refs)
    stack = members * GROUP
    per_row = LANES // members
    sums = jnp.sum(partial_ref[...], axis=0)
    spread_rows = jnp.concatenate(
        [jnp.broadcast_to(sums[r : r + 1], (per_row, LANES)) for r in range(members // per_row)], axis=0
    )
    keep = iota((members, LANES), 0) % per_row == iota((members, LANES), 1) // members
    folded = (iota((LANES, members), 0) % members == iota((LANES, members), 1)).astype(F32)
    gram = exact_dot(jnp.where(keep, spread_rows, 0.0), folded)
    proj_row = jnp.broadcast_to(sums[members // per_row : members // per_row + 1], (members, LANES))
    on_diagonal = iota((members, LANES), 0) == iota((members, LANES), 1)
    proj = jnp.sum(jnp.where(on_diagonal, proj_row, 0.0), axis=1, keepdims=True)
    transform = ensemble_transform(gram, proj)
    held = global_member(iota((stack, members), 0) // GROUP, index_ref[0], own_members)
    pick = (held == iota((stack, members), 1)).astype(F32).astype(BF16)
    same = iota((stack, stack), 0) % GROUP == iota((stack, stack), 1) % GROUP
    mixers = []
    for piece in halves(transform):
        rows_of = dot(pick, piece, ((1,), (1,))).astype(BF16)
        mixers.append(jnp.where(same, dot(rows_of, pick, ((1,), (1,))), 0.0).astype(BF16))
    for lower in range(0, rows, GROUP):
        part = slice(lower, lower + GROUP)
        fields = jnp.concatenate([ref[:, part, :].reshape(-1, feat_width) for ref in share_refs], axis=0)
        mixed = (dot(mixers[0], fields) + dot(mixers[1], fields)).astype(BF16)
        own_stack = own_members * GROUP
        for at, out_ref in enumerate(out_refs):
            piece = mixed[at * own_stack : (at + 1) * own_stack]
            out_ref[:, part, :] = piece.reshape(own_members, GROUP, feat_width)


def combine(index, partials, shares):
    size = shares[0].size * len(shares)
    members = shares[0].shape[0] * len(shares)
    return pl.pallas_call(
        combine_kernel,
        out_shape=[jax.ShapeDtypeStruct(v.shape, BF16) for v in shares],
        in_specs=[smem_spec()] + [vmem_spec()] * (1 + len(shares)),
        out_specs=[vmem_spec()] * len(shares),
        compiler_params=pltpu.CompilerParams(vmem_limit_bytes=VMEM_LIMIT),
        cost_estimate=pl.CostEstimate(flops=4 * GROUP * members * size, bytes_accessed=4 * size, transcendentals=0),
        name="combine",
    )(index, partials, *shares)


def assemble_kernel(index_ref, *refs):
    part_refs, out_ref, sems = refs[:-2], refs[-2], refs[-1]
    rows = part_refs[0].shape[1]
    copies = []
    for part, ref in enumerate(part_refs):
        lower = pl.multiple_of((index_ref[0] ^ part) * rows, rows)
        copies.append(pltpu.make_async_copy(ref, out_ref.at[:, pl.ds(lower, rows), :], sems.at[part]))
    for copy in copies:
        copy.start()
    for copy in copies:
        copy.wait()


def assemble(index, parts):
    members, rows, feat_width = parts[0].shape
    return pl.pallas_call(
        assemble_kernel,
        out_shape=jax.ShapeDtypeStruct((members, len(parts) * rows, feat_width), BF16),
        in_specs=[smem_spec()] + [vmem_spec()] * len(parts),
        out_specs=pl.BlockSpec(memory_space=pl.ANY),
        scratch_shapes=[pltpu.SemaphoreType.DMA((len(parts),))],
        compiler_params=pltpu.CompilerParams(vmem_limit_bytes=VMEM_LIMIT),
        cost_estimate=pl.CostEstimate(flops=0, bytes_accessed=4 * len(parts) * parts[0].size, transcendentals=0),
        name="assemble",
    )(index, *parts)


def exchanged(parts):
    count = lax.axis_size("mem")
    return [
        lax.ppermute(v, "mem", [(i, i ^ part) for i in range(count)]) if part else v for part, v in enumerate(parts)
    ]


def halos(own, reach):
    count = lax.axis_size("tok")
    odd = lax.axis_index("tok") % 2
    last = own.shape[1] - reach
    near = lax.dynamic_slice_in_dim(own, (1 - odd) * last, reach, axis=1)
    far = lax.dynamic_slice_in_dim(own, odd * last, reach, axis=1)
    near_pairs = [(i, i ^ 1) for i in range(count)]
    far_pairs = [pair for i in range(1, count - 1, 2) for pair in ((i, i + 1), (i + 1, i))]
    return lax.ppermute(near, "tok", near_pairs), lax.ppermute(far, "tok", far_pairs)


def local(
    ens_state,
    attn_gain,
    ffn_gain,
    w_query,
    w_key,
    w_value,
    w_out,
    w_gate,
    w_up,
    down_weight,
    head_window,
    obs_token,
    obs_channel,
    obs_value,
    obs_var,
):
    own_members, row_count, feat_width = ens_state.shape
    mem_count = lax.axis_size("mem")
    tok_count = lax.axis_size("tok")
    device_count = mem_count * tok_count
    share_rows = row_count // mem_count
    first_pos = lax.axis_index("tok") * row_count
    near_halo, far_halo = halos(ens_state, WIN)
    share_start = first_pos + lax.axis_index("mem") * share_rows
    grid = sample_grid(
        share_start.astype(jnp.int32).reshape(1), obs_token, obs_channel, obs_value, obs_var, share_rows, feat_width
    )
    mem_index = lax.axis_index("mem").astype(jnp.int32).reshape(1)
    tok_index = lax.axis_index("tok").astype(jnp.int32).reshape(1)
    gains = [attn_gain.reshape(1, -1), ffn_gain.reshape(1, -1)]
    inner_parts = inner(head_window, ens_state, gains[0], w_query, w_key, w_value, WIN)
    weights = [w_key, w_value, w_out, w_gate, w_up, down_weight]
    total_len = row_count * tok_count
    forecast = forward(
        total_len, tok_index, mem_index, head_window, ens_state, inner_parts, near_halo, far_halo, gains, weights, mem_count
    )
    shares = exchanged(forecast)
    partial = gram_partial(mem_index, shares, grid)
    partials = lax.all_to_all(
        jnp.broadcast_to(partial[None], (device_count, *partial.shape)),
        ("mem", "tok"),
        split_axis=0,
        concat_axis=0,
        tiled=True,
    )
    return assemble(mem_index, exchanged(combine(mem_index, partials, shares)))


def solution(mesh):
    in_specs = (P("mem", "tok", None), *[P()] * 10, *[P("tok")] * 4)
    return jax.shard_map(local, mesh=mesh, in_specs=in_specs, out_specs=P("mem", "tok", None), check_vma=False)
```

```python
import functools
import math

import jax
import jax.numpy as jnp
from jax import lax
from jax.experimental import pallas as pl
from jax.experimental.pallas import tpu as pltpu
from jax.sharding import PartitionSpec as P

WIN = 256
NS_STEPS = 8
EPS = 1e-05
Q_ROWS = 128
GROUP = 16
LANES = 128
VMEM_LIMIT = 32 * 1024 * 1024
SAFE_SCORE = 100.0
FOLD = 4
BATCH = 2
PASSES = 6
HIDDEN_CHUNK = 256

F32 = jnp.float32
BF16 = jnp.bfloat16


def dot(a, b, contract=((1,), (0,)), precision=None):
    return lax.dot_general(a, b, (contract, ((), ())), precision=precision, preferred_element_type=F32)


def exact_dot(a, b, contract=((1,), (0,))):
    return dot(a, b, contract, lax.Precision.HIGHEST)


def iota(shape, axis):
    return lax.broadcasted_iota(jnp.int32, shape, axis)


def halves(values):
    high = values.astype(BF16)
    return high, (values - high.astype(F32)).astype(BF16)


def rms_scaled(values, gain):
    return values * lax.rsqrt(jnp.mean(values * values, axis=-1, keepdims=True) + EPS) * gain


def vmem_spec():
    return pl.BlockSpec(memory_space=pltpu.VMEM)


def smem_spec():
    return pl.BlockSpec(memory_space=pltpu.SMEM)


def sample_grid_kernel(start_ref, token_ref, channel_ref, value_ref, var_ref, out_ref):
    rows, feat_width = out_ref.shape[1:]
    count = token_ref.shape[1]
    chunk = min(1024, count)
    total = jnp.zeros((4 * rows, feat_width), F32)
    for lower in range(0, count, chunk):
        part = slice(lower, lower + chunk)
        inv_var = 1.0 / var_ref[:, part]
        weighted = value_ref[:, part] * inv_var
        here = iota((rows, chunk), 0) == token_ref[:, part] - start_ref[0]
        pieces = []
        for row in (inv_var, weighted):
            high = row.astype(BF16).astype(F32)
            pieces.append(jnp.where(here, high, 0.0).astype(BF16))
            pieces.append(jnp.where(here, row - high, 0.0).astype(BF16))
        channel_hot = jnp.where(iota((feat_width, chunk), 0) == channel_ref[:, part], 1.0, 0.0).astype(BF16)
        total += dot(jnp.concatenate(pieces, axis=0), channel_hot, ((1,), (1,)))
    out_ref[0] = total[:rows] + total[rows : 2 * rows]
    out_ref[1] = total[2 * rows : 3 * rows] + total[3 * rows :]


def sample_grid(start, obs_token, obs_channel, obs_value, obs_var, rows, feat_width):
    count = obs_token.shape[0]
    return pl.pallas_call(
        sample_grid_kernel,
        out_shape=jax.ShapeDtypeStruct((2, rows, feat_width), F32),
        in_specs=[smem_spec()] + [vmem_spec()] * 4,
        out_specs=vmem_spec(),
        compiler_params=pltpu.CompilerParams(vmem_limit_bytes=VMEM_LIMIT),
        cost_estimate=pl.CostEstimate(flops=8 * rows * count * feat_width, bytes_accessed=16 * count, transcendentals=0),
        name="sample_grid",
    )(start, *(v.reshape(1, count) for v in (obs_token, obs_channel, obs_value, obs_var)))


def head_lanes(feat_width, heads):
    lane_head = iota((feat_width, LANES), 0) // (feat_width // heads)
    return (lane_head == iota((feat_width, LANES), 1)).astype(F32).astype(BF16)


def norm_bounds(values, heads):
    rows = values.shape[0] // FOLD
    squares = values * values
    folded = squares[:rows]
    for part in range(1, FOLD):
        folded = jnp.maximum(folded, squares[part * rows : (part + 1) * rows])
    return jnp.max(dot(folded.astype(BF16), head_lanes(values.shape[1], heads)), axis=0, keepdims=True)


def is_safe(query_norms, key_norms):
    return jnp.max(query_norms * key_norms) * 1.05 <= SAFE_SCORE * SAFE_SCORE


def query_scale(head_size):
    return math.log2(math.e) / math.sqrt(head_size)


def in_band(window, lower, upper, reach):
    apart = jnp.abs(iota((Q_ROWS, upper - lower), 1) + (lower - reach) - iota((Q_ROWS, upper - lower), 0))
    return apart <= window


def factor(mask):
    return jnp.where(mask, 1.0, 0.0).astype(BF16)


def group_lanes(group):
    return slice(group * LANES, (group + 1) * LANES)


def stacked_heads(queries, head_size):
    lane_head = iota((1, LANES), 1) // head_size
    masks = [(lane_head == head).astype(F32).astype(BF16) for head in range(LANES // head_size)]
    return jnp.concatenate([queries * mask for mask in masks], axis=0)


def put_values(buf, lower, values):
    for group in range(values.shape[1] // LANES):
        lanes = slice(2 * group * LANES, (2 * group + 1) * LANES)
        buf[lower : lower + values.shape[0], lanes] = values[:, group_lanes(group)]


def weighted_sums(weights, values, head_size):
    mixed_all = dot(weights, values)
    heads = LANES // head_size
    count = mixed_all.shape[0] // heads
    lane_head = iota((1, LANES), 1) // head_size
    mixed, totals = mixed_all[:count, :LANES], mixed_all[:count, LANES:]
    for head in range(1, heads):
        part = mixed_all[head * count : (head + 1) * count]
        mixed = jnp.where(lane_head == head, part[:, :LANES], mixed)
        totals = jnp.where(lane_head == head, part[:, LANES:], totals)
    return mixed, totals


def padded_lanes(values, before, after):
    pieces = [jnp.zeros((values.shape[0], before), BF16)] if before else []
    pieces.append(values)
    if after:
        pieces.append(jnp.zeros((values.shape[0], after), BF16))
    return jnp.concatenate(pieces, axis=1) if len(pieces) > 1 else pieces[0]


def unit_weights(scores, spans, band_of):
    width = scores.shape[1]
    count = len(spans) * Q_ROWS
    weights = []
    for head in range(scores.shape[0] // count):
        for block, (lower, upper) in enumerate(spans):
            top = head * count + block * Q_ROWS
            expo = jnp.exp2(scores[top : top + Q_ROWS, lower:upper]).astype(BF16)
            weights.append(padded_lanes(expo * band_of(head, block), lower, width - upper))
    return jnp.concatenate(weights, axis=0)


def inner_kernel(
    window_ref,
    own_ref,
    gain_ref,
    w_query_ref,
    w_key_ref,
    w_value_ref,
    query_ref,
    norm_ref,
    mixed_ref,
    total_ref,
    key_buf,
    value_buf,
    band_buf,
):
    rows, feat_width = own_ref.shape[1:]
    heads = window_ref.shape[0]
    head_size = feat_width // heads
    group_heads = LANES // head_size
    key_count = band_buf.shape[2]
    reach = (key_count - Q_ROWS) // 2
    reach_blocks = reach // Q_ROWS
    blocks = rows // Q_ROWS

    @pl.when(pl.program_id(0) == 0)
    def _():
        for head in range(heads):
            band_buf[head] = factor(in_band(window_ref[head], 0, key_count, reach))
        value_buf[...] = jnp.ones(value_buf.shape, BF16)

    batch = own_ref.shape[0]
    own = own_ref[...].reshape(batch * rows, feat_width).astype(F32)
    normed = rms_scaled(own, gain_ref[...]).astype(BF16)
    query_rows = dot(normed, w_query_ref[...]) * query_scale(head_size)
    key_rows = dot(normed, w_key_ref[...])
    value_rows = dot(normed, w_value_ref[...]).astype(BF16)
    query_norms, key_norms = norm_bounds(query_rows, heads), norm_bounds(key_rows, heads)
    blank = jnp.zeros((norm_ref.shape[1] - 2, LANES), F32)
    for member in range(batch):
        here = slice(member * rows, (member + 1) * rows)
        query_ref[member] = query_rows[here].astype(BF16)
        key_buf[member] = key_rows[here].astype(BF16).T
        put_values(value_buf.at[member], 0, value_rows[here])
        norm_ref[member] = jnp.concatenate([query_norms, key_norms, blank], axis=0)

    @pl.when(is_safe(query_norms, key_norms))
    def _():
        pairs = range(0, blocks, 2)
        groups = range(heads // group_heads)
        units = [(member, first, group) for member in range(batch) for first in pairs for group in groups]

        def scores_of(member, first, group):
            queries = query_ref[member, first * Q_ROWS : (first + 2) * Q_ROWS, group_lanes(group)]
            return dot(stacked_heads(queries, head_size), key_buf[member, group_lanes(group), :])

        scores = scores_of(*units[0])
        for at, (member, first, group) in enumerate(units):
            following = scores_of(*units[at + 1]) if at + 1 < len(units) else None
            ranges = [(max(0, b - reach_blocks), min(blocks, b + reach_blocks + 1)) for b in (first, first + 1)]
            spans = [(lower * Q_ROWS, upper * Q_ROWS) for lower, upper in ranges]

            def band_of(head, block):
                shift = (reach_blocks - first - block) * Q_ROWS
                lower, upper = spans[block]
                return band_buf[group * group_heads + head, :, lower + shift : upper + shift]

            values = value_buf[member, :, 2 * group * LANES : 2 * (group + 1) * LANES]
            mixed, totals = weighted_sums(unit_weights(scores, spans, band_of), values, head_size)
            here = slice(first * Q_ROWS, (first + 2) * Q_ROWS)
            mixed_ref[member, here, group_lanes(group)] = mixed
            total_ref[member, here, group_lanes(group)] = totals
            scores = following


def batch_of(members):
    return BATCH if members % BATCH == 0 else 1


def inner(head_window, own, gain, w_query, w_key, w_value, reach):
    members, rows, feat_width = own.shape
    heads = head_window.shape[0]
    key_count = Q_ROWS + 2 * reach
    shapes = [(own.shape, BF16), ((members, 8, LANES), F32), (own.shape, F32), (own.shape, F32)]

    batch = batch_of(members)

    def spec(shape):
        return pl.BlockSpec((batch, *shape[1:]), lambda m: (m, 0, 0))

    return pl.pallas_call(
        inner_kernel,
        grid=(members // batch,),
        out_shape=[jax.ShapeDtypeStruct(*v) for v in shapes],
        in_specs=[smem_spec(), spec(own.shape)] + [vmem_spec()] * 4,
        out_specs=[spec(shape) for shape, _ in shapes],
        scratch_shapes=[
            pltpu.VMEM((batch, feat_width, rows), BF16),
            pltpu.VMEM((batch, rows, 2 * feat_width), BF16),
            pltpu.VMEM((heads, Q_ROWS, key_count), BF16),
        ],
        compiler_params=pltpu.CompilerParams(vmem_limit_bytes=VMEM_LIMIT),
        cost_estimate=pl.CostEstimate(
            flops=own.size * (6 * feat_width + 16 * rows), bytes_accessed=14 * own.size, transcendentals=0
        ),
        name="inner",
    )(head_window, own, gain, w_query, w_key, w_value)


def forward_kernel(
    total_len,
    tok_ref,
    mem_ref,
    window_ref,
    state_ref,
    query_ref,
    norm_ref,
    inner_mixed_ref,
    inner_total_ref,
    near_ref,
    far_ref,
    attn_gain_ref,
    ffn_gain_ref,
    w_key_ref,
    w_value_ref,
    w_out_ref,
    w_gate_ref,
    w_up_ref,
    down_weight_ref,
    *refs,
):
    out_refs, (halo_key_buf, halo_value_buf, band_buf, mixed_buf, key_buf, value_buf, forecast_buf) = (
        refs[:-7],
        refs[-7:],
    )
    rows, feat_width = state_ref.shape[1:]
    reach = near_ref.shape[1]
    heads = window_ref.shape[0]
    head_size = feat_width // heads
    group_heads = LANES // head_size
    groups = heads // group_heads
    blocks = rows // Q_ROWS
    key_count = Q_ROWS + 2 * reach
    count = 2 * Q_ROWS
    first_pos = tok_ref[0] * rows

    @pl.when(pl.program_id(0) == 0)
    def _():
        first_valid = first_pos - reach >= 0
        last_valid = first_pos + rows + reach <= total_len
        for head in range(heads):
            window = window_ref[head]
            band_buf[0, head] = factor(in_band(jnp.where(first_valid, window, -1), 0, reach, reach))
            right_window = jnp.where(last_valid, window, -1)
            band_buf[1, head] = factor(in_band(right_window, key_count - reach, key_count, reach))
        halo_value_buf[...] = jnp.ones(halo_value_buf.shape, BF16)

    def keys_of(normed):
        return dot(normed, w_key_ref[...])

    def values_of(normed):
        return dot(normed, w_value_ref[...]).astype(BF16)

    odd = tok_ref[0] % 2 == 1
    batch = state_ref.shape[0]
    halo = []
    for member in range(batch):
        near, far = near_ref[member].astype(F32), far_ref[member].astype(F32)
        halo += [jnp.where(odd, near, far), jnp.where(odd, far, near)]
    normed = rms_scaled(jnp.concatenate(halo, axis=0), attn_gain_ref[...]).astype(BF16)
    halo_keys = keys_of(normed)
    halo_values = values_of(normed)
    query_norms = jnp.max(norm_ref[:, 0, :], axis=0, keepdims=True)
    key_norms = jnp.maximum(jnp.max(norm_ref[:, 1, :], axis=0, keepdims=True), norm_bounds(halo_keys, heads))
    for at in range(2 * batch):
        here = slice(at * reach, (at + 1) * reach)
        halo_key_buf[at] = halo_keys[here].astype(BF16).T
        put_values(halo_value_buf.at[at], 0, halo_values[here])
    safe = is_safe(query_norms, key_norms)

    @pl.when(safe)
    def _():
        units = [(member, side, group) for member in range(batch) for side in range(2) for group in range(groups)]

        def scores_of(member, side, group):
            start = side * (rows - count)
            queries = query_ref[member, start : start + count, group_lanes(group)]
            return dot(stacked_heads(queries, head_size), halo_key_buf[2 * member + side, group_lanes(group), :])

        scores = scores_of(*units[0])
        for at, (member, side, group) in enumerate(units):
            following = scores_of(*units[at + 1]) if at + 1 < len(units) else None
            spans = [(0, reach), (Q_ROWS, reach)] if side == 0 else [(0, reach - Q_ROWS), (0, reach)]

            def band_of(head, block):
                lower, upper = spans[block]
                shift = -block * Q_ROWS if side == 0 else (1 - block) * Q_ROWS
                return band_buf[side, group * group_heads + head, :, lower + shift : upper + shift]

            values = halo_value_buf[2 * member + side, :, 2 * group * LANES : 2 * (group + 1) * LANES]
            mixed, totals = weighted_sums(unit_weights(scores, spans, band_of), values, head_size)
            start = side * (rows - count)
            here = slice(start, start + count)
            mixed = mixed + inner_mixed_ref[member, here, group_lanes(group)]
            totals = totals + inner_total_ref[member, here, group_lanes(group)]
            start += member * rows
            mixed_buf[start : start + count, group_lanes(group)] = (mixed / totals).astype(BF16)
            scores = following

    @pl.when(jnp.logical_not(safe))
    def _():
        for member in range(batch):
            normed = rms_scaled(state_ref[member].astype(F32), attn_gain_ref[...]).astype(BF16)
            key_buf[:, :reach] = halo_key_buf[2 * member]
            key_buf[:, reach : reach + rows] = keys_of(normed).astype(BF16).T
            key_buf[:, reach + rows :] = halo_key_buf[2 * member + 1]
            value_buf[...] = jnp.ones(value_buf.shape, BF16)
            put_values(value_buf, reach, values_of(normed))
            value_buf[:reach] = halo_value_buf[2 * member]
            value_buf[reach + rows :] = halo_value_buf[2 * member + 1]
            for block in range(blocks):
                start = block * Q_ROWS
                k_pos = first_pos - reach + start + iota((Q_ROWS, key_count), 1)
                inside = (k_pos >= 0) & (k_pos < total_len)
                for group in range(groups):
                    queries = query_ref[member, start : start + Q_ROWS, group_lanes(group)]
                    keys = key_buf[group_lanes(group), start : start + key_count]
                    scores = dot(stacked_heads(queries, head_size), keys)
                    weights = []
                    for head in range(group_heads):
                        allowed = inside & in_band(window_ref[group * group_heads + head], 0, key_count, reach)
                        score_matrix = jnp.where(allowed, scores[head * Q_ROWS : (head + 1) * Q_ROWS], -1e30)
                        row_top = jnp.max(score_matrix, axis=-1, keepdims=True)
                        weights.append(jnp.exp2(score_matrix - row_top).astype(BF16))
                    values = value_buf[start : start + key_count, 2 * group * LANES : 2 * (group + 1) * LANES]
                    mixed, totals = weighted_sums(jnp.concatenate(weights, axis=0), values, head_size)
                    here = slice(member * rows + start, member * rows + start + Q_ROWS)
                    mixed_buf[here, group_lanes(group)] = (mixed / totals).astype(BF16)

    state = state_ref[...].reshape(batch * rows, feat_width).astype(F32)
    after = (state + dot(mixed_buf[...], w_out_ref[...])).astype(BF16)
    normed_mid = rms_scaled(after.astype(F32), ffn_gain_ref[...]).astype(BF16)
    forecast = after.astype(F32)
    chunks = [slice(lower, lower + HIDDEN_CHUNK) for lower in range(0, w_gate_ref.shape[1], HIDDEN_CHUNK)]

    def gate_and_up(part):
        return dot(normed_mid, w_gate_ref[:, part]), dot(normed_mid, w_up_ref[:, part])

    gate, up = gate_and_up(chunks[0])
    for at, part in enumerate(chunks):
        following = gate_and_up(chunks[at + 1]) if at + 1 < len(chunks) else (None, None)
        gate = 0.5 * gate
        hidden = (gate * (1.0 + jnp.tanh(gate.astype(BF16)).astype(F32)) * up).astype(BF16)
        forecast += dot(hidden, down_weight_ref[part, :])
        gate, up = following
    forecast_buf[...] = forecast.astype(BF16)
    share_rows = out_refs[0].shape[1]
    for part, out_ref in enumerate(out_refs):
        lower = pl.multiple_of((mem_ref[0] ^ part) * share_rows, share_rows)
        for member in range(batch):
            out_ref[member] = forecast_buf[pl.ds(member * rows + lower, share_rows), :]


def forward(total_len, tok_index, mem_index, head_window, own, inner_parts, near, far, gains, weights, shares):
    members, row_count, feat_width = own.shape
    reach = near.shape[1]
    heads = head_window.shape[0]
    hidden_width = weights[3].shape[1]
    macs = members * row_count * feat_width * (3 * feat_width + 3 * hidden_width + 4 * reach)
    batch = batch_of(members)
    share_rows = row_count // shares

    def spec(array):
        return pl.BlockSpec((batch, *array.shape[1:]), lambda m: (m, 0, 0))

    return pl.pallas_call(
        functools.partial(forward_kernel, total_len),
        grid=(members // batch,),
        out_shape=[jax.ShapeDtypeStruct((members, share_rows, feat_width), BF16)] * shares,
        in_specs=[smem_spec()] * 3
        + [spec(v) for v in (own, *inner_parts, near, far)]
        + [vmem_spec()] * (len(gains) + len(weights)),
        out_specs=[pl.BlockSpec((batch, share_rows, feat_width), lambda m: (m, 0, 0))] * shares,
        scratch_shapes=[
            pltpu.VMEM((2 * batch, feat_width, reach), BF16),
            pltpu.VMEM((2 * batch, reach, 2 * feat_width), BF16),
            pltpu.VMEM((2, heads, Q_ROWS, reach), BF16),
            pltpu.VMEM((batch * row_count, feat_width), BF16),
            pltpu.VMEM((feat_width, row_count + 2 * reach), BF16),
            pltpu.VMEM((row_count + 2 * reach, 2 * feat_width), BF16),
            pltpu.VMEM((batch * row_count, feat_width), BF16),
        ],
        compiler_params=pltpu.CompilerParams(vmem_limit_bytes=VMEM_LIMIT),
        cost_estimate=pl.CostEstimate(flops=2 * macs, bytes_accessed=10 * own.size, transcendentals=0),
        name="forward",
    )(tok_index, mem_index, head_window, own, *inner_parts, near, far, *gains, *weights)


def global_member(held, index, own_members):
    return ((held // own_members) ^ index) * own_members + held % own_members


def gram_kernel(index_ref, *refs):
    share_refs, grid_ref, out_ref = refs[:-2], refs[-2], refs[-1]
    own_members, rows, feat_width = share_refs[0].shape
    members = own_members * len(share_refs)
    index = index_ref[0]
    stack = members * GROUP
    total = jnp.zeros((stack, stack), F32)
    crossed = jnp.zeros((stack, stack), F32)
    proj = jnp.zeros((members, GROUP, feat_width), F32)
    for lower in range(0, rows, GROUP):
        part = slice(lower, lower + GROUP)
        fields = jnp.concatenate([ref[:, part, :] for ref in share_refs], axis=0).astype(F32)
        mean = jnp.sum(fields, axis=0) * (1.0 / members)
        spread = fields - mean[None]
        weight = grid_ref[0, part, :]
        proj += spread * (grid_ref[1, part, :] - weight * mean)[None]
        scaled = spread * jnp.sqrt(jnp.maximum(weight, 0.0))[None]
        high, low = halves(scaled.reshape(stack, feat_width))
        total += dot(high, high, ((1,), (1,)))
        crossed += dot(high, low, ((1,), (1,)))
    total += crossed + crossed.T
    same = iota((stack, stack), 0) % GROUP == iota((stack, stack), 1) % GROUP
    by_row = jnp.sum(jnp.where(same, total, 0.0).reshape(members, GROUP, stack), axis=1)
    column = global_member(iota((stack, LANES), 0) // GROUP, index, own_members)
    folded = (column == iota((stack, LANES), 1) % members).astype(F32)
    held = global_member(iota((members, members), 1), index, own_members)
    in_order = (held == iota((members, members), 0)).astype(F32)
    tiled = exact_dot(in_order, exact_dot(by_row, folded))
    per_row = LANES // members
    keep = iota((members, LANES), 0) % per_row == iota((members, LANES), 1) // members
    packed = jnp.sum(jnp.where(keep, tiled, 0.0).reshape(members // per_row, per_row, LANES), axis=1)
    proj_col = jnp.sum(jnp.sum(proj, axis=1), axis=1, keepdims=True)
    at_lane = global_member(iota((members, LANES), 0), index, own_members) == iota((members, LANES), 1)
    proj_row = jnp.sum(jnp.where(at_lane, proj_col, 0.0), axis=0, keepdims=True)
    filled = members // per_row + 1
    blank = jnp.zeros((out_ref.shape[0] - filled, LANES), F32)
    out_ref[...] = jnp.concatenate([packed, proj_row, blank], axis=0)


def gram_partial(index, shares, grid):
    members = shares[0].shape[0] * len(shares)
    filled = members * members // LANES + 1
    return pl.pallas_call(
        gram_kernel,
        out_shape=jax.ShapeDtypeStruct((-(-filled // 8) * 8, LANES), F32),
        in_specs=[smem_spec()] + [vmem_spec()] * (len(shares) + 1),
        out_specs=vmem_spec(),
        compiler_params=pltpu.CompilerParams(vmem_limit_bytes=VMEM_LIMIT),
        cost_estimate=pl.CostEstimate(
            flops=3 * GROUP * members * members * grid.size, bytes_accessed=members * grid.size, transcendentals=0
        ),
        name="gram",
    )(index, *shares, grid)


def repeated_dot(a, b):
    size = a.shape[0]

    def pieces(values):
        first = values.astype(BF16).astype(F32)
        rest = values - first
        second = rest.astype(BF16).astype(F32)
        return first, second, rest - second

    block = iota(a.shape, 1) // size
    a_first, a_second, a_third = pieces(a)
    b_first, b_second, b_third = (piece.astype(BF16) for piece in pieces(b))
    left = jnp.where((block == 2) | (block == 4), a_second, jnp.where(block == 5, a_third, a_first))
    right = jnp.concatenate([b_first, b_second, b_first, b_third, b_second, b_first], axis=0)
    return dot(left.astype(BF16), right)


def ensemble_transform(gram, proj):
    members = gram.shape[0]
    row, column = iota((members, members), 0), iota((members, members), 1)
    identity = (row == column).astype(F32)
    system = gram + (members - 1.0) * identity
    left, right = system, proj
    for pivot in range(members):
        is_pivot = iota((members, 1), 0) == pivot
        scale = 1.0 / left[pivot : pivot + 1, pivot : pivot + 1]
        pivot_row = left[pivot : pivot + 1, :] * scale
        pivot_right = right[pivot : pivot + 1, :] * scale
        factor = left[:, pivot : pivot + 1]
        left = jnp.where(is_pivot, pivot_row, left - factor * pivot_row)
        right = jnp.where(is_pivot, pivot_right, right - factor * pivot_right)
    mean_weights = right
    mean_level = jnp.sum(jnp.sum(system * identity, axis=1, keepdims=True), axis=0, keepdims=True) / members
    lifted = system + (mean_level - (members - 1.0)) * (1.0 / members)
    frobenius = jnp.sqrt(jnp.sum(jnp.sum(lifted * lifted, axis=1, keepdims=True), axis=0, keepdims=True))
    root_iter = jnp.concatenate([lifted / frobenius] * PASSES, axis=1)
    repeated = iota((members, PASSES * members), 1) % members == iota((members, PASSES * members), 0)
    repeated = repeated.astype(F32)
    inv_iter = repeated
    for sweep in range(NS_STEPS):
        product = root_iter if sweep == 0 else repeated_dot(inv_iter, root_iter)
        correction = 1.5 * repeated - 0.5 * product
        inv_iter = correction if sweep == 0 else repeated_dot(correction, inv_iter)
        if sweep < NS_STEPS - 1:
            root_iter = repeated_dot(root_iter, correction)
    inv_iter = inv_iter[:, :members]
    inv_root = inv_iter / jnp.sqrt(frobenius) + (1.0 / math.sqrt(members - 1.0) - 1.0 / jnp.sqrt(mean_level)) * (
        1.0 / members
    )
    moved = mean_weights + math.sqrt(members - 1.0) * inv_root
    return 1.0 / members + moved - jnp.sum(moved, axis=0, keepdims=True) * (1.0 / members)


def combine_kernel(index_ref, partial_ref, *refs):
    share_refs, out_refs = refs[: len(refs) // 2], refs[len(refs) // 2 :]
    own_members, rows, feat_width = share_refs[0].shape
    members = own_members * len(share_refs)
    stack = members * GROUP
    per_row = LANES // members
    sums = jnp.sum(partial_ref[...], axis=0)
    spread_rows = jnp.concatenate(
        [jnp.broadcast_to(sums[r : r + 1], (per_row, LANES)) for r in range(members // per_row)], axis=0
    )
    keep = iota((members, LANES), 0) % per_row == iota((members, LANES), 1) // members
    folded = (iota((LANES, members), 0) % members == iota((LANES, members), 1)).astype(F32)
    gram = exact_dot(jnp.where(keep, spread_rows, 0.0), folded)
    proj_row = jnp.broadcast_to(sums[members // per_row : members // per_row + 1], (members, LANES))
    on_diagonal = iota((members, LANES), 0) == iota((members, LANES), 1)
    proj = jnp.sum(jnp.where(on_diagonal, proj_row, 0.0), axis=1, keepdims=True)
    transform = ensemble_transform(gram, proj)
    held = global_member(iota((stack, members), 0) // GROUP, index_ref[0], own_members)
    pick = (held == iota((stack, members), 1)).astype(F32).astype(BF16)
    same = iota((stack, stack), 0) % GROUP == iota((stack, stack), 1) % GROUP
    mixers = []
    for piece in halves(transform):
        rows_of = dot(pick, piece, ((1,), (1,))).astype(BF16)
        mixers.append(jnp.where(same, dot(rows_of, pick, ((1,), (1,))), 0.0).astype(BF16))
    for lower in range(0, rows, GROUP):
        part = slice(lower, lower + GROUP)
        fields = jnp.concatenate([ref[:, part, :].reshape(-1, feat_width) for ref in share_refs], axis=0)
        mixed = (dot(mixers[0], fields) + dot(mixers[1], fields)).astype(BF16)
        own_stack = own_members * GROUP
        for at, out_ref in enumerate(out_refs):
            piece = mixed[at * own_stack : (at + 1) * own_stack]
            out_ref[:, part, :] = piece.reshape(own_members, GROUP, feat_width)


def combine(index, partials, shares):
    size = shares[0].size * len(shares)
    members = shares[0].shape[0] * len(shares)
    return pl.pallas_call(
        combine_kernel,
        out_shape=[jax.ShapeDtypeStruct(v.shape, BF16) for v in shares],
        in_specs=[smem_spec()] + [vmem_spec()] * (1 + len(shares)),
        out_specs=[vmem_spec()] * len(shares),
        compiler_params=pltpu.CompilerParams(vmem_limit_bytes=VMEM_LIMIT),
        cost_estimate=pl.CostEstimate(flops=4 * GROUP * members * size, bytes_accessed=4 * size, transcendentals=0),
        name="combine",
    )(index, partials, *shares)


def assemble_kernel(index_ref, *refs):
    part_refs, out_ref, sems = refs[:-2], refs[-2], refs[-1]
    rows = part_refs[0].shape[1]
    copies = []
    for part, ref in enumerate(part_refs):
        lower = pl.multiple_of((index_ref[0] ^ part) * rows, rows)
        copies.append(pltpu.make_async_copy(ref, out_ref.at[:, pl.ds(lower, rows), :], sems.at[part]))
    for copy in copies:
        copy.start()
    for copy in copies:
        copy.wait()


def assemble(index, parts):
    members, rows, feat_width = parts[0].shape
    return pl.pallas_call(
        assemble_kernel,
        out_shape=jax.ShapeDtypeStruct((members, len(parts) * rows, feat_width), BF16),
        in_specs=[smem_spec()] + [vmem_spec()] * len(parts),
        out_specs=pl.BlockSpec(memory_space=pl.ANY),
        scratch_shapes=[pltpu.SemaphoreType.DMA((len(parts),))],
        compiler_params=pltpu.CompilerParams(vmem_limit_bytes=VMEM_LIMIT),
        cost_estimate=pl.CostEstimate(flops=0, bytes_accessed=4 * len(parts) * parts[0].size, transcendentals=0),
        name="assemble",
    )(index, *parts)


def exchanged(parts):
    count = lax.axis_size("mem")
    return [
        lax.ppermute(v, "mem", [(i, i ^ part) for i in range(count)]) if part else v for part, v in enumerate(parts)
    ]


def halos(own, reach):
    count = lax.axis_size("tok")
    odd = lax.axis_index("tok") % 2
    last = own.shape[1] - reach
    near_pairs = [(i, i ^ 1) for i in range(count)]
    far_pairs = [pair for i in range(1, count - 1, 2) for pair in ((i, i + 1), (i + 1, i))]
    far = lax.dynamic_slice_in_dim(own, odd * last, reach, axis=1)
    far, own = lax.optimization_barrier((far, own))
    far_halo = lax.ppermute(far, "tok", far_pairs)
    near = lax.dynamic_slice_in_dim(own, (1 - odd) * last, reach, axis=1)
    return lax.ppermute(near, "tok", near_pairs), far_halo


def local(
    ens_state,
    attn_gain,
    ffn_gain,
    w_query,
    w_key,
    w_value,
    w_out,
    w_gate,
    w_up,
    down_weight,
    head_window,
    obs_token,
    obs_channel,
    obs_value,
    obs_var,
):
    own_members, row_count, feat_width = ens_state.shape
    mem_count = lax.axis_size("mem")
    tok_count = lax.axis_size("tok")
    device_count = mem_count * tok_count
    share_rows = row_count // mem_count
    first_pos = lax.axis_index("tok") * row_count
    near_halo, far_halo = halos(ens_state, WIN)
    share_start = first_pos + lax.axis_index("mem") * share_rows
    grid = sample_grid(
        share_start.astype(jnp.int32).reshape(1), obs_token, obs_channel, obs_value, obs_var, share_rows, feat_width
    )
    mem_index = lax.axis_index("mem").astype(jnp.int32).reshape(1)
    tok_index = lax.axis_index("tok").astype(jnp.int32).reshape(1)
    gains = [attn_gain.reshape(1, -1), ffn_gain.reshape(1, -1)]
    inner_parts = inner(head_window, ens_state, gains[0], w_query, w_key, w_value, WIN)
    weights = [w_key, w_value, w_out, w_gate, w_up, down_weight]
    total_len = row_count * tok_count
    forecast = forward(
        total_len, tok_index, mem_index, head_window, ens_state, inner_parts, near_halo, far_halo, gains, weights, mem_count
    )
    shares = exchanged(forecast)
    partial = gram_partial(mem_index, shares, grid)
    partials = lax.all_to_all(
        jnp.broadcast_to(partial[None], (device_count, *partial.shape)),
        ("mem", "tok"),
        split_axis=0,
        concat_axis=0,
        tiled=True,
    )
    return assemble(mem_index, exchanged(combine(mem_index, partials, shares)))


def solution(mesh):
    in_specs = (P("mem", "tok", None), *[P()] * 10, *[P("tok")] * 4)
    return jax.shard_map(local, mesh=mesh, in_specs=in_specs, out_specs=P("mem", "tok", None), check_vma=False)
```

```python
import functools
import math

import jax
import jax.numpy as jnp
from jax import lax
from jax.experimental import pallas as pl
from jax.experimental.pallas import tpu as pltpu
from jax.sharding import PartitionSpec as P

WIN = 256
NS_STEPS = 8
EPS = 1e-05
Q_ROWS = 128
GROUP = 16
LANES = 128
VMEM_LIMIT = 32 * 1024 * 1024
SAFE_SCORE = 100.0
FOLD = 4
BATCH = 2
PASSES = 6
HIDDEN_CHUNK = 256

F32 = jnp.float32
BF16 = jnp.bfloat16


def dot(a, b, contract=((1,), (0,)), precision=None):
    return lax.dot_general(a, b, (contract, ((), ())), precision=precision, preferred_element_type=F32)


def exact_dot(a, b, contract=((1,), (0,))):
    return dot(a, b, contract, lax.Precision.HIGHEST)


def iota(shape, axis):
    return lax.broadcasted_iota(jnp.int32, shape, axis)


def halves(values):
    high = values.astype(BF16)
    return high, (values - high.astype(F32)).astype(BF16)


def rms_scaled(values, gain):
    return values * lax.rsqrt(jnp.mean(values * values, axis=-1, keepdims=True) + EPS) * gain


def vmem_spec():
    return pl.BlockSpec(memory_space=pltpu.VMEM)


def smem_spec():
    return pl.BlockSpec(memory_space=pltpu.SMEM)


def sample_grid_kernel(start_ref, token_ref, channel_ref, value_ref, var_ref, out_ref):
    rows, feat_width = out_ref.shape[1:]
    count = token_ref.shape[1]
    chunk = min(1024, count)
    total = jnp.zeros((4 * rows, feat_width), F32)
    for lower in range(0, count, chunk):
        part = slice(lower, lower + chunk)
        inv_var = 1.0 / var_ref[:, part]
        weighted = value_ref[:, part] * inv_var
        here = iota((rows, chunk), 0) == token_ref[:, part] - start_ref[0]
        pieces = []
        for row in (inv_var, weighted):
            high = row.astype(BF16).astype(F32)
            pieces.append(jnp.where(here, high, 0.0).astype(BF16))
            pieces.append(jnp.where(here, row - high, 0.0).astype(BF16))
        channel_hot = jnp.where(iota((feat_width, chunk), 0) == channel_ref[:, part], 1.0, 0.0).astype(BF16)
        total += dot(jnp.concatenate(pieces, axis=0), channel_hot, ((1,), (1,)))
    out_ref[0] = total[:rows] + total[rows : 2 * rows]
    out_ref[1] = total[2 * rows : 3 * rows] + total[3 * rows :]


def sample_grid(start, obs_token, obs_channel, obs_value, obs_var, rows, feat_width):
    count = obs_token.shape[0]
    return pl.pallas_call(
        sample_grid_kernel,
        out_shape=jax.ShapeDtypeStruct((2, rows, feat_width), F32),
        in_specs=[smem_spec()] + [vmem_spec()] * 4,
        out_specs=vmem_spec(),
        compiler_params=pltpu.CompilerParams(vmem_limit_bytes=VMEM_LIMIT),
        cost_estimate=pl.CostEstimate(flops=8 * rows * count * feat_width, bytes_accessed=16 * count, transcendentals=0),
        name="sample_grid",
    )(start, *(v.reshape(1, count) for v in (obs_token, obs_channel, obs_value, obs_var)))


def head_lanes(feat_width, heads):
    lane_head = iota((feat_width, LANES), 0) // (feat_width // heads)
    return (lane_head == iota((feat_width, LANES), 1)).astype(F32).astype(BF16)


def norm_bounds(values, heads):
    rows = values.shape[0] // FOLD
    squares = values * values
    folded = squares[:rows]
    for part in range(1, FOLD):
        folded = jnp.maximum(folded, squares[part * rows : (part + 1) * rows])
    return jnp.max(dot(folded.astype(BF16), head_lanes(values.shape[1], heads)), axis=0, keepdims=True)


def is_safe(query_norms, key_norms):
    return jnp.max(query_norms * key_norms) * 1.05 <= SAFE_SCORE * SAFE_SCORE


def query_scale(head_size):
    return math.log2(math.e) / math.sqrt(head_size)


def in_band(window, lower, upper, reach):
    apart = jnp.abs(iota((Q_ROWS, upper - lower), 1) + (lower - reach) - iota((Q_ROWS, upper - lower), 0))
    return apart <= window


def factor(mask):
    return jnp.where(mask, 1.0, 0.0).astype(BF16)


def group_lanes(group):
    return slice(group * LANES, (group + 1) * LANES)


def stacked_heads(queries, head_size):
    lane_head = iota((1, LANES), 1) // head_size
    masks = [(lane_head == head).astype(F32).astype(BF16) for head in range(LANES // head_size)]
    return jnp.concatenate([queries * mask for mask in masks], axis=0)


def put_values(buf, lower, values):
    for group in range(values.shape[1] // LANES):
        lanes = slice(2 * group * LANES, (2 * group + 1) * LANES)
        buf[lower : lower + values.shape[0], lanes] = values[:, group_lanes(group)]


def weighted_sums(weights, values, head_size):
    mixed_all = dot(weights, values)
    heads = LANES // head_size
    count = mixed_all.shape[0] // heads
    lane_head = iota((1, LANES), 1) // head_size
    mixed, totals = mixed_all[:count, :LANES], mixed_all[:count, LANES:]
    for head in range(1, heads):
        part = mixed_all[head * count : (head + 1) * count]
        mixed = jnp.where(lane_head == head, part[:, :LANES], mixed)
        totals = jnp.where(lane_head == head, part[:, LANES:], totals)
    return mixed, totals


def padded_lanes(values, before, after):
    pieces = [jnp.zeros((values.shape[0], before), BF16)] if before else []
    pieces.append(values)
    if after:
        pieces.append(jnp.zeros((values.shape[0], after), BF16))
    return jnp.concatenate(pieces, axis=1) if len(pieces) > 1 else pieces[0]


def unit_weights(scores, spans, band_of):
    width = scores.shape[1]
    count = len(spans) * Q_ROWS
    weights = []
    for head in range(scores.shape[0] // count):
        for block, (lower, upper) in enumerate(spans):
            top = head * count + block * Q_ROWS
            expo = jnp.exp2(scores[top : top + Q_ROWS, lower:upper]).astype(BF16)
            weights.append(padded_lanes(expo * band_of(head, block), lower, width - upper))
    return jnp.concatenate(weights, axis=0)


def inner_kernel(
    window_ref,
    own_ref,
    gain_ref,
    w_query_ref,
    w_key_ref,
    w_value_ref,
    query_ref,
    norm_ref,
    mixed_ref,
    total_ref,
    key_buf,
    value_buf,
    band_buf,
):
    rows, feat_width = own_ref.shape[1:]
    heads = window_ref.shape[0]
    head_size = feat_width // heads
    group_heads = LANES // head_size
    key_count = band_buf.shape[2]
    reach = (key_count - Q_ROWS) // 2
    reach_blocks = reach // Q_ROWS
    blocks = rows // Q_ROWS

    @pl.when(pl.program_id(0) == 0)
    def _():
        for head in range(heads):
            band_buf[head] = factor(in_band(window_ref[head], 0, key_count, reach))
        value_buf[...] = jnp.ones(value_buf.shape, BF16)

    batch = own_ref.shape[0]
    own = own_ref[...].reshape(batch * rows, feat_width).astype(F32)
    normed = rms_scaled(own, gain_ref[...]).astype(BF16)
    query_rows = dot(normed, w_query_ref[...]) * query_scale(head_size)
    key_rows = dot(normed, w_key_ref[...])
    value_rows = dot(normed, w_value_ref[...]).astype(BF16)
    query_norms, key_norms = norm_bounds(query_rows, heads), norm_bounds(key_rows, heads)
    blank = jnp.zeros((norm_ref.shape[1] - 2, LANES), F32)
    for member in range(batch):
        here = slice(member * rows, (member + 1) * rows)
        query_ref[member] = query_rows[here].astype(BF16)
        key_buf[member] = key_rows[here].astype(BF16).T
        put_values(value_buf.at[member], 0, value_rows[here])
        norm_ref[member] = jnp.concatenate([query_norms, key_norms, blank], axis=0)

    @pl.when(is_safe(query_norms, key_norms))
    def _():
        pairs = range(0, blocks, 2)
        groups = range(heads // group_heads)
        units = [(member, first, group) for member in range(batch) for first in pairs for group in groups]

        def scores_of(member, first, group):
            queries = query_ref[member, first * Q_ROWS : (first + 2) * Q_ROWS, group_lanes(group)]
            return dot(stacked_heads(queries, head_size), key_buf[member, group_lanes(group), :])

        scores = scores_of(*units[0])
        for at, (member, first, group) in enumerate(units):
            following = scores_of(*units[at + 1]) if at + 1 < len(units) else None
            ranges = [(max(0, b - reach_blocks), min(blocks, b + reach_blocks + 1)) for b in (first, first + 1)]
            spans = [(lower * Q_ROWS, upper * Q_ROWS) for lower, upper in ranges]

            def band_of(head, block):
                shift = (reach_blocks - first - block) * Q_ROWS
                lower, upper = spans[block]
                return band_buf[group * group_heads + head, :, lower + shift : upper + shift]

            values = value_buf[member, :, 2 * group * LANES : 2 * (group + 1) * LANES]
            mixed, totals = weighted_sums(unit_weights(scores, spans, band_of), values, head_size)
            here = slice(first * Q_ROWS, (first + 2) * Q_ROWS)
            mixed_ref[member, here, group_lanes(group)] = mixed
            total_ref[member, here, group_lanes(group)] = totals
            scores = following


def batch_of(members):
    return BATCH if members % BATCH == 0 else 1


def inner(head_window, own, gain, w_query, w_key, w_value, reach):
    members, rows, feat_width = own.shape
    heads = head_window.shape[0]
    key_count = Q_ROWS + 2 * reach
    shapes = [(own.shape, BF16), ((members, 8, LANES), F32), (own.shape, F32), (own.shape, F32)]

    batch = batch_of(members)

    def spec(shape):
        return pl.BlockSpec((batch, *shape[1:]), lambda m: (m, 0, 0))

    return pl.pallas_call(
        inner_kernel,
        grid=(members // batch,),
        out_shape=[jax.ShapeDtypeStruct(*v) for v in shapes],
        in_specs=[smem_spec(), spec(own.shape)] + [vmem_spec()] * 4,
        out_specs=[spec(shape) for shape, _ in shapes],
        scratch_shapes=[
            pltpu.VMEM((batch, feat_width, rows), BF16),
            pltpu.VMEM((batch, rows, 2 * feat_width), BF16),
            pltpu.VMEM((heads, Q_ROWS, key_count), BF16),
        ],
        compiler_params=pltpu.CompilerParams(vmem_limit_bytes=VMEM_LIMIT),
        cost_estimate=pl.CostEstimate(
            flops=own.size * (6 * feat_width + 16 * rows), bytes_accessed=14 * own.size, transcendentals=0
        ),
        name="inner",
    )(head_window, own, gain, w_query, w_key, w_value)


def forward_kernel(
    total_len,
    tok_ref,
    mem_ref,
    window_ref,
    state_ref,
    query_ref,
    norm_ref,
    inner_mixed_ref,
    inner_total_ref,
    near_ref,
    far_ref,
    attn_gain_ref,
    ffn_gain_ref,
    w_key_ref,
    w_value_ref,
    w_out_ref,
    w_gate_ref,
    w_up_ref,
    down_weight_ref,
    *refs,
):
    out_refs, (halo_key_buf, halo_value_buf, band_buf, mixed_buf, key_buf, value_buf, forecast_buf) = (
        refs[:-7],
        refs[-7:],
    )
    rows, feat_width = state_ref.shape[1:]
    reach = near_ref.shape[1]
    heads = window_ref.shape[0]
    head_size = feat_width // heads
    group_heads = LANES // head_size
    groups = heads // group_heads
    blocks = rows // Q_ROWS
    key_count = Q_ROWS + 2 * reach
    count = 2 * Q_ROWS
    first_pos = tok_ref[0] * rows

    @pl.when(pl.program_id(0) == 0)
    def _():
        first_valid = first_pos - reach >= 0
        last_valid = first_pos + rows + reach <= total_len
        for head in range(heads):
            window = window_ref[head]
            band_buf[0, head] = factor(in_band(jnp.where(first_valid, window, -1), 0, reach, reach))
            right_window = jnp.where(last_valid, window, -1)
            band_buf[1, head] = factor(in_band(right_window, key_count - reach, key_count, reach))
        halo_value_buf[...] = jnp.ones(halo_value_buf.shape, BF16)

    def keys_of(normed):
        return dot(normed, w_key_ref[...])

    def values_of(normed):
        return dot(normed, w_value_ref[...]).astype(BF16)

    odd = tok_ref[0] % 2 == 1
    batch = state_ref.shape[0]
    halo = []
    for member in range(batch):
        near, far = near_ref[member].astype(F32), far_ref[member].astype(F32)
        halo += [jnp.where(odd, near, far), jnp.where(odd, far, near)]
    normed = rms_scaled(jnp.concatenate(halo, axis=0), attn_gain_ref[...]).astype(BF16)
    halo_keys = keys_of(normed)
    halo_values = values_of(normed)
    query_norms = jnp.max(norm_ref[:, 0, :], axis=0, keepdims=True)
    key_norms = jnp.maximum(jnp.max(norm_ref[:, 1, :], axis=0, keepdims=True), norm_bounds(halo_keys, heads))
    for at in range(2 * batch):
        here = slice(at * reach, (at + 1) * reach)
        halo_key_buf[at] = halo_keys[here].astype(BF16).T
        put_values(halo_value_buf.at[at], 0, halo_values[here])
    safe = is_safe(query_norms, key_norms)

    @pl.when(safe)
    def _():
        units = [(member, side, group) for member in range(batch) for side in range(2) for group in range(groups)]

        def scores_of(member, side, group):
            start = side * (rows - count)
            queries = query_ref[member, start : start + count, group_lanes(group)]
            return dot(stacked_heads(queries, head_size), halo_key_buf[2 * member + side, group_lanes(group), :])

        scores = scores_of(*units[0])
        for at, (member, side, group) in enumerate(units):
            following = scores_of(*units[at + 1]) if at + 1 < len(units) else None
            spans = [(0, reach), (Q_ROWS, reach)] if side == 0 else [(0, reach - Q_ROWS), (0, reach)]

            def band_of(head, block):
                lower, upper = spans[block]
                shift = -block * Q_ROWS if side == 0 else (1 - block) * Q_ROWS
                return band_buf[side, group * group_heads + head, :, lower + shift : upper + shift]

            values = halo_value_buf[2 * member + side, :, 2 * group * LANES : 2 * (group + 1) * LANES]
            mixed, totals = weighted_sums(unit_weights(scores, spans, band_of), values, head_size)
            start = side * (rows - count)
            here = slice(start, start + count)
            mixed = mixed + inner_mixed_ref[member, here, group_lanes(group)]
            totals = totals + inner_total_ref[member, here, group_lanes(group)]
            start += member * rows
            mixed_buf[start : start + count, group_lanes(group)] = (mixed / totals).astype(BF16)
            scores = following

    @pl.when(jnp.logical_not(safe))
    def _():
        for member in range(batch):
            normed = rms_scaled(state_ref[member].astype(F32), attn_gain_ref[...]).astype(BF16)
            key_buf[:, :reach] = halo_key_buf[2 * member]
            key_buf[:, reach : reach + rows] = keys_of(normed).astype(BF16).T
            key_buf[:, reach + rows :] = halo_key_buf[2 * member + 1]
            value_buf[...] = jnp.ones(value_buf.shape, BF16)
            put_values(value_buf, reach, values_of(normed))
            value_buf[:reach] = halo_value_buf[2 * member]
            value_buf[reach + rows :] = halo_value_buf[2 * member + 1]
            for block in range(blocks):
                start = block * Q_ROWS
                k_pos = first_pos - reach + start + iota((Q_ROWS, key_count), 1)
                inside = (k_pos >= 0) & (k_pos < total_len)
                for group in range(groups):
                    queries = query_ref[member, start : start + Q_ROWS, group_lanes(group)]
                    keys = key_buf[group_lanes(group), start : start + key_count]
                    scores = dot(stacked_heads(queries, head_size), keys)
                    weights = []
                    for head in range(group_heads):
                        allowed = inside & in_band(window_ref[group * group_heads + head], 0, key_count, reach)
                        score_matrix = jnp.where(allowed, scores[head * Q_ROWS : (head + 1) * Q_ROWS], -1e30)
                        row_top = jnp.max(score_matrix, axis=-1, keepdims=True)
                        weights.append(jnp.exp2(score_matrix - row_top).astype(BF16))
                    values = value_buf[start : start + key_count, 2 * group * LANES : 2 * (group + 1) * LANES]
                    mixed, totals = weighted_sums(jnp.concatenate(weights, axis=0), values, head_size)
                    here = slice(member * rows + start, member * rows + start + Q_ROWS)
                    mixed_buf[here, group_lanes(group)] = (mixed / totals).astype(BF16)

    state = state_ref[...].reshape(batch * rows, feat_width).astype(F32)
    after = (state + dot(mixed_buf[...], w_out_ref[...])).astype(BF16)
    normed_mid = rms_scaled(after.astype(F32), ffn_gain_ref[...]).astype(BF16)
    forecast = after.astype(F32)
    chunks = [slice(lower, lower + HIDDEN_CHUNK) for lower in range(0, w_gate_ref.shape[1], HIDDEN_CHUNK)]

    def gate_and_up(part):
        return dot(normed_mid, w_gate_ref[:, part]), dot(normed_mid, w_up_ref[:, part])

    gate, up = gate_and_up(chunks[0])
    for at, part in enumerate(chunks):
        following = gate_and_up(chunks[at + 1]) if at + 1 < len(chunks) else (None, None)
        gate = 0.5 * gate
        hidden = (gate * (1.0 + jnp.tanh(gate.astype(BF16)).astype(F32)) * up).astype(BF16)
        forecast += dot(hidden, down_weight_ref[part, :])
        gate, up = following
    forecast_buf[...] = forecast.astype(BF16)
    share_rows = out_refs[0].shape[1]
    for part, out_ref in enumerate(out_refs):
        lower = pl.multiple_of((mem_ref[0] ^ part) * share_rows, share_rows)
        for member in range(batch):
            out_ref[member] = forecast_buf[pl.ds(member * rows + lower, share_rows), :]


def forward(total_len, tok_index, mem_index, head_window, own, inner_parts, near, far, gains, weights, shares):
    members, row_count, feat_width = own.shape
    reach = near.shape[1]
    heads = head_window.shape[0]
    hidden_width = weights[3].shape[1]
    macs = members * row_count * feat_width * (3 * feat_width + 3 * hidden_width + 4 * reach)
    batch = batch_of(members)
    share_rows = row_count // shares

    def spec(array):
        return pl.BlockSpec((batch, *array.shape[1:]), lambda m: (m, 0, 0))

    return pl.pallas_call(
        functools.partial(forward_kernel, total_len),
        grid=(members // batch,),
        out_shape=[jax.ShapeDtypeStruct((members, share_rows, feat_width), BF16)] * shares,
        in_specs=[smem_spec()] * 3
        + [spec(v) for v in (own, *inner_parts, near, far)]
        + [vmem_spec()] * (len(gains) + len(weights)),
        out_specs=[pl.BlockSpec((batch, share_rows, feat_width), lambda m: (m, 0, 0))] * shares,
        scratch_shapes=[
            pltpu.VMEM((2 * batch, feat_width, reach), BF16),
            pltpu.VMEM((2 * batch, reach, 2 * feat_width), BF16),
            pltpu.VMEM((2, heads, Q_ROWS, reach), BF16),
            pltpu.VMEM((batch * row_count, feat_width), BF16),
            pltpu.VMEM((feat_width, row_count + 2 * reach), BF16),
            pltpu.VMEM((row_count + 2 * reach, 2 * feat_width), BF16),
            pltpu.VMEM((batch * row_count, feat_width), BF16),
        ],
        compiler_params=pltpu.CompilerParams(vmem_limit_bytes=VMEM_LIMIT),
        cost_estimate=pl.CostEstimate(flops=2 * macs, bytes_accessed=10 * own.size, transcendentals=0),
        name="forward",
    )(tok_index, mem_index, head_window, own, *inner_parts, near, far, *gains, *weights)


def global_member(held, index, own_members):
    return ((held // own_members) ^ index) * own_members + held % own_members


def gram_kernel(index_ref, *refs):
    share_refs, grid_ref, out_ref = refs[:-2], refs[-2], refs[-1]
    own_members, rows, feat_width = share_refs[0].shape
    members = own_members * len(share_refs)
    index = index_ref[0]
    stack = members * GROUP
    total = jnp.zeros((stack, stack), F32)
    crossed = jnp.zeros((stack, stack), F32)
    proj = jnp.zeros((members, GROUP, feat_width), F32)
    for lower in range(0, rows, GROUP):
        part = slice(lower, lower + GROUP)
        fields = jnp.concatenate([ref[:, part, :] for ref in share_refs], axis=0).astype(F32)
        mean = jnp.sum(fields, axis=0) * (1.0 / members)
        spread = fields - mean[None]
        weight = grid_ref[0, part, :]
        proj += spread * (grid_ref[1, part, :] - weight * mean)[None]
        scaled = spread * jnp.sqrt(jnp.maximum(weight, 0.0))[None]
        high, low = halves(scaled.reshape(stack, feat_width))
        total += dot(high, high, ((1,), (1,)))
        crossed += dot(high, low, ((1,), (1,)))
    total += crossed + crossed.T
    same = iota((stack, stack), 0) % GROUP == iota((stack, stack), 1) % GROUP
    by_row = jnp.sum(jnp.where(same, total, 0.0).reshape(members, GROUP, stack), axis=1)
    column = global_member(iota((stack, LANES), 0) // GROUP, index, own_members)
    folded = (column == iota((stack, LANES), 1) % members).astype(F32)
    held = global_member(iota((members, members), 1), index, own_members)
    in_order = (held == iota((members, members), 0)).astype(F32)
    tiled = exact_dot(in_order, exact_dot(by_row, folded))
    per_row = LANES // members
    keep = iota((members, LANES), 0) % per_row == iota((members, LANES), 1) // members
    packed = jnp.sum(jnp.where(keep, tiled, 0.0).reshape(members // per_row, per_row, LANES), axis=1)
    proj_col = jnp.sum(jnp.sum(proj, axis=1), axis=1, keepdims=True)
    at_lane = global_member(iota((members, LANES), 0), index, own_members) == iota((members, LANES), 1)
    proj_row = jnp.sum(jnp.where(at_lane, proj_col, 0.0), axis=0, keepdims=True)
    filled = members // per_row + 1
    blank = jnp.zeros((out_ref.shape[0] - filled, LANES), F32)
    out_ref[...] = jnp.concatenate([packed, proj_row, blank], axis=0)


def gram_partial(index, shares, grid):
    members = shares[0].shape[0] * len(shares)
    filled = members * members // LANES + 1
    return pl.pallas_call(
        gram_kernel,
        out_shape=jax.ShapeDtypeStruct((-(-filled // 8) * 8, LANES), F32),
        in_specs=[smem_spec()] + [vmem_spec()] * (len(shares) + 1),
        out_specs=vmem_spec(),
        compiler_params=pltpu.CompilerParams(vmem_limit_bytes=VMEM_LIMIT),
        cost_estimate=pl.CostEstimate(
            flops=3 * GROUP * members * members * grid.size, bytes_accessed=members * grid.size, transcendentals=0
        ),
        name="gram",
    )(index, *shares, grid)


def repeated_dot(a, b):
    size = a.shape[0]

    def pieces(values):
        first = values.astype(BF16).astype(F32)
        rest = values - first
        second = rest.astype(BF16).astype(F32)
        return first, second, rest - second

    block = iota(a.shape, 1) // size
    a_first, a_second, a_third = pieces(a)
    b_first, b_second, b_third = (piece.astype(BF16) for piece in pieces(b))
    left = jnp.where((block == 2) | (block == 4), a_second, jnp.where(block == 5, a_third, a_first))
    right = jnp.concatenate([b_first, b_second, b_first, b_third, b_second, b_first], axis=0)
    return dot(left.astype(BF16), right)


def ensemble_transform(gram, proj):
    members = gram.shape[0]
    row, column = iota((members, members), 0), iota((members, members), 1)
    identity = (row == column).astype(F32)
    system = gram + (members - 1.0) * identity
    left, right = system, proj
    for pivot in range(members):
        is_pivot = iota((members, 1), 0) == pivot
        scale = 1.0 / left[pivot : pivot + 1, pivot : pivot + 1]
        pivot_row = left[pivot : pivot + 1, :] * scale
        pivot_right = right[pivot : pivot + 1, :] * scale
        factor = left[:, pivot : pivot + 1]
        left = jnp.where(is_pivot, pivot_row, left - factor * pivot_row)
        right = jnp.where(is_pivot, pivot_right, right - factor * pivot_right)
    mean_weights = right
    mean_level = jnp.sum(jnp.sum(system * identity, axis=1, keepdims=True), axis=0, keepdims=True) / members
    lifted = system + (mean_level - (members - 1.0)) * (1.0 / members)
    frobenius = jnp.sqrt(jnp.sum(jnp.sum(lifted * lifted, axis=1, keepdims=True), axis=0, keepdims=True))
    root_iter = jnp.concatenate([lifted / frobenius] * PASSES, axis=1)
    repeated = iota((members, PASSES * members), 1) % members == iota((members, PASSES * members), 0)
    repeated = repeated.astype(F32)
    inv_iter = repeated
    for sweep in range(NS_STEPS):
        product = root_iter if sweep == 0 else repeated_dot(inv_iter, root_iter)
        correction = 1.5 * repeated - 0.5 * product
        inv_iter = correction if sweep == 0 else repeated_dot(correction, inv_iter)
        if sweep < NS_STEPS - 1:
            root_iter = repeated_dot(root_iter, correction)
    inv_iter = inv_iter[:, :members]
    inv_root = inv_iter / jnp.sqrt(frobenius) + (1.0 / math.sqrt(members - 1.0) - 1.0 / jnp.sqrt(mean_level)) * (
        1.0 / members
    )
    moved = mean_weights + math.sqrt(members - 1.0) * inv_root
    return 1.0 / members + moved - jnp.sum(moved, axis=0, keepdims=True) * (1.0 / members)


def combine_kernel(index_ref, partial_ref, *refs):
    share_refs, out_refs = refs[: len(refs) // 2], refs[len(refs) // 2 :]
    own_members, rows, feat_width = share_refs[0].shape
    members = own_members * len(share_refs)
    stack = members * GROUP
    per_row = LANES // members
    sums = jnp.sum(partial_ref[...], axis=0)
    spread_rows = jnp.concatenate(
        [jnp.broadcast_to(sums[r : r + 1], (per_row, LANES)) for r in range(members // per_row)], axis=0
    )
    keep = iota((members, LANES), 0) % per_row == iota((members, LANES), 1) // members
    folded = (iota((LANES, members), 0) % members == iota((LANES, members), 1)).astype(F32)
    gram = exact_dot(jnp.where(keep, spread_rows, 0.0), folded)
    proj_row = jnp.broadcast_to(sums[members // per_row : members // per_row + 1], (members, LANES))
    on_diagonal = iota((members, LANES), 0) == iota((members, LANES), 1)
    proj = jnp.sum(jnp.where(on_diagonal, proj_row, 0.0), axis=1, keepdims=True)
    transform = ensemble_transform(gram, proj)
    held = global_member(iota((stack, members), 0) // GROUP, index_ref[0], own_members)
    pick = (held == iota((stack, members), 1)).astype(F32).astype(BF16)
    same = iota((stack, stack), 0) % GROUP == iota((stack, stack), 1) % GROUP
    mixers = []
    for piece in halves(transform):
        rows_of = dot(pick, piece, ((1,), (1,))).astype(BF16)
        mixers.append(jnp.where(same, dot(rows_of, pick, ((1,), (1,))), 0.0).astype(BF16))
    for lower in range(0, rows, GROUP):
        part = slice(lower, lower + GROUP)
        fields = jnp.concatenate([ref[:, part, :].reshape(-1, feat_width) for ref in share_refs], axis=0)
        mixed = (dot(mixers[0], fields) + dot(mixers[1], fields)).astype(BF16)
        own_stack = own_members * GROUP
        for at, out_ref in enumerate(out_refs):
            piece = mixed[at * own_stack : (at + 1) * own_stack]
            out_ref[:, part, :] = piece.reshape(own_members, GROUP, feat_width)


def combine(index, partials, shares):
    size = shares[0].size * len(shares)
    members = shares[0].shape[0] * len(shares)
    return pl.pallas_call(
        combine_kernel,
        out_shape=[jax.ShapeDtypeStruct(v.shape, BF16) for v in shares],
        in_specs=[smem_spec()] + [vmem_spec()] * (1 + len(shares)),
        out_specs=[vmem_spec()] * len(shares),
        compiler_params=pltpu.CompilerParams(vmem_limit_bytes=VMEM_LIMIT),
        cost_estimate=pl.CostEstimate(flops=4 * GROUP * members * size, bytes_accessed=4 * size, transcendentals=0),
        name="combine",
    )(index, partials, *shares)


def place_kernel(first, count, index_ref, *refs):
    part_refs, out_ref, sems = refs[:count], refs[-2], refs[-1]
    rows = part_refs[0].shape[1]
    copies = []
    for at, ref in enumerate(part_refs):
        lower = pl.multiple_of((index_ref[0] ^ (first + at)) * rows, rows)
        copies.append(pltpu.make_async_copy(ref, out_ref.at[:, pl.ds(lower, rows), :], sems.at[at]))
    for copy in copies:
        copy.start()
    for copy in copies:
        copy.wait()


def place(index, parts, first, shares, result=()):
    members, rows, feat_width = parts[0].shape
    anywhere = pl.BlockSpec(memory_space=pl.ANY)
    return pl.pallas_call(
        functools.partial(place_kernel, first, len(parts)),
        out_shape=jax.ShapeDtypeStruct((members, shares * rows, feat_width), BF16),
        in_specs=[smem_spec()] + [vmem_spec()] * len(parts) + [anywhere] * len(result),
        out_specs=anywhere,
        input_output_aliases={1 + len(parts): 0} if result else {},
        scratch_shapes=[pltpu.SemaphoreType.DMA((len(parts),))],
        compiler_params=pltpu.CompilerParams(vmem_limit_bytes=VMEM_LIMIT),
        cost_estimate=pl.CostEstimate(flops=0, bytes_accessed=4 * len(parts) * parts[0].size, transcendentals=0),
        name="place",
    )(index, *parts, *result)


def assemble(index, parts):
    result = place(index, parts[:-1], 0, len(parts))
    return place(index, parts[-1:], len(parts) - 1, len(parts), (result,))


def exchanged(parts):
    count = lax.axis_size("mem")
    return [
        lax.ppermute(v, "mem", [(i, i ^ part) for i in range(count)]) if part else v for part, v in enumerate(parts)
    ]


def halos(own, reach):
    count = lax.axis_size("tok")
    odd = lax.axis_index("tok") % 2
    last = own.shape[1] - reach
    near = lax.dynamic_slice_in_dim(own, (1 - odd) * last, reach, axis=1)
    far = lax.dynamic_slice_in_dim(own, odd * last, reach, axis=1)
    near_pairs = [(i, i ^ 1) for i in range(count)]
    far_pairs = [pair for i in range(1, count - 1, 2) for pair in ((i, i + 1), (i + 1, i))]
    far_halo = lax.ppermute(far, "tok", far_pairs)
    return lax.ppermute(near, "tok", near_pairs), far_halo


def local(
    ens_state,
    attn_gain,
    ffn_gain,
    w_query,
    w_key,
    w_value,
    w_out,
    w_gate,
    w_up,
    down_weight,
    head_window,
    obs_token,
    obs_channel,
    obs_value,
    obs_var,
):
    own_members, row_count, feat_width = ens_state.shape
    mem_count = lax.axis_size("mem")
    tok_count = lax.axis_size("tok")
    device_count = mem_count * tok_count
    share_rows = row_count // mem_count
    first_pos = lax.axis_index("tok") * row_count
    near_halo, far_halo = halos(ens_state, WIN)
    share_start = first_pos + lax.axis_index("mem") * share_rows
    grid = sample_grid(
        share_start.astype(jnp.int32).reshape(1), obs_token, obs_channel, obs_value, obs_var, share_rows, feat_width
    )
    mem_index = lax.axis_index("mem").astype(jnp.int32).reshape(1)
    tok_index = lax.axis_index("tok").astype(jnp.int32).reshape(1)
    gains = [attn_gain.reshape(1, -1), ffn_gain.reshape(1, -1)]
    inner_parts = inner(head_window, ens_state, gains[0], w_query, w_key, w_value, WIN)
    weights = [w_key, w_value, w_out, w_gate, w_up, down_weight]
    total_len = row_count * tok_count
    forecast = forward(
        total_len, tok_index, mem_index, head_window, ens_state, inner_parts, near_halo, far_halo, gains, weights, mem_count
    )
    shares = exchanged(forecast)
    partial = gram_partial(mem_index, shares, grid)
    partials = lax.all_to_all(
        jnp.broadcast_to(partial[None], (device_count, *partial.shape)),
        ("mem", "tok"),
        split_axis=0,
        concat_axis=0,
        tiled=True,
    )
    return assemble(mem_index, exchanged(combine(mem_index, partials, shares)))


def solution(mesh):
    in_specs = (P("mem", "tok", None), *[P()] * 10, *[P("tok")] * 4)
    return jax.shard_map(local, mesh=mesh, in_specs=in_specs, out_specs=P("mem", "tok", None), check_vma=False)
```

```python
import functools
import math

import jax
import jax.numpy as jnp
from jax import lax
from jax.experimental import pallas as pl
from jax.experimental.pallas import tpu as pltpu
from jax.sharding import PartitionSpec as P

WIN = 256
NS_STEPS = 8
EPS = 1e-05
Q_ROWS = 128
GROUP = 16
LANES = 128
VMEM_LIMIT = 32 * 1024 * 1024
SAFE_SCORE = 100.0
FOLD = 4
BATCH = 2
PASSES = 6
HIDDEN_CHUNK = 256

F32 = jnp.float32
BF16 = jnp.bfloat16


def dot(a, b, contract=((1,), (0,)), precision=None):
    return lax.dot_general(a, b, (contract, ((), ())), precision=precision, preferred_element_type=F32)


def exact_dot(a, b, contract=((1,), (0,))):
    return dot(a, b, contract, lax.Precision.HIGHEST)


def iota(shape, axis):
    return lax.broadcasted_iota(jnp.int32, shape, axis)


def halves(values):
    high = values.astype(BF16)
    return high, (values - high.astype(F32)).astype(BF16)


def rms_scaled(values, gain):
    return values * lax.rsqrt(jnp.mean(values * values, axis=-1, keepdims=True) + EPS) * gain


def vmem_spec():
    return pl.BlockSpec(memory_space=pltpu.VMEM)


def smem_spec():
    return pl.BlockSpec(memory_space=pltpu.SMEM)


def sample_grid_kernel(start_ref, token_ref, channel_ref, value_ref, var_ref, out_ref):
    rows, feat_width = out_ref.shape[1:]
    count = token_ref.shape[1]
    chunk = min(1024, count)
    total = jnp.zeros((4 * rows, feat_width), F32)
    for lower in range(0, count, chunk):
        part = slice(lower, lower + chunk)
        inv_var = 1.0 / var_ref[:, part]
        weighted = value_ref[:, part] * inv_var
        here = iota((rows, chunk), 0) == token_ref[:, part] - start_ref[0]
        pieces = []
        for row in (inv_var, weighted):
            high = row.astype(BF16).astype(F32)
            pieces.append(jnp.where(here, high, 0.0).astype(BF16))
            pieces.append(jnp.where(here, row - high, 0.0).astype(BF16))
        channel_hot = jnp.where(iota((feat_width, chunk), 0) == channel_ref[:, part], 1.0, 0.0).astype(BF16)
        total += dot(jnp.concatenate(pieces, axis=0), channel_hot, ((1,), (1,)))
    out_ref[0] = total[:rows] + total[rows : 2 * rows]
    out_ref[1] = total[2 * rows : 3 * rows] + total[3 * rows :]


def sample_grid(start, obs_token, obs_channel, obs_value, obs_var, rows, feat_width):
    count = obs_token.shape[0]
    return pl.pallas_call(
        sample_grid_kernel,
        out_shape=jax.ShapeDtypeStruct((2, rows, feat_width), F32),
        in_specs=[smem_spec()] + [vmem_spec()] * 4,
        out_specs=vmem_spec(),
        compiler_params=pltpu.CompilerParams(vmem_limit_bytes=VMEM_LIMIT),
        cost_estimate=pl.CostEstimate(flops=8 * rows * count * feat_width, bytes_accessed=16 * count, transcendentals=0),
        name="sample_grid",
    )(start, *(v.reshape(1, count) for v in (obs_token, obs_channel, obs_value, obs_var)))


def head_lanes(feat_width, heads):
    lane_head = iota((feat_width, LANES), 0) // (feat_width // heads)
    return (lane_head == iota((feat_width, LANES), 1)).astype(F32).astype(BF16)


def norm_bounds(values, heads):
    rows = values.shape[0] // FOLD
    squares = values * values
    folded = squares[:rows]
    for part in range(1, FOLD):
        folded = jnp.maximum(folded, squares[part * rows : (part + 1) * rows])
    return jnp.max(dot(folded.astype(BF16), head_lanes(values.shape[1], heads)), axis=0, keepdims=True)


def is_safe(query_norms, key_norms):
    return jnp.max(query_norms * key_norms) * 1.05 <= SAFE_SCORE * SAFE_SCORE


def query_scale(head_size):
    return math.log2(math.e) / math.sqrt(head_size)


def in_band(window, lower, upper, reach):
    apart = jnp.abs(iota((Q_ROWS, upper - lower), 1) + (lower - reach) - iota((Q_ROWS, upper - lower), 0))
    return apart <= window


def factor(mask):
    return jnp.where(mask, 1.0, 0.0).astype(BF16)


def group_lanes(group):
    return slice(group * LANES, (group + 1) * LANES)


def stacked_heads(queries, head_size):
    lane_head = iota((1, LANES), 1) // head_size
    masks = [(lane_head == head).astype(F32).astype(BF16) for head in range(LANES // head_size)]
    return jnp.concatenate([queries * mask for mask in masks], axis=0)


def put_values(buf, lower, values):
    for group in range(values.shape[1] // LANES):
        lanes = slice(2 * group * LANES, (2 * group + 1) * LANES)
        buf[lower : lower + values.shape[0], lanes] = values[:, group_lanes(group)]


def weighted_sums(weights, values, head_size):
    mixed_all = dot(weights, values)
    heads = LANES // head_size
    count = mixed_all.shape[0] // heads
    lane_head = iota((1, LANES), 1) // head_size
    mixed, totals = mixed_all[:count, :LANES], mixed_all[:count, LANES:]
    for head in range(1, heads):
        part = mixed_all[head * count : (head + 1) * count]
        mixed = jnp.where(lane_head == head, part[:, :LANES], mixed)
        totals = jnp.where(lane_head == head, part[:, LANES:], totals)
    return mixed, totals


def padded_lanes(values, before, after):
    pieces = [jnp.zeros((values.shape[0], before), BF16)] if before else []
    pieces.append(values)
    if after:
        pieces.append(jnp.zeros((values.shape[0], after), BF16))
    return jnp.concatenate(pieces, axis=1) if len(pieces) > 1 else pieces[0]


def unit_weights(scores, spans, band_of):
    width = scores.shape[1]
    count = len(spans) * Q_ROWS
    weights = []
    for head in range(scores.shape[0] // count):
        for block, (lower, upper) in enumerate(spans):
            top = head * count + block * Q_ROWS
            expo = jnp.exp2(scores[top : top + Q_ROWS, lower:upper]).astype(BF16)
            weights.append(padded_lanes(expo * band_of(head, block), lower, width - upper))
    return jnp.concatenate(weights, axis=0)


def inner_kernel(
    window_ref,
    own_ref,
    gain_ref,
    w_query_ref,
    w_key_ref,
    w_value_ref,
    query_ref,
    norm_ref,
    mixed_ref,
    total_ref,
    key_buf,
    value_buf,
    band_buf,
):
    rows, feat_width = own_ref.shape[1:]
    heads = window_ref.shape[0]
    head_size = feat_width // heads
    group_heads = LANES // head_size
    key_count = band_buf.shape[2]
    reach = (key_count - Q_ROWS) // 2
    reach_blocks = reach // Q_ROWS
    blocks = rows // Q_ROWS

    @pl.when(pl.program_id(0) == 0)
    def _():
        for head in range(heads):
            band_buf[head] = factor(in_band(window_ref[head], 0, key_count, reach))
        value_buf[...] = jnp.ones(value_buf.shape, BF16)

    batch = own_ref.shape[0]
    own = own_ref[...].reshape(batch * rows, feat_width).astype(F32)
    normed = rms_scaled(own, gain_ref[...]).astype(BF16)
    query_rows = dot(normed, w_query_ref[...]) * query_scale(head_size)
    key_rows = dot(normed, w_key_ref[...])
    value_rows = dot(normed, w_value_ref[...]).astype(BF16)
    query_norms, key_norms = norm_bounds(query_rows, heads), norm_bounds(key_rows, heads)
    blank = jnp.zeros((norm_ref.shape[1] - 2, LANES), F32)
    for member in range(batch):
        here = slice(member * rows, (member + 1) * rows)
        query_ref[member] = query_rows[here].astype(BF16)
        key_buf[member] = key_rows[here].astype(BF16).T
        put_values(value_buf.at[member], 0, value_rows[here])
        norm_ref[member] = jnp.concatenate([query_norms, key_norms, blank], axis=0)

    @pl.when(is_safe(query_norms, key_norms))
    def _():
        pairs = range(0, blocks, 2)
        groups = range(heads // group_heads)
        units = [(member, first, group) for member in range(batch) for first in pairs for group in groups]

        def scores_of(member, first, group):
            queries = query_ref[member, first * Q_ROWS : (first + 2) * Q_ROWS, group_lanes(group)]
            return dot(stacked_heads(queries, head_size), key_buf[member, group_lanes(group), :])

        scores = scores_of(*units[0])
        for at, (member, first, group) in enumerate(units):
            following = scores_of(*units[at + 1]) if at + 1 < len(units) else None
            ranges = [(max(0, b - reach_blocks), min(blocks, b + reach_blocks + 1)) for b in (first, first + 1)]
            spans = [(lower * Q_ROWS, upper * Q_ROWS) for lower, upper in ranges]

            def band_of(head, block):
                shift = (reach_blocks - first - block) * Q_ROWS
                lower, upper = spans[block]
                return band_buf[group * group_heads + head, :, lower + shift : upper + shift]

            values = value_buf[member, :, 2 * group * LANES : 2 * (group + 1) * LANES]
            mixed, totals = weighted_sums(unit_weights(scores, spans, band_of), values, head_size)
            here = slice(first * Q_ROWS, (first + 2) * Q_ROWS)
            mixed_ref[member, here, group_lanes(group)] = mixed
            total_ref[member, here, group_lanes(group)] = totals
            scores = following


def batch_of(members):
    return BATCH if members % BATCH == 0 else 1


def inner(head_window, own, gain, w_query, w_key, w_value, reach):
    members, rows, feat_width = own.shape
    heads = head_window.shape[0]
    key_count = Q_ROWS + 2 * reach
    shapes = [(own.shape, BF16), ((members, 8, LANES), F32), (own.shape, F32), (own.shape, F32)]

    batch = batch_of(members)

    def spec(shape):
        return pl.BlockSpec((batch, *shape[1:]), lambda m: (m, 0, 0))

    return pl.pallas_call(
        inner_kernel,
        grid=(members // batch,),
        out_shape=[jax.ShapeDtypeStruct(*v) for v in shapes],
        in_specs=[smem_spec(), spec(own.shape)] + [vmem_spec()] * 4,
        out_specs=[spec(shape) for shape, _ in shapes],
        scratch_shapes=[
            pltpu.VMEM((batch, feat_width, rows), BF16),
            pltpu.VMEM((batch, rows, 2 * feat_width), BF16),
            pltpu.VMEM((heads, Q_ROWS, key_count), BF16),
        ],
        compiler_params=pltpu.CompilerParams(vmem_limit_bytes=VMEM_LIMIT),
        cost_estimate=pl.CostEstimate(
            flops=own.size * (6 * feat_width + 16 * rows), bytes_accessed=14 * own.size, transcendentals=0
        ),
        name="inner",
    )(head_window, own, gain, w_query, w_key, w_value)


def forward_kernel(
    total_len,
    tok_ref,
    mem_ref,
    window_ref,
    state_ref,
    query_ref,
    norm_ref,
    inner_mixed_ref,
    inner_total_ref,
    near_ref,
    far_ref,
    attn_gain_ref,
    ffn_gain_ref,
    w_key_ref,
    w_value_ref,
    w_out_ref,
    w_gate_ref,
    w_up_ref,
    down_weight_ref,
    *refs,
):
    out_refs, (halo_key_buf, halo_value_buf, band_buf, mixed_buf, key_buf, value_buf, forecast_buf) = (
        refs[:-7],
        refs[-7:],
    )
    rows, feat_width = state_ref.shape[1:]
    reach = near_ref.shape[1]
    heads = window_ref.shape[0]
    head_size = feat_width // heads
    group_heads = LANES // head_size
    groups = heads // group_heads
    blocks = rows // Q_ROWS
    key_count = Q_ROWS + 2 * reach
    count = 2 * Q_ROWS
    first_pos = tok_ref[0] * rows

    @pl.when(pl.program_id(0) == 0)
    def _():
        first_valid = first_pos - reach >= 0
        last_valid = first_pos + rows + reach <= total_len
        for head in range(heads):
            window = window_ref[head]
            band_buf[0, head] = factor(in_band(jnp.where(first_valid, window, -1), 0, reach, reach))
            right_window = jnp.where(last_valid, window, -1)
            band_buf[1, head] = factor(in_band(right_window, key_count - reach, key_count, reach))
        halo_value_buf[...] = jnp.ones(halo_value_buf.shape, BF16)

    def keys_of(normed):
        return dot(normed, w_key_ref[...])

    def values_of(normed):
        return dot(normed, w_value_ref[...]).astype(BF16)

    odd = tok_ref[0] % 2 == 1
    batch = state_ref.shape[0]
    halo = []
    for member in range(batch):
        near, far = near_ref[member].astype(F32), far_ref[member].astype(F32)
        halo += [jnp.where(odd, near, far), jnp.where(odd, far, near)]
    normed = rms_scaled(jnp.concatenate(halo, axis=0), attn_gain_ref[...]).astype(BF16)
    halo_keys = keys_of(normed)
    halo_values = values_of(normed)
    query_norms = jnp.max(norm_ref[:, 0, :], axis=0, keepdims=True)
    key_norms = jnp.maximum(jnp.max(norm_ref[:, 1, :], axis=0, keepdims=True), norm_bounds(halo_keys, heads))
    for at in range(2 * batch):
        here = slice(at * reach, (at + 1) * reach)
        halo_key_buf[at] = halo_keys[here].astype(BF16).T
        put_values(halo_value_buf.at[at], 0, halo_values[here])
    safe = is_safe(query_norms, key_norms)

    @pl.when(safe)
    def _():
        units = [(member, side, group) for member in range(batch) for side in range(2) for group in range(groups)]

        def scores_of(member, side, group):
            start = side * (rows - count)
            queries = query_ref[member, start : start + count, group_lanes(group)]
            return dot(stacked_heads(queries, head_size), halo_key_buf[2 * member + side, group_lanes(group), :])

        scores = scores_of(*units[0])
        for at, (member, side, group) in enumerate(units):
            following = scores_of(*units[at + 1]) if at + 1 < len(units) else None
            spans = [(0, reach), (Q_ROWS, reach)] if side == 0 else [(0, reach - Q_ROWS), (0, reach)]

            def band_of(head, block):
                lower, upper = spans[block]
                shift = -block * Q_ROWS if side == 0 else (1 - block) * Q_ROWS
                return band_buf[side, group * group_heads + head, :, lower + shift : upper + shift]

            values = halo_value_buf[2 * member + side, :, 2 * group * LANES : 2 * (group + 1) * LANES]
            mixed, totals = weighted_sums(unit_weights(scores, spans, band_of), values, head_size)
            start = side * (rows - count)
            here = slice(start, start + count)
            mixed = mixed + inner_mixed_ref[member, here, group_lanes(group)]
            totals = totals + inner_total_ref[member, here, group_lanes(group)]
            start += member * rows
            mixed_buf[start : start + count, group_lanes(group)] = (mixed / totals).astype(BF16)
            scores = following

    @pl.when(jnp.logical_not(safe))
    def _():
        for member in range(batch):
            normed = rms_scaled(state_ref[member].astype(F32), attn_gain_ref[...]).astype(BF16)
            key_buf[:, :reach] = halo_key_buf[2 * member]
            key_buf[:, reach : reach + rows] = keys_of(normed).astype(BF16).T
            key_buf[:, reach + rows :] = halo_key_buf[2 * member + 1]
            value_buf[...] = jnp.ones(value_buf.shape, BF16)
            put_values(value_buf, reach, values_of(normed))
            value_buf[:reach] = halo_value_buf[2 * member]
            value_buf[reach + rows :] = halo_value_buf[2 * member + 1]
            for block in range(blocks):
                start = block * Q_ROWS
                k_pos = first_pos - reach + start + iota((Q_ROWS, key_count), 1)
                inside = (k_pos >= 0) & (k_pos < total_len)
                for group in range(groups):
                    queries = query_ref[member, start : start + Q_ROWS, group_lanes(group)]
                    keys = key_buf[group_lanes(group), start : start + key_count]
                    scores = dot(stacked_heads(queries, head_size), keys)
                    weights = []
                    for head in range(group_heads):
                        allowed = inside & in_band(window_ref[group * group_heads + head], 0, key_count, reach)
                        score_matrix = jnp.where(allowed, scores[head * Q_ROWS : (head + 1) * Q_ROWS], -1e30)
                        row_top = jnp.max(score_matrix, axis=-1, keepdims=True)
                        weights.append(jnp.exp2(score_matrix - row_top).astype(BF16))
                    values = value_buf[start : start + key_count, 2 * group * LANES : 2 * (group + 1) * LANES]
                    mixed, totals = weighted_sums(jnp.concatenate(weights, axis=0), values, head_size)
                    here = slice(member * rows + start, member * rows + start + Q_ROWS)
                    mixed_buf[here, group_lanes(group)] = (mixed / totals).astype(BF16)

    state = state_ref[...].reshape(batch * rows, feat_width).astype(F32)
    after = (state + dot(mixed_buf[...], w_out_ref[...])).astype(BF16)
    normed_mid = rms_scaled(after.astype(F32), ffn_gain_ref[...]).astype(BF16)
    forecast = after.astype(F32)
    chunks = [slice(lower, lower + HIDDEN_CHUNK) for lower in range(0, w_gate_ref.shape[1], HIDDEN_CHUNK)]

    def gate_and_up(part):
        return dot(normed_mid, w_gate_ref[:, part]), dot(normed_mid, w_up_ref[:, part])

    gate, up = gate_and_up(chunks[0])
    for at, part in enumerate(chunks):
        following = gate_and_up(chunks[at + 1]) if at + 1 < len(chunks) else (None, None)
        gate = 0.5 * gate
        hidden = (gate * (1.0 + jnp.tanh(gate.astype(BF16)).astype(F32)) * up).astype(BF16)
        forecast += dot(hidden, down_weight_ref[part, :])
        gate, up = following
    forecast_buf[...] = forecast.astype(BF16)
    share_rows = out_refs[0].shape[1]
    for part, out_ref in enumerate(out_refs):
        lower = pl.multiple_of((mem_ref[0] ^ part) * share_rows, share_rows)
        for member in range(batch):
            out_ref[member] = forecast_buf[pl.ds(member * rows + lower, share_rows), :]


def forward(total_len, tok_index, mem_index, head_window, own, inner_parts, near, far, gains, weights, shares):
    members, row_count, feat_width = own.shape
    reach = near.shape[1]
    heads = head_window.shape[0]
    hidden_width = weights[3].shape[1]
    macs = members * row_count * feat_width * (3 * feat_width + 3 * hidden_width + 4 * reach)
    batch = batch_of(members)
    share_rows = row_count // shares

    def spec(array):
        return pl.BlockSpec((batch, *array.shape[1:]), lambda m: (m, 0, 0))

    return pl.pallas_call(
        functools.partial(forward_kernel, total_len),
        grid=(members // batch,),
        out_shape=[jax.ShapeDtypeStruct((members, share_rows, feat_width), BF16)] * shares,
        in_specs=[smem_spec()] * 3
        + [spec(v) for v in (own, *inner_parts, near, far)]
        + [vmem_spec()] * (len(gains) + len(weights)),
        out_specs=[pl.BlockSpec((batch, share_rows, feat_width), lambda m: (m, 0, 0))] * shares,
        scratch_shapes=[
            pltpu.VMEM((2 * batch, feat_width, reach), BF16),
            pltpu.VMEM((2 * batch, reach, 2 * feat_width), BF16),
            pltpu.VMEM((2, heads, Q_ROWS, reach), BF16),
            pltpu.VMEM((batch * row_count, feat_width), BF16),
            pltpu.VMEM((feat_width, row_count + 2 * reach), BF16),
            pltpu.VMEM((row_count + 2 * reach, 2 * feat_width), BF16),
            pltpu.VMEM((batch * row_count, feat_width), BF16),
        ],
        compiler_params=pltpu.CompilerParams(vmem_limit_bytes=VMEM_LIMIT),
        cost_estimate=pl.CostEstimate(flops=2 * macs, bytes_accessed=10 * own.size, transcendentals=0),
        name="forward",
    )(tok_index, mem_index, head_window, own, *inner_parts, near, far, *gains, *weights)


def global_member(held, index, own_members):
    return ((held // own_members) ^ index) * own_members + held % own_members


def gram_kernel(index_ref, *refs):
    share_refs, grid_ref, out_ref = refs[:-2], refs[-2], refs[-1]
    own_members, rows, feat_width = share_refs[0].shape
    members = own_members * len(share_refs)
    index = index_ref[0]
    stack = members * GROUP
    total = jnp.zeros((stack, stack), F32)
    crossed = jnp.zeros((stack, stack), F32)
    proj = jnp.zeros((members, GROUP, feat_width), F32)
    for lower in range(0, rows, GROUP):
        part = slice(lower, lower + GROUP)
        fields = jnp.concatenate([ref[:, part, :] for ref in share_refs], axis=0).astype(F32)
        mean = jnp.sum(fields, axis=0) * (1.0 / members)
        spread = fields - mean[None]
        weight = grid_ref[0, part, :]
        proj += spread * (grid_ref[1, part, :] - weight * mean)[None]
        scaled = spread * jnp.sqrt(jnp.maximum(weight, 0.0))[None]
        high, low = halves(scaled.reshape(stack, feat_width))
        total += dot(high, high, ((1,), (1,)))
        crossed += dot(high, low, ((1,), (1,)))
    total += crossed + crossed.T
    same = iota((stack, stack), 0) % GROUP == iota((stack, stack), 1) % GROUP
    by_row = jnp.sum(jnp.where(same, total, 0.0).reshape(members, GROUP, stack), axis=1)
    column = global_member(iota((stack, LANES), 0) // GROUP, index, own_members)
    folded = (column == iota((stack, LANES), 1) % members).astype(F32)
    held = global_member(iota((members, members), 1), index, own_members)
    in_order = (held == iota((members, members), 0)).astype(F32)
    tiled = exact_dot(in_order, exact_dot(by_row, folded))
    per_row = LANES // members
    keep = iota((members, LANES), 0) % per_row == iota((members, LANES), 1) // members
    packed = jnp.sum(jnp.where(keep, tiled, 0.0).reshape(members // per_row, per_row, LANES), axis=1)
    proj_col = jnp.sum(jnp.sum(proj, axis=1), axis=1, keepdims=True)
    at_lane = global_member(iota((members, LANES), 0), index, own_members) == iota((members, LANES), 1)
    proj_row = jnp.sum(jnp.where(at_lane, proj_col, 0.0), axis=0, keepdims=True)
    filled = members // per_row + 1
    blank = jnp.zeros((out_ref.shape[0] - filled, LANES), F32)
    out_ref[...] = jnp.concatenate([packed, proj_row, blank], axis=0)


def gram_partial(index, shares, grid):
    members = shares[0].shape[0] * len(shares)
    filled = members * members // LANES + 1
    return pl.pallas_call(
        gram_kernel,
        out_shape=jax.ShapeDtypeStruct((-(-filled // 8) * 8, LANES), F32),
        in_specs=[smem_spec()] + [vmem_spec()] * (len(shares) + 1),
        out_specs=vmem_spec(),
        compiler_params=pltpu.CompilerParams(vmem_limit_bytes=VMEM_LIMIT),
        cost_estimate=pl.CostEstimate(
            flops=3 * GROUP * members * members * grid.size, bytes_accessed=members * grid.size, transcendentals=0
        ),
        name="gram",
    )(index, *shares, grid)


def repeated_dot(a, b):
    size = a.shape[0]

    def pieces(values):
        first = values.astype(BF16).astype(F32)
        rest = values - first
        second = rest.astype(BF16).astype(F32)
        return first, second, rest - second

    block = iota(a.shape, 1) // size
    a_first, a_second, a_third = pieces(a)
    b_first, b_second, b_third = (piece.astype(BF16) for piece in pieces(b))
    left = jnp.where((block == 2) | (block == 4), a_second, jnp.where(block == 5, a_third, a_first))
    right = jnp.concatenate([b_first, b_second, b_first, b_third, b_second, b_first], axis=0)
    return dot(left.astype(BF16), right)


def ensemble_transform(gram, proj):
    members = gram.shape[0]
    row, column = iota((members, members), 0), iota((members, members), 1)
    identity = (row == column).astype(F32)
    system = gram + (members - 1.0) * identity
    left, right = system, proj
    for pivot in range(members):
        is_pivot = iota((members, 1), 0) == pivot
        scale = 1.0 / left[pivot : pivot + 1, pivot : pivot + 1]
        pivot_row = left[pivot : pivot + 1, :] * scale
        pivot_right = right[pivot : pivot + 1, :] * scale
        factor = left[:, pivot : pivot + 1]
        left = jnp.where(is_pivot, pivot_row, left - factor * pivot_row)
        right = jnp.where(is_pivot, pivot_right, right - factor * pivot_right)
    mean_weights = right
    mean_level = jnp.sum(jnp.sum(system * identity, axis=1, keepdims=True), axis=0, keepdims=True) / members
    lifted = system + (mean_level - (members - 1.0)) * (1.0 / members)
    frobenius = jnp.sqrt(jnp.sum(jnp.sum(lifted * lifted, axis=1, keepdims=True), axis=0, keepdims=True))
    root_iter = jnp.concatenate([lifted / frobenius] * PASSES, axis=1)
    repeated = iota((members, PASSES * members), 1) % members == iota((members, PASSES * members), 0)
    repeated = repeated.astype(F32)
    inv_iter = repeated
    for sweep in range(NS_STEPS):
        product = root_iter if sweep == 0 else repeated_dot(inv_iter, root_iter)
        correction = 1.5 * repeated - 0.5 * product
        inv_iter = correction if sweep == 0 else repeated_dot(correction, inv_iter)
        if sweep < NS_STEPS - 1:
            root_iter = repeated_dot(root_iter, correction)
    inv_iter = inv_iter[:, :members]
    inv_root = inv_iter / jnp.sqrt(frobenius) + (1.0 / math.sqrt(members - 1.0) - 1.0 / jnp.sqrt(mean_level)) * (
        1.0 / members
    )
    moved = mean_weights + math.sqrt(members - 1.0) * inv_root
    return 1.0 / members + moved - jnp.sum(moved, axis=0, keepdims=True) * (1.0 / members)


def combine_kernel(index_ref, partial_ref, *refs):
    share_refs, out_refs = refs[: len(refs) // 2], refs[len(refs) // 2 :]
    own_members, rows, feat_width = share_refs[0].shape
    members = own_members * len(share_refs)
    stack = members * GROUP
    per_row = LANES // members
    sums = jnp.sum(partial_ref[...], axis=0)
    spread_rows = jnp.concatenate(
        [jnp.broadcast_to(sums[r : r + 1], (per_row, LANES)) for r in range(members // per_row)], axis=0
    )
    keep = iota((members, LANES), 0) % per_row == iota((members, LANES), 1) // members
    folded = (iota((LANES, members), 0) % members == iota((LANES, members), 1)).astype(F32)
    gram = exact_dot(jnp.where(keep, spread_rows, 0.0), folded)
    proj_row = jnp.broadcast_to(sums[members // per_row : members // per_row + 1], (members, LANES))
    on_diagonal = iota((members, LANES), 0) == iota((members, LANES), 1)
    proj = jnp.sum(jnp.where(on_diagonal, proj_row, 0.0), axis=1, keepdims=True)
    transform = ensemble_transform(gram, proj)
    held = global_member(iota((stack, members), 0) // GROUP, index_ref[0], own_members)
    pick = (held == iota((stack, members), 1)).astype(F32).astype(BF16)
    same = iota((stack, stack), 0) % GROUP == iota((stack, stack), 1) % GROUP
    mixers = []
    for piece in halves(transform):
        rows_of = dot(pick, piece, ((1,), (1,))).astype(BF16)
        mixers.append(jnp.where(same, dot(rows_of, pick, ((1,), (1,))), 0.0).astype(BF16))
    for lower in range(0, rows, GROUP):
        part = slice(lower, lower + GROUP)
        fields = jnp.concatenate([ref[:, part, :].reshape(-1, feat_width) for ref in share_refs], axis=0)
        mixed = (dot(mixers[0], fields) + dot(mixers[1], fields)).astype(BF16)
        own_stack = own_members * GROUP
        for at, out_ref in enumerate(out_refs):
            piece = mixed[at * own_stack : (at + 1) * own_stack]
            out_ref[:, part, :] = piece.reshape(own_members, GROUP, feat_width)


def combine(index, partials, shares):
    size = shares[0].size * len(shares)
    members = shares[0].shape[0] * len(shares)
    return pl.pallas_call(
        combine_kernel,
        out_shape=[jax.ShapeDtypeStruct(v.shape, BF16) for v in shares],
        in_specs=[smem_spec()] + [vmem_spec()] * (1 + len(shares)),
        out_specs=[vmem_spec()] * len(shares),
        compiler_params=pltpu.CompilerParams(vmem_limit_bytes=VMEM_LIMIT),
        cost_estimate=pl.CostEstimate(flops=4 * GROUP * members * size, bytes_accessed=4 * size, transcendentals=0),
        name="combine",
    )(index, partials, *shares)


def assemble_kernel(index_ref, *refs):
    part_refs, out_ref, sems = refs[:-2], refs[-2], refs[-1]
    rows = part_refs[0].shape[1]
    copies = []
    for part, ref in enumerate(part_refs):
        lower = pl.multiple_of((index_ref[0] ^ part) * rows, rows)
        copies.append(pltpu.make_async_copy(ref, out_ref.at[:, pl.ds(lower, rows), :], sems.at[part]))
    for copy in copies:
        copy.start()
    for copy in copies:
        copy.wait()


def assemble(index, parts):
    members, rows, feat_width = parts[0].shape
    return pl.pallas_call(
        assemble_kernel,
        out_shape=jax.ShapeDtypeStruct((members, len(parts) * rows, feat_width), BF16),
        in_specs=[smem_spec()] + [vmem_spec()] * len(parts),
        out_specs=pl.BlockSpec(memory_space=pl.ANY),
        scratch_shapes=[pltpu.SemaphoreType.DMA((len(parts),))],
        compiler_params=pltpu.CompilerParams(vmem_limit_bytes=VMEM_LIMIT),
        cost_estimate=pl.CostEstimate(flops=0, bytes_accessed=4 * len(parts) * parts[0].size, transcendentals=0),
        name="assemble",
    )(index, *parts)


def exchanged(parts):
    count = lax.axis_size("mem")
    return [
        lax.ppermute(v, "mem", [(i, i ^ part) for i in range(count)]) if part else v for part, v in enumerate(parts)
    ]


def halos(own, reach):
    count = lax.axis_size("tok")
    odd = lax.axis_index("tok") % 2
    last = own.shape[1] - reach
    near = lax.dynamic_slice_in_dim(own, (1 - odd) * last, reach, axis=1)
    far = lax.dynamic_slice_in_dim(own, odd * last, reach, axis=1)
    near_pairs = [(i, i ^ 1) for i in range(count)]
    far_pairs = [pair for i in range(1, count - 1, 2) for pair in ((i, i + 1), (i + 1, i))]
    far_halo = lax.ppermute(far, "tok", far_pairs)
    return lax.ppermute(near, "tok", near_pairs), far_halo


def local(
    ens_state,
    attn_gain,
    ffn_gain,
    w_query,
    w_key,
    w_value,
    w_out,
    w_gate,
    w_up,
    down_weight,
    head_window,
    obs_token,
    obs_channel,
    obs_value,
    obs_var,
):
    own_members, row_count, feat_width = ens_state.shape
    mem_count = lax.axis_size("mem")
    tok_count = lax.axis_size("tok")
    device_count = mem_count * tok_count
    share_rows = row_count // mem_count
    first_pos = lax.axis_index("tok") * row_count
    near_halo, far_halo = halos(ens_state, WIN)
    share_start = first_pos + lax.axis_index("mem") * share_rows
    grid = sample_grid(
        share_start.astype(jnp.int32).reshape(1), obs_token, obs_channel, obs_value, obs_var, share_rows, feat_width
    )
    mem_index = lax.axis_index("mem").astype(jnp.int32).reshape(1)
    tok_index = lax.axis_index("tok").astype(jnp.int32).reshape(1)
    gains = [attn_gain.reshape(1, -1), ffn_gain.reshape(1, -1)]
    inner_parts = inner(head_window, ens_state, gains[0], w_query, w_key, w_value, WIN)
    weights = [w_key, w_value, w_out, w_gate, w_up, down_weight]
    total_len = row_count * tok_count
    forecast = forward(
        total_len, tok_index, mem_index, head_window, ens_state, inner_parts, near_halo, far_halo, gains, weights, mem_count
    )
    shares = exchanged(forecast)
    partial = gram_partial(mem_index, shares, grid)
    partials = lax.all_to_all(
        jnp.broadcast_to(partial[None], (device_count, *partial.shape)),
        ("mem", "tok"),
        split_axis=0,
        concat_axis=0,
        tiled=True,
    )
    return assemble(mem_index, exchanged(combine(mem_index, partials, shares)))


def solution(mesh):
    in_specs = (P("mem", "tok", None), *[P()] * 10, *[P("tok")] * 4)
    return jax.shard_map(local, mesh=mesh, in_specs=in_specs, out_specs=P("mem", "tok", None), check_vma=False)
```
